32 devices in a mesh: dp: 16 (over z, x, core), tp: 2 (over y).
Axes of the slice: x: 2, y: 2, z: 4, core: 2. Of those that a mesh axis runs over, the one named last changes fastest.
Arguments:
- tokens: float32 [16384, 1024], P(('dp', 'tp')), may hold values from -6 to 6
- v_first: bfloat16 [16384, 1024], P('dp', 'tp'), may hold values from -6 to 6
- w_query: bfloat16 [1024, 1024], P(None, 'tp'), may hold values from -0.1875 to 0.1875
- w_key: bfloat16 [1024, 1024], P(None, 'tp'), may hold values from -0.1875 to 0.1875
- w_value: bfloat16 [1024, 1024], P(None, 'tp'), may hold values from -0.1875 to 0.1875
- w_out: bfloat16 [1024, 1024], P('tp'), may hold values from -3 to 3
- w_gate: bfloat16 [1024, 2816], P(None, 'tp'), may hold values from -0.1875 to 0.1875
- w_up: bfloat16 [1024, 2816], P(None, 'tp'), may hold values from -0.1875 to 0.1875
- w_down: bfloat16 [2816, 1024], P('tp'), may hold values from -0.109375 to 0.109375
- gain_attn: float32 [1024], replicated, may hold values from 0.5 to 1.5
- gain_mlp: float32 [1024], replicated, may hold values from 0.5 to 1.5
- seq_lens: int32 [16, 1], P('dp'), may hold values from 0 to 1024, as said below
- cotangent: float32 [16384, 1024], P(('dp', 'tp')), may hold values from -6 to 6
Outputs:
- layer_out: float32 [16384, 1024], P(('dp', 'tp'))
- grad_tokens: float32 [16384, 1024], P(('dp', 'tp'))
- grad_first: float32 [16384, 1024], P('dp', 'tp')
- grad_query: float32 [1024, 1024], P(None, 'tp')
- grad_key: float32 [1024, 1024], P(None, 'tp')
- grad_value: float32 [1024, 1024], P(None, 'tp')
- grad_output: float32 [1024, 1024], P('tp')
- grad_gate: float32 [1024, 2816], P(None, 'tp')
- grad_up: float32 [1024, 2816], P(None, 'tp')
- grad_down: float32 [2816, 1024], P('tp')
- grad_gain_attn: float32 [1024], replicated
- grad_gain_mlp: float32 [1024], replicated
The draws below stay inside these ranges and needn't reach their ends.
Inputs may be any that keep to these rules, and one draw needn't show every extreme that they name: `seq_lens`: in each data group the nonzero lengths are 1024, 2048 or 4096 and all lengths sum to 1024; some group holds a sequence of the largest length.
All inputs are finite; a program needn't handle non-finite values.
Results may differ from the reference program's by a relative error of at most 0.02.
Values may be sent and summed in bfloat16 or wider, within the bound.
A program may use at most 192 MiB of HBM per device.

```python
import jax
import jax.numpy as jnp
from jax import lax

HDIM = 64
D = 1024
FF = 2816
TOK_DEV = 512
MINLEN = 1024
SEQS = 1
GROUPS = 16
TOKENS = 16384
N_DP = 16
N_TP = 2


def draw_seq_lens(key, part):
    key = jax.random.fold_in(key, 7)
    chosen = jax.random.randint(jax.random.fold_in(key, 1), (), 0, GROUPS)
    group_ids = jnp.arange(GROUPS, dtype=jnp.int32)
    remaining = jnp.full((GROUPS,), SEQS, jnp.int32)
    columns = []
    for slot_index in range(SEQS):
        largest = jnp.where(remaining >= 4, 4, jnp.where(remaining >= 2, 2, jnp.where(remaining >= 1, 1, 0)))
        draw_index = jax.random.randint(jax.random.fold_in(key, slot_index + 2), (GROUPS,), 0, 3)
        length_units = jnp.where(draw_index == 0, 1, jnp.where(draw_index == 1, 2, 4))
        if slot_index == 0:
            length_units = jnp.where(group_ids == chosen, largest, length_units)
        length_units = jnp.minimum(length_units, largest)
        remaining = remaining - length_units
        columns.append(length_units * MINLEN)
    return jnp.stack(columns, axis=1).astype(jnp.int32)


def shard_levels(own_key, dims, shards, low, top_value):
    level = 1.0
    for dim, blocks in shards:
        draws = jax.random.uniform(jax.random.fold_in(jax.random.fold_in(own_key, 6), dim), (blocks,), jnp.float32, low / len(shards), top_value / len(shards))
        level = level * jnp.repeat(jnp.exp(draws), dims[dim] // blocks).reshape((-1,) + (1,) * (len(dims) - 1 - dim))
    return level


def normal_values(own_key, shape, deviation, bound, cuts=(), kind=jnp.bfloat16):
    result = deviation * jax.random.normal(own_key, shape, jnp.float32)
    if cuts:
        result = result * shard_levels(own_key, shape, cuts, -0.22, 0.18)
    return jnp.clip(result, -bound, bound).astype(kind)


def setup_inputs(seed: int = 0) -> dict:
    splits = jax.random.split(jax.random.key(seed), 14)
    return {
        "tokens": normal_values(splits[0], (TOKENS, D), 1.0, 6.0, ((0, 32),), jnp.float32),
        "v_first": normal_values(splits[1], (TOKENS, D), 1.0, 6.0, ((0, 16), (1, 2))),
        "w_query": normal_values(splits[2], (D, D), D ** -0.5, 0.1875, ((1, 2),)),
        "w_key": normal_values(splits[3], (D, D), D ** -0.5, 0.1875, ((1, 2),)),
        "w_value": normal_values(splits[4], (D, D), D ** -0.5, 0.1875, ((1, 2),)),
        "w_out": normal_values(splits[5], (D, D), (max(D // 256, 1)) ** -0.5, 3.0, ((0, 2),)),
        "w_gate": normal_values(splits[6], (D, FF), D ** -0.5, 0.1875, ((1, 2),)),
        "w_up": normal_values(splits[7], (D, FF), D ** -0.5, 0.1875, ((1, 2),)),
        "w_down": normal_values(splits[8], (FF, D), FF ** -0.5, 0.109375, ((0, 2),)),
        "gain_attn": jnp.clip(1.0 + 0.1 * jax.random.normal(splits[9], (D,), jnp.float32), 0.5, 1.5),
        "gain_mlp": jnp.clip(1.0 + 0.1 * jax.random.normal(splits[10], (D,), jnp.float32), 0.5, 1.5),
        "seq_lens": draw_seq_lens(jax.random.fold_in(splits[13], 71), 0),
        "cotangent": normal_values(splits[12], (TOKENS, D), 1.0, 6.0, ((0, 32),), jnp.float32),
    }


EPS = 1e-06
HIGHEST = lax.Precision.HIGHEST

@jax.custom_vjp
def low(v):
    return lax.optimization_barrier(v.astype(jnp.bfloat16)).astype(jnp.float32)

@jax.custom_vjp
def low_back(v):
    return v

def low_keep(v):
    return (low(v), None)

def low_pass(kept, grad):
    return (grad,)

def back_keep(v):
    return (v, None)

def back_low(kept, grad):
    return (low(grad),)
low.defvjp(low_keep, low_pass)
low_back.defvjp(back_keep, back_low)

def layout(seq_row, row_share, tp_count):
    group_rows = row_share * tp_count
    row_ids = jnp.arange(group_rows, dtype=jnp.int32)
    device = row_ids // row_share
    local_row = row_ids % row_share
    pieces = (seq_row // (2 * tp_count)).astype(jnp.int32)
    slot_ends = jnp.cumsum(2 * pieces).astype(jnp.int32)
    starts = slot_ends - 2 * pieces
    offset = local_row[:, None] - starts[None, :]
    inside = (offset >= 0) & (offset < 2 * pieces[None, :])
    first_half = offset < pieces[None, :]
    mirror = 2 * tp_count - 1 - device[:, None]
    position = jnp.where(first_half, device[:, None] * pieces[None, :] + offset, mirror * pieces[None, :] + offset - pieces[None, :])
    slot_ids = jnp.arange(seq_row.shape[0], dtype=jnp.int32)
    doc_ids = lax.optimization_barrier(jnp.sum(jnp.where(inside, slot_ids[None, :], 0), axis=1)).astype(jnp.int32)
    positions = lax.optimization_barrier(jnp.sum(jnp.where(inside, position, 0), axis=1)).astype(jnp.int32)
    return (doc_ids, positions)

def rotate(values, positions, head_dim, turn_sign):
    row_count, width_all = values.shape
    half_dim = head_dim // 2
    shaped = values.reshape(row_count, width_all // head_dim, head_dim)
    freqs = 10000.0 ** (-jnp.arange(half_dim, dtype=jnp.float32) / half_dim)
    angles = positions.astype(jnp.float32)[:, None] * freqs[None, :]
    cosine = jnp.cos(angles)[:, None, :]
    sine = turn_sign * jnp.sin(angles)[:, None, :]
    front = shaped[..., :half_dim]
    behind = shaped[..., half_dim:]
    turned = jnp.concatenate([front * cosine - behind * sine, behind * cosine + front * sine], axis=-1)
    return turned.reshape(row_count, width_all)

def normalize(values, gain):
    return values * lax.rsqrt(lax.optimization_barrier(jnp.mean(values * values, axis=-1, keepdims=True)) + EPS) * gain

def matmul(left, right):
    return jnp.dot(left, right, precision=HIGHEST, preferred_element_type=jnp.float32)

def attend(query, keys, values, doc_ids, positions, head_dim):
    group_rows, width_local = query.shape
    head_count = width_local // head_dim
    block_rows = min(512, group_rows)
    block_count = group_rows // block_rows
    score_scale = head_dim ** (-0.5)
    key_heads = keys.reshape(group_rows, head_count, head_dim)
    value_heads = values.reshape(group_rows, head_count, head_dim)

    def one_block(block_index):
        first_row = block_index * block_rows
        query_rows = lax.dynamic_slice_in_dim(query, first_row, block_rows, 0).reshape(block_rows, head_count, head_dim)
        row_doc = lax.dynamic_slice_in_dim(doc_ids, first_row, block_rows, 0)
        row_pos = lax.dynamic_slice_in_dim(positions, first_row, block_rows, 0)
        scores = low_back(jnp.einsum('qhd,khd->hqk', query_rows, key_heads, precision=HIGHEST) * score_scale)
        allowed = (row_doc[:, None] == doc_ids[None, :]) & (positions[None, :] <= row_pos[:, None])
        scores = jnp.where(allowed[None], scores, -1e+30)
        row_max = lax.optimization_barrier(jnp.max(scores, axis=-1, keepdims=True))
        exponent = jnp.exp(scores - row_max)
        weights = low(exponent / lax.optimization_barrier(jnp.sum(exponent, axis=-1, keepdims=True)))
        mixture = jnp.einsum('hqk,khd->qhd', weights, value_heads, precision=HIGHEST)
        return mixture.reshape(block_rows, width_local)
    mixture = lax.map(jax.checkpoint(one_block), jnp.arange(block_count, dtype=jnp.int32))
    return mixture.reshape(group_rows, width_local)

def block_forward(residual, first_values, weights, doc_ids, positions):
    query_weight, key_weight, value_weight, out_weight, gate_weight, up_weight, down_weight, attn_gain, mlp_gain = weights
    normed = low(normalize(residual, attn_gain))
    query = low(low_back(rotate(low_back(matmul(normed, query_weight)), positions, HDIM, 1.0)))
    keys = low(low_back(rotate(low_back(matmul(normed, key_weight)), positions, HDIM, 1.0)))
    values = low_back(matmul(normed, value_weight))
    mixed_values = low(low_back(0.5 * values + 0.5 * first_values))
    attended = low(low_back(attend(query, keys, mixed_values, doc_ids, positions, HDIM)))
    middle = residual + low_back(matmul(attended, out_weight))
    mlp_in = low(normalize(middle, mlp_gain))
    gate = low_back(matmul(mlp_in, gate_weight))
    up_values = low_back(matmul(mlp_in, up_weight))
    hidden = low(jax.nn.silu(gate) * up_values)
    return middle + low_back(matmul(hidden, down_weight))

def reference(tokens, v_first, w_query, w_key, w_value, w_out, w_gate, w_up, w_down, gain_attn, gain_mlp, seq_lens, cotangent):
    group_rows = TOK_DEV * N_TP
    weights = tuple((weight.astype(jnp.float32) for weight in (w_query, w_key, w_value, w_out, w_gate, w_up, w_down))) + (gain_attn.astype(jnp.float32), gain_mlp.astype(jnp.float32))

    def group_step(totals, inputs):
        residual, first_values, cot_rows, seq_row = inputs
        doc_ids, positions = layout(seq_row, TOK_DEV, N_TP)

        def apply_block(residual, first_values, weights):
            return block_forward(residual, first_values, weights, doc_ids, positions)
        output, pullback = jax.vjp(apply_block, residual, first_values, weights)
        grad_rows, grad_values, grad_weights = pullback(cot_rows)
        totals = jax.tree.map(jnp.add, totals, grad_weights)
        return (totals, (output, grad_rows, grad_values))
    zero_grads = jax.tree.map(jnp.zeros_like, weights)
    stacked = (tokens.astype(jnp.float32).reshape(N_DP, group_rows, D), v_first.astype(jnp.float32).reshape(N_DP, group_rows, D), cotangent.astype(jnp.float32).reshape(N_DP, group_rows, D), seq_lens)
    totals, (outputs, grad_rows, grad_values) = lax.scan(group_step, zero_grads, stacked)
    return (outputs.reshape(N_DP * group_rows, D), grad_rows.reshape(N_DP * group_rows, D), grad_values.reshape(N_DP * group_rows, D), totals[0], totals[1], totals[2], totals[3], totals[4], totals[5], totals[6], totals[7], totals[8])
```

```python
import functools

import jax
import jax.numpy as jnp
import numpy as np
from jax import lax
from jax.experimental import pallas as pl
from jax.experimental.pallas import tpu as pltpu
from jax.sharding import PartitionSpec as P

HDIM = 64


EPS = 1e-06


def layout(seq_row, row_share, tp_count):
    group_rows = row_share * tp_count
    row_ids = jnp.arange(group_rows, dtype=jnp.int32)
    device = row_ids // row_share
    local_row = row_ids % row_share
    pieces = seq_row // (2 * tp_count)
    slot_ends = jnp.cumsum(2 * pieces)
    starts = slot_ends - 2 * pieces
    offset = local_row[:, None] - starts[None, :]
    inside = (offset >= 0) & (offset < 2 * pieces[None, :])
    first_half = offset < pieces[None, :]
    mirror = 2 * tp_count - 1 - device[:, None]
    position = jnp.where(
        first_half,
        device[:, None] * pieces[None, :] + offset,
        mirror * pieces[None, :] + offset - pieces[None, :],
    )
    slot_ids = jnp.arange(seq_row.shape[0], dtype=jnp.int32)
    doc_ids = jnp.sum(jnp.where(inside, slot_ids[None, :], 0), axis=1)
    positions = jnp.sum(jnp.where(inside, position, 0), axis=1)
    return (doc_ids, positions)


def rotate(values, positions, head_dim, turn_sign):
    row_count, width_all = values.shape
    half_dim = head_dim // 2
    shaped = values.reshape(row_count, width_all // head_dim, head_dim)
    freqs = 10000.0 ** (-jnp.arange(half_dim, dtype=jnp.float32) / half_dim)
    angles = positions.astype(jnp.float32)[:, None] * freqs[None, :]
    cosine = jnp.cos(angles)[:, None, :]
    sine = turn_sign * jnp.sin(angles)[:, None, :]
    front = shaped[..., :half_dim]
    behind = shaped[..., half_dim:]
    turned = jnp.concatenate(
        [front * cosine - behind * sine, behind * cosine + front * sine], axis=-1
    )
    return turned.reshape(row_count, width_all)


def normalize(values, gain):
    return values * lax.rsqrt(jnp.mean(values * values, axis=-1, keepdims=True) + EPS) * gain


def normalize_back(values, gain, grad_in):
    factor = lax.rsqrt(jnp.mean(values * values, axis=-1, keepdims=True) + EPS)
    normed = values * factor
    grad_normed = grad_in * gain
    grad_values = factor * (
        grad_normed - normed * jnp.mean(grad_normed * normed, axis=-1, keepdims=True)
    )
    return (grad_values, jnp.sum(grad_in * normed, axis=0))


def inner_rows(left, right):
    return lax.dot_general(
        left, right, (((0,), (0,)), ((), ())), preferred_element_type=jnp.float32
    )


def outer_cols(left, right):
    return lax.dot_general(
        left, right, (((1,), (1,)), ((), ())), preferred_element_type=jnp.float32
    )


def swiglu_back(gate, up_values, grad_hidden):
    sigma = jax.nn.sigmoid(gate)
    grad_gate = grad_hidden * up_values * (sigma * (1.0 + gate * (1.0 - sigma)))
    grad_upper = grad_hidden * (gate * sigma)
    return (grad_gate.astype(jnp.bfloat16), grad_upper.astype(jnp.bfloat16))


def block_mask(doc_ids, positions, first_row, block_rows):
    row_doc = lax.dynamic_slice_in_dim(doc_ids, first_row, block_rows, 0)
    row_pos = lax.dynamic_slice_in_dim(positions, first_row, block_rows, 0)
    return (row_doc[:, None] == doc_ids[None, :]) & (positions[None, :] <= row_pos[:, None])


def attention_forward(query, keys, values, doc_ids, positions, head_dim):
    group_rows, width_local = query.shape
    head_count = width_local // head_dim
    block_rows = min(512, group_rows)
    block_count = group_rows // block_rows
    score_scale = head_dim ** (-0.5)
    key_heads = keys.reshape(group_rows, head_count, head_dim)
    value_heads = values.reshape(group_rows, head_count, head_dim)

    def forward_block(block_index):
        first_row = block_index * block_rows
        query_rows = lax.dynamic_slice_in_dim(query, first_row, block_rows, 0).reshape(
            block_rows, head_count, head_dim
        )
        scores = (
            jnp.einsum("qhd,khd->hqk", query_rows, key_heads, preferred_element_type=jnp.float32)
            * score_scale
        )
        allowed = block_mask(doc_ids, positions, first_row, block_rows)
        scores = jnp.where(allowed[None], scores, -1e30)
        row_max = jnp.max(scores, axis=-1, keepdims=True)
        exponent = jnp.exp(scores - row_max)
        row_total = jnp.sum(exponent, axis=-1, keepdims=True)
        weights = (exponent / row_total).astype(jnp.bfloat16)
        mixture = jnp.einsum(
            "hqk,khd->qhd", weights, value_heads, preferred_element_type=jnp.float32
        )
        return (
            mixture.astype(jnp.bfloat16).reshape(block_rows, width_local),
            (row_max + jnp.log(row_total))[..., 0],
        )

    mixture, row_lse = lax.map(forward_block, jnp.arange(block_count, dtype=jnp.int32))
    return (mixture.reshape(group_rows, width_local), row_lse)


def attention_backward(query, keys, values, grad_mixture, row_lse, doc_ids, positions, head_dim):
    group_rows, width_local = query.shape
    head_count = width_local // head_dim
    block_rows = min(512, group_rows)
    block_count = group_rows // block_rows
    score_scale = head_dim ** (-0.5)
    key_heads = keys.reshape(group_rows, head_count, head_dim)
    value_heads = values.reshape(group_rows, head_count, head_dim)

    def backward_block(carry, block_index):
        key_total, value_total = carry
        first_row = block_index * block_rows
        query_rows = lax.dynamic_slice_in_dim(query, first_row, block_rows, 0).reshape(
            block_rows, head_count, head_dim
        )
        grad_rows = lax.dynamic_slice_in_dim(grad_mixture, first_row, block_rows, 0).reshape(
            block_rows, head_count, head_dim
        )
        scores = (
            jnp.einsum("qhd,khd->hqk", query_rows, key_heads, preferred_element_type=jnp.float32)
            * score_scale
        )
        allowed = block_mask(doc_ids, positions, first_row, block_rows)
        scores = jnp.where(allowed[None], scores, -1e30)
        weights = jnp.exp(scores - row_lse[block_index][..., None])
        weights_low = weights.astype(jnp.bfloat16)
        grad_weights = jnp.einsum(
            "qhd,khd->hqk", grad_rows, value_heads, preferred_element_type=jnp.float32
        )
        weighted_sum = jnp.sum(weights * grad_weights, axis=-1, keepdims=True)
        score_grad = (weights * (grad_weights - weighted_sum)).astype(jnp.bfloat16)
        query_grad = (
            jnp.einsum("hqk,khd->qhd", score_grad, key_heads, preferred_element_type=jnp.float32)
            * score_scale
        )
        key_total = (
            key_total
            + jnp.einsum("hqk,qhd->khd", score_grad, query_rows, preferred_element_type=jnp.float32)
            * score_scale
        )
        value_total = value_total + jnp.einsum(
            "hqk,qhd->khd", weights_low, grad_rows, preferred_element_type=jnp.float32
        )
        return (
            (key_total, value_total),
            query_grad.astype(jnp.bfloat16).reshape(block_rows, width_local),
        )

    zero_heads = jnp.zeros((group_rows, head_count, head_dim), jnp.float32)
    (key_total, value_total), query_grad = lax.scan(
        backward_block, (zero_heads, zero_heads), jnp.arange(block_count, dtype=jnp.int32)
    )
    return (
        query_grad.reshape(group_rows, width_local),
        key_total.reshape(group_rows, width_local).astype(jnp.bfloat16),
        value_total.reshape(group_rows, width_local).astype(jnp.bfloat16),
    )


BF, F32 = jnp.bfloat16, jnp.float32
BLK = 256
POS_OF = (0, 3, 1, 2)
NT = (((1,), (1,)), ((), ()))

def nt(a, b):
    return lax.dot_general(a, b, NT, preferred_element_type=F32)

def nn(a, b):
    return jnp.dot(a, b, preferred_element_type=F32)

def rows(block):
    return pl.ds(block * BLK, BLK)

def turn(u, cosine, sine, lane):
    near = jnp.where(lane % 64 < 32, pltpu.roll(u, 96, 1), pltpu.roll(u, 32, 1))
    return u * cosine + near * sine

def fwd_kernel(x_ref, wq_ref, wk_ref, wv_ref, vf_ref, cos_ref, sin_ref,
               q_ref, k_ref, v_ref, o_ref, lse_ref, vt_ref):
    lane = lax.broadcasted_iota(jnp.int32, (BLK, 128), 1)
    for m in range(4):
        at = rows(POS_OF[m])
        x = x_ref[rows(m), :]
        cosine, sine = cos_ref[rows(m), :], sin_ref[rows(m), :]
        qf, kf = nn(x, wq_ref[...]), nn(x, wk_ref[...])
        vf = 0.5 * nn(x, wv_ref[...]) + 0.5 * vf_ref[rows(m), :].astype(F32)
        for t in range(2):
            cols = slice(t * 128, t * 128 + 128)
            q_ref[at, cols] = turn(qf[:, cols], cosine, sine, lane).astype(BF) * 0.125
            k_ref[at, cols] = turn(kf[:, cols], cosine, sine, lane).astype(BF)
        low = vf.astype(BF)
        v_ref[at, :] = low
        vt_ref[:, at] = low.T
    lse_ref[...] = jnp.zeros_like(lse_ref)
    causal = lax.broadcasted_iota(jnp.int32, (BLK, BLK), 0) <= lax.broadcasted_iota(jnp.int32, (BLK, BLK), 1)
    for t in range(2):
        cols = slice(t * 128, t * 128 + 128)
        for m in range(4):
            i = POS_OF[m]
            n = BLK * (i + 1)
            q = q_ref[rows(i), cols]
            parts = []
            for h in range(2):
                qm = jnp.where((lane < 64) == (h == 0), q, jnp.zeros_like(q))
                scores = [nt(k_ref[rows(j), cols], qm) for j in range(i + 1)]
                scores[i] = jnp.where(causal, scores[i], -1e30)
                top = functools.reduce(jnp.maximum, [jnp.max(s, axis=0, keepdims=True) for s in scores])
                es = [jnp.exp(s - top) for s in scores]
                total = functools.reduce(jnp.add, [jnp.sum(e, axis=0, keepdims=True) for e in es])
                head = slice(t * 128 + h * 64, t * 128 + h * 64 + 64)
                ot = functools.reduce(jnp.add, [nn(vt_ref[head, rows(j)], es[j].astype(BF)) for j in range(i + 1)])
                parts.append(ot * (1.0 / total))
                lse_ref[t * 2 + h : t * 2 + h + 1, rows(i)] = top + jnp.log(total)
            o_ref[rows(m), cols] = jnp.concatenate(parts, axis=0).T.astype(BF)

def attn_fwd(x, wq, wk, wv, vf, cos, sin):
    R = 1024
    full = lambda s: pl.BlockSpec(s, lambda g: (0, 0))
    col = pl.BlockSpec((R, 256), lambda g: (0, g))
    return pl.pallas_call(
        fwd_kernel, grid=(2,),
        in_specs=[full((R, 1024)), col, col, col, col, full((R, 128)), full((R, 128))],
        out_specs=[col, col, col, col, pl.BlockSpec((None, 8, R), lambda g: (g, 0, 0))],
        out_shape=[jax.ShapeDtypeStruct((R, 512), BF)] * 4 + [jax.ShapeDtypeStruct((2, 8, R), F32)],
        scratch_shapes=[pltpu.VMEM((256, R), BF)],
        compiler_params=pltpu.CompilerParams(vmem_limit_bytes=50 << 20),
        cost_estimate=pl.CostEstimate(flops=10 * 10**9, bytes_accessed=12 << 20, transcendentals=5 << 20),
    )(x, wq, wk, wv, vf, cos, sin)

def bwd_kernel(c_ref, wo_ref, q_ref, k_ref, v_ref, o_ref, lse_ref, cos_ref, sin_ref,
               dq_ref, dk_ref, dv_ref, gf_ref, do_ref, kt_ref, dka_ref, dva_ref, dl_ref):
    lane = lax.broadcasted_iota(jnp.int32, (BLK, 128), 1)
    for m in range(4):
        at = rows(POS_OF[m])
        low = nt(c_ref[rows(m), :], wo_ref[...]).astype(BF)
        do_ref[at, :] = low
        prod = (low.astype(F32) * o_ref[rows(m), :].astype(F32)).T
        for h in range(4):
            dl_ref[h : h + 1, at] = jnp.sum(prod[h * 64 : h * 64 + 64, :], axis=0, keepdims=True)
        kt_ref[:, at] = k_ref[at, :].T
    causal = lax.broadcasted_iota(jnp.int32, (BLK, BLK), 0) <= lax.broadcasted_iota(jnp.int32, (BLK, BLK), 1)
    for t in range(2):
        cols = slice(t * 128, t * 128 + 128)
        for m in range(4):
            i = POS_OF[m]
            q, do = q_ref[rows(i), cols], do_ref[rows(i), cols]
            parts = []
            for h in range(2):
                mine = (lane < 64) == (h == 0)
                qm = jnp.where(mine, q, jnp.zeros_like(q))
                dom = jnp.where(mine, do, jnp.zeros_like(do))
                lse = lse_ref[t * 2 + h : t * 2 + h + 1, rows(i)]
                delta = dl_ref[t * 2 + h : t * 2 + h + 1, rows(i)]
                head = slice(t * 128 + h * 64, t * 128 + h * 64 + 64)
                dqt = None
                for j in range(i + 1):
                    p = jnp.exp(nt(k_ref[rows(j), cols], qm) - lse)
                    if j == i:
                        p = jnp.where(causal, p, 0.0)
                    ds = (p * (nt(v_ref[rows(j), cols], dom) - delta)).astype(BF)
                    dv, dk = nn(p.astype(BF), dom), nn(ds, qm)
                    dva_ref[rows(j), cols] = dv if (m, h) == FIRST[j] else dva_ref[rows(j), cols] + dv
                    dka_ref[rows(j), cols] = dk if (m, h) == FIRST[j] else dka_ref[rows(j), cols] + dk
                    part = nn(kt_ref[head, rows(j)], ds)
                    dqt = part if dqt is None else dqt + part
                parts.append(dqt)
            dq = (jnp.concatenate(parts, axis=0).T * 0.125).astype(BF).astype(F32)
            dq_ref[rows(m), cols] = turn(dq, cos_ref[rows(m), :], -sin_ref[rows(m), :], lane).astype(BF)
    for m in range(4):
        at = rows(POS_OF[m])
        cosine, sine = cos_ref[rows(m), :], -sin_ref[rows(m), :]
        for t in range(2):
            cols = slice(t * 128, t * 128 + 128)
            dk = dka_ref[at, cols].astype(BF).astype(F32)
            dk_ref[rows(m), cols] = turn(dk, cosine, sine, lane).astype(BF)
        half = 0.5 * dva_ref[at, :].astype(BF).astype(F32)
        dv_ref[rows(m), :] = half.astype(BF)
        gf_ref[rows(m), :] = half

FIRST = {}
for _m in range(4):
    for _j in range(POS_OF[_m] + 1):
        FIRST.setdefault(_j, (_m, 0))

def attn_bwd(c, wo, q, k, v, o, lse, cos, sin):
    R = 1024
    full = lambda s: pl.BlockSpec(s, lambda g: (0, 0))
    col = pl.BlockSpec((R, 256), lambda g: (0, g))
    return pl.pallas_call(
        bwd_kernel, grid=(2,),
        in_specs=[full((R, 1024)), pl.BlockSpec((256, 1024), lambda g: (g, 0)), col, col, col, col,
                  pl.BlockSpec((None, 8, R), lambda g: (g, 0, 0)), full((R, 128)), full((R, 128))],
        out_specs=[col] * 4,
        out_shape=[jax.ShapeDtypeStruct((R, 512), BF)] * 3 + [jax.ShapeDtypeStruct((R, 512), F32)],
        scratch_shapes=[pltpu.VMEM((R, 256), BF), pltpu.VMEM((256, R), BF), pltpu.VMEM((R, 256), F32),
                        pltpu.VMEM((R, 256), F32), pltpu.VMEM((8, R), F32)],
        compiler_params=pltpu.CompilerParams(vmem_limit_bytes=50 << 20),
        cost_estimate=pl.CostEstimate(flops=20 * 10**9, bytes_accessed=12 << 20, transcendentals=5 << 20),
    )(c, wo, q, k, v, o, lse, cos, sin)

def tables():
    pos = np.zeros(1024, np.float32)
    for m in range(4):
        pos[m*256:(m+1)*256] = POS_OF[m]*256 + np.arange(256)
    freqs = np.float32(10000.0) ** (-np.arange(32, dtype=np.float32) / np.float32(32))
    ang = pos[:, None] * freqs[None]
    c, s = np.cos(ang.astype(np.float32)), np.sin(ang.astype(np.float32))
    return np.tile(c, (1, 4)).astype(np.float32), np.concatenate([-s, s, -s, s], 1).astype(np.float32)

def swap(block):
    return lax.ppermute(block, "tp", [(0, 1), (1, 0)])


def joined(mine, other):
    pair = jnp.concatenate([mine, other], axis=0)
    return jnp.where(lax.axis_index("tp") == 0, pair, jnp.roll(pair, mine.shape[0], axis=0))


def local_pair(
    tokens,
    v_first,
    w_query,
    w_key,
    w_value,
    w_out,
    w_gate,
    w_up,
    w_down,
    gain_attn,
    gain_mlp,
    seq_lens,
    cotangent,
):
    row_share = tokens.shape[0]
    me = lax.axis_index("tp")
    cosine, sine = tables()
    own = lambda whole: lax.dynamic_slice_in_dim(whole, me * row_share, row_share, 0)
    theirs = lambda whole: lax.dynamic_slice_in_dim(whole, (1 - me) * row_share, row_share, 0)

    def scatter(partial):
        return own(partial) + swap(theirs(partial).astype(jnp.bfloat16)).astype(jnp.float32)

    def gather(mine):
        return joined(mine, swap(mine))

    normed_attn = gather(normalize(tokens, gain_attn).astype(jnp.bfloat16))
    query, keys, mixed_values, attended, row_lse = attn_fwd(
        normed_attn, w_query, w_key, w_value, v_first, cosine, sine
    )
    middle = tokens + scatter(jnp.dot(attended, w_out, preferred_element_type=jnp.float32))
    mlp_rows = gather(normalize(middle, gain_mlp).astype(jnp.bfloat16))
    cot_rows = gather(cotangent.astype(jnp.bfloat16))
    gate = jnp.dot(mlp_rows, w_gate, preferred_element_type=jnp.float32)
    up_values = jnp.dot(mlp_rows, w_up, preferred_element_type=jnp.float32)
    hidden = (jax.nn.silu(gate) * up_values).astype(jnp.bfloat16)
    layer_out = middle + scatter(jnp.dot(hidden, w_down, preferred_element_type=jnp.float32))
    gate_grad, up_grad = swiglu_back(gate, up_values, outer_cols(cot_rows, w_down))
    grad_mlp_in = scatter(outer_cols(gate_grad, w_gate) + outer_cols(up_grad, w_up))
    grad_down = inner_rows(hidden, cot_rows)
    grad_gate = inner_rows(mlp_rows, gate_grad)
    grad_up = inner_rows(mlp_rows, up_grad)
    grad_gate, grad_up, grad_down = lax.psum(
        tuple(g.astype(jnp.bfloat16) for g in (grad_gate, grad_up, grad_down)), "dp"
    )
    middle_back, grad_gain_mlp = normalize_back(middle, gain_mlp, grad_mlp_in)
    grad_middle = cotangent + middle_back
    attn_cot_rows = gather(grad_middle.astype(jnp.bfloat16))
    query_pre_grad, key_pre_grad, value_grad, grad_first = attn_bwd(
        attn_cot_rows, w_out, query, keys, mixed_values, attended, row_lse, cosine, sine
    )
    grad_attn_in = scatter(
        outer_cols(query_pre_grad, w_query)
        + outer_cols(key_pre_grad, w_key)
        + outer_cols(value_grad, w_value)
    )
    grad_output = inner_rows(attended, attn_cot_rows)
    grad_query = inner_rows(normed_attn, query_pre_grad)
    grad_key = inner_rows(normed_attn, key_pre_grad)
    grad_value = inner_rows(normed_attn, value_grad)
    tokens_back, grad_gain_attn = normalize_back(tokens, gain_attn, grad_attn_in)
    grad_tokens = grad_middle + tokens_back
    grad_query, grad_key, grad_value, grad_output = lax.psum(
        tuple(g.astype(jnp.bfloat16) for g in (grad_query, grad_key, grad_value, grad_output)), "dp"
    )
    grad_gain_attn, grad_gain_mlp = lax.psum((grad_gain_attn, grad_gain_mlp), ("dp", "tp"))
    wide = [
        g.astype(jnp.float32)
        for g in (grad_query, grad_key, grad_value, grad_output, grad_gate, grad_up, grad_down)
    ]
    return (layer_out, grad_tokens, grad_first, *wide, grad_gain_attn, grad_gain_mlp)


def local(
    tokens,
    v_first,
    w_query,
    w_key,
    w_value,
    w_out,
    w_gate,
    w_up,
    w_down,
    gain_attn,
    gain_mlp,
    seq_lens,
    cotangent,
):
    tp_count = lax.axis_size("tp")
    row_share = tokens.shape[0]
    doc_ids, positions = layout(seq_lens[0], row_share, tp_count)
    normed_attn = lax.all_gather(
        normalize(tokens, gain_attn).astype(jnp.bfloat16), "tp", axis=0, tiled=True
    )
    query = rotate(
        jnp.dot(normed_attn, w_query, preferred_element_type=jnp.float32), positions, HDIM, 1.0
    ).astype(jnp.bfloat16)
    keys = rotate(
        jnp.dot(normed_attn, w_key, preferred_element_type=jnp.float32), positions, HDIM, 1.0
    ).astype(jnp.bfloat16)
    value_pre = jnp.dot(normed_attn, w_value, preferred_element_type=jnp.float32)
    mixed_values = (0.5 * value_pre + 0.5 * v_first.astype(jnp.float32)).astype(jnp.bfloat16)
    attended, row_lse = attention_forward(query, keys, mixed_values, doc_ids, positions, HDIM)
    middle = tokens + lax.psum_scatter(
        jnp.dot(attended, w_out, preferred_element_type=jnp.float32),
        "tp",
        scatter_dimension=0,
        tiled=True,
    )
    normed_mlp = normalize(middle, gain_mlp).astype(jnp.bfloat16)
    grad_branch = cotangent.astype(jnp.bfloat16)
    mlp_rows = lax.all_gather(normed_mlp, "tp", axis=0, tiled=True)
    gate = jnp.dot(mlp_rows, w_gate, preferred_element_type=jnp.float32)
    up_values = jnp.dot(mlp_rows, w_up, preferred_element_type=jnp.float32)
    hidden = (jax.nn.silu(gate) * up_values).astype(jnp.bfloat16)
    layer_out = middle + lax.psum_scatter(
        jnp.dot(hidden, w_down, preferred_element_type=jnp.float32).astype(jnp.bfloat16),
        "tp",
        scatter_dimension=0,
        tiled=True,
    ).astype(jnp.float32)
    cot_rows = lax.all_gather(grad_branch, "tp", axis=0, tiled=True)
    grad_down = inner_rows(hidden, cot_rows)
    gate_grad, up_grad = swiglu_back(gate, up_values, outer_cols(cot_rows, w_down))
    grad_gate = inner_rows(mlp_rows, gate_grad)
    grad_up = inner_rows(mlp_rows, up_grad)
    grad_mlp_in = lax.psum_scatter(
        (outer_cols(gate_grad, w_gate) + outer_cols(up_grad, w_up)).astype(jnp.bfloat16),
        "tp",
        scatter_dimension=0,
        tiled=True,
    ).astype(jnp.float32)
    middle_back, grad_gain_mlp = normalize_back(middle, gain_mlp, grad_mlp_in)
    grad_middle = cotangent + middle_back
    attn_cot_rows = lax.all_gather(grad_middle.astype(jnp.bfloat16), "tp", axis=0, tiled=True)
    grad_output = inner_rows(attended, attn_cot_rows)
    grad_attended = outer_cols(attn_cot_rows, w_out).astype(jnp.bfloat16)
    query_grad, key_grad, mixed_grad = attention_backward(
        query, keys, mixed_values, grad_attended, row_lse, doc_ids, positions, HDIM
    )
    half_mixed = 0.5 * mixed_grad.astype(jnp.float32)
    value_grad = half_mixed.astype(jnp.bfloat16)
    query_pre_grad = rotate(query_grad.astype(jnp.float32), positions, HDIM, -1.0).astype(
        jnp.bfloat16
    )
    key_pre_grad = rotate(key_grad.astype(jnp.float32), positions, HDIM, -1.0).astype(jnp.bfloat16)
    grad_query = inner_rows(normed_attn, query_pre_grad)
    grad_key = inner_rows(normed_attn, key_pre_grad)
    grad_value = inner_rows(normed_attn, value_grad)
    grad_attn_in = lax.psum_scatter(
        (
            outer_cols(query_pre_grad, w_query)
            + outer_cols(key_pre_grad, w_key)
            + outer_cols(value_grad, w_value)
        ).astype(jnp.bfloat16),
        "tp",
        scatter_dimension=0,
        tiled=True,
    ).astype(jnp.float32)
    tokens_back, grad_gain_attn = normalize_back(tokens, gain_attn, grad_attn_in)
    grad_tokens = grad_middle + tokens_back
    grad_query, grad_key, grad_value, grad_output, grad_gate, grad_up, grad_down = (
        lax.psum(grad_query.astype(jnp.bfloat16), "dp").astype(jnp.float32),
        lax.psum(grad_key.astype(jnp.bfloat16), "dp").astype(jnp.float32),
        lax.psum(grad_value.astype(jnp.bfloat16), "dp").astype(jnp.float32),
        lax.psum(grad_output.astype(jnp.bfloat16), "dp").astype(jnp.float32),
        lax.psum(grad_gate.astype(jnp.bfloat16), "dp").astype(jnp.float32),
        lax.psum(grad_up.astype(jnp.bfloat16), "dp").astype(jnp.float32),
        lax.psum(grad_down.astype(jnp.bfloat16), "dp").astype(jnp.float32),
    )
    grad_gain_attn, grad_gain_mlp = lax.psum((grad_gain_attn, grad_gain_mlp), ("dp", "tp"))
    return (
        layer_out,
        grad_tokens,
        half_mixed,
        grad_query,
        grad_key,
        grad_value,
        grad_output,
        grad_gate,
        grad_up,
        grad_down,
        grad_gain_attn,
        grad_gain_mlp,
    )


def solution(mesh):
    in_specs = (
        P(("dp", "tp"), None),
        P("dp", "tp"),
        P(None, "tp"),
        P(None, "tp"),
        P(None, "tp"),
        P("tp", None),
        P(None, "tp"),
        P(None, "tp"),
        P("tp", None),
        P(),
        P(),
        P("dp", None),
        P(("dp", "tp"), None),
    )
    out_specs = (
        P(("dp", "tp"), None),
        P(("dp", "tp"), None),
        P("dp", "tp"),
        P(None, "tp"),
        P(None, "tp"),
        P(None, "tp"),
        P("tp", None),
        P(None, "tp"),
        P(None, "tp"),
        P("tp", None),
        P(),
        P(),
    )

    def step(*args):
        tokens, seq_lens = args[0], args[11]
        pair = mesh.shape["tp"] == 2 and seq_lens.shape[1] == 1 and tokens.shape == (512, 1024)
        return (local_pair if pair else local)(*args)

    return jax.shard_map(step, mesh=mesh, in_specs=in_specs, out_specs=out_specs, check_vma=False)
```

```python
import functools

import jax
import jax.numpy as jnp
import numpy as np
from jax import lax
from jax.experimental import pallas as pl
from jax.experimental.pallas import tpu as pltpu
from jax.sharding import PartitionSpec as P

HDIM = 64


EPS = 1e-06


def layout(seq_row, row_share, tp_count):
    group_rows = row_share * tp_count
    row_ids = jnp.arange(group_rows, dtype=jnp.int32)
    device = row_ids // row_share
    local_row = row_ids % row_share
    pieces = seq_row // (2 * tp_count)
    slot_ends = jnp.cumsum(2 * pieces)
    starts = slot_ends - 2 * pieces
    offset = local_row[:, None] - starts[None, :]
    inside = (offset >= 0) & (offset < 2 * pieces[None, :])
    first_half = offset < pieces[None, :]
    mirror = 2 * tp_count - 1 - device[:, None]
    position = jnp.where(
        first_half,
        device[:, None] * pieces[None, :] + offset,
        mirror * pieces[None, :] + offset - pieces[None, :],
    )
    slot_ids = jnp.arange(seq_row.shape[0], dtype=jnp.int32)
    doc_ids = jnp.sum(jnp.where(inside, slot_ids[None, :], 0), axis=1)
    positions = jnp.sum(jnp.where(inside, position, 0), axis=1)
    return (doc_ids, positions)


def rotate(values, positions, head_dim, turn_sign):
    row_count, width_all = values.shape
    half_dim = head_dim // 2
    shaped = values.reshape(row_count, width_all // head_dim, head_dim)
    freqs = 10000.0 ** (-jnp.arange(half_dim, dtype=jnp.float32) / half_dim)
    angles = positions.astype(jnp.float32)[:, None] * freqs[None, :]
    cosine = jnp.cos(angles)[:, None, :]
    sine = turn_sign * jnp.sin(angles)[:, None, :]
    front = shaped[..., :half_dim]
    behind = shaped[..., half_dim:]
    turned = jnp.concatenate(
        [front * cosine - behind * sine, behind * cosine + front * sine], axis=-1
    )
    return turned.reshape(row_count, width_all)


def normalize(values, gain):
    return values * lax.rsqrt(jnp.mean(values * values, axis=-1, keepdims=True) + EPS) * gain


def normalize_back(values, gain, grad_in):
    factor = lax.rsqrt(jnp.mean(values * values, axis=-1, keepdims=True) + EPS)
    normed = values * factor
    grad_normed = grad_in * gain
    grad_values = factor * (
        grad_normed - normed * jnp.mean(grad_normed * normed, axis=-1, keepdims=True)
    )
    return (grad_values, jnp.sum(grad_in * normed, axis=0))


def inner_rows(left, right):
    return lax.dot_general(
        left, right, (((0,), (0,)), ((), ())), preferred_element_type=jnp.float32
    )


def outer_cols(left, right):
    return lax.dot_general(
        left, right, (((1,), (1,)), ((), ())), preferred_element_type=jnp.float32
    )


def swiglu_back(gate, up_values, grad_hidden):
    sigma = jax.nn.sigmoid(gate)
    grad_gate = grad_hidden * up_values * (sigma * (1.0 + gate * (1.0 - sigma)))
    grad_upper = grad_hidden * (gate * sigma)
    return (grad_gate.astype(jnp.bfloat16), grad_upper.astype(jnp.bfloat16))


def block_mask(doc_ids, positions, first_row, block_rows):
    row_doc = lax.dynamic_slice_in_dim(doc_ids, first_row, block_rows, 0)
    row_pos = lax.dynamic_slice_in_dim(positions, first_row, block_rows, 0)
    return (row_doc[:, None] == doc_ids[None, :]) & (positions[None, :] <= row_pos[:, None])


def attention_forward(query, keys, values, doc_ids, positions, head_dim):
    group_rows, width_local = query.shape
    head_count = width_local // head_dim
    block_rows = min(512, group_rows)
    block_count = group_rows // block_rows
    score_scale = head_dim ** (-0.5)
    key_heads = keys.reshape(group_rows, head_count, head_dim)
    value_heads = values.reshape(group_rows, head_count, head_dim)

    def forward_block(block_index):
        first_row = block_index * block_rows
        query_rows = lax.dynamic_slice_in_dim(query, first_row, block_rows, 0).reshape(
            block_rows, head_count, head_dim
        )
        scores = (
            jnp.einsum("qhd,khd->hqk", query_rows, key_heads, preferred_element_type=jnp.float32)
            * score_scale
        )
        allowed = block_mask(doc_ids, positions, first_row, block_rows)
        scores = jnp.where(allowed[None], scores, -1e30)
        row_max = jnp.max(scores, axis=-1, keepdims=True)
        exponent = jnp.exp(scores - row_max)
        row_total = jnp.sum(exponent, axis=-1, keepdims=True)
        weights = (exponent / row_total).astype(jnp.bfloat16)
        mixture = jnp.einsum(
            "hqk,khd->qhd", weights, value_heads, preferred_element_type=jnp.float32
        )
        return (
            mixture.astype(jnp.bfloat16).reshape(block_rows, width_local),
            (row_max + jnp.log(row_total))[..., 0],
        )

    mixture, row_lse = lax.map(forward_block, jnp.arange(block_count, dtype=jnp.int32))
    return (mixture.reshape(group_rows, width_local), row_lse)


def attention_backward(query, keys, values, grad_mixture, row_lse, doc_ids, positions, head_dim):
    group_rows, width_local = query.shape
    head_count = width_local // head_dim
    block_rows = min(512, group_rows)
    block_count = group_rows // block_rows
    score_scale = head_dim ** (-0.5)
    key_heads = keys.reshape(group_rows, head_count, head_dim)
    value_heads = values.reshape(group_rows, head_count, head_dim)

    def backward_block(carry, block_index):
        key_total, value_total = carry
        first_row = block_index * block_rows
        query_rows = lax.dynamic_slice_in_dim(query, first_row, block_rows, 0).reshape(
            block_rows, head_count, head_dim
        )
        grad_rows = lax.dynamic_slice_in_dim(grad_mixture, first_row, block_rows, 0).reshape(
            block_rows, head_count, head_dim
        )
        scores = (
            jnp.einsum("qhd,khd->hqk", query_rows, key_heads, preferred_element_type=jnp.float32)
            * score_scale
        )
        allowed = block_mask(doc_ids, positions, first_row, block_rows)
        scores = jnp.where(allowed[None], scores, -1e30)
        weights = jnp.exp(scores - row_lse[block_index][..., None])
        weights_low = weights.astype(jnp.bfloat16)
        grad_weights = jnp.einsum(
            "qhd,khd->hqk", grad_rows, value_heads, preferred_element_type=jnp.float32
        )
        weighted_sum = jnp.sum(weights * grad_weights, axis=-1, keepdims=True)
        score_grad = (weights * (grad_weights - weighted_sum)).astype(jnp.bfloat16)
        query_grad = (
            jnp.einsum("hqk,khd->qhd", score_grad, key_heads, preferred_element_type=jnp.float32)
            * score_scale
        )
        key_total = (
            key_total
            + jnp.einsum("hqk,qhd->khd", score_grad, query_rows, preferred_element_type=jnp.float32)
            * score_scale
        )
        value_total = value_total + jnp.einsum(
            "hqk,qhd->khd", weights_low, grad_rows, preferred_element_type=jnp.float32
        )
        return (
            (key_total, value_total),
            query_grad.astype(jnp.bfloat16).reshape(block_rows, width_local),
        )

    zero_heads = jnp.zeros((group_rows, head_count, head_dim), jnp.float32)
    (key_total, value_total), query_grad = lax.scan(
        backward_block, (zero_heads, zero_heads), jnp.arange(block_count, dtype=jnp.int32)
    )
    return (
        query_grad.reshape(group_rows, width_local),
        key_total.reshape(group_rows, width_local).astype(jnp.bfloat16),
        value_total.reshape(group_rows, width_local).astype(jnp.bfloat16),
    )


BF, F32 = jnp.bfloat16, jnp.float32
BLK = 256
POS_OF = (0, 3, 1, 2)
NT = (((1,), (1,)), ((), ()))

def nt(a, b):
    return lax.dot_general(a, b, NT, preferred_element_type=F32)

def nn(a, b):
    return jnp.dot(a, b, preferred_element_type=F32)

def rows(block):
    return pl.ds(block * BLK, BLK)

def turn(u, cosine, sine, lane):
    near = jnp.where(lane % 64 < 32, pltpu.roll(u, 96, 1), pltpu.roll(u, 32, 1))
    return u * cosine + near * sine

def fwd_kernel(x_ref, wq_ref, wk_ref, wv_ref, vf_ref, cos_ref, sin_ref,
               q_ref, k_ref, v_ref, o_ref, ot_ref, lse_ref, vt_ref):
    lane = lax.broadcasted_iota(jnp.int32, (BLK, 128), 1)
    for m in range(4):
        at = rows(POS_OF[m])
        x = x_ref[rows(m), :]
        cosine, sine = cos_ref[rows(m), :], sin_ref[rows(m), :]
        qf, kf = nn(x, wq_ref[...]), nn(x, wk_ref[...])
        vf = 0.5 * nn(x, wv_ref[...]) + 0.5 * vf_ref[rows(m), :].astype(F32)
        for t in range(2):
            cols = slice(t * 128, t * 128 + 128)
            q_ref[at, cols] = turn(qf[:, cols], cosine, sine, lane).astype(BF) * 0.125
            k_ref[at, cols] = turn(kf[:, cols], cosine, sine, lane).astype(BF)
        low = vf.astype(BF)
        v_ref[at, :] = low
        vt_ref[:, at] = low.T
    lse_ref[...] = jnp.zeros_like(lse_ref)
    causal = lax.broadcasted_iota(jnp.int32, (BLK, BLK), 0) <= lax.broadcasted_iota(jnp.int32, (BLK, BLK), 1)
    for t in range(2):
        cols = slice(t * 128, t * 128 + 128)
        for m in range(4):
            i = POS_OF[m]
            n = BLK * (i + 1)
            q = q_ref[rows(i), cols]
            parts = []
            for h in range(2):
                qm = jnp.where((lane < 64) == (h == 0), q, jnp.zeros_like(q))
                scores = [nt(k_ref[rows(j), cols], qm) for j in range(i + 1)]
                scores[i] = jnp.where(causal, scores[i], -1e30)
                top = functools.reduce(jnp.maximum, [jnp.max(s, axis=0, keepdims=True) for s in scores])
                es = [jnp.exp(s - top) for s in scores]
                total = functools.reduce(jnp.add, [jnp.sum(e, axis=0, keepdims=True) for e in es])
                head = slice(t * 128 + h * 64, t * 128 + h * 64 + 64)
                ot = functools.reduce(jnp.add, [nn(vt_ref[head, rows(j)], es[j].astype(BF)) for j in range(i + 1)])
                parts.append(ot * (1.0 / total))
                lse_ref[t * 2 + h : t * 2 + h + 1, rows(i)] = top + jnp.log(total)
            flat = jnp.concatenate(parts, axis=0)
            ot_ref[cols, rows(m)] = flat.astype(BF)
            o_ref[rows(m), cols] = flat.T.astype(BF)

def attn_fwd(x, wq, wk, wv, vf, cos, sin):
    R = 1024
    full = lambda s: pl.BlockSpec(s, lambda g: (0, 0))
    col = pl.BlockSpec((R, 256), lambda g: (0, g))
    return pl.pallas_call(
        fwd_kernel, grid=(2,),
        in_specs=[full((R, 1024)), col, col, col, col, full((R, 128)), full((R, 128))],
        out_specs=[col, col, col, col, pl.BlockSpec((256, R), lambda g: (g, 0)), pl.BlockSpec((None, 8, R), lambda g: (g, 0, 0))],
        out_shape=[jax.ShapeDtypeStruct((R, 512), BF)] * 4 + [jax.ShapeDtypeStruct((512, R), BF), jax.ShapeDtypeStruct((2, 8, R), F32)],
        scratch_shapes=[pltpu.VMEM((256, R), BF)],
        compiler_params=pltpu.CompilerParams(vmem_limit_bytes=50 << 20),
        cost_estimate=pl.CostEstimate(flops=10 * 10**9, bytes_accessed=12 << 20, transcendentals=5 << 20),
    )(x, wq, wk, wv, vf, cos, sin)

FIRST = {}
for _m in range(4):
    for _j in range(POS_OF[_m] + 1):
        FIRST.setdefault(_j, (_m, 0))

def tables():
    pos = np.zeros(1024, np.float32)
    for m in range(4):
        pos[m*256:(m+1)*256] = POS_OF[m]*256 + np.arange(256)
    freqs = np.float32(10000.0) ** (-np.arange(32, dtype=np.float32) / np.float32(32))
    ang = pos[:, None] * freqs[None]
    c, s = np.cos(ang.astype(np.float32)), np.sin(ang.astype(np.float32))
    return np.tile(c, (1, 4)).astype(np.float32), np.concatenate([-s, s, -s, s], 1).astype(np.float32)


def ring_place(dp):
    core, x, z = lax.rem(dp, 2), lax.rem(lax.div(dp, 2), 2), lax.div(dp, 4)
    place = z + x * (7 - 2 * z)

    def device(where):
        side = lax.div(where, 4)
        return ((where + side * (7 - 2 * where)) * 2 + side) * 2 + core

    turn_no = lax.rem(place + core * (8 - 2 * place), 8)
    after = device(lax.rem(place + 1 + 6 * core, 8))
    before = device(lax.rem(place + 7 - 6 * core, 8))
    cube = (dp + 1 - 2 * core, dp + 2 - 4 * x, dp + 4 - 8 * lax.rem(z, 2), dp + 8 - 16 * lax.div(z, 2))
    return core, turn_no, after, before, cube


def remote(src, dst, send, recv, dp):
    return pltpu.make_async_remote_copy(
        src, dst, send, recv, device_id={"dp": dp}, device_id_type=pl.DeviceIdType.MESH
    )


class Ring:
    def __init__(self, place, takes, outs, own, sib, slots, sems):
        self.core, self.turn_no, self.after, self.before, self.cube = place
        self.takes, self.outs, self.own, self.sib, self.slots = takes, outs, own, sib, slots
        self.trade, self.rs, self.ag, self.over, self.keep = sems

    def piece(self, g, chunk):
        size = self.slots[g].shape[1]
        return pl.ds(pl.multiple_of(chunk * size, size), size)

    def traded(self, g):
        return remote(self.takes[g](1 - self.core), self.sib[g], self.trade.at[0, g], self.trade.at[1, g], self.cube[0])

    def total(self, g, chunk):
        at = self.piece(g, chunk)
        return self.own[g][at, :].astype(F32) + self.sib[g][at, :].astype(F32)

    def first(self, g, chunk):
        return remote(
            self.own[g].at[self.piece(g, chunk)], self.slots[g].at[0], self.rs.at[0, g, 0], self.rs.at[1, g, 0], self.after
        )

    def begin(self, g):
        self.traded(g).wait()
        chunk = lax.rem(self.turn_no + 7, 8)
        self.own[g][self.piece(g, chunk), :] = self.total(g, chunk).astype(BF)
        self.first(g, chunk).start()

    def add(self, g, t):
        chunk = lax.rem(self.turn_no + 14 - t, 8)
        remote(self.slots[g].at[t], self.slots[g].at[t], self.rs.at[0, g, t], self.rs.at[1, g, t], self.after).wait_recv()
        self.slots[g][t] = (self.slots[g][t].astype(F32) + self.total(g, chunk)).astype(BF)

    def add_on(self, g, t):
        self.add(g, t)
        remote(self.slots[g].at[t], self.slots[g].at[t + 1], self.rs.at[0, g, t + 1], self.rs.at[1, g, t + 1], self.after).start()

    def spot(self, g, chunk):
        return self.outs[g](self.core, chunk)

    def turn_over(self, g):
        self.add(g, 6)
        spot = self.spot(g, self.turn_no)
        last = self.slots[g].at[6]
        remote(last, spot, self.ag.at[0, g, 0], self.ag.at[1, g, 0], self.after).start()
        remote(last, spot, self.over.at[0, g, 0], self.over.at[1, g, 0], self.cube[0]).start()
        pltpu.make_async_copy(last, spot, self.keep.at[g]).start()

    def pass_on(self, g, t):
        spot = self.spot(g, lax.rem(self.turn_no + 15 - t, 8))
        remote(spot, spot, self.ag.at[0, g, t], self.ag.at[1, g, t], self.after).wait_recv()

        @pl.when(t < 6)
        def _():
            remote(spot, spot, self.ag.at[0, g, t + 1], self.ag.at[1, g, t + 1], self.after).start()

        remote(spot, spot, self.over.at[0, g, t + 1], self.over.at[1, g, t + 1], self.cube[0]).start()

    def end(self, g):
        spot = self.spot(g, self.turn_no)
        pltpu.make_async_copy(self.slots[g].at[6], spot, self.keep.at[g]).wait()

        def finish(t, _):
            remote(self.slots[g].at[0], self.slots[g].at[0], self.rs.at[0, g, t], self.rs.at[1, g, t], self.after).wait_send()
            remote(spot, spot, self.ag.at[0, g, t], self.ag.at[1, g, t], self.after).wait_send()
            return _

        lax.fori_loop(0, 7, finish, 0)

        def crossed(t, _):
            there = self.outs[g](1 - self.core, lax.rem(self.turn_no + t, 8))
            remote(spot, there, self.over.at[0, g, t], self.over.at[1, g, t], self.cube[0]).wait()
            return _

        lax.fori_loop(0, 8, crossed, 0)


def strip(ref, axis, halves, length):
    if axis == 0:
        return lambda core, chunk: ref.at[pl.ds(pl.multiple_of(core * halves + chunk * length, length), length)]
    return lambda core, chunk: ref.at[
        pl.ds(pl.multiple_of(chunk * length, length), length), pl.ds(pl.multiple_of(core * halves, halves), halves)
    ]


def half_of(ref, axis, halves):
    if axis == 0:
        return lambda core: ref.at[pl.ds(pl.multiple_of(core * halves, halves), halves)]
    return lambda core: ref.at[:, pl.ds(pl.multiple_of(core * halves, halves), halves)]


def norm_back_rows(values, gain, grad_in):
    factor = lax.rsqrt(jnp.mean(values * values, axis=-1, keepdims=True) + EPS)
    normed = values * factor
    grad_normed = grad_in * gain
    grad = factor * (grad_normed - normed * jnp.mean(grad_normed * normed, axis=-1, keepdims=True))
    return grad, jnp.sum(grad_in * normed, axis=0, keepdims=True)


def back_kernel(
    own6_h, send6_h, own4_h, send4_h, middle_h, cot_h, tokens_h, gain_attn_ref, gain_mlp_ref,
    wo_h, wq_h, wk_h, wv_h, q_h, k_h, v_h, o_h, ot_h, xt_h, lse_ref, cos_ref, sin_ref, gg_h, gu_h, gd_h,
    out_h, gt_h, gf_h, rq_h, rk_h, rv_h, ro_h, rg_h, ru_h, rd_h, gains_ref,
    f1, f2, f3, recv6, recv4, recv8, send8, c, wo, wq, wk, wv, q, k, v, o, ot, xt,
    dq, dk, dv, do, kt, dka, dva, dl, own8, dwq, dwk, dwv, dwo,
    mg, mu, md, sg, su, sd, lg, lu, ld, bq, bk, bv, bo, aq, ak, av, ao,
    load, ysem, trade1, rs1, ag1, over1, keep1, trade2, rs2, ag2, over2, keep2, gain_in, gain_sem, store,
):
    dp, tp = lax.axis_index("dp"), lax.axis_index("tp")
    place = ring_place(dp)
    core, turn_no, after, before, cube = place
    mesh_id = pl.DeviceIdType.MESH
    barrier = pltpu.get_barrier_semaphore()
    for other in (*cube, after, before):
        pl.semaphore_signal(barrier, inc=1, device_id={"dp": other}, device_id_type=mesh_id)
    pl.semaphore_signal(barrier, inc=1, device_id={"tp": 1 - tp}, device_id_type=mesh_id)

    loads = {}

    def fetch(name, src, dst):
        loads[name] = pltpu.make_async_copy(src, dst, load.at[len(loads)])
        loads[name].start()

    one = Ring(
        place, (half_of(gg_h, 0, 512), half_of(gu_h, 0, 512), half_of(gd_h, 1, 512)),
        (strip(rg_h, 0, 512, 64), strip(ru_h, 0, 512, 64), strip(rd_h, 1, 512, 176)),
        (mg, mu, md), (sg, su, sd), (lg, lu, ld), (trade1, rs1, ag1, over1, keep1),
    )
    two = Ring(
        place, (half_of(dwq, 0, 512), half_of(dwk, 0, 512), half_of(dwv, 0, 512), half_of(dwo, 0, 256)),
        (strip(rq_h, 0, 512, 64), strip(rk_h, 0, 512, 64), strip(rv_h, 0, 512, 64), strip(ro_h, 0, 256, 32)),
        (half_of(dwq, 0, 512)(core), half_of(dwk, 0, 512)(core), half_of(dwv, 0, 512)(core), half_of(dwo, 0, 256)(core)),
        (bq, bk, bv, bo), (aq, ak, av, ao), (trade2, rs2, ag2, over2, keep2),
    )
    for g, (whole, mine) in enumerate(((gg_h, mg), (gu_h, mu), (gd_h, md))):
        fetch(("m", g), one.takes[g](core), mine)
    for name, src, dst in (
        ("own6", own6_h, f1), ("middle", middle_h, f2), ("cot", cot_h, f3), ("wo", wo_h, wo), ("q", q_h, q), ("k", k_h, k),
        ("v", v_h, v), ("o", o_h, o), ("wq", wq_h, wq), ("wk", wk_h, wk), ("wv", wv_h, wv), ("ot", ot_h, ot), ("xt", xt_h, xt),
    ):
        fetch(name, src, dst)
    pl.semaphore_wait(barrier, 7)

    def peer(n, src, dst):
        return pltpu.make_async_remote_copy(
            src, dst, ysem.at[0, n], ysem.at[1, n], device_id={"tp": 1 - tp}, device_id_type=mesh_id
        )

    half = lambda b: pl.ds(b * BLK, BLK)
    six = [peer(b, send6_h.at[half(b)], recv6.at[half(b)]) for b in range(2)]
    for b in range(2):
        six[b].start()
    for g in range(3):
        one.traded(g).start()
    for g in range(3):
        loads["m", g].wait()
        one.begin(g)

    def ring_steps(first, last):
        def body(t, carry):
            for g in range(3):
                one.add_on(g, t)
            return carry

        lax.fori_loop(first, last, body, 0)

    lane = lax.broadcasted_iota(jnp.int32, (BLK, 128), 1)
    causal = lax.broadcasted_iota(jnp.int32, (BLK, BLK), 0) <= lax.broadcasted_iota(jnp.int32, (BLK, BLK), 1)
    gain_mlp, gain_attn = gain_mlp_ref[...], gain_attn_ref[...]
    ring_steps(0, 3)
    for name in ("own6", "middle", "cot", "wo"):
        loads[name].wait()
    gain_sum = jnp.zeros((1, 1024), F32)
    seven = []
    for b in range(2):
        six[b].wait_recv()

        def rows_back(n, total):
            at = pl.ds(pl.multiple_of(b * BLK + n * 64, 64), 64)
            grad_in = f1[at, :] + recv6[at, :].astype(F32)
            grad, part = norm_back_rows(f2[at, :], gain_mlp, grad_in)
            grad = f3[at, :] + grad
            f1[at, :] = grad
            c[pl.ds(pl.multiple_of(tp * 512 + b * BLK + n * 64, 64), 64), :] = grad.astype(BF)
            return total + part

        gain_sum = lax.fori_loop(0, 4, rows_back, gain_sum)
        mine = c.at[pl.ds(pl.multiple_of(tp * 512 + b * BLK, BLK), BLK)]
        seven.append(peer(2 + b, mine, mine))
        seven[b].start()
        ring_steps(3 + b, 4 + b)
    four = peer(4, send4_h, recv4)
    four.start()
    late = pltpu.make_async_copy(own4_h, f3, load.at[len(loads)])
    late.start()
    gains_ref[...] = jnp.zeros_like(gains_ref)
    gains_ref[0:1, :] = gain_sum
    for name in ("o", "k"):
        loads[name].wait()

    def branch_back(m):
        at = rows(m)
        low = nt(c[at, :], wo[...]).astype(BF)
        do[at, :] = low
        prod = (low.astype(F32) * o[at, :].astype(F32)).T
        for h in range(8):
            dl[h : h + 1, at] = jnp.sum(prod[h * 64 : h * 64 + 64, :], axis=0, keepdims=True)

    ring_steps(5, 6)
    for b in range(2):
        seven[b].wait_recv()
    for g in range(3):
        one.turn_over(g)
    for m in range(4):
        branch_back(m)
    for name in ("q", "v"):
        loads[name].wait()

    def pair(p, carry):
        cols = pl.ds(pl.multiple_of(p * 128, 128), 128)
        for j in range(4):
            kt[:, rows(j)] = k[rows(j), cols].T
        for m in range(4):
            i = POS_OF[m]
            qb, dob = q[rows(i), cols], do[rows(m), cols]
            parts = []
            for h in range(2):
                mine = (lane < 64) == (h == 0)
                qm = jnp.where(mine, qb, jnp.zeros_like(qb))
                dom = jnp.where(mine, dob, jnp.zeros_like(dob))
                lse = lse_ref[lax.div(p, 2), pl.ds(2 * lax.rem(p, 2) + h, 1), rows(i)]
                delta = dl[pl.ds(2 * p + h, 1), rows(m)]
                head = slice(h * 64, h * 64 + 64)
                dqt = None
                for j in range(i + 1):
                    weights = jnp.exp(nt(k[rows(j), cols], qm) - lse)
                    if j == i:
                        weights = jnp.where(causal, weights, 0.0)
                    ds = (weights * (nt(v[rows(j), cols], dom) - delta)).astype(BF)
                    dvp, dkp = nn(weights.astype(BF), dom), nn(ds, qm)
                    fresh = (m, h) == FIRST[j]
                    dva[rows(j), :] = dvp if fresh else dva[rows(j), :] + dvp
                    dka[rows(j), :] = dkp if fresh else dka[rows(j), :] + dkp
                    part = nn(kt[head, rows(j)], ds)
                    dqt = part if dqt is None else dqt + part
                parts.append(dqt)
            grad = (jnp.concatenate(parts, axis=0).T * 0.125).astype(BF).astype(F32)
            dq[rows(m), cols] = turn(grad, cos_ref[rows(m), :], -sin_ref[rows(m), :], lane).astype(BF)
            if m < 3:
                one.pass_on(m, 2 * p)
        for m in range(4):
            at = rows(POS_OF[m])
            grad = dka[at, :].astype(BF).astype(F32)
            dk[rows(m), cols] = turn(grad, cos_ref[rows(m), :], -sin_ref[rows(m), :], lane).astype(BF)
            dv[rows(m), cols] = (0.5 * dva[at, :].astype(BF).astype(F32)).astype(BF)

        @pl.when(p < 3)
        def _():
            for g in range(3):
                one.pass_on(g, 2 * p + 1)

        return carry

    lax.fori_loop(0, 4, pair, 0)
    keep_gf = pltpu.make_async_copy(dv, gf_h, store.at[0])
    keep_gf.start()
    for name in ("wq", "wk", "wv"):
        loads[name].wait()

    def into_rows(at):
        return nt(dq[at, :], wq[...]) + nt(dk[at, :], wk[...]) + nt(dv[at, :], wv[...])

    eight = []
    for b in range(2):
        at = pl.ds(pl.multiple_of((1 - tp) * 512 + b * BLK, BLK), BLK)
        send8[half(b), :] = into_rows(at).astype(BF)
        eight.append(peer(5 + b, send8.at[half(b)], recv8.at[half(b)]))
        eight[b].start()
    for name in ("xt", "ot"):
        loads[name].wait()
    for which in range(2):
        side = (1 - core) * (1 - which) + core * which
        at = pl.ds(pl.multiple_of(side * 512, 512), 512)
        for dst, src in ((dwq, dq), (dwk, dk), (dwv, dv)):
            dst[at, :] = nn(xt[at, :], src[...]).astype(BF)
        at = pl.ds(pl.multiple_of(side * 256, 256), 256)
        dwo[at, :] = nn(ot[at, :], c[...]).astype(BF)
        if which == 0:
            for g in range(4):
                two.traded(g).start()
    for g in range(4):
        two.begin(g)

    def second(t, carry):
        for g in range(4):
            two.add_on(g, t)
        return carry

    for b in range(2):
        own8[half(b), :] = into_rows(pl.ds(pl.multiple_of(tp * 512 + b * BLK, BLK), BLK))
    fetch_tokens = pltpu.make_async_copy(tokens_h, f2, load.at[len(loads) + 1])
    fetch_tokens.start()
    lax.fori_loop(0, 3, second, 0)
    four.wait_recv()
    late.wait()
    fetch_tokens.wait()

    def out_rows(n, carry):
        at = pl.ds(pl.multiple_of(n * 64, 64), 64)
        f3[at, :] = f3[at, :] + recv4[at, :].astype(F32)
        return carry

    lax.fori_loop(0, 8, out_rows, 0)
    keep_out = pltpu.make_async_copy(f3, out_h, store.at[1])
    keep_out.start()
    lax.fori_loop(3, 6, second, 0)
    for g in range(4):
        two.turn_over(g)
    gain_sum = jnp.zeros((1, 1024), F32)
    for b in range(2):
        eight[b].wait_recv()

        def rows_last(n, total):
            at = pl.ds(pl.multiple_of(b * BLK + n * 64, 64), 64)
            grad, part = norm_back_rows(f2[at, :], gain_attn, own8[at, :] + recv8[at, :].astype(F32))
            f1[at, :] = f1[at, :] + grad
            return total + part

        gain_sum = lax.fori_loop(0, 4, rows_last, gain_sum)
    keep_gt = pltpu.make_async_copy(f1, gt_h, store.at[2])
    keep_gt.start()
    gains_ref[1:2, :] = gain_sum

    def gain_swap(n):
        where = {"tp": 1 - tp} if n == 4 else {"dp": cube[n]}
        return pltpu.make_async_remote_copy(
            gains_ref, gain_in.at[n], gain_sem.at[0, n], gain_sem.at[1, n], device_id=where, device_id_type=mesh_id
        )

    for t in range(7):
        for g in range(4):
            two.pass_on(g, t)
        if t < 5:
            move = gain_swap(t)
            move.start()
            move.wait()
            gains_ref[...] = gains_ref[...] + gain_in[t]
    for g in range(3):
        one.end(g)
    for g in range(4):
        two.end(g)
    for copy in (*six, *seven, *eight, four):
        copy.wait_send()
    for copy in (keep_gf, keep_out, keep_gt):
        copy.wait()


def back(own6, send6, own4, send4, middle, cot, tokens, gain_attn, gain_mlp, wo, wq, wk, wv, q, k, v, o, ot, xt, lse, cos, sin, gg, gu, gd):
    V = lambda shape, kind=BF: pltpu.VMEM(shape, kind)
    D = lambda *shape: pltpu.SemaphoreType.DMA(shape)
    hbm, vmem = pl.BlockSpec(memory_space=pl.ANY), pl.BlockSpec(memory_space=pltpu.VMEM)
    S = jax.ShapeDtypeStruct
    wide = (1024, 1024)
    return pl.pallas_call(
        back_kernel,
        in_specs=[hbm] * 7 + [vmem] * 2 + [hbm] * 10 + [vmem] * 3 + [hbm] * 3,
        out_specs=[hbm] * 10 + [vmem],
        out_shape=[S((512, 1024), F32), S((512, 1024), F32), S((1024, 512), BF), *[S((1024, 512), BF)] * 3, S((512, 1024), BF),
                   S((1024, 1408), BF), S((1024, 1408), BF), S((1408, 1024), BF), S((8, 1024), F32)],
        scratch_shapes=[
            *[V((512, 1024), F32)] * 3, *[V((512, 1024))] * 4, V(wide), V((512, 1024)), *[V((1024, 512))] * 7, V((512, 1024)), V(wide),
            *[V((1024, 512))] * 4, V((128, 1024)), *[V((1024, 128), F32)] * 2, V((8, 1024), F32), V((512, 1024), F32),
            *[V((1024, 512))] * 3, V((512, 1024)),
            *[V((512, 1408)), V((512, 1408)), V((1408, 512))] * 2, V((7, 64, 1408)), V((7, 64, 1408)), V((7, 176, 512)),
            *[V((512, 512))] * 3, V((256, 1024)), *[V((7, 64, 512))] * 3, V((7, 32, 1024)),
            D(18), D(2, 7), D(2, 3), D(2, 3, 7), D(2, 3, 7), D(2, 3, 8), D(3), D(2, 4), D(2, 4, 7), D(2, 4, 7), D(2, 4, 8), D(4),
            V((5, 8, 1024), F32), D(2, 5), D(3),
        ],
        compiler_params=pltpu.CompilerParams(collective_id=3, has_side_effects=True, vmem_limit_bytes=62 << 20),
        cost_estimate=pl.CostEstimate(flops=30 * 10**9, bytes_accessed=60 << 20, transcendentals=5 << 20),
    )(own6, send6, own4, send4, middle, cot, tokens, gain_attn, gain_mlp, wo, wq, wk, wv, q, k, v, o, ot, xt, lse, cos, sin, gg, gu, gd)

def swap(block):
    return lax.ppermute(block, "tp", [(0, 1), (1, 0)])


def joined(mine, other):
    pair = jnp.concatenate([mine, other], axis=0)
    return jnp.where(lax.axis_index("tp") == 0, pair, jnp.roll(pair, mine.shape[0], axis=0))


def local_pair(
    tokens,
    v_first,
    w_query,
    w_key,
    w_value,
    w_out,
    w_gate,
    w_up,
    w_down,
    gain_attn,
    gain_mlp,
    seq_lens,
    cotangent,
):
    row_share = tokens.shape[0]
    me = lax.axis_index("tp")
    cosine, sine = tables()
    own = lambda whole: lax.dynamic_slice_in_dim(whole, me * row_share, row_share, 0)
    theirs = lambda whole: lax.dynamic_slice_in_dim(whole, (1 - me) * row_share, row_share, 0)

    def scatter(partial):
        return own(partial) + swap(theirs(partial).astype(jnp.bfloat16)).astype(jnp.float32)

    def gather(mine):
        return joined(mine, swap(mine))

    normed_attn = gather(normalize(tokens, gain_attn).astype(jnp.bfloat16))
    query, keys, mixed_values, attended, attended_t, row_lse = attn_fwd(
        normed_attn, w_query, w_key, w_value, v_first, cosine, sine
    )
    middle = tokens + scatter(jnp.dot(attended, w_out, preferred_element_type=jnp.float32))
    mlp_rows = gather(normalize(middle, gain_mlp).astype(jnp.bfloat16))
    cot_rows = gather(cotangent.astype(jnp.bfloat16))
    gate = jnp.dot(mlp_rows, w_gate, preferred_element_type=jnp.float32)
    up_values = jnp.dot(mlp_rows, w_up, preferred_element_type=jnp.float32)
    hidden = (jax.nn.silu(gate) * up_values).astype(jnp.bfloat16)
    branch = jnp.dot(hidden, w_down, preferred_element_type=jnp.float32)
    gate_grad, up_grad = swiglu_back(gate, up_values, outer_cols(cot_rows, w_down))
    mlp_in = outer_cols(gate_grad, w_gate) + outer_cols(up_grad, w_up)
    grad_down = inner_rows(hidden, cot_rows).astype(jnp.bfloat16)
    grad_gate = inner_rows(mlp_rows, gate_grad).astype(jnp.bfloat16)
    grad_up = inner_rows(mlp_rows, up_grad).astype(jnp.bfloat16)
    low = lambda part: theirs(part).astype(jnp.bfloat16)
    layer_out, grad_tokens, grad_first, *low_grads, gains = back(
        own(mlp_in), low(mlp_in), middle + own(branch), low(branch), middle, cotangent, tokens,
        gain_attn[None], gain_mlp[None], w_out, w_query, w_key, w_value, query, keys, mixed_values, attended, attended_t,
        normed_attn.T, row_lse, cosine, sine, grad_gate, grad_up, grad_down,
    )
    wide = [g.astype(jnp.float32) for g in low_grads]
    grad_first = grad_first.astype(jnp.float32)
    grad_gain_mlp, grad_gain_attn = gains[0], gains[1]
    return (layer_out, grad_tokens, grad_first, *wide, grad_gain_attn, grad_gain_mlp)


def local(
    tokens,
    v_first,
    w_query,
    w_key,
    w_value,
    w_out,
    w_gate,
    w_up,
    w_down,
    gain_attn,
    gain_mlp,
    seq_lens,
    cotangent,
):
    tp_count = lax.axis_size("tp")
    row_share = tokens.shape[0]
    doc_ids, positions = layout(seq_lens[0], row_share, tp_count)
    normed_attn = lax.all_gather(
        normalize(tokens, gain_attn).astype(jnp.bfloat16), "tp", axis=0, tiled=True
    )
    query = rotate(
        jnp.dot(normed_attn, w_query, preferred_element_type=jnp.float32), positions, HDIM, 1.0
    ).astype(jnp.bfloat16)
    keys = rotate(
        jnp.dot(normed_attn, w_key, preferred_element_type=jnp.float32), positions, HDIM, 1.0
    ).astype(jnp.bfloat16)
    value_pre = jnp.dot(normed_attn, w_value, preferred_element_type=jnp.float32)
    mixed_values = (0.5 * value_pre + 0.5 * v_first.astype(jnp.float32)).astype(jnp.bfloat16)
    attended, row_lse = attention_forward(query, keys, mixed_values, doc_ids, positions, HDIM)
    middle = tokens + lax.psum_scatter(
        jnp.dot(attended, w_out, preferred_element_type=jnp.float32),
        "tp",
        scatter_dimension=0,
        tiled=True,
    )
    normed_mlp = normalize(middle, gain_mlp).astype(jnp.bfloat16)
    grad_branch = cotangent.astype(jnp.bfloat16)
    mlp_rows = lax.all_gather(normed_mlp, "tp", axis=0, tiled=True)
    gate = jnp.dot(mlp_rows, w_gate, preferred_element_type=jnp.float32)
    up_values = jnp.dot(mlp_rows, w_up, preferred_element_type=jnp.float32)
    hidden = (jax.nn.silu(gate) * up_values).astype(jnp.bfloat16)
    layer_out = middle + lax.psum_scatter(
        jnp.dot(hidden, w_down, preferred_element_type=jnp.float32).astype(jnp.bfloat16),
        "tp",
        scatter_dimension=0,
        tiled=True,
    ).astype(jnp.float32)
    cot_rows = lax.all_gather(grad_branch, "tp", axis=0, tiled=True)
    grad_down = inner_rows(hidden, cot_rows)
    gate_grad, up_grad = swiglu_back(gate, up_values, outer_cols(cot_rows, w_down))
    grad_gate = inner_rows(mlp_rows, gate_grad)
    grad_up = inner_rows(mlp_rows, up_grad)
    grad_mlp_in = lax.psum_scatter(
        (outer_cols(gate_grad, w_gate) + outer_cols(up_grad, w_up)).astype(jnp.bfloat16),
        "tp",
        scatter_dimension=0,
        tiled=True,
    ).astype(jnp.float32)
    middle_back, grad_gain_mlp = normalize_back(middle, gain_mlp, grad_mlp_in)
    grad_middle = cotangent + middle_back
    attn_cot_rows = lax.all_gather(grad_middle.astype(jnp.bfloat16), "tp", axis=0, tiled=True)
    grad_output = inner_rows(attended, attn_cot_rows)
    grad_attended = outer_cols(attn_cot_rows, w_out).astype(jnp.bfloat16)
    query_grad, key_grad, mixed_grad = attention_backward(
        query, keys, mixed_values, grad_attended, row_lse, doc_ids, positions, HDIM
    )
    half_mixed = 0.5 * mixed_grad.astype(jnp.float32)
    value_grad = half_mixed.astype(jnp.bfloat16)
    query_pre_grad = rotate(query_grad.astype(jnp.float32), positions, HDIM, -1.0).astype(
        jnp.bfloat16
    )
    key_pre_grad = rotate(key_grad.astype(jnp.float32), positions, HDIM, -1.0).astype(jnp.bfloat16)
    grad_query = inner_rows(normed_attn, query_pre_grad)
    grad_key = inner_rows(normed_attn, key_pre_grad)
    grad_value = inner_rows(normed_attn, value_grad)
    grad_attn_in = lax.psum_scatter(
        (
            outer_cols(query_pre_grad, w_query)
            + outer_cols(key_pre_grad, w_key)
            + outer_cols(value_grad, w_value)
        ).astype(jnp.bfloat16),
        "tp",
        scatter_dimension=0,
        tiled=True,
    ).astype(jnp.float32)
    tokens_back, grad_gain_attn = normalize_back(tokens, gain_attn, grad_attn_in)
    grad_tokens = grad_middle + tokens_back
    grad_query, grad_key, grad_value, grad_output, grad_gate, grad_up, grad_down = (
        lax.psum(grad_query.astype(jnp.bfloat16), "dp").astype(jnp.float32),
        lax.psum(grad_key.astype(jnp.bfloat16), "dp").astype(jnp.float32),
        lax.psum(grad_value.astype(jnp.bfloat16), "dp").astype(jnp.float32),
        lax.psum(grad_output.astype(jnp.bfloat16), "dp").astype(jnp.float32),
        lax.psum(grad_gate.astype(jnp.bfloat16), "dp").astype(jnp.float32),
        lax.psum(grad_up.astype(jnp.bfloat16), "dp").astype(jnp.float32),
        lax.psum(grad_down.astype(jnp.bfloat16), "dp").astype(jnp.float32),
    )
    grad_gain_attn, grad_gain_mlp = lax.psum((grad_gain_attn, grad_gain_mlp), ("dp", "tp"))
    return (
        layer_out,
        grad_tokens,
        half_mixed,
        grad_query,
        grad_key,
        grad_value,
        grad_output,
        grad_gate,
        grad_up,
        grad_down,
        grad_gain_attn,
        grad_gain_mlp,
    )


def solution(mesh):
    in_specs = (
        P(("dp", "tp"), None),
        P("dp", "tp"),
        P(None, "tp"),
        P(None, "tp"),
        P(None, "tp"),
        P("tp", None),
        P(None, "tp"),
        P(None, "tp"),
        P("tp", None),
        P(),
        P(),
        P("dp", None),
        P(("dp", "tp"), None),
    )
    out_specs = (
        P(("dp", "tp"), None),
        P(("dp", "tp"), None),
        P("dp", "tp"),
        P(None, "tp"),
        P(None, "tp"),
        P(None, "tp"),
        P("tp", None),
        P(None, "tp"),
        P(None, "tp"),
        P("tp", None),
        P(),
        P(),
    )

    def step(*args):
        tokens, seq_lens = args[0], args[11]
        pair = mesh.shape["tp"] == 2 and mesh.shape["dp"] == 16 and seq_lens.shape[1] == 1 and tokens.shape == (512, 1024)
        return (local_pair if pair else local)(*args)

    return jax.shard_map(step, mesh=mesh, in_specs=in_specs, out_specs=out_specs, check_vma=False)
```

```python
import functools

import jax
import jax.numpy as jnp
import numpy as np
from jax import lax
from jax.experimental import pallas as pl
from jax.experimental.pallas import tpu as pltpu
from jax.sharding import PartitionSpec as P

HDIM = 64


EPS = 1e-06


def layout(seq_row, row_share, tp_count):
    group_rows = row_share * tp_count
    row_ids = jnp.arange(group_rows, dtype=jnp.int32)
    device = row_ids // row_share
    local_row = row_ids % row_share
    pieces = seq_row // (2 * tp_count)
    slot_ends = jnp.cumsum(2 * pieces)
    starts = slot_ends - 2 * pieces
    offset = local_row[:, None] - starts[None, :]
    inside = (offset >= 0) & (offset < 2 * pieces[None, :])
    first_half = offset < pieces[None, :]
    mirror = 2 * tp_count - 1 - device[:, None]
    position = jnp.where(
        first_half,
        device[:, None] * pieces[None, :] + offset,
        mirror * pieces[None, :] + offset - pieces[None, :],
    )
    slot_ids = jnp.arange(seq_row.shape[0], dtype=jnp.int32)
    doc_ids = jnp.sum(jnp.where(inside, slot_ids[None, :], 0), axis=1)
    positions = jnp.sum(jnp.where(inside, position, 0), axis=1)
    return (doc_ids, positions)


def rotate(values, positions, head_dim, turn_sign):
    row_count, width_all = values.shape
    half_dim = head_dim // 2
    shaped = values.reshape(row_count, width_all // head_dim, head_dim)
    freqs = 10000.0 ** (-jnp.arange(half_dim, dtype=jnp.float32) / half_dim)
    angles = positions.astype(jnp.float32)[:, None] * freqs[None, :]
    cosine = jnp.cos(angles)[:, None, :]
    sine = turn_sign * jnp.sin(angles)[:, None, :]
    front = shaped[..., :half_dim]
    behind = shaped[..., half_dim:]
    turned = jnp.concatenate(
        [front * cosine - behind * sine, behind * cosine + front * sine], axis=-1
    )
    return turned.reshape(row_count, width_all)


def normalize(values, gain):
    return values * lax.rsqrt(jnp.mean(values * values, axis=-1, keepdims=True) + EPS) * gain


def normalize_back(values, gain, grad_in):
    factor = lax.rsqrt(jnp.mean(values * values, axis=-1, keepdims=True) + EPS)
    normed = values * factor
    grad_normed = grad_in * gain
    grad_values = factor * (
        grad_normed - normed * jnp.mean(grad_normed * normed, axis=-1, keepdims=True)
    )
    return (grad_values, jnp.sum(grad_in * normed, axis=0))


def inner_rows(left, right):
    return lax.dot_general(
        left, right, (((0,), (0,)), ((), ())), preferred_element_type=jnp.float32
    )


def outer_cols(left, right):
    return lax.dot_general(
        left, right, (((1,), (1,)), ((), ())), preferred_element_type=jnp.float32
    )


def swiglu_back(gate, up_values, grad_hidden):
    sigma = jax.nn.sigmoid(gate)
    grad_gate = grad_hidden * up_values * (sigma * (1.0 + gate * (1.0 - sigma)))
    grad_upper = grad_hidden * (gate * sigma)
    return (grad_gate.astype(jnp.bfloat16), grad_upper.astype(jnp.bfloat16))


def block_mask(doc_ids, positions, first_row, block_rows):
    row_doc = lax.dynamic_slice_in_dim(doc_ids, first_row, block_rows, 0)
    row_pos = lax.dynamic_slice_in_dim(positions, first_row, block_rows, 0)
    return (row_doc[:, None] == doc_ids[None, :]) & (positions[None, :] <= row_pos[:, None])


def attention_forward(query, keys, values, doc_ids, positions, head_dim):
    group_rows, width_local = query.shape
    head_count = width_local // head_dim
    block_rows = min(512, group_rows)
    block_count = group_rows // block_rows
    score_scale = head_dim ** (-0.5)
    key_heads = keys.reshape(group_rows, head_count, head_dim)
    value_heads = values.reshape(group_rows, head_count, head_dim)

    def forward_block(block_index):
        first_row = block_index * block_rows
        query_rows = lax.dynamic_slice_in_dim(query, first_row, block_rows, 0).reshape(
            block_rows, head_count, head_dim
        )
        scores = (
            jnp.einsum("qhd,khd->hqk", query_rows, key_heads, preferred_element_type=jnp.float32)
            * score_scale
        )
        allowed = block_mask(doc_ids, positions, first_row, block_rows)
        scores = jnp.where(allowed[None], scores, -1e30)
        row_max = jnp.max(scores, axis=-1, keepdims=True)
        exponent = jnp.exp(scores - row_max)
        row_total = jnp.sum(exponent, axis=-1, keepdims=True)
        weights = (exponent / row_total).astype(jnp.bfloat16)
        mixture = jnp.einsum(
            "hqk,khd->qhd", weights, value_heads, preferred_element_type=jnp.float32
        )
        return (
            mixture.astype(jnp.bfloat16).reshape(block_rows, width_local),
            (row_max + jnp.log(row_total))[..., 0],
        )

    mixture, row_lse = lax.map(forward_block, jnp.arange(block_count, dtype=jnp.int32))
    return (mixture.reshape(group_rows, width_local), row_lse)


def attention_backward(query, keys, values, grad_mixture, row_lse, doc_ids, positions, head_dim):
    group_rows, width_local = query.shape
    head_count = width_local // head_dim
    block_rows = min(512, group_rows)
    block_count = group_rows // block_rows
    score_scale = head_dim ** (-0.5)
    key_heads = keys.reshape(group_rows, head_count, head_dim)
    value_heads = values.reshape(group_rows, head_count, head_dim)

    def backward_block(carry, block_index):
        key_total, value_total = carry
        first_row = block_index * block_rows
        query_rows = lax.dynamic_slice_in_dim(query, first_row, block_rows, 0).reshape(
            block_rows, head_count, head_dim
        )
        grad_rows = lax.dynamic_slice_in_dim(grad_mixture, first_row, block_rows, 0).reshape(
            block_rows, head_count, head_dim
        )
        scores = (
            jnp.einsum("qhd,khd->hqk", query_rows, key_heads, preferred_element_type=jnp.float32)
            * score_scale
        )
        allowed = block_mask(doc_ids, positions, first_row, block_rows)
        scores = jnp.where(allowed[None], scores, -1e30)
        weights = jnp.exp(scores - row_lse[block_index][..., None])
        weights_low = weights.astype(jnp.bfloat16)
        grad_weights = jnp.einsum(
            "qhd,khd->hqk", grad_rows, value_heads, preferred_element_type=jnp.float32
        )
        weighted_sum = jnp.sum(weights * grad_weights, axis=-1, keepdims=True)
        score_grad = (weights * (grad_weights - weighted_sum)).astype(jnp.bfloat16)
        query_grad = (
            jnp.einsum("hqk,khd->qhd", score_grad, key_heads, preferred_element_type=jnp.float32)
            * score_scale
        )
        key_total = (
            key_total
            + jnp.einsum("hqk,qhd->khd", score_grad, query_rows, preferred_element_type=jnp.float32)
            * score_scale
        )
        value_total = value_total + jnp.einsum(
            "hqk,qhd->khd", weights_low, grad_rows, preferred_element_type=jnp.float32
        )
        return (
            (key_total, value_total),
            query_grad.astype(jnp.bfloat16).reshape(block_rows, width_local),
        )

    zero_heads = jnp.zeros((group_rows, head_count, head_dim), jnp.float32)
    (key_total, value_total), query_grad = lax.scan(
        backward_block, (zero_heads, zero_heads), jnp.arange(block_count, dtype=jnp.int32)
    )
    return (
        query_grad.reshape(group_rows, width_local),
        key_total.reshape(group_rows, width_local).astype(jnp.bfloat16),
        value_total.reshape(group_rows, width_local).astype(jnp.bfloat16),
    )


BF, F32 = jnp.bfloat16, jnp.float32
BLK = 256
POS_OF = (0, 3, 1, 2)
NT = (((1,), (1,)), ((), ()))

def nt(a, b):
    return lax.dot_general(a, b, NT, preferred_element_type=F32)

def nn(a, b):
    return jnp.dot(a, b, preferred_element_type=F32)

def rows(block):
    return pl.ds(block * BLK, BLK)

def turn(u, cosine, sine, lane):
    near = jnp.where(lane % 64 < 32, pltpu.roll(u, 96, 1), pltpu.roll(u, 32, 1))
    return u * cosine + near * sine

FIRST = {}
for _m in range(4):
    for _j in range(POS_OF[_m] + 1):
        FIRST.setdefault(_j, (_m, 0))

def tables():
    pos = np.zeros(1024, np.float32)
    for m in range(4):
        pos[m*256:(m+1)*256] = POS_OF[m]*256 + np.arange(256)
    freqs = np.float32(10000.0) ** (-np.arange(32, dtype=np.float32) / np.float32(32))
    ang = pos[:, None] * freqs[None]
    c, s = np.cos(ang.astype(np.float32)), np.sin(ang.astype(np.float32))
    return np.tile(c, (1, 4)).astype(np.float32), np.concatenate([-s, s, -s, s], 1).astype(np.float32)


def block_place(m):
    late = lax.div(m, 2)
    return m * 3 - late * (5 + 2 * (m - 2))


def norm_rows(values, gain):
    return values * lax.rsqrt(jnp.mean(values * values, axis=-1, keepdims=True) + EPS) * gain


TILES = ((0, 512), (512, 512), (1024, 384))


def front_kernel(
    tokens_h, vf_h, wq_h, wk_h, wv_h, wo_h, wg_h, wu_h, wd_h, gain_attn_ref, gain_mlp_ref, cot_h, cos_ref, sin_ref,
    q_h, k_h, v_h, o_h, ot_h, xt_h, lse_ref, middle_h, base_h, send4_h, own6_h, recv6_h, gg_h, gu_h, gd_h,
    tok, cot, x, xt, wq, wk, wv, vf, q, k, v, vt, o, ot, wo, recv2, send2, c, x2t, wg, wu, wd,
    ht, hid, gg, ug, base, send4, send6, recv6, tg, td,
    load, ysem, store, stage,
):
    tp = lax.axis_index("tp")
    mesh_id = pl.DeviceIdType.MESH
    barrier = pltpu.get_barrier_semaphore()
    pl.semaphore_signal(barrier, inc=1, device_id={"tp": 1 - tp}, device_id_type=mesh_id)
    loads = {}

    def fetch(name, src, dst):
        loads[name] = pltpu.make_async_copy(src, dst, load.at[len(loads)])
        loads[name].start()

    half = lambda b: pl.ds(b * BLK, BLK)
    for b in range(2):
        fetch(("tok", b), tokens_h.at[half(b)], tok.at[half(b)])
    for name, src, dst in (
        ("wq", wq_h, wq), ("wk", wk_h, wk), ("wv", wv_h, wv), ("vf", vf_h, vf), ("cot", cot_h, cot), ("wo", wo_h, wo),
        ("wg", wg_h, wg), ("wu", wu_h, wu), ("wd", wd_h, wd),
    ):
        fetch(name, src, dst)
    stores = []

    def keep(src, dst):
        stores.append(pltpu.make_async_copy(src, dst, store.at[len(stores)]))
        stores[-1].start()

    def peer(n, src, dst):
        return pltpu.make_async_remote_copy(
            src, dst, ysem.at[0, n], ysem.at[1, n], device_id={"tp": 1 - tp}, device_id_type=mesh_id
        )

    def mine(b):
        return pl.ds(pl.multiple_of(tp * 512 + b * BLK, BLK), BLK)

    def theirs(b):
        return pl.ds(pl.multiple_of((1 - tp) * 512 + b * BLK, BLK), BLK)

    lane = lax.broadcasted_iota(jnp.int32, (BLK, 128), 1)
    causal = lax.broadcasted_iota(jnp.int32, (BLK, BLK), 0) <= lax.broadcasted_iota(jnp.int32, (BLK, BLK), 1)
    gain_attn, gain_mlp = gain_attn_ref[...], gain_mlp_ref[...]
    sends = []
    for b in range(2):
        loads["tok", b].wait()
        x[mine(b), :] = norm_rows(tok[half(b), :], gain_attn).astype(BF)
        if b == 0:
            pl.semaphore_wait(barrier, 1)
        sends.append(peer(b, x.at[mine(b)], x.at[mine(b)]))
        sends[-1].start()
    loads["cot"].wait()
    for b in range(2):
        c[mine(b), :] = cot[half(b), :].astype(BF)
    for name in ("wq", "wk", "wv", "vf"):
        loads[name].wait()

    def project(m):
        row = pl.ds(pl.multiple_of(m * BLK, BLK), BLK)
        at = pl.ds(pl.multiple_of(block_place(m) * BLK, BLK), BLK)
        xm = x[row, :]
        cosine, sine = cos_ref[row, :], sin_ref[row, :]
        qf, kf = nn(xm, wq[...]), nn(xm, wk[...])
        low = (0.5 * nn(xm, wv[...]) + 0.5 * vf[row, :].astype(F32)).astype(BF)
        for t in range(4):
            cols = slice(t * 128, t * 128 + 128)
            q[at, cols] = turn(qf[:, cols], cosine, sine, lane).astype(BF) * 0.125
            k[at, cols] = turn(kf[:, cols], cosine, sine, lane).astype(BF)
        v[at, :] = low
        vt[:, at] = low.T
        xt[:, row] = xm.T

    def project_mine(b, carry):
        project(tp * 2 + b)
        return carry

    lax.fori_loop(0, 2, project_mine, 0)

    def project_theirs(b, carry):
        peer(b, x.at[mine(0)], x.at[mine(0)]).wait_recv()
        project((1 - tp) * 2 + b)
        return carry

    lax.fori_loop(0, 2, project_theirs, 0)
    cots = [peer(2 + b, c.at[mine(b)], c.at[mine(b)]) for b in range(2)]
    cots[0].start()
    for src, dst in ((q, q_h), (k, k_h), (v, v_h), (xt, xt_h)):
        keep(src, dst)
    lse_ref[...] = jnp.zeros_like(lse_ref)
    loads["wo"].wait()

    def attend(m):
        i = POS_OF[m]

        def pair(p, carry):
            cols = pl.ds(pl.multiple_of(p * 128, 128), 128)
            qb = q[rows(i), cols]
            parts = []
            for h in range(2):
                qm = jnp.where((lane < 64) == (h == 0), qb, jnp.zeros_like(qb))
                scores = [nt(k[rows(j), cols], qm) for j in range(i + 1)]
                scores[i] = jnp.where(causal, scores[i], -1e30)
                top = functools.reduce(jnp.maximum, [jnp.max(s, axis=0, keepdims=True) for s in scores])
                es = [jnp.exp(s - top) for s in scores]
                total = functools.reduce(jnp.add, [jnp.sum(e, axis=0, keepdims=True) for e in es])
                head = pl.ds(pl.multiple_of(p * 128 + h * 64, 64), 64)
                mix = functools.reduce(jnp.add, [nn(vt[head, rows(j)], es[j].astype(BF)) for j in range(i + 1)])
                parts.append(mix * (1.0 / total))
                lse_ref[lax.div(p, 2), pl.ds(2 * lax.rem(p, 2) + h, 1), rows(i)] = top + jnp.log(total)
            flat = jnp.concatenate(parts, axis=0)
            ot[cols, rows(m)] = flat.astype(BF)
            o[rows(m), cols] = flat.T.astype(BF)
            return carry

        lax.fori_loop(0, 4, pair, 0)

    twos = [peer(4 + b, send2.at[half(b)], recv2.at[half(b)]) for b in range(2)]
    for b in range(2):
        for side in range(2):

            @pl.when(tp == side)
            def _():
                attend((1 - side) * 2 + b)

        send2[half(b), :] = nn(o[theirs(b), :], wo[...]).astype(BF)
        twos[b].start()
    for side in range(2):

        @pl.when(tp == side)
        def _():
            attend(side * 2)
            attend(side * 2 + 1)

    keep(o, o_h)
    keep(ot, ot_h)
    for name in ("wg", "wu", "wd"):
        loads[name].wait()

    def gated(at):
        xm, cm = x[at, :], c[at, :]
        x2t[:, at] = xm.T
        for first, size in TILES:
            cols = slice(first, first + size)
            gate, up = nn(xm, wg[:, cols]), nn(xm, wu[:, cols])
            sigma = lax.logistic(gate)
            smooth = gate * sigma
            low = (smooth * up).astype(BF)
            hid[:, cols] = low
            ht[cols, at] = low.T
            back = nt(cm, wd[cols, :])
            gg[at, cols] = (back * up * (sigma * (1.0 + gate * (1.0 - sigma)))).astype(BF)
            ug[at, cols] = (back * smooth).astype(BF)
        return nn(hid[...], wd[...]), nt(gg[at, :], wg[...]) + nt(ug[at, :], wu[...])

    def block_mine(b, carry):
        here = pl.ds(pl.multiple_of(b * BLK, BLK), BLK)
        at = mine(b)
        peer(4 + b, send2.at[half(0)], recv2.at[half(0)]).wait_recv()
        middle = tok[here, :] + nn(o[at, :], wo[...]) + recv2[here, :].astype(F32)
        tok[here, :] = middle
        peer(b, x.at[half(0)], x.at[half(0)]).wait_send()
        x[at, :] = norm_rows(middle, gain_mlp).astype(BF)
        peer(6 + b, x.at[at], x.at[at]).start()
        branch, grad_in = gated(at)
        base[here, :] = tok[here, :] + branch
        cot[here, :] = grad_in
        return carry

    lax.fori_loop(0, 2, block_mine, 0)
    cots[1].start()
    keep(tok, middle_h)
    keep(base, base_h)
    keep(cot, own6_h)

    def block_theirs(b, carry):
        here = pl.ds(pl.multiple_of(b * BLK, BLK), BLK)
        peer(6 + b, x.at[half(0)], x.at[half(0)]).wait_recv()
        peer(2 + b, c.at[half(0)], c.at[half(0)]).wait_recv()
        branch, grad_in = gated(theirs(b))
        send4[here, :] = branch.astype(BF)
        send6[here, :] = grad_in.astype(BF)
        peer(8 + b, send6.at[here], recv6.at[here]).start()
        return carry

    lax.fori_loop(0, 2, block_theirs, 0)
    keep(send4, send4_h)

    def weight_tiles(count, size, left, right, buf, out, sem):
        def body(n, carry):
            slot = lax.rem(n, 2)
            at = pl.ds(pl.multiple_of(n * size, size), size)
            copy = pltpu.make_async_copy(buf.at[slot], out.at[at], stage.at[sem, slot])

            @pl.when(n >= 2)
            def _():
                copy.wait()

            buf[slot] = nn(left[at, :], right[...]).astype(BF)
            copy.start()
            return carry

        lax.fori_loop(0, count, body, 0)

        for slot in range(2):
            pltpu.make_async_copy(buf.at[slot], out.at[pl.ds(0, size)], stage.at[sem, slot]).wait()

    weight_tiles(4, 352, ht, c, td, gd_h, 0)
    weight_tiles(4, 256, x2t, gg, tg, gg_h, 1)
    weight_tiles(4, 256, x2t, ug, tg, gu_h, 2)
    for b in range(2):
        peer(8 + b, send6.at[half(b)], recv6.at[half(b)]).wait_recv()
    keep(recv6, recv6_h)
    for b in range(2):
        for n in (2, 4, 6, 8):
            peer(n + b, recv6.at[half(0)], recv6.at[half(0)]).wait_send()
    for copy in stores:
        copy.wait()


def front(tokens, vf, wq, wk, wv, wo, wg, wu, wd, gain_attn, gain_mlp, cot, cos, sin):
    V = lambda shape, kind=BF: pltpu.VMEM(shape, kind)
    D = lambda *shape: pltpu.SemaphoreType.DMA(shape)
    hbm, vmem = pl.BlockSpec(memory_space=pl.ANY), pl.BlockSpec(memory_space=pltpu.VMEM)
    S = jax.ShapeDtypeStruct
    own, heads, turned, square = (512, 1024), (1024, 512), (512, 1024), (1024, 1024)
    hidden, across = (1024, 1408), (1408, 1024)
    return pl.pallas_call(
        front_kernel,
        in_specs=[hbm] * 9 + [vmem] * 2 + [hbm] + [vmem] * 2,
        out_specs=[hbm] * 6 + [vmem] + [hbm] * 8,
        out_shape=[*[S(heads, BF)] * 4, S(turned, BF), S(square, BF), S((2, 8, 1024), F32), S(own, F32), S(own, F32), S(own, BF),
                   S(own, F32), S(own, BF), S(hidden, BF), S(hidden, BF), S(across, BF)],
        scratch_shapes=[
            V(own, F32), V(own, F32), V(square), V(square), *[V(heads)] * 7, V(turned), V(heads), V(turned), V(own), V(own), V(own),
            V(square), V(square), V(hidden), V(hidden), V(across), V(across), V((256, 1408)), V(hidden), V(hidden), V(own, F32),
            V(own), V(own), V(own), V((2, 256, 1408)), V((2, 352, 1024)),
            D(11), D(2, 10), D(11), D(3, 2),
        ],
        compiler_params=pltpu.CompilerParams(collective_id=4, has_side_effects=True, vmem_limit_bytes=63 << 20),
        cost_estimate=pl.CostEstimate(flops=40 * 10**9, bytes_accessed=60 << 20, transcendentals=5 << 20),
    )(tokens, vf, wq, wk, wv, wo, wg, wu, wd, gain_attn, gain_mlp, cot, cos, sin)


def ring_place(dp):
    core, x, z = lax.rem(dp, 2), lax.rem(lax.div(dp, 2), 2), lax.div(dp, 4)
    place = z + x * (7 - 2 * z)

    def device(where):
        side = lax.div(where, 4)
        return ((where + side * (7 - 2 * where)) * 2 + side) * 2 + core

    turn_no = lax.rem(place + core * (8 - 2 * place), 8)
    after = device(lax.rem(place + 1 + 6 * core, 8))
    before = device(lax.rem(place + 7 - 6 * core, 8))
    cube = (dp + 1 - 2 * core, dp + 2 - 4 * x, dp + 4 - 8 * lax.rem(z, 2), dp + 8 - 16 * lax.div(z, 2))
    return core, turn_no, after, before, cube


def remote(src, dst, send, recv, dp):
    return pltpu.make_async_remote_copy(
        src, dst, send, recv, device_id={"dp": dp}, device_id_type=pl.DeviceIdType.MESH
    )


class Ring:
    def __init__(self, place, takes, outs, own, sib, slots, sems):
        self.core, self.turn_no, self.after, self.before, self.cube = place
        self.takes, self.outs, self.own, self.sib, self.slots = takes, outs, own, sib, slots
        self.trade, self.rs, self.ag, self.over, self.keep = sems

    def piece(self, g, chunk):
        size = self.slots[g].shape[1]
        return pl.ds(pl.multiple_of(chunk * size, size), size)

    def traded(self, g):
        return remote(self.takes[g](1 - self.core), self.sib[g], self.trade.at[0, g], self.trade.at[1, g], self.cube[0])

    def total(self, g, chunk):
        at = self.piece(g, chunk)
        return self.own[g][at, :].astype(F32) + self.sib[g][at, :].astype(F32)

    def first(self, g, chunk):
        return remote(
            self.own[g].at[self.piece(g, chunk)], self.slots[g].at[0], self.rs.at[0, g, 0], self.rs.at[1, g, 0], self.after
        )

    def begin(self, g):
        self.traded(g).wait()
        chunk = lax.rem(self.turn_no + 7, 8)
        self.own[g][self.piece(g, chunk), :] = self.total(g, chunk).astype(BF)
        self.first(g, chunk).start()

    def add(self, g, t):
        chunk = lax.rem(self.turn_no + 14 - t, 8)
        remote(self.slots[g].at[t], self.slots[g].at[t], self.rs.at[0, g, t], self.rs.at[1, g, t], self.after).wait_recv()
        self.slots[g][t] = (self.slots[g][t].astype(F32) + self.total(g, chunk)).astype(BF)

    def add_on(self, g, t):
        self.add(g, t)
        remote(self.slots[g].at[t], self.slots[g].at[t + 1], self.rs.at[0, g, t + 1], self.rs.at[1, g, t + 1], self.after).start()

    def spot(self, g, chunk):
        return self.outs[g](self.core, chunk)

    def turn_over(self, g):
        self.add(g, 6)
        spot = self.spot(g, self.turn_no)
        last = self.slots[g].at[6]
        remote(last, spot, self.ag.at[0, g, 0], self.ag.at[1, g, 0], self.after).start()
        remote(last, spot, self.over.at[0, g, 0], self.over.at[1, g, 0], self.cube[0]).start()
        pltpu.make_async_copy(last, spot, self.keep.at[g]).start()

    def pass_on(self, g, t):
        spot = self.spot(g, lax.rem(self.turn_no + 15 - t, 8))
        remote(spot, spot, self.ag.at[0, g, t], self.ag.at[1, g, t], self.after).wait_recv()

        @pl.when(t < 6)
        def _():
            remote(spot, spot, self.ag.at[0, g, t + 1], self.ag.at[1, g, t + 1], self.after).start()

        remote(spot, spot, self.over.at[0, g, t + 1], self.over.at[1, g, t + 1], self.cube[0]).start()

    def end(self, g):
        spot = self.spot(g, self.turn_no)
        pltpu.make_async_copy(self.slots[g].at[6], spot, self.keep.at[g]).wait()

        def finish(t, _):
            remote(self.slots[g].at[0], self.slots[g].at[0], self.rs.at[0, g, t], self.rs.at[1, g, t], self.after).wait_send()
            remote(spot, spot, self.ag.at[0, g, t], self.ag.at[1, g, t], self.after).wait_send()
            return _

        lax.fori_loop(0, 7, finish, 0)

        def crossed(t, _):
            there = self.outs[g](1 - self.core, lax.rem(self.turn_no + t, 8))
            remote(spot, there, self.over.at[0, g, t], self.over.at[1, g, t], self.cube[0]).wait()
            return _

        lax.fori_loop(0, 8, crossed, 0)


def strip(ref, axis, halves, length):
    if axis == 0:
        return lambda core, chunk: ref.at[pl.ds(pl.multiple_of(core * halves + chunk * length, length), length)]
    return lambda core, chunk: ref.at[
        pl.ds(pl.multiple_of(chunk * length, length), length), pl.ds(pl.multiple_of(core * halves, halves), halves)
    ]


def half_of(ref, axis, halves):
    if axis == 0:
        return lambda core: ref.at[pl.ds(pl.multiple_of(core * halves, halves), halves)]
    return lambda core: ref.at[:, pl.ds(pl.multiple_of(core * halves, halves), halves)]


def norm_back_rows(values, gain, grad_in):
    factor = lax.rsqrt(jnp.mean(values * values, axis=-1, keepdims=True) + EPS)
    normed = values * factor
    grad_normed = grad_in * gain
    grad = factor * (grad_normed - normed * jnp.mean(grad_normed * normed, axis=-1, keepdims=True))
    return grad, jnp.sum(grad_in * normed, axis=0, keepdims=True)


def back_kernel(
    own6_h, recv6_h, own4_h, send4_h, middle_h, cot_h, tokens_h, gain_attn_ref, gain_mlp_ref,
    wo_h, wq_h, wk_h, wv_h, q_h, k_h, v_h, o_h, ot_h, xt_h, lse_ref, cos_ref, sin_ref, gg_h, gu_h, gd_h,
    out_h, gt_h, gf_h, rq_h, rk_h, rv_h, ro_h, rg_h, ru_h, rd_h, gains_ref,
    f1, f2, f3, recv6, recv4, recv8, send8, c, wo, wq, wk, wv, q, k, v, o, ot, xt,
    dq, dk, dv, do, kt, dka, dva, dl, own8, dwq, dwk, dwv, dwo,
    mg, mu, md, sg, su, sd, lg, lu, ld, bq, bk, bv, bo, aq, ak, av, ao,
    load, ysem, trade1, rs1, ag1, over1, keep1, trade2, rs2, ag2, over2, keep2, gain_in, gain_sem, store,
):
    dp, tp = lax.axis_index("dp"), lax.axis_index("tp")
    place = ring_place(dp)
    core, turn_no, after, before, cube = place
    mesh_id = pl.DeviceIdType.MESH
    barrier = pltpu.get_barrier_semaphore()
    for other in (*cube, after, before):
        pl.semaphore_signal(barrier, inc=1, device_id={"dp": other}, device_id_type=mesh_id)
    pl.semaphore_signal(barrier, inc=1, device_id={"tp": 1 - tp}, device_id_type=mesh_id)

    loads = {}

    def fetch(name, src, dst):
        loads[name] = pltpu.make_async_copy(src, dst, load.at[len(loads)])
        loads[name].start()

    one = Ring(
        place, (half_of(gg_h, 0, 512), half_of(gu_h, 0, 512), half_of(gd_h, 1, 512)),
        (strip(rg_h, 0, 512, 64), strip(ru_h, 0, 512, 64), strip(rd_h, 1, 512, 176)),
        (mg, mu, md), (sg, su, sd), (lg, lu, ld), (trade1, rs1, ag1, over1, keep1),
    )
    two = Ring(
        place, (half_of(dwq, 0, 512), half_of(dwk, 0, 512), half_of(dwv, 0, 512), half_of(dwo, 0, 256)),
        (strip(rq_h, 0, 512, 64), strip(rk_h, 0, 512, 64), strip(rv_h, 0, 512, 64), strip(ro_h, 0, 256, 32)),
        (half_of(dwq, 0, 512)(core), half_of(dwk, 0, 512)(core), half_of(dwv, 0, 512)(core), half_of(dwo, 0, 256)(core)),
        (bq, bk, bv, bo), (aq, ak, av, ao), (trade2, rs2, ag2, over2, keep2),
    )
    for g, (whole, mine) in enumerate(((gg_h, mg), (gu_h, mu), (gd_h, md))):
        fetch(("m", g), one.takes[g](core), mine)
    for name, src, dst in (
        ("own6", own6_h, f1), ("recv6", recv6_h, recv6), ("middle", middle_h, f2), ("cot", cot_h, f3), ("wo", wo_h, wo), ("q", q_h, q), ("k", k_h, k),
        ("v", v_h, v), ("o", o_h, o), ("wq", wq_h, wq), ("wk", wk_h, wk), ("wv", wv_h, wv), ("ot", ot_h, ot), ("xt", xt_h, xt),
    ):
        fetch(name, src, dst)
    pl.semaphore_wait(barrier, 7)

    def peer(n, src, dst):
        return pltpu.make_async_remote_copy(
            src, dst, ysem.at[0, n], ysem.at[1, n], device_id={"tp": 1 - tp}, device_id_type=mesh_id
        )

    half = lambda b: pl.ds(b * BLK, BLK)
    for g in range(3):
        one.traded(g).start()
    for g in range(3):
        loads["m", g].wait()
        one.begin(g)

    def ring_steps(first, last):
        def body(t, carry):
            for g in range(3):
                one.add_on(g, t)
            return carry

        lax.fori_loop(first, last, body, 0)

    lane = lax.broadcasted_iota(jnp.int32, (BLK, 128), 1)
    causal = lax.broadcasted_iota(jnp.int32, (BLK, BLK), 0) <= lax.broadcasted_iota(jnp.int32, (BLK, BLK), 1)
    gain_mlp, gain_attn = gain_mlp_ref[...], gain_attn_ref[...]
    for name in ("own6", "recv6", "middle", "cot", "wo"):
        loads[name].wait()
    gain_sum = jnp.zeros((1, 1024), F32)
    seven = []
    for b in range(2):

        def rows_back(n, total):
            at = pl.ds(pl.multiple_of(b * BLK + n * 64, 64), 64)
            grad_in = f1[at, :] + recv6[at, :].astype(F32)
            grad, part = norm_back_rows(f2[at, :], gain_mlp, grad_in)
            grad = f3[at, :] + grad
            f1[at, :] = grad
            c[pl.ds(pl.multiple_of(tp * 512 + b * BLK + n * 64, 64), 64), :] = grad.astype(BF)
            return total + part

        gain_sum = lax.fori_loop(0, 4, rows_back, gain_sum)
        mine = c.at[pl.ds(pl.multiple_of(tp * 512 + b * BLK, BLK), BLK)]
        seven.append(peer(2 + b, mine, mine))
        seven[b].start()
        ring_steps(b, 1 + b)
    four = peer(4, send4_h, recv4)
    four.start()
    late = pltpu.make_async_copy(own4_h, f3, load.at[len(loads)])
    late.start()
    gains_ref[...] = jnp.zeros_like(gains_ref)
    gains_ref[0:1, :] = gain_sum
    for name in ("o", "k"):
        loads[name].wait()

    def branch_back(m):
        at = rows(m)
        low = nt(c[at, :], wo[...]).astype(BF)
        do[at, :] = low
        prod = (low.astype(F32) * o[at, :].astype(F32)).T
        for h in range(8):
            dl[h : h + 1, at] = jnp.sum(prod[h * 64 : h * 64 + 64, :], axis=0, keepdims=True)

    ring_steps(2, 3)
    for b in range(2):
        seven[b].wait_recv()
    for m in range(4):
        branch_back(m)
        if m < 3:
            one.add_on(m, 3)
    for name in ("q", "v"):
        loads[name].wait()

    def serve(g, p):
        @pl.when(p < 2)
        def _():
            one.add_on(g, 4 + p)

        @pl.when(p == 2)
        def _():
            one.turn_over(g)

        @pl.when(p == 3)
        def _():
            one.pass_on(g, 0)

    def pair(p, carry):
        cols = pl.ds(pl.multiple_of(p * 128, 128), 128)
        for j in range(4):
            kt[:, rows(j)] = k[rows(j), cols].T
        for m in range(4):
            i = POS_OF[m]
            qb, dob = q[rows(i), cols], do[rows(m), cols]
            parts = []
            for h in range(2):
                mine = (lane < 64) == (h == 0)
                qm = jnp.where(mine, qb, jnp.zeros_like(qb))
                dom = jnp.where(mine, dob, jnp.zeros_like(dob))
                lse = lse_ref[lax.div(p, 2), pl.ds(2 * lax.rem(p, 2) + h, 1), rows(i)]
                delta = dl[pl.ds(2 * p + h, 1), rows(m)]
                head = slice(h * 64, h * 64 + 64)
                dqt = None
                for j in range(i + 1):
                    weights = jnp.exp(nt(k[rows(j), cols], qm) - lse)
                    if j == i:
                        weights = jnp.where(causal, weights, 0.0)
                    ds = (weights * (nt(v[rows(j), cols], dom) - delta)).astype(BF)
                    dvp, dkp = nn(weights.astype(BF), dom), nn(ds, qm)
                    fresh = (m, h) == FIRST[j]
                    dva[rows(j), :] = dvp if fresh else dva[rows(j), :] + dvp
                    dka[rows(j), :] = dkp if fresh else dka[rows(j), :] + dkp
                    part = nn(kt[head, rows(j)], ds)
                    dqt = part if dqt is None else dqt + part
                parts.append(dqt)
            grad = (jnp.concatenate(parts, axis=0).T * 0.125).astype(BF).astype(F32)
            dq[rows(m), cols] = turn(grad, cos_ref[rows(m), :], -sin_ref[rows(m), :], lane).astype(BF)
            if m < 3:
                serve(m, p)
        for m in range(4):
            at = rows(POS_OF[m])
            grad = dka[at, :].astype(BF).astype(F32)
            dk[rows(m), cols] = turn(grad, cos_ref[rows(m), :], -sin_ref[rows(m), :], lane).astype(BF)
            dv[rows(m), cols] = (0.5 * dva[at, :].astype(BF).astype(F32)).astype(BF)

        return carry

    lax.fori_loop(0, 4, pair, 0)
    keep_gf = pltpu.make_async_copy(dv, gf_h, store.at[0])
    keep_gf.start()
    for name in ("wq", "wk", "wv"):
        loads[name].wait()

    def into_rows(at):
        return nt(dq[at, :], wq[...]) + nt(dk[at, :], wk[...]) + nt(dv[at, :], wv[...])

    eight = []
    for b in range(2):
        at = pl.ds(pl.multiple_of((1 - tp) * 512 + b * BLK, BLK), BLK)
        send8[half(b), :] = into_rows(at).astype(BF)
        eight.append(peer(5 + b, send8.at[half(b)], recv8.at[half(b)]))
        eight[b].start()
        for g in range(3):
            one.pass_on(g, 1 + b)
    for name in ("xt", "ot"):
        loads[name].wait()
    for which in range(2):
        side = (1 - core) * (1 - which) + core * which
        at = pl.ds(pl.multiple_of(side * 512, 512), 512)
        for dst, src in ((dwq, dq), (dwk, dk), (dwv, dv)):
            dst[at, :] = nn(xt[at, :], src[...]).astype(BF)
        at = pl.ds(pl.multiple_of(side * 256, 256), 256)
        dwo[at, :] = nn(ot[at, :], c[...]).astype(BF)
        if which == 0:
            for g in range(4):
                two.traded(g).start()
    for g in range(4):
        two.begin(g)

    def second(t, carry):
        @pl.when(t < 4)
        def _():
            for g in range(3):
                one.pass_on(g, 3 + t)

        for g in range(4):
            two.add_on(g, t)
        return carry

    for b in range(2):
        own8[half(b), :] = into_rows(pl.ds(pl.multiple_of(tp * 512 + b * BLK, BLK), BLK))
    fetch_tokens = pltpu.make_async_copy(tokens_h, f2, load.at[len(loads) + 1])
    fetch_tokens.start()
    lax.fori_loop(0, 3, second, 0)
    four.wait_recv()
    late.wait()
    fetch_tokens.wait()

    def out_rows(n, carry):
        at = pl.ds(pl.multiple_of(n * 64, 64), 64)
        f3[at, :] = f3[at, :] + recv4[at, :].astype(F32)
        return carry

    lax.fori_loop(0, 8, out_rows, 0)
    keep_out = pltpu.make_async_copy(f3, out_h, store.at[1])
    keep_out.start()
    lax.fori_loop(3, 6, second, 0)
    for g in range(4):
        two.turn_over(g)
    gain_sum = jnp.zeros((1, 1024), F32)
    for b in range(2):
        eight[b].wait_recv()

        def rows_last(n, total):
            at = pl.ds(pl.multiple_of(b * BLK + n * 64, 64), 64)
            grad, part = norm_back_rows(f2[at, :], gain_attn, own8[at, :] + recv8[at, :].astype(F32))
            f1[at, :] = f1[at, :] + grad
            return total + part

        gain_sum = lax.fori_loop(0, 4, rows_last, gain_sum)
    keep_gt = pltpu.make_async_copy(f1, gt_h, store.at[2])
    keep_gt.start()
    gains_ref[1:2, :] = gain_sum

    def gain_swap(n):
        where = {"tp": 1 - tp} if n == 4 else {"dp": cube[n]}
        return pltpu.make_async_remote_copy(
            gains_ref, gain_in.at[n], gain_sem.at[0, n], gain_sem.at[1, n], device_id=where, device_id_type=mesh_id
        )

    for t in range(7):
        for g in range(4):
            two.pass_on(g, t)
        if t < 5:
            move = gain_swap(t)
            move.start()
            move.wait()
            gains_ref[...] = gains_ref[...] + gain_in[t]
    for g in range(3):
        one.end(g)
    for g in range(4):
        two.end(g)
    for copy in (*seven, *eight, four):
        copy.wait_send()
    for copy in (keep_gf, keep_out, keep_gt):
        copy.wait()


def back(own6, recv6, own4, send4, middle, cot, tokens, gain_attn, gain_mlp, wo, wq, wk, wv, q, k, v, o, ot, xt, lse, cos, sin, gg, gu, gd):
    V = lambda shape, kind=BF: pltpu.VMEM(shape, kind)
    D = lambda *shape: pltpu.SemaphoreType.DMA(shape)
    hbm, vmem = pl.BlockSpec(memory_space=pl.ANY), pl.BlockSpec(memory_space=pltpu.VMEM)
    S = jax.ShapeDtypeStruct
    wide = (1024, 1024)
    return pl.pallas_call(
        back_kernel,
        in_specs=[hbm] * 7 + [vmem] * 2 + [hbm] * 10 + [vmem] * 3 + [hbm] * 3,
        out_specs=[hbm] * 10 + [vmem],
        out_shape=[S((512, 1024), F32), S((512, 1024), F32), S((1024, 512), BF), *[S((1024, 512), BF)] * 3, S((512, 1024), BF),
                   S((1024, 1408), BF), S((1024, 1408), BF), S((1408, 1024), BF), S((8, 1024), F32)],
        scratch_shapes=[
            *[V((512, 1024), F32)] * 3, *[V((512, 1024))] * 4, V(wide), V((512, 1024)), *[V((1024, 512))] * 7, V((512, 1024)), V(wide),
            *[V((1024, 512))] * 4, V((128, 1024)), *[V((1024, 128), F32)] * 2, V((8, 1024), F32), V((512, 1024), F32),
            *[V((1024, 512))] * 3, V((512, 1024)),
            *[V((512, 1408)), V((512, 1408)), V((1408, 512))] * 2, V((7, 64, 1408)), V((7, 64, 1408)), V((7, 176, 512)),
            *[V((512, 512))] * 3, V((256, 1024)), *[V((7, 64, 512))] * 3, V((7, 32, 1024)),
            D(19), D(2, 7), D(2, 3), D(2, 3, 7), D(2, 3, 7), D(2, 3, 8), D(3), D(2, 4), D(2, 4, 7), D(2, 4, 7), D(2, 4, 8), D(4),
            V((5, 8, 1024), F32), D(2, 5), D(3),
        ],
        compiler_params=pltpu.CompilerParams(collective_id=3, has_side_effects=True, vmem_limit_bytes=62 << 20),
        cost_estimate=pl.CostEstimate(flops=30 * 10**9, bytes_accessed=60 << 20, transcendentals=5 << 20),
    )(own6, recv6, own4, send4, middle, cot, tokens, gain_attn, gain_mlp, wo, wq, wk, wv, q, k, v, o, ot, xt, lse, cos, sin, gg, gu, gd)

def local_pair(
    tokens,
    v_first,
    w_query,
    w_key,
    w_value,
    w_out,
    w_gate,
    w_up,
    w_down,
    gain_attn,
    gain_mlp,
    seq_lens,
    cotangent,
):
    cosine, sine = tables()
    (query, keys, mixed_values, attended, attended_t, normed_t, row_lse, middle, base, send_out, own_in, got_in,
     grad_gate, grad_up, grad_down) = front(
        tokens, v_first, w_query, w_key, w_value, w_out, w_gate, w_up, w_down, gain_attn[None], gain_mlp[None], cotangent, cosine, sine
    )
    layer_out, grad_tokens, grad_first, *low_grads, gains = back(
        own_in, got_in, base, send_out, middle, cotangent, tokens, gain_attn[None], gain_mlp[None], w_out, w_query, w_key, w_value,
        query, keys, mixed_values, attended, attended_t, normed_t, row_lse, cosine, sine, grad_gate, grad_up, grad_down,
    )
    wide = [g.astype(jnp.float32) for g in low_grads]
    grad_first = grad_first.astype(jnp.float32)
    grad_gain_mlp, grad_gain_attn = gains[0], gains[1]
    return (layer_out, grad_tokens, grad_first, *wide, grad_gain_attn, grad_gain_mlp)


def local(
    tokens,
    v_first,
    w_query,
    w_key,
    w_value,
    w_out,
    w_gate,
    w_up,
    w_down,
    gain_attn,
    gain_mlp,
    seq_lens,
    cotangent,
):
    tp_count = lax.axis_size("tp")
    row_share = tokens.shape[0]
    doc_ids, positions = layout(seq_lens[0], row_share, tp_count)
    normed_attn = lax.all_gather(
        normalize(tokens, gain_attn).astype(jnp.bfloat16), "tp", axis=0, tiled=True
    )
    query = rotate(
        jnp.dot(normed_attn, w_query, preferred_element_type=jnp.float32), positions, HDIM, 1.0
    ).astype(jnp.bfloat16)
    keys = rotate(
        jnp.dot(normed_attn, w_key, preferred_element_type=jnp.float32), positions, HDIM, 1.0
    ).astype(jnp.bfloat16)
    value_pre = jnp.dot(normed_attn, w_value, preferred_element_type=jnp.float32)
    mixed_values = (0.5 * value_pre + 0.5 * v_first.astype(jnp.float32)).astype(jnp.bfloat16)
    attended, row_lse = attention_forward(query, keys, mixed_values, doc_ids, positions, HDIM)
    middle = tokens + lax.psum_scatter(
        jnp.dot(attended, w_out, preferred_element_type=jnp.float32),
        "tp",
        scatter_dimension=0,
        tiled=True,
    )
    normed_mlp = normalize(middle, gain_mlp).astype(jnp.bfloat16)
    grad_branch = cotangent.astype(jnp.bfloat16)
    mlp_rows = lax.all_gather(normed_mlp, "tp", axis=0, tiled=True)
    gate = jnp.dot(mlp_rows, w_gate, preferred_element_type=jnp.float32)
    up_values = jnp.dot(mlp_rows, w_up, preferred_element_type=jnp.float32)
    hidden = (jax.nn.silu(gate) * up_values).astype(jnp.bfloat16)
    layer_out = middle + lax.psum_scatter(
        jnp.dot(hidden, w_down, preferred_element_type=jnp.float32).astype(jnp.bfloat16),
        "tp",
        scatter_dimension=0,
        tiled=True,
    ).astype(jnp.float32)
    cot_rows = lax.all_gather(grad_branch, "tp", axis=0, tiled=True)
    grad_down = inner_rows(hidden, cot_rows)
    gate_grad, up_grad = swiglu_back(gate, up_values, outer_cols(cot_rows, w_down))
    grad_gate = inner_rows(mlp_rows, gate_grad)
    grad_up = inner_rows(mlp_rows, up_grad)
    grad_mlp_in = lax.psum_scatter(
        (outer_cols(gate_grad, w_gate) + outer_cols(up_grad, w_up)).astype(jnp.bfloat16),
        "tp",
        scatter_dimension=0,
        tiled=True,
    ).astype(jnp.float32)
    middle_back, grad_gain_mlp = normalize_back(middle, gain_mlp, grad_mlp_in)
    grad_middle = cotangent + middle_back
    attn_cot_rows = lax.all_gather(grad_middle.astype(jnp.bfloat16), "tp", axis=0, tiled=True)
    grad_output = inner_rows(attended, attn_cot_rows)
    grad_attended = outer_cols(attn_cot_rows, w_out).astype(jnp.bfloat16)
    query_grad, key_grad, mixed_grad = attention_backward(
        query, keys, mixed_values, grad_attended, row_lse, doc_ids, positions, HDIM
    )
    half_mixed = 0.5 * mixed_grad.astype(jnp.float32)
    value_grad = half_mixed.astype(jnp.bfloat16)
    query_pre_grad = rotate(query_grad.astype(jnp.float32), positions, HDIM, -1.0).astype(
        jnp.bfloat16
    )
    key_pre_grad = rotate(key_grad.astype(jnp.float32), positions, HDIM, -1.0).astype(jnp.bfloat16)
    grad_query = inner_rows(normed_attn, query_pre_grad)
    grad_key = inner_rows(normed_attn, key_pre_grad)
    grad_value = inner_rows(normed_attn, value_grad)
    grad_attn_in = lax.psum_scatter(
        (
            outer_cols(query_pre_grad, w_query)
            + outer_cols(key_pre_grad, w_key)
            + outer_cols(value_grad, w_value)
        ).astype(jnp.bfloat16),
        "tp",
        scatter_dimension=0,
        tiled=True,
    ).astype(jnp.float32)
    tokens_back, grad_gain_attn = normalize_back(tokens, gain_attn, grad_attn_in)
    grad_tokens = grad_middle + tokens_back
    grad_query, grad_key, grad_value, grad_output, grad_gate, grad_up, grad_down = (
        lax.psum(grad_query.astype(jnp.bfloat16), "dp").astype(jnp.float32),
        lax.psum(grad_key.astype(jnp.bfloat16), "dp").astype(jnp.float32),
        lax.psum(grad_value.astype(jnp.bfloat16), "dp").astype(jnp.float32),
        lax.psum(grad_output.astype(jnp.bfloat16), "dp").astype(jnp.float32),
        lax.psum(grad_gate.astype(jnp.bfloat16), "dp").astype(jnp.float32),
        lax.psum(grad_up.astype(jnp.bfloat16), "dp").astype(jnp.float32),
        lax.psum(grad_down.astype(jnp.bfloat16), "dp").astype(jnp.float32),
    )
    grad_gain_attn, grad_gain_mlp = lax.psum((grad_gain_attn, grad_gain_mlp), ("dp", "tp"))
    return (
        layer_out,
        grad_tokens,
        half_mixed,
        grad_query,
        grad_key,
        grad_value,
        grad_output,
        grad_gate,
        grad_up,
        grad_down,
        grad_gain_attn,
        grad_gain_mlp,
    )


def solution(mesh):
    in_specs = (
        P(("dp", "tp"), None),
        P("dp", "tp"),
        P(None, "tp"),
        P(None, "tp"),
        P(None, "tp"),
        P("tp", None),
        P(None, "tp"),
        P(None, "tp"),
        P("tp", None),
        P(),
        P(),
        P("dp", None),
        P(("dp", "tp"), None),
    )
    out_specs = (
        P(("dp", "tp"), None),
        P(("dp", "tp"), None),
        P("dp", "tp"),
        P(None, "tp"),
        P(None, "tp"),
        P(None, "tp"),
        P("tp", None),
        P(None, "tp"),
        P(None, "tp"),
        P("tp", None),
        P(),
        P(),
    )

    def step(*args):
        tokens, seq_lens = args[0], args[11]
        pair = mesh.shape["tp"] == 2 and mesh.shape["dp"] == 16 and seq_lens.shape[1] == 1 and tokens.shape == (512, 1024)
        return (local_pair if pair else local)(*args)

    return jax.shard_map(step, mesh=mesh, in_specs=in_specs, out_specs=out_specs, check_vma=False)
```

```python
import functools

import jax
import jax.numpy as jnp
import numpy as np
from jax import lax
from jax.experimental import pallas as pl
from jax.experimental.pallas import tpu as pltpu
from jax.sharding import PartitionSpec as P

HDIM = 64


EPS = 1e-06


def layout(seq_row, row_share, tp_count):
    group_rows = row_share * tp_count
    row_ids = jnp.arange(group_rows, dtype=jnp.int32)
    device = row_ids // row_share
    local_row = row_ids % row_share
    pieces = seq_row // (2 * tp_count)
    slot_ends = jnp.cumsum(2 * pieces)
    starts = slot_ends - 2 * pieces
    offset = local_row[:, None] - starts[None, :]
    inside = (offset >= 0) & (offset < 2 * pieces[None, :])
    first_half = offset < pieces[None, :]
    mirror = 2 * tp_count - 1 - device[:, None]
    position = jnp.where(
        first_half,
        device[:, None] * pieces[None, :] + offset,
        mirror * pieces[None, :] + offset - pieces[None, :],
    )
    slot_ids = jnp.arange(seq_row.shape[0], dtype=jnp.int32)
    doc_ids = jnp.sum(jnp.where(inside, slot_ids[None, :], 0), axis=1)
    positions = jnp.sum(jnp.where(inside, position, 0), axis=1)
    return (doc_ids, positions)


def rotate(values, positions, head_dim, turn_sign):
    row_count, width_all = values.shape
    half_dim = head_dim // 2
    shaped = values.reshape(row_count, width_all // head_dim, head_dim)
    freqs = 10000.0 ** (-jnp.arange(half_dim, dtype=jnp.float32) / half_dim)
    angles = positions.astype(jnp.float32)[:, None] * freqs[None, :]
    cosine = jnp.cos(angles)[:, None, :]
    sine = turn_sign * jnp.sin(angles)[:, None, :]
    front = shaped[..., :half_dim]
    behind = shaped[..., half_dim:]
    turned = jnp.concatenate(
        [front * cosine - behind * sine, behind * cosine + front * sine], axis=-1
    )
    return turned.reshape(row_count, width_all)


def normalize(values, gain):
    return values * lax.rsqrt(jnp.mean(values * values, axis=-1, keepdims=True) + EPS) * gain


def normalize_back(values, gain, grad_in):
    factor = lax.rsqrt(jnp.mean(values * values, axis=-1, keepdims=True) + EPS)
    normed = values * factor
    grad_normed = grad_in * gain
    grad_values = factor * (
        grad_normed - normed * jnp.mean(grad_normed * normed, axis=-1, keepdims=True)
    )
    return (grad_values, jnp.sum(grad_in * normed, axis=0))


def inner_rows(left, right):
    return lax.dot_general(
        left, right, (((0,), (0,)), ((), ())), preferred_element_type=jnp.float32
    )


def outer_cols(left, right):
    return lax.dot_general(
        left, right, (((1,), (1,)), ((), ())), preferred_element_type=jnp.float32
    )


def swiglu_back(gate, up_values, grad_hidden):
    sigma = jax.nn.sigmoid(gate)
    grad_gate = grad_hidden * up_values * (sigma * (1.0 + gate * (1.0 - sigma)))
    grad_upper = grad_hidden * (gate * sigma)
    return (grad_gate.astype(jnp.bfloat16), grad_upper.astype(jnp.bfloat16))


def block_mask(doc_ids, positions, first_row, block_rows):
    row_doc = lax.dynamic_slice_in_dim(doc_ids, first_row, block_rows, 0)
    row_pos = lax.dynamic_slice_in_dim(positions, first_row, block_rows, 0)
    return (row_doc[:, None] == doc_ids[None, :]) & (positions[None, :] <= row_pos[:, None])


def attention_forward(query, keys, values, doc_ids, positions, head_dim):
    group_rows, width_local = query.shape
    head_count = width_local // head_dim
    block_rows = min(512, group_rows)
    block_count = group_rows // block_rows
    score_scale = head_dim ** (-0.5)
    key_heads = keys.reshape(group_rows, head_count, head_dim)
    value_heads = values.reshape(group_rows, head_count, head_dim)

    def forward_block(block_index):
        first_row = block_index * block_rows
        query_rows = lax.dynamic_slice_in_dim(query, first_row, block_rows, 0).reshape(
            block_rows, head_count, head_dim
        )
        scores = (
            jnp.einsum("qhd,khd->hqk", query_rows, key_heads, preferred_element_type=jnp.float32)
            * score_scale
        )
        allowed = block_mask(doc_ids, positions, first_row, block_rows)
        scores = jnp.where(allowed[None], scores, -1e30)
        row_max = jnp.max(scores, axis=-1, keepdims=True)
        exponent = jnp.exp(scores - row_max)
        row_total = jnp.sum(exponent, axis=-1, keepdims=True)
        weights = (exponent / row_total).astype(jnp.bfloat16)
        mixture = jnp.einsum(
            "hqk,khd->qhd", weights, value_heads, preferred_element_type=jnp.float32
        )
        return (
            mixture.astype(jnp.bfloat16).reshape(block_rows, width_local),
            (row_max + jnp.log(row_total))[..., 0],
        )

    mixture, row_lse = lax.map(forward_block, jnp.arange(block_count, dtype=jnp.int32))
    return (mixture.reshape(group_rows, width_local), row_lse)


def attention_backward(query, keys, values, grad_mixture, row_lse, doc_ids, positions, head_dim):
    group_rows, width_local = query.shape
    head_count = width_local // head_dim
    block_rows = min(512, group_rows)
    block_count = group_rows // block_rows
    score_scale = head_dim ** (-0.5)
    key_heads = keys.reshape(group_rows, head_count, head_dim)
    value_heads = values.reshape(group_rows, head_count, head_dim)

    def backward_block(carry, block_index):
        key_total, value_total = carry
        first_row = block_index * block_rows
        query_rows = lax.dynamic_slice_in_dim(query, first_row, block_rows, 0).reshape(
            block_rows, head_count, head_dim
        )
        grad_rows = lax.dynamic_slice_in_dim(grad_mixture, first_row, block_rows, 0).reshape(
            block_rows, head_count, head_dim
        )
        scores = (
            jnp.einsum("qhd,khd->hqk", query_rows, key_heads, preferred_element_type=jnp.float32)
            * score_scale
        )
        allowed = block_mask(doc_ids, positions, first_row, block_rows)
        scores = jnp.where(allowed[None], scores, -1e30)
        weights = jnp.exp(scores - row_lse[block_index][..., None])
        weights_low = weights.astype(jnp.bfloat16)
        grad_weights = jnp.einsum(
            "qhd,khd->hqk", grad_rows, value_heads, preferred_element_type=jnp.float32
        )
        weighted_sum = jnp.sum(weights * grad_weights, axis=-1, keepdims=True)
        score_grad = (weights * (grad_weights - weighted_sum)).astype(jnp.bfloat16)
        query_grad = (
            jnp.einsum("hqk,khd->qhd", score_grad, key_heads, preferred_element_type=jnp.float32)
            * score_scale
        )
        key_total = (
            key_total
            + jnp.einsum("hqk,qhd->khd", score_grad, query_rows, preferred_element_type=jnp.float32)
            * score_scale
        )
        value_total = value_total + jnp.einsum(
            "hqk,qhd->khd", weights_low, grad_rows, preferred_element_type=jnp.float32
        )
        return (
            (key_total, value_total),
            query_grad.astype(jnp.bfloat16).reshape(block_rows, width_local),
        )

    zero_heads = jnp.zeros((group_rows, head_count, head_dim), jnp.float32)
    (key_total, value_total), query_grad = lax.scan(
        backward_block, (zero_heads, zero_heads), jnp.arange(block_count, dtype=jnp.int32)
    )
    return (
        query_grad.reshape(group_rows, width_local),
        key_total.reshape(group_rows, width_local).astype(jnp.bfloat16),
        value_total.reshape(group_rows, width_local).astype(jnp.bfloat16),
    )


BF, F32 = jnp.bfloat16, jnp.float32
BLK = 256
POS_OF = (0, 3, 1, 2)
NT = (((1,), (1,)), ((), ()))

def nt(a, b):
    return lax.dot_general(a, b, NT, preferred_element_type=F32)

def nn(a, b):
    return jnp.dot(a, b, preferred_element_type=F32)

def rows(block):
    return pl.ds(block * BLK, BLK)

def turn(u, cosine, sine, lane):
    near = jnp.where(lane % 64 < 32, pltpu.roll(u, 96, 1), pltpu.roll(u, 32, 1))
    return u * cosine + near * sine

FIRST = {}
for _m in range(4):
    for _j in range(POS_OF[_m] + 1):
        FIRST.setdefault(_j, (_m, 0))

def tables():
    pos = np.zeros(1024, np.float32)
    for m in range(4):
        pos[m*256:(m+1)*256] = POS_OF[m]*256 + np.arange(256)
    freqs = np.float32(10000.0) ** (-np.arange(32, dtype=np.float32) / np.float32(32))
    ang = pos[:, None] * freqs[None]
    c, s = np.cos(ang.astype(np.float32)), np.sin(ang.astype(np.float32))
    return np.tile(c, (1, 4)).astype(np.float32), np.concatenate([-s, s, -s, s], 1).astype(np.float32)


def block_place(m):
    late = lax.div(m, 2)
    return m * 3 - late * (5 + 2 * (m - 2))


def norm_rows(values, gain):
    return values * lax.rsqrt(jnp.mean(values * values, axis=-1, keepdims=True) + EPS) * gain


TILES = ((0, 512), (512, 512), (1024, 384))


def front_kernel(
    tokens_h, vf_h, wq_h, wk_h, wv_h, wo_h, wg_h, wu_h, wd_h, gain_attn_ref, gain_mlp_ref, cot_h, cos_ref, sin_ref,
    q_h, k_h, v_h, o_h, ot_h, xt_h, lse_ref, middle_h, base_h, send4_h, own6_h, send6_h, recv6_h, gg_h, gu_h, gd_h,
    tok, cot, x, xt, wq, wk, wv, vf, q, k, v, vt, o, ot, wo, recv2, send2, c, x2t, wg, wu, wd,
    ht, hid, gg, ug, base, send4, send6, recv6,
    load, ysem, store,
):
    tp = lax.axis_index("tp")
    mesh_id = pl.DeviceIdType.MESH
    barrier = pltpu.get_barrier_semaphore()
    pl.semaphore_signal(barrier, inc=1, device_id={"tp": 1 - tp}, device_id_type=mesh_id)
    loads = {}

    def fetch(name, src, dst):
        loads[name] = pltpu.make_async_copy(src, dst, load.at[len(loads)])
        loads[name].start()

    half = lambda b: pl.ds(b * BLK, BLK)
    for b in range(2):
        fetch(("tok", b), tokens_h.at[half(b)], tok.at[half(b)])
    for name, src, dst in (
        ("wq", wq_h, wq), ("wk", wk_h, wk), ("wv", wv_h, wv), ("vf", vf_h, vf), ("cot", cot_h, cot), ("wo", wo_h, wo),
        ("wg", wg_h, wg), ("wu", wu_h, wu), ("wd", wd_h, wd),
    ):
        fetch(name, src, dst)
    stores = []

    def keep(src, dst):
        stores.append(pltpu.make_async_copy(src, dst, store.at[len(stores)]))
        stores[-1].start()

    def peer(n, src, dst):
        return pltpu.make_async_remote_copy(
            src, dst, ysem.at[0, n], ysem.at[1, n], device_id={"tp": 1 - tp}, device_id_type=mesh_id
        )

    def mine(b):
        return pl.ds(pl.multiple_of(tp * 512 + b * BLK, BLK), BLK)

    def theirs(b):
        return pl.ds(pl.multiple_of((1 - tp) * 512 + b * BLK, BLK), BLK)

    lane = lax.broadcasted_iota(jnp.int32, (BLK, 128), 1)
    causal = lax.broadcasted_iota(jnp.int32, (BLK, BLK), 0) <= lax.broadcasted_iota(jnp.int32, (BLK, BLK), 1)
    gain_attn, gain_mlp = gain_attn_ref[...], gain_mlp_ref[...]
    sends = []
    for b in range(2):
        loads["tok", b].wait()
        x[mine(b), :] = norm_rows(tok[half(b), :], gain_attn).astype(BF)
        if b == 0:
            pl.semaphore_wait(barrier, 1)
        sends.append(peer(b, x.at[mine(b)], x.at[mine(b)]))
        sends[-1].start()
    loads["cot"].wait()
    for b in range(2):
        c[mine(b), :] = cot[half(b), :].astype(BF)
    for name in ("wq", "wk", "wv", "vf"):
        loads[name].wait()

    def project(m):
        row = pl.ds(pl.multiple_of(m * BLK, BLK), BLK)
        at = pl.ds(pl.multiple_of(block_place(m) * BLK, BLK), BLK)
        xm = x[row, :]
        cosine, sine = cos_ref[row, :], sin_ref[row, :]
        qf, kf = nn(xm, wq[...]), nn(xm, wk[...])
        low = (0.5 * nn(xm, wv[...]) + 0.5 * vf[row, :].astype(F32)).astype(BF)
        for t in range(4):
            cols = slice(t * 128, t * 128 + 128)
            q[at, cols] = turn(qf[:, cols], cosine, sine, lane).astype(BF) * 0.125
            k[at, cols] = turn(kf[:, cols], cosine, sine, lane).astype(BF)
        v[at, :] = low
        vt[:, at] = low.T
        xt[:, row] = xm.T

    def project_mine(b, carry):
        project(tp * 2 + b)
        return carry

    lax.fori_loop(0, 2, project_mine, 0)

    def project_theirs(b, carry):
        peer(b, x.at[mine(0)], x.at[mine(0)]).wait_recv()
        project((1 - tp) * 2 + b)
        return carry

    lax.fori_loop(0, 2, project_theirs, 0)
    cots = [peer(2 + b, c.at[mine(b)], c.at[mine(b)]) for b in range(2)]
    cots[0].start()
    for src, dst in ((q, q_h), (k, k_h), (v, v_h), (xt, xt_h)):
        keep(src, dst)
    lse_ref[...] = jnp.zeros_like(lse_ref)
    loads["wo"].wait()

    def attend(m):
        i = POS_OF[m]

        def pair(p, carry):
            cols = pl.ds(pl.multiple_of(p * 128, 128), 128)
            qb = q[rows(i), cols]
            parts = []
            for h in range(2):
                qm = jnp.where((lane < 64) == (h == 0), qb, jnp.zeros_like(qb))
                scores = [nt(k[rows(j), cols], qm) for j in range(i + 1)]
                scores[i] = jnp.where(causal, scores[i], -1e30)
                top = functools.reduce(jnp.maximum, [jnp.max(s, axis=0, keepdims=True) for s in scores])
                es = [jnp.exp(s - top) for s in scores]
                total = functools.reduce(jnp.add, [jnp.sum(e, axis=0, keepdims=True) for e in es])
                head = pl.ds(pl.multiple_of(p * 128 + h * 64, 64), 64)
                mix = functools.reduce(jnp.add, [nn(vt[head, rows(j)], es[j].astype(BF)) for j in range(i + 1)])
                parts.append(mix * (1.0 / total))
                lse_ref[lax.div(p, 2), pl.ds(2 * lax.rem(p, 2) + h, 1), rows(i)] = top + jnp.log(total)
            flat = jnp.concatenate(parts, axis=0)
            ot[cols, rows(m)] = flat.astype(BF)
            o[rows(m), cols] = flat.T.astype(BF)
            return carry

        lax.fori_loop(0, 4, pair, 0)

    twos = [peer(4 + b, send2.at[half(b)], recv2.at[half(b)]) for b in range(2)]
    for b in range(2):
        for side in range(2):

            @pl.when(tp == side)
            def _():
                attend((1 - side) * 2 + b)

        send2[half(b), :] = nn(o[theirs(b), :], wo[...]).astype(BF)
        twos[b].start()
    for side in range(2):

        @pl.when(tp == side)
        def _():
            attend(side * 2)
            attend(side * 2 + 1)

    keep(o, o_h)
    keep(ot, ot_h)
    for name in ("wg", "wu", "wd"):
        loads[name].wait()

    def gated(at):
        xm, cm = x[at, :], c[at, :]
        x2t[:, at] = xm.T
        for first, size in TILES:
            cols = slice(first, first + size)
            gate, up = nn(xm, wg[:, cols]), nn(xm, wu[:, cols])
            sigma = lax.logistic(gate)
            smooth = gate * sigma
            low = (smooth * up).astype(BF)
            hid[:, cols] = low
            ht[cols, at] = low.T
            back = nt(cm, wd[cols, :])
            gg[at, cols] = (back * up * (sigma * (1.0 + gate * (1.0 - sigma)))).astype(BF)
            ug[at, cols] = (back * smooth).astype(BF)
        return nn(hid[...], wd[...]), nt(gg[at, :], wg[...]) + nt(ug[at, :], wu[...])

    def block_mine(b, carry):
        here = pl.ds(pl.multiple_of(b * BLK, BLK), BLK)
        at = mine(b)
        peer(4 + b, send2.at[half(0)], recv2.at[half(0)]).wait_recv()
        middle = tok[here, :] + nn(o[at, :], wo[...]) + recv2[here, :].astype(F32)
        tok[here, :] = middle
        peer(b, x.at[half(0)], x.at[half(0)]).wait_send()
        x[at, :] = norm_rows(middle, gain_mlp).astype(BF)
        peer(6 + b, x.at[at], x.at[at]).start()
        branch, grad_in = gated(at)
        base[here, :] = tok[here, :] + branch
        cot[here, :] = grad_in
        return carry

    lax.fori_loop(0, 2, block_mine, 0)
    cots[1].start()
    keep(tok, middle_h)
    keep(base, base_h)
    keep(cot, own6_h)
    for copy in stores[:6]:
        copy.wait()
    columns = lambda t: slice(TILES[t][0], sum(TILES[t]))
    across = [(buf.at[:, : TILES[t][1]], gg, columns(t), gg_h) for t, buf in enumerate((wq, wk, wv))]
    across += [(buf.at[:, : TILES[t][1]], ug, columns(t), gu_h) for t, buf in enumerate((q, k, v))]
    down = [(buf.at[: TILES[t][1]], columns(t)) for t, buf in enumerate((ot, wo, recv2))]

    def gather(at, fresh):
        for buf, cols in down:
            new = nn(ht[cols, at], c[at, :])
            buf[...] = (new if fresh else buf[...].astype(F32) + new).astype(BF)

        def body(n, carry):
            tile = pl.ds(pl.multiple_of(n * BLK, BLK), BLK)
            turned = x2t[tile, at]
            for buf, right, cols, _ in across:
                new = nn(turned, right[at, cols])
                buf[tile, :] = (new if fresh else buf[tile, :].astype(F32) + new).astype(BF)
            return carry

        lax.fori_loop(0, 4, body, 0)

    gather(pl.ds(pl.multiple_of(tp * 512, 512), 512), True)
    for b in range(2):
        peer(6 + b, x.at[half(0)], x.at[half(0)]).wait_recv()
        peer(2 + b, c.at[half(0)], c.at[half(0)]).wait_recv()
        branch, grad_in = gated(theirs(b))
        send4[half(b), :] = branch.astype(BF)
        send6[half(b), :] = grad_in.astype(BF)
        if b == 0:
            peer(8, send6.at[half(0)], recv6.at[half(0)]).start()
        else:
            keep(send6, send6_h)
            keep(send4, send4_h)
        gather(theirs(b), False)
    last = [(buf, gd_h.at[cols]) for buf, cols in down] + [(buf, out.at[:, cols]) for buf, _, cols, out in across]
    for buf, out in last:
        keep(buf, out)
    peer(8, send6.at[half(0)], recv6.at[half(0)]).wait_recv()
    keep(recv6, recv6_h)
    for b in range(2):
        for n in (2, 4, 6):
            peer(n + b, recv6.at[half(0)], recv6.at[half(0)]).wait_send()
    peer(8, send6.at[half(0)], recv6.at[half(0)]).wait_send()
    for copy in stores[6:]:
        copy.wait()


def front(tokens, vf, wq, wk, wv, wo, wg, wu, wd, gain_attn, gain_mlp, cot, cos, sin):
    V = lambda shape, kind=BF: pltpu.VMEM(shape, kind)
    D = lambda *shape: pltpu.SemaphoreType.DMA(shape)
    hbm, vmem = pl.BlockSpec(memory_space=pl.ANY), pl.BlockSpec(memory_space=pltpu.VMEM)
    S = jax.ShapeDtypeStruct
    own, heads, turned, square = (512, 1024), (1024, 512), (512, 1024), (1024, 1024)
    hidden, across, half = (1024, 1408), (1408, 1024), (256, 1024)
    return pl.pallas_call(
        front_kernel,
        in_specs=[hbm] * 9 + [vmem] * 2 + [hbm] + [vmem] * 2,
        out_specs=[hbm] * 6 + [vmem] + [hbm] * 9,
        out_shape=[*[S(heads, BF)] * 4, S(turned, BF), S(square, BF), S((2, 8, 1024), F32), S(own, F32), S(own, F32), S(own, BF),
                   S(own, F32), S(own, BF), S(half, BF), S(hidden, BF), S(hidden, BF), S(across, BF)],
        scratch_shapes=[
            V(own, F32), V(own, F32), V(square), V(square), *[V(heads)] * 7, V(turned), V(heads), V(turned), V(own), V(own), V(own),
            V(square), V(square), V(hidden), V(hidden), V(across), V(across), V((256, 1408)), V(hidden), V(hidden), V(own, F32),
            V(own), V(own), V(half),
            D(11), D(2, 9), D(22),
        ],
        compiler_params=pltpu.CompilerParams(collective_id=4, has_side_effects=True, vmem_limit_bytes=63 << 20),
        cost_estimate=pl.CostEstimate(flops=40 * 10**9, bytes_accessed=60 << 20, transcendentals=5 << 20),
    )(tokens, vf, wq, wk, wv, wo, wg, wu, wd, gain_attn, gain_mlp, cot, cos, sin)


def ring_place(dp):
    core, x, z = lax.rem(dp, 2), lax.rem(lax.div(dp, 2), 2), lax.div(dp, 4)
    place = z + x * (7 - 2 * z)

    def device(where):
        side = lax.div(where, 4)
        return ((where + side * (7 - 2 * where)) * 2 + side) * 2 + core

    turn_no = lax.rem(place + core * (8 - 2 * place), 8)
    after = device(lax.rem(place + 1 + 6 * core, 8))
    before = device(lax.rem(place + 7 - 6 * core, 8))
    cube = (dp + 1 - 2 * core, dp + 2 - 4 * x, dp + 4 - 8 * lax.rem(z, 2), dp + 8 - 16 * lax.div(z, 2))
    return core, turn_no, after, before, cube


def remote(src, dst, send, recv, dp):
    return pltpu.make_async_remote_copy(
        src, dst, send, recv, device_id={"dp": dp}, device_id_type=pl.DeviceIdType.MESH
    )


class Ring:
    def __init__(self, place, takes, outs, own, sib, slots, sems):
        self.core, self.turn_no, self.after, self.before, self.cube = place
        self.takes, self.outs, self.own, self.sib, self.slots = takes, outs, own, sib, slots
        self.trade, self.rs, self.ag, self.over, self.keep = sems

    def piece(self, g, chunk):
        size = self.slots[g].shape[1]
        return pl.ds(pl.multiple_of(chunk * size, size), size)

    def traded(self, g):
        return remote(self.takes[g](1 - self.core), self.sib[g], self.trade.at[0, g], self.trade.at[1, g], self.cube[0])

    def total(self, g, chunk):
        at = self.piece(g, chunk)
        return self.own[g][at, :].astype(F32) + self.sib[g][at, :].astype(F32)

    def first(self, g, chunk):
        return remote(
            self.own[g].at[self.piece(g, chunk)], self.slots[g].at[0], self.rs.at[0, g, 0], self.rs.at[1, g, 0], self.after
        )

    def begin(self, g):
        self.traded(g).wait()
        chunk = lax.rem(self.turn_no + 7, 8)
        self.own[g][self.piece(g, chunk), :] = self.total(g, chunk).astype(BF)
        self.first(g, chunk).start()

    def add(self, g, t):
        chunk = lax.rem(self.turn_no + 14 - t, 8)
        remote(self.slots[g].at[t], self.slots[g].at[t], self.rs.at[0, g, t], self.rs.at[1, g, t], self.after).wait_recv()
        self.slots[g][t] = (self.slots[g][t].astype(F32) + self.total(g, chunk)).astype(BF)

    def add_on(self, g, t):
        self.add(g, t)
        remote(self.slots[g].at[t], self.slots[g].at[t + 1], self.rs.at[0, g, t + 1], self.rs.at[1, g, t + 1], self.after).start()

    def spot(self, g, chunk):
        return self.outs[g](self.core, chunk)

    def turn_over(self, g):
        self.add(g, 6)
        spot = self.spot(g, self.turn_no)
        last = self.slots[g].at[6]
        remote(last, spot, self.ag.at[0, g, 0], self.ag.at[1, g, 0], self.after).start()
        remote(last, spot, self.over.at[0, g, 0], self.over.at[1, g, 0], self.cube[0]).start()
        pltpu.make_async_copy(last, spot, self.keep.at[g]).start()

    def pass_on(self, g, t):
        spot = self.spot(g, lax.rem(self.turn_no + 15 - t, 8))
        remote(spot, spot, self.ag.at[0, g, t], self.ag.at[1, g, t], self.after).wait_recv()

        @pl.when(t < 6)
        def _():
            remote(spot, spot, self.ag.at[0, g, t + 1], self.ag.at[1, g, t + 1], self.after).start()

        remote(spot, spot, self.over.at[0, g, t + 1], self.over.at[1, g, t + 1], self.cube[0]).start()

    def end(self, g):
        spot = self.spot(g, self.turn_no)
        pltpu.make_async_copy(self.slots[g].at[6], spot, self.keep.at[g]).wait()

        def finish(t, _):
            remote(self.slots[g].at[0], self.slots[g].at[0], self.rs.at[0, g, t], self.rs.at[1, g, t], self.after).wait_send()
            remote(spot, spot, self.ag.at[0, g, t], self.ag.at[1, g, t], self.after).wait_send()
            return _

        lax.fori_loop(0, 7, finish, 0)

        def crossed(t, _):
            there = self.outs[g](1 - self.core, lax.rem(self.turn_no + t, 8))
            remote(spot, there, self.over.at[0, g, t], self.over.at[1, g, t], self.cube[0]).wait()
            return _

        lax.fori_loop(0, 8, crossed, 0)


def strip(ref, axis, halves, length):
    if axis == 0:
        return lambda core, chunk: ref.at[pl.ds(pl.multiple_of(core * halves + chunk * length, length), length)]
    return lambda core, chunk: ref.at[
        pl.ds(pl.multiple_of(chunk * length, length), length), pl.ds(pl.multiple_of(core * halves, halves), halves)
    ]


def half_of(ref, axis, halves):
    if axis == 0:
        return lambda core: ref.at[pl.ds(pl.multiple_of(core * halves, halves), halves)]
    return lambda core: ref.at[:, pl.ds(pl.multiple_of(core * halves, halves), halves)]


def norm_back_rows(values, gain, grad_in):
    factor = lax.rsqrt(jnp.mean(values * values, axis=-1, keepdims=True) + EPS)
    normed = values * factor
    grad_normed = grad_in * gain
    grad = factor * (grad_normed - normed * jnp.mean(grad_normed * normed, axis=-1, keepdims=True))
    return grad, jnp.sum(grad_in * normed, axis=0, keepdims=True)


def back_kernel(
    own6_h, send6_h, recv6_h, own4_h, send4_h, middle_h, cot_h, tokens_h, gain_attn_ref, gain_mlp_ref,
    wo_h, wq_h, wk_h, wv_h, q_h, k_h, v_h, o_h, ot_h, xt_h, lse_ref, cos_ref, sin_ref, gg_h, gu_h, gd_h,
    out_h, gt_h, gf_h, rq_h, rk_h, rv_h, ro_h, rg_h, ru_h, rd_h, gains_ref,
    f1, f2, f3, recv6, recv4, recv8, send8, c, wo, wq, wk, wv, q, k, v, o, ot, xt,
    dq, dk, dv, do, kt, dka, dva, dl, own8, dwq, dwk, dwv, dwo,
    mg, mu, md, sg, su, sd, lg, lu, ld, bq, bk, bv, bo, aq, ak, av, ao,
    load, ysem, trade1, rs1, ag1, over1, keep1, trade2, rs2, ag2, over2, keep2, gain_in, gain_sem, store,
):
    dp, tp = lax.axis_index("dp"), lax.axis_index("tp")
    place = ring_place(dp)
    core, turn_no, after, before, cube = place
    mesh_id = pl.DeviceIdType.MESH
    barrier = pltpu.get_barrier_semaphore()
    for other in (*cube, after, before):
        pl.semaphore_signal(barrier, inc=1, device_id={"dp": other}, device_id_type=mesh_id)
    pl.semaphore_signal(barrier, inc=1, device_id={"tp": 1 - tp}, device_id_type=mesh_id)

    loads = {}

    def fetch(name, src, dst):
        loads[name] = pltpu.make_async_copy(src, dst, load.at[len(loads)])
        loads[name].start()

    one = Ring(
        place, (half_of(gg_h, 0, 512), half_of(gu_h, 0, 512), half_of(gd_h, 1, 512)),
        (strip(rg_h, 0, 512, 64), strip(ru_h, 0, 512, 64), strip(rd_h, 1, 512, 176)),
        (mg, mu, md), (sg, su, sd), (lg, lu, ld), (trade1, rs1, ag1, over1, keep1),
    )
    two = Ring(
        place, (half_of(dwq, 0, 512), half_of(dwk, 0, 512), half_of(dwv, 0, 512), half_of(dwo, 0, 256)),
        (strip(rq_h, 0, 512, 64), strip(rk_h, 0, 512, 64), strip(rv_h, 0, 512, 64), strip(ro_h, 0, 256, 32)),
        (half_of(dwq, 0, 512)(core), half_of(dwk, 0, 512)(core), half_of(dwv, 0, 512)(core), half_of(dwo, 0, 256)(core)),
        (bq, bk, bv, bo), (aq, ak, av, ao), (trade2, rs2, ag2, over2, keep2),
    )
    for g, (whole, mine) in enumerate(((gg_h, mg), (gu_h, mu), (gd_h, md))):
        fetch(("m", g), one.takes[g](core), mine)
    for name, src, dst in (
        ("own6", own6_h, f1), ("recv6", recv6_h, recv6.at[pl.ds(0, BLK)]), ("middle", middle_h, f2), ("cot", cot_h, f3), ("wo", wo_h, wo), ("q", q_h, q), ("k", k_h, k),
        ("v", v_h, v), ("o", o_h, o), ("wq", wq_h, wq), ("wk", wk_h, wk), ("wv", wv_h, wv), ("ot", ot_h, ot), ("xt", xt_h, xt),
    ):
        fetch(name, src, dst)
    pl.semaphore_wait(barrier, 7)

    def peer(n, src, dst):
        return pltpu.make_async_remote_copy(
            src, dst, ysem.at[0, n], ysem.at[1, n], device_id={"tp": 1 - tp}, device_id_type=mesh_id
        )

    half = lambda b: pl.ds(b * BLK, BLK)
    six = peer(0, send6_h.at[half(1)], recv6.at[half(1)])
    six.start()
    for g in range(3):
        one.traded(g).start()
    for g in range(3):
        loads["m", g].wait()
        one.begin(g)

    def ring_steps(first, last):
        def body(t, carry):
            for g in range(3):
                one.add_on(g, t)
            return carry

        lax.fori_loop(first, last, body, 0)

    lane = lax.broadcasted_iota(jnp.int32, (BLK, 128), 1)
    causal = lax.broadcasted_iota(jnp.int32, (BLK, BLK), 0) <= lax.broadcasted_iota(jnp.int32, (BLK, BLK), 1)
    gain_mlp, gain_attn = gain_mlp_ref[...], gain_attn_ref[...]
    for name in ("own6", "recv6", "middle", "cot", "wo"):
        loads[name].wait()
    gain_sum = jnp.zeros((1, 1024), F32)
    seven = []
    for b in range(2):
        if b == 1:
            six.wait_recv()

        def rows_back(n, total):
            at = pl.ds(pl.multiple_of(b * BLK + n * 64, 64), 64)
            grad_in = f1[at, :] + recv6[at, :].astype(F32)
            grad, part = norm_back_rows(f2[at, :], gain_mlp, grad_in)
            grad = f3[at, :] + grad
            f1[at, :] = grad
            c[pl.ds(pl.multiple_of(tp * 512 + b * BLK + n * 64, 64), 64), :] = grad.astype(BF)
            return total + part

        gain_sum = lax.fori_loop(0, 4, rows_back, gain_sum)
        mine = c.at[pl.ds(pl.multiple_of(tp * 512 + b * BLK, BLK), BLK)]
        seven.append(peer(2 + b, mine, mine))
        seven[b].start()
        ring_steps(b, 1 + b)
    four = peer(4, send4_h, recv4)
    four.start()
    late = pltpu.make_async_copy(own4_h, f3, load.at[len(loads)])
    late.start()
    gains_ref[...] = jnp.zeros_like(gains_ref)
    gains_ref[0:1, :] = gain_sum
    for name in ("o", "k"):
        loads[name].wait()

    def branch_back(m):
        at = rows(m)
        low = nt(c[at, :], wo[...]).astype(BF)
        do[at, :] = low
        prod = (low.astype(F32) * o[at, :].astype(F32)).T
        for h in range(8):
            dl[h : h + 1, at] = jnp.sum(prod[h * 64 : h * 64 + 64, :], axis=0, keepdims=True)

    ring_steps(2, 3)
    for b in range(2):
        seven[b].wait_recv()
    for m in range(4):
        branch_back(m)
        if m < 3:
            one.add_on(m, 3)
    for name in ("q", "v"):
        loads[name].wait()

    def serve(g, p):
        @pl.when(p < 2)
        def _():
            one.add_on(g, 4 + p)

        @pl.when(p == 2)
        def _():
            one.turn_over(g)

        @pl.when(p == 3)
        def _():
            one.pass_on(g, 0)

    def pair(p, carry):
        cols = pl.ds(pl.multiple_of(p * 128, 128), 128)
        for j in range(4):
            kt[:, rows(j)] = k[rows(j), cols].T
        for m in range(4):
            i = POS_OF[m]
            qb, dob = q[rows(i), cols], do[rows(m), cols]
            parts = []
            for h in range(2):
                mine = (lane < 64) == (h == 0)
                qm = jnp.where(mine, qb, jnp.zeros_like(qb))
                dom = jnp.where(mine, dob, jnp.zeros_like(dob))
                lse = lse_ref[lax.div(p, 2), pl.ds(2 * lax.rem(p, 2) + h, 1), rows(i)]
                delta = dl[pl.ds(2 * p + h, 1), rows(m)]
                head = slice(h * 64, h * 64 + 64)
                dqt = None
                for j in range(i + 1):
                    weights = jnp.exp(nt(k[rows(j), cols], qm) - lse)
                    if j == i:
                        weights = jnp.where(causal, weights, 0.0)
                    ds = (weights * (nt(v[rows(j), cols], dom) - delta)).astype(BF)
                    dvp, dkp = nn(weights.astype(BF), dom), nn(ds, qm)
                    fresh = (m, h) == FIRST[j]
                    dva[rows(j), :] = dvp if fresh else dva[rows(j), :] + dvp
                    dka[rows(j), :] = dkp if fresh else dka[rows(j), :] + dkp
                    part = nn(kt[head, rows(j)], ds)
                    dqt = part if dqt is None else dqt + part
                parts.append(dqt)
            grad = (jnp.concatenate(parts, axis=0).T * 0.125).astype(BF).astype(F32)
            dq[rows(m), cols] = turn(grad, cos_ref[rows(m), :], -sin_ref[rows(m), :], lane).astype(BF)
            if m < 3:
                serve(m, p)
        for m in range(4):
            at = rows(POS_OF[m])
            grad = dka[at, :].astype(BF).astype(F32)
            dk[rows(m), cols] = turn(grad, cos_ref[rows(m), :], -sin_ref[rows(m), :], lane).astype(BF)
            dv[rows(m), cols] = (0.5 * dva[at, :].astype(BF).astype(F32)).astype(BF)

        return carry

    lax.fori_loop(0, 4, pair, 0)
    keep_gf = pltpu.make_async_copy(dv, gf_h, store.at[0])
    keep_gf.start()
    for name in ("wq", "wk", "wv"):
        loads[name].wait()

    def into_rows(at):
        return nt(dq[at, :], wq[...]) + nt(dk[at, :], wk[...]) + nt(dv[at, :], wv[...])

    eight = []
    for b in range(2):
        at = pl.ds(pl.multiple_of((1 - tp) * 512 + b * BLK, BLK), BLK)
        send8[half(b), :] = into_rows(at).astype(BF)
        eight.append(peer(5 + b, send8.at[half(b)], recv8.at[half(b)]))
        eight[b].start()
        for g in range(3):
            one.pass_on(g, 1 + b)
    for name in ("xt", "ot"):
        loads[name].wait()
    for which in range(2):
        side = (1 - core) * (1 - which) + core * which
        at = pl.ds(pl.multiple_of(side * 512, 512), 512)
        for dst, src in ((dwq, dq), (dwk, dk), (dwv, dv)):
            dst[at, :] = nn(xt[at, :], src[...]).astype(BF)
        at = pl.ds(pl.multiple_of(side * 256, 256), 256)
        dwo[at, :] = nn(ot[at, :], c[...]).astype(BF)
        if which == 0:
            for g in range(4):
                two.traded(g).start()
    for g in range(4):
        two.begin(g)

    def second(t, carry):
        @pl.when(t < 4)
        def _():
            for g in range(3):
                one.pass_on(g, 3 + t)

        for g in range(4):
            two.add_on(g, t)
        return carry

    for b in range(2):
        own8[half(b), :] = into_rows(pl.ds(pl.multiple_of(tp * 512 + b * BLK, BLK), BLK))
    fetch_tokens = pltpu.make_async_copy(tokens_h, f2, load.at[len(loads) + 1])
    fetch_tokens.start()
    lax.fori_loop(0, 3, second, 0)
    four.wait_recv()
    late.wait()
    fetch_tokens.wait()

    def out_rows(n, carry):
        at = pl.ds(pl.multiple_of(n * 64, 64), 64)
        f3[at, :] = f3[at, :] + recv4[at, :].astype(F32)
        return carry

    lax.fori_loop(0, 8, out_rows, 0)
    keep_out = pltpu.make_async_copy(f3, out_h, store.at[1])
    keep_out.start()
    lax.fori_loop(3, 6, second, 0)
    for g in range(4):
        two.turn_over(g)
    gain_sum = jnp.zeros((1, 1024), F32)
    for b in range(2):
        eight[b].wait_recv()

        def rows_last(n, total):
            at = pl.ds(pl.multiple_of(b * BLK + n * 64, 64), 64)
            grad, part = norm_back_rows(f2[at, :], gain_attn, own8[at, :] + recv8[at, :].astype(F32))
            f1[at, :] = f1[at, :] + grad
            return total + part

        gain_sum = lax.fori_loop(0, 4, rows_last, gain_sum)
    keep_gt = pltpu.make_async_copy(f1, gt_h, store.at[2])
    keep_gt.start()
    gains_ref[1:2, :] = gain_sum

    def gain_swap(n):
        where = {"tp": 1 - tp} if n == 4 else {"dp": cube[n]}
        return pltpu.make_async_remote_copy(
            gains_ref, gain_in.at[n], gain_sem.at[0, n], gain_sem.at[1, n], device_id=where, device_id_type=mesh_id
        )

    for t in range(7):
        for g in range(4):
            two.pass_on(g, t)
        if t < 5:
            move = gain_swap(t)
            move.start()
            move.wait()
            gains_ref[...] = gains_ref[...] + gain_in[t]
    for g in range(3):
        one.end(g)
    for g in range(4):
        two.end(g)
    for copy in (six, *seven, *eight, four):
        copy.wait_send()
    for copy in (keep_gf, keep_out, keep_gt):
        copy.wait()


def back(own6, send6, recv6, own4, send4, middle, cot, tokens, gain_attn, gain_mlp, wo, wq, wk, wv, q, k, v, o, ot, xt, lse, cos, sin, gg, gu, gd):
    V = lambda shape, kind=BF: pltpu.VMEM(shape, kind)
    D = lambda *shape: pltpu.SemaphoreType.DMA(shape)
    hbm, vmem = pl.BlockSpec(memory_space=pl.ANY), pl.BlockSpec(memory_space=pltpu.VMEM)
    S = jax.ShapeDtypeStruct
    wide = (1024, 1024)
    return pl.pallas_call(
        back_kernel,
        in_specs=[hbm] * 8 + [vmem] * 2 + [hbm] * 10 + [vmem] * 3 + [hbm] * 3,
        out_specs=[hbm] * 10 + [vmem],
        out_shape=[S((512, 1024), F32), S((512, 1024), F32), S((1024, 512), BF), *[S((1024, 512), BF)] * 3, S((512, 1024), BF),
                   S((1024, 1408), BF), S((1024, 1408), BF), S((1408, 1024), BF), S((8, 1024), F32)],
        scratch_shapes=[
            *[V((512, 1024), F32)] * 3, *[V((512, 1024))] * 4, V(wide), V((512, 1024)), *[V((1024, 512))] * 7, V((512, 1024)), V(wide),
            *[V((1024, 512))] * 4, V((128, 1024)), *[V((1024, 128), F32)] * 2, V((8, 1024), F32), V((512, 1024), F32),
            *[V((1024, 512))] * 3, V((512, 1024)),
            *[V((512, 1408)), V((512, 1408)), V((1408, 512))] * 2, V((7, 64, 1408)), V((7, 64, 1408)), V((7, 176, 512)),
            *[V((512, 512))] * 3, V((256, 1024)), *[V((7, 64, 512))] * 3, V((7, 32, 1024)),
            D(19), D(2, 7), D(2, 3), D(2, 3, 7), D(2, 3, 7), D(2, 3, 8), D(3), D(2, 4), D(2, 4, 7), D(2, 4, 7), D(2, 4, 8), D(4),
            V((5, 8, 1024), F32), D(2, 5), D(3),
        ],
        compiler_params=pltpu.CompilerParams(collective_id=3, has_side_effects=True, vmem_limit_bytes=62 << 20),
        cost_estimate=pl.CostEstimate(flops=30 * 10**9, bytes_accessed=60 << 20, transcendentals=5 << 20),
    )(own6, send6, recv6, own4, send4, middle, cot, tokens, gain_attn, gain_mlp, wo, wq, wk, wv, q, k, v, o, ot, xt, lse, cos, sin, gg, gu, gd)


PIECES = 4


def finish_kernel(*refs):
    ins, outs, wide = refs[:10], refs[10:20], refs[20:36]
    through, load, store = refs[36:]
    into = [pltpu.make_async_copy(ins[n], through.at[n], load.at[8, n]) for n in range(2)]
    whole = [pltpu.make_async_copy(through.at[n], outs[n], store.at[n, 0]) for n in range(2)]
    for copy in into:
        copy.start()
    low, high = wide[:8], wide[8:]
    order = (5, 6, 7, 1, 2, 3, 4, 0)

    def part(ref, piece):
        size = ref.shape[0] // PIECES
        return ref.at[pl.ds(piece * size, size)]

    for a in order:
        for piece in range(PIECES):
            pltpu.make_async_copy(part(ins[a + 2], piece), part(low[a], piece), load.at[a, piece]).start()
    for n in range(2):
        into[n].wait()
        whole[n].start()
    for a in order:
        for piece in range(PIECES):
            pltpu.make_async_copy(part(ins[a + 2], piece), part(low[a], piece), load.at[a, piece]).wait()
            size = low[a].shape[0] // PIECES

            def widen(n, carry):
                at = pl.ds(pl.multiple_of(piece * size + n * 16, 16), 16)
                high[a][at, :] = low[a][at, :].astype(F32)
                return carry

            lax.fori_loop(0, size // 16, widen, 0, unroll=2)
            pltpu.make_async_copy(part(high[a], piece), part(outs[a + 2], piece), store.at[a + 2, piece]).start()
    for a in order:
        for piece in range(PIECES):
            pltpu.make_async_copy(part(high[a], piece), part(outs[a + 2], piece), store.at[a + 2, piece]).wait()
    for copy in whole:
        copy.wait()


def finish(*arrays):
    hbm = pl.BlockSpec(memory_space=pl.ANY)
    return pl.pallas_call(
        finish_kernel,
        in_specs=[hbm] * 10,
        out_specs=[hbm] * 10,
        out_shape=[jax.ShapeDtypeStruct(a.shape, F32) for a in arrays],
        scratch_shapes=[
            *[pltpu.VMEM(a.shape, BF) for a in arrays[2:]], *[pltpu.VMEM(a.shape, F32) for a in arrays[2:]],
            pltpu.VMEM((2, *arrays[0].shape), F32), pltpu.SemaphoreType.DMA((9, PIECES)), pltpu.SemaphoreType.DMA((10, PIECES)),
        ],
        compiler_params=pltpu.CompilerParams(vmem_limit_bytes=60 << 20),
        cost_estimate=pl.CostEstimate(flops=10**7, bytes_accessed=48 << 20, transcendentals=0),
    )(*arrays)

def local_pair(
    tokens,
    v_first,
    w_query,
    w_key,
    w_value,
    w_out,
    w_gate,
    w_up,
    w_down,
    gain_attn,
    gain_mlp,
    seq_lens,
    cotangent,
):
    cosine, sine = tables()
    (query, keys, mixed_values, attended, attended_t, normed_t, row_lse, middle, base, send_out, own_in, send_in, got_in,
     grad_gate, grad_up, grad_down) = front(
        tokens, v_first, w_query, w_key, w_value, w_out, w_gate, w_up, w_down, gain_attn[None], gain_mlp[None], cotangent, cosine, sine
    )
    layer_out, grad_tokens, grad_first, *low_grads, gains = back(
        own_in, send_in, got_in, base, send_out, middle, cotangent, tokens, gain_attn[None], gain_mlp[None], w_out, w_query, w_key, w_value,
        query, keys, mixed_values, attended, attended_t, normed_t, row_lse, cosine, sine, grad_gate, grad_up, grad_down,
    )
    layer_out, grad_tokens, grad_first, *wide = finish(layer_out, grad_tokens, grad_first, *low_grads)
    grad_gain_mlp, grad_gain_attn = gains[0], gains[1]
    return (layer_out, grad_tokens, grad_first, *wide, grad_gain_attn, grad_gain_mlp)


def local(
    tokens,
    v_first,
    w_query,
    w_key,
    w_value,
    w_out,
    w_gate,
    w_up,
    w_down,
    gain_attn,
    gain_mlp,
    seq_lens,
    cotangent,
):
    tp_count = lax.axis_size("tp")
    row_share = tokens.shape[0]
    doc_ids, positions = layout(seq_lens[0], row_share, tp_count)
    normed_attn = lax.all_gather(
        normalize(tokens, gain_attn).astype(jnp.bfloat16), "tp", axis=0, tiled=True
    )
    query = rotate(
        jnp.dot(normed_attn, w_query, preferred_element_type=jnp.float32), positions, HDIM, 1.0
    ).astype(jnp.bfloat16)
    keys = rotate(
        jnp.dot(normed_attn, w_key, preferred_element_type=jnp.float32), positions, HDIM, 1.0
    ).astype(jnp.bfloat16)
    value_pre = jnp.dot(normed_attn, w_value, preferred_element_type=jnp.float32)
    mixed_values = (0.5 * value_pre + 0.5 * v_first.astype(jnp.float32)).astype(jnp.bfloat16)
    attended, row_lse = attention_forward(query, keys, mixed_values, doc_ids, positions, HDIM)
    middle = tokens + lax.psum_scatter(
        jnp.dot(attended, w_out, preferred_element_type=jnp.float32),
        "tp",
        scatter_dimension=0,
        tiled=True,
    )
    normed_mlp = normalize(middle, gain_mlp).astype(jnp.bfloat16)
    grad_branch = cotangent.astype(jnp.bfloat16)
    mlp_rows = lax.all_gather(normed_mlp, "tp", axis=0, tiled=True)
    gate = jnp.dot(mlp_rows, w_gate, preferred_element_type=jnp.float32)
    up_values = jnp.dot(mlp_rows, w_up, preferred_element_type=jnp.float32)
    hidden = (jax.nn.silu(gate) * up_values).astype(jnp.bfloat16)
    layer_out = middle + lax.psum_scatter(
        jnp.dot(hidden, w_down, preferred_element_type=jnp.float32).astype(jnp.bfloat16),
        "tp",
        scatter_dimension=0,
        tiled=True,
    ).astype(jnp.float32)
    cot_rows = lax.all_gather(grad_branch, "tp", axis=0, tiled=True)
    grad_down = inner_rows(hidden, cot_rows)
    gate_grad, up_grad = swiglu_back(gate, up_values, outer_cols(cot_rows, w_down))
    grad_gate = inner_rows(mlp_rows, gate_grad)
    grad_up = inner_rows(mlp_rows, up_grad)
    grad_mlp_in = lax.psum_scatter(
        (outer_cols(gate_grad, w_gate) + outer_cols(up_grad, w_up)).astype(jnp.bfloat16),
        "tp",
        scatter_dimension=0,
        tiled=True,
    ).astype(jnp.float32)
    middle_back, grad_gain_mlp = normalize_back(middle, gain_mlp, grad_mlp_in)
    grad_middle = cotangent + middle_back
    attn_cot_rows = lax.all_gather(grad_middle.astype(jnp.bfloat16), "tp", axis=0, tiled=True)
    grad_output = inner_rows(attended, attn_cot_rows)
    grad_attended = outer_cols(attn_cot_rows, w_out).astype(jnp.bfloat16)
    query_grad, key_grad, mixed_grad = attention_backward(
        query, keys, mixed_values, grad_attended, row_lse, doc_ids, positions, HDIM
    )
    half_mixed = 0.5 * mixed_grad.astype(jnp.float32)
    value_grad = half_mixed.astype(jnp.bfloat16)
    query_pre_grad = rotate(query_grad.astype(jnp.float32), positions, HDIM, -1.0).astype(
        jnp.bfloat16
    )
    key_pre_grad = rotate(key_grad.astype(jnp.float32), positions, HDIM, -1.0).astype(jnp.bfloat16)
    grad_query = inner_rows(normed_attn, query_pre_grad)
    grad_key = inner_rows(normed_attn, key_pre_grad)
    grad_value = inner_rows(normed_attn, value_grad)
    grad_attn_in = lax.psum_scatter(
        (
            outer_cols(query_pre_grad, w_query)
            + outer_cols(key_pre_grad, w_key)
            + outer_cols(value_grad, w_value)
        ).astype(jnp.bfloat16),
        "tp",
        scatter_dimension=0,
        tiled=True,
    ).astype(jnp.float32)
    tokens_back, grad_gain_attn = normalize_back(tokens, gain_attn, grad_attn_in)
    grad_tokens = grad_middle + tokens_back
    grad_query, grad_key, grad_value, grad_output, grad_gate, grad_up, grad_down = (
        lax.psum(grad_query.astype(jnp.bfloat16), "dp").astype(jnp.float32),
        lax.psum(grad_key.astype(jnp.bfloat16), "dp").astype(jnp.float32),
        lax.psum(grad_value.astype(jnp.bfloat16), "dp").astype(jnp.float32),
        lax.psum(grad_output.astype(jnp.bfloat16), "dp").astype(jnp.float32),
        lax.psum(grad_gate.astype(jnp.bfloat16), "dp").astype(jnp.float32),
        lax.psum(grad_up.astype(jnp.bfloat16), "dp").astype(jnp.float32),
        lax.psum(grad_down.astype(jnp.bfloat16), "dp").astype(jnp.float32),
    )
    grad_gain_attn, grad_gain_mlp = lax.psum((grad_gain_attn, grad_gain_mlp), ("dp", "tp"))
    return (
        layer_out,
        grad_tokens,
        half_mixed,
        grad_query,
        grad_key,
        grad_value,
        grad_output,
        grad_gate,
        grad_up,
        grad_down,
        grad_gain_attn,
        grad_gain_mlp,
    )


def solution(mesh):
    in_specs = (
        P(("dp", "tp"), None),
        P("dp", "tp"),
        P(None, "tp"),
        P(None, "tp"),
        P(None, "tp"),
        P("tp", None),
        P(None, "tp"),
        P(None, "tp"),
        P("tp", None),
        P(),
        P(),
        P("dp", None),
        P(("dp", "tp"), None),
    )
    out_specs = (
        P(("dp", "tp"), None),
        P(("dp", "tp"), None),
        P("dp", "tp"),
        P(None, "tp"),
        P(None, "tp"),
        P(None, "tp"),
        P("tp", None),
        P(None, "tp"),
        P(None, "tp"),
        P("tp", None),
        P(),
        P(),
    )

    def step(*args):
        tokens, seq_lens = args[0], args[11]
        pair = mesh.shape["tp"] == 2 and mesh.shape["dp"] == 16 and seq_lens.shape[1] == 1 and tokens.shape == (512, 1024)
        return (local_pair if pair else local)(*args)

    return jax.shard_map(step, mesh=mesh, in_specs=in_specs, out_specs=out_specs, check_vma=False)
```

```python
import functools

import jax
import jax.numpy as jnp
import numpy as np
from jax import lax
from jax.experimental import pallas as pl
from jax.experimental.pallas import tpu as pltpu
from jax.sharding import PartitionSpec as P

HDIM = 64


EPS = 1e-06


def layout(seq_row, row_share, tp_count):
    group_rows = row_share * tp_count
    row_ids = jnp.arange(group_rows, dtype=jnp.int32)
    device = row_ids // row_share
    local_row = row_ids % row_share
    pieces = seq_row // (2 * tp_count)
    slot_ends = jnp.cumsum(2 * pieces)
    starts = slot_ends - 2 * pieces
    offset = local_row[:, None] - starts[None, :]
    inside = (offset >= 0) & (offset < 2 * pieces[None, :])
    first_half = offset < pieces[None, :]
    mirror = 2 * tp_count - 1 - device[:, None]
    position = jnp.where(
        first_half,
        device[:, None] * pieces[None, :] + offset,
        mirror * pieces[None, :] + offset - pieces[None, :],
    )
    slot_ids = jnp.arange(seq_row.shape[0], dtype=jnp.int32)
    doc_ids = jnp.sum(jnp.where(inside, slot_ids[None, :], 0), axis=1)
    positions = jnp.sum(jnp.where(inside, position, 0), axis=1)
    return (doc_ids, positions)


def rotate(values, positions, head_dim, turn_sign):
    row_count, width_all = values.shape
    half_dim = head_dim // 2
    shaped = values.reshape(row_count, width_all // head_dim, head_dim)
    freqs = 10000.0 ** (-jnp.arange(half_dim, dtype=jnp.float32) / half_dim)
    angles = positions.astype(jnp.float32)[:, None] * freqs[None, :]
    cosine = jnp.cos(angles)[:, None, :]
    sine = turn_sign * jnp.sin(angles)[:, None, :]
    front = shaped[..., :half_dim]
    behind = shaped[..., half_dim:]
    turned = jnp.concatenate(
        [front * cosine - behind * sine, behind * cosine + front * sine], axis=-1
    )
    return turned.reshape(row_count, width_all)


def normalize(values, gain):
    return values * lax.rsqrt(jnp.mean(values * values, axis=-1, keepdims=True) + EPS) * gain


def normalize_back(values, gain, grad_in):
    factor = lax.rsqrt(jnp.mean(values * values, axis=-1, keepdims=True) + EPS)
    normed = values * factor
    grad_normed = grad_in * gain
    grad_values = factor * (
        grad_normed - normed * jnp.mean(grad_normed * normed, axis=-1, keepdims=True)
    )
    return (grad_values, jnp.sum(grad_in * normed, axis=0))


def inner_rows(left, right):
    return lax.dot_general(
        left, right, (((0,), (0,)), ((), ())), preferred_element_type=jnp.float32
    )


def outer_cols(left, right):
    return lax.dot_general(
        left, right, (((1,), (1,)), ((), ())), preferred_element_type=jnp.float32
    )


def swiglu_back(gate, up_values, grad_hidden):
    sigma = jax.nn.sigmoid(gate)
    grad_gate = grad_hidden * up_values * (sigma * (1.0 + gate * (1.0 - sigma)))
    grad_upper = grad_hidden * (gate * sigma)
    return (grad_gate.astype(jnp.bfloat16), grad_upper.astype(jnp.bfloat16))


def block_mask(doc_ids, positions, first_row, block_rows):
    row_doc = lax.dynamic_slice_in_dim(doc_ids, first_row, block_rows, 0)
    row_pos = lax.dynamic_slice_in_dim(positions, first_row, block_rows, 0)
    return (row_doc[:, None] == doc_ids[None, :]) & (positions[None, :] <= row_pos[:, None])


def attention_forward(query, keys, values, doc_ids, positions, head_dim):
    group_rows, width_local = query.shape
    head_count = width_local // head_dim
    block_rows = min(512, group_rows)
    block_count = group_rows // block_rows
    score_scale = head_dim ** (-0.5)
    key_heads = keys.reshape(group_rows, head_count, head_dim)
    value_heads = values.reshape(group_rows, head_count, head_dim)

    def forward_block(block_index):
        first_row = block_index * block_rows
        query_rows = lax.dynamic_slice_in_dim(query, first_row, block_rows, 0).reshape(
            block_rows, head_count, head_dim
        )
        scores = (
            jnp.einsum("qhd,khd->hqk", query_rows, key_heads, preferred_element_type=jnp.float32)
            * score_scale
        )
        allowed = block_mask(doc_ids, positions, first_row, block_rows)
        scores = jnp.where(allowed[None], scores, -1e30)
        row_max = jnp.max(scores, axis=-1, keepdims=True)
        exponent = jnp.exp(scores - row_max)
        row_total = jnp.sum(exponent, axis=-1, keepdims=True)
        weights = (exponent / row_total).astype(jnp.bfloat16)
        mixture = jnp.einsum(
            "hqk,khd->qhd", weights, value_heads, preferred_element_type=jnp.float32
        )
        return (
            mixture.astype(jnp.bfloat16).reshape(block_rows, width_local),
            (row_max + jnp.log(row_total))[..., 0],
        )

    mixture, row_lse = lax.map(forward_block, jnp.arange(block_count, dtype=jnp.int32))
    return (mixture.reshape(group_rows, width_local), row_lse)


def attention_backward(query, keys, values, grad_mixture, row_lse, doc_ids, positions, head_dim):
    group_rows, width_local = query.shape
    head_count = width_local // head_dim
    block_rows = min(512, group_rows)
    block_count = group_rows // block_rows
    score_scale = head_dim ** (-0.5)
    key_heads = keys.reshape(group_rows, head_count, head_dim)
    value_heads = values.reshape(group_rows, head_count, head_dim)

    def backward_block(carry, block_index):
        key_total, value_total = carry
        first_row = block_index * block_rows
        query_rows = lax.dynamic_slice_in_dim(query, first_row, block_rows, 0).reshape(
            block_rows, head_count, head_dim
        )
        grad_rows = lax.dynamic_slice_in_dim(grad_mixture, first_row, block_rows, 0).reshape(
            block_rows, head_count, head_dim
        )
        scores = (
            jnp.einsum("qhd,khd->hqk", query_rows, key_heads, preferred_element_type=jnp.float32)
            * score_scale
        )
        allowed = block_mask(doc_ids, positions, first_row, block_rows)
        scores = jnp.where(allowed[None], scores, -1e30)
        weights = jnp.exp(scores - row_lse[block_index][..., None])
        weights_low = weights.astype(jnp.bfloat16)
        grad_weights = jnp.einsum(
            "qhd,khd->hqk", grad_rows, value_heads, preferred_element_type=jnp.float32
        )
        weighted_sum = jnp.sum(weights * grad_weights, axis=-1, keepdims=True)
        score_grad = (weights * (grad_weights - weighted_sum)).astype(jnp.bfloat16)
        query_grad = (
            jnp.einsum("hqk,khd->qhd", score_grad, key_heads, preferred_element_type=jnp.float32)
            * score_scale
        )
        key_total = (
            key_total
            + jnp.einsum("hqk,qhd->khd", score_grad, query_rows, preferred_element_type=jnp.float32)
            * score_scale
        )
        value_total = value_total + jnp.einsum(
            "hqk,qhd->khd", weights_low, grad_rows, preferred_element_type=jnp.float32
        )
        return (
            (key_total, value_total),
            query_grad.astype(jnp.bfloat16).reshape(block_rows, width_local),
        )

    zero_heads = jnp.zeros((group_rows, head_count, head_dim), jnp.float32)
    (key_total, value_total), query_grad = lax.scan(
        backward_block, (zero_heads, zero_heads), jnp.arange(block_count, dtype=jnp.int32)
    )
    return (
        query_grad.reshape(group_rows, width_local),
        key_total.reshape(group_rows, width_local).astype(jnp.bfloat16),
        value_total.reshape(group_rows, width_local).astype(jnp.bfloat16),
    )


BF, F32 = jnp.bfloat16, jnp.float32
BLK = 256
POS_OF = (0, 3, 1, 2)
NT = (((1,), (1,)), ((), ()))

def nt(a, b):
    return lax.dot_general(a, b, NT, preferred_element_type=F32)

def nn(a, b):
    return jnp.dot(a, b, preferred_element_type=F32)

def rows(block):
    return pl.ds(block * BLK, BLK)

def turn(u, cosine, sine, lane):
    near = jnp.where(lane % 64 < 32, pltpu.roll(u, 96, 1), pltpu.roll(u, 32, 1))
    return u * cosine + near * sine

FIRST = {}
for _m in range(4):
    for _j in range(POS_OF[_m] + 1):
        FIRST.setdefault(_j, (_m, 0))

def tables():
    pos = np.zeros(1024, np.float32)
    for m in range(4):
        pos[m*256:(m+1)*256] = POS_OF[m]*256 + np.arange(256)
    freqs = np.float32(10000.0) ** (-np.arange(32, dtype=np.float32) / np.float32(32))
    ang = pos[:, None] * freqs[None]
    c, s = np.cos(ang.astype(np.float32)), np.sin(ang.astype(np.float32))
    return np.tile(c, (1, 4)).astype(np.float32), np.concatenate([-s, s, -s, s], 1).astype(np.float32)


def block_place(m):
    late = lax.div(m, 2)
    return m * 3 - late * (5 + 2 * (m - 2))


def norm_rows(values, gain):
    return values * lax.rsqrt(jnp.mean(values * values, axis=-1, keepdims=True) + EPS) * gain


TILES = ((0, 512), (512, 512), (1024, 384))


def front_kernel(
    tokens_h, vf_h, wq_h, wk_h, wv_h, wo_h, wg_h, wu_h, wd_h, gain_attn_ref, gain_mlp_ref, cot_h, cos_ref, sin_ref,
    q_h, k_h, v_h, o_h, ot_h, xt_h, lse_ref, middle_h, base_h, send4_h, own6_h, send6_h, recv6_h, gg_h, gu_h, gd_h,
    tok, cot, x, xt, wq, wk, wv, vf, q, k, v, vt, o, ot, wo, recv2, send2, c, x2t, wg, wu, wd,
    ht, hid, gg, ug, base, send4, send6, recv6,
    load, ysem, store,
):
    tp = lax.axis_index("tp")
    mesh_id = pl.DeviceIdType.MESH
    barrier = pltpu.get_barrier_semaphore()
    pl.semaphore_signal(barrier, inc=1, device_id={"tp": 1 - tp}, device_id_type=mesh_id)
    loads = {}

    def fetch(name, src, dst):
        loads[name] = pltpu.make_async_copy(src, dst, load.at[len(loads)])
        loads[name].start()

    half = lambda b: pl.ds(b * BLK, BLK)
    for b in range(2):
        fetch(("tok", b), tokens_h.at[half(b)], tok.at[half(b)])
    for name, src, dst in (
        ("wq", wq_h, wq), ("wk", wk_h, wk), ("wv", wv_h, wv), ("vf", vf_h, vf), ("cot", cot_h, cot), ("wo", wo_h, wo),
        ("wg", wg_h, wg), ("wu", wu_h, wu), ("wd", wd_h, wd),
    ):
        fetch(name, src, dst)
    stores = []

    def keep(src, dst):
        stores.append(pltpu.make_async_copy(src, dst, store.at[len(stores)]))
        stores[-1].start()

    def peer(n, src, dst):
        return pltpu.make_async_remote_copy(
            src, dst, ysem.at[0, n], ysem.at[1, n], device_id={"tp": 1 - tp}, device_id_type=mesh_id
        )

    def mine(b):
        return pl.ds(pl.multiple_of(tp * 512 + b * BLK, BLK), BLK)

    def theirs(b):
        return pl.ds(pl.multiple_of((1 - tp) * 512 + b * BLK, BLK), BLK)

    lane = lax.broadcasted_iota(jnp.int32, (BLK, 128), 1)
    causal = lax.broadcasted_iota(jnp.int32, (BLK, BLK), 0) <= lax.broadcasted_iota(jnp.int32, (BLK, BLK), 1)
    gain_attn, gain_mlp = gain_attn_ref[...], gain_mlp_ref[...]
    sends = []
    for b in range(2):
        loads["tok", b].wait()
        x[mine(b), :] = norm_rows(tok[half(b), :], gain_attn).astype(BF)
        if b == 0:
            pl.semaphore_wait(barrier, 1)
        sends.append(peer(b, x.at[mine(b)], x.at[mine(b)]))
        sends[-1].start()
    loads["cot"].wait()
    for b in range(2):
        c[mine(b), :] = cot[half(b), :].astype(BF)
    for name in ("wq", "wk", "wv", "vf"):
        loads[name].wait()

    def project(m):
        row = pl.ds(pl.multiple_of(m * BLK, BLK), BLK)
        at = pl.ds(pl.multiple_of(block_place(m) * BLK, BLK), BLK)
        xm = x[row, :]
        cosine, sine = cos_ref[row, :], sin_ref[row, :]
        qf, kf = nn(xm, wq[...]), nn(xm, wk[...])
        low = (0.5 * nn(xm, wv[...]) + 0.5 * vf[row, :].astype(F32)).astype(BF)
        for t in range(4):
            cols = slice(t * 128, t * 128 + 128)
            q[at, cols] = turn(qf[:, cols], cosine, sine, lane).astype(BF) * 0.125
            k[at, cols] = turn(kf[:, cols], cosine, sine, lane).astype(BF)
        v[at, :] = low
        vt[:, at] = low.T
        xt[:, row] = xm.T

    def project_mine(b, carry):
        project(tp * 2 + b)
        return carry

    lax.fori_loop(0, 2, project_mine, 0)

    def project_theirs(b, carry):
        peer(b, x.at[mine(0)], x.at[mine(0)]).wait_recv()
        project((1 - tp) * 2 + b)
        return carry

    lax.fori_loop(0, 2, project_theirs, 0)
    cots = [peer(2 + b, c.at[mine(b)], c.at[mine(b)]) for b in range(2)]
    cots[0].start()
    for src, dst in ((q, q_h), (k, k_h), (v, v_h), (xt, xt_h)):
        keep(src, dst)
    lse_ref[...] = jnp.zeros_like(lse_ref)
    loads["wo"].wait()

    def attend(m):
        i = POS_OF[m]

        def pair(p, carry):
            cols = pl.ds(pl.multiple_of(p * 128, 128), 128)
            qb = q[rows(i), cols]
            parts = []
            for h in range(2):
                qm = jnp.where((lane < 64) == (h == 0), qb, jnp.zeros_like(qb))
                scores = [nt(k[rows(j), cols], qm) for j in range(i + 1)]
                scores[i] = jnp.where(causal, scores[i], -1e30)
                top = functools.reduce(jnp.maximum, [jnp.max(s, axis=0, keepdims=True) for s in scores])
                es = [jnp.exp(s - top) for s in scores]
                total = functools.reduce(jnp.add, [jnp.sum(e, axis=0, keepdims=True) for e in es])
                head = pl.ds(pl.multiple_of(p * 128 + h * 64, 64), 64)
                mix = functools.reduce(jnp.add, [nn(vt[head, rows(j)], es[j].astype(BF)) for j in range(i + 1)])
                parts.append(mix * (1.0 / total))
                lse_ref[lax.div(p, 2), pl.ds(2 * lax.rem(p, 2) + h, 1), rows(i)] = top + jnp.log(total)
            flat = jnp.concatenate(parts, axis=0)
            ot[cols, rows(m)] = flat.astype(BF)
            o[rows(m), cols] = flat.T.astype(BF)
            return carry

        lax.fori_loop(0, 4, pair, 0)

    twos = [peer(4 + b, send2.at[half(b)], recv2.at[half(b)]) for b in range(2)]
    for b in range(2):
        for side in range(2):

            @pl.when(tp == side)
            def _():
                attend((1 - side) * 2 + b)

        send2[half(b), :] = nn(o[theirs(b), :], wo[...]).astype(BF)
        twos[b].start()
    for side in range(2):

        @pl.when(tp == side)
        def _():
            attend(side * 2)
            attend(side * 2 + 1)

    keep(o, o_h)
    keep(ot, ot_h)
    for name in ("wg", "wu", "wd"):
        loads[name].wait()

    def gated(at):
        xm, cm = x[at, :], c[at, :]
        x2t[:, at] = xm.T
        for first, size in TILES:
            cols = slice(first, first + size)
            gate, up = nn(xm, wg[:, cols]), nn(xm, wu[:, cols])
            sigma = lax.logistic(gate)
            smooth = gate * sigma
            low = (smooth * up).astype(BF)
            hid[:, cols] = low
            ht[cols, at] = low.T
            back = nt(cm, wd[cols, :])
            gg[at, cols] = (back * up * (sigma * (1.0 + gate * (1.0 - sigma)))).astype(BF)
            ug[at, cols] = (back * smooth).astype(BF)
        return nn(hid[...], wd[...]), nt(gg[at, :], wg[...]) + nt(ug[at, :], wu[...])

    def block_mine(b, carry):
        here = pl.ds(pl.multiple_of(b * BLK, BLK), BLK)
        at = mine(b)
        peer(4 + b, send2.at[half(0)], recv2.at[half(0)]).wait_recv()
        middle = tok[here, :] + nn(o[at, :], wo[...]) + recv2[here, :].astype(F32)
        tok[here, :] = middle
        peer(b, x.at[half(0)], x.at[half(0)]).wait_send()
        x[at, :] = norm_rows(middle, gain_mlp).astype(BF)
        peer(6 + b, x.at[at], x.at[at]).start()
        branch, grad_in = gated(at)
        base[here, :] = tok[here, :] + branch
        cot[here, :] = grad_in
        return carry

    lax.fori_loop(0, 2, block_mine, 0)
    cots[1].start()
    keep(tok, middle_h)
    keep(base, base_h)
    keep(cot, own6_h)
    for copy in stores[:6]:
        copy.wait()
    columns = lambda t: slice(TILES[t][0], sum(TILES[t]))
    across = [(buf.at[:, : TILES[t][1]], gg, columns(t), gg_h) for t, buf in enumerate((wq, wk, wv))]
    across += [(buf.at[:, : TILES[t][1]], ug, columns(t), gu_h) for t, buf in enumerate((q, k, v))]
    down = [(buf.at[: TILES[t][1]], columns(t)) for t, buf in enumerate((ot, wo, recv2))]

    def gather(at, fresh):
        for buf, cols in down:
            new = nn(ht[cols, at], c[at, :])
            buf[...] = (new if fresh else buf[...].astype(F32) + new).astype(BF)

        def body(n, carry):
            tile = pl.ds(pl.multiple_of(n * BLK, BLK), BLK)
            turned = x2t[tile, at]
            for buf, right, cols, _ in across:
                new = nn(turned, right[at, cols])
                buf[tile, :] = (new if fresh else buf[tile, :].astype(F32) + new).astype(BF)
            return carry

        lax.fori_loop(0, 4, body, 0)

    gather(pl.ds(pl.multiple_of(tp * 512, 512), 512), True)
    for b in range(2):
        peer(6 + b, x.at[half(0)], x.at[half(0)]).wait_recv()
        peer(2 + b, c.at[half(0)], c.at[half(0)]).wait_recv()
        branch, grad_in = gated(theirs(b))
        send4[half(b), :] = branch.astype(BF)
        send6[half(b), :] = grad_in.astype(BF)
        if b == 0:
            peer(8, send6.at[half(0)], recv6.at[half(0)]).start()
        else:
            keep(send6, send6_h)
            keep(send4, send4_h)
        gather(theirs(b), False)
    last = [(buf, gd_h.at[cols]) for buf, cols in down] + [(buf, out.at[:, cols]) for buf, _, cols, out in across]
    for buf, out in last:
        keep(buf, out)
    peer(8, send6.at[half(0)], recv6.at[half(0)]).wait_recv()
    keep(recv6, recv6_h)
    for b in range(2):
        for n in (2, 4, 6):
            peer(n + b, recv6.at[half(0)], recv6.at[half(0)]).wait_send()
    peer(8, send6.at[half(0)], recv6.at[half(0)]).wait_send()
    for copy in stores[6:]:
        copy.wait()


def front(tokens, vf, wq, wk, wv, wo, wg, wu, wd, gain_attn, gain_mlp, cot, cos, sin):
    V = lambda shape, kind=BF: pltpu.VMEM(shape, kind)
    D = lambda *shape: pltpu.SemaphoreType.DMA(shape)
    hbm, vmem = pl.BlockSpec(memory_space=pl.ANY), pl.BlockSpec(memory_space=pltpu.VMEM)
    S = jax.ShapeDtypeStruct
    own, heads, turned, square = (512, 1024), (1024, 512), (512, 1024), (1024, 1024)
    hidden, across, half = (1024, 1408), (1408, 1024), (256, 1024)
    return pl.pallas_call(
        front_kernel,
        in_specs=[hbm] * 9 + [vmem] * 2 + [hbm] + [vmem] * 2,
        out_specs=[hbm] * 6 + [vmem] + [hbm] * 9,
        out_shape=[*[S(heads, BF)] * 4, S(turned, BF), S(square, BF), S((2, 8, 1024), F32), S(own, F32), S(own, F32), S(own, BF),
                   S(own, F32), S(own, BF), S(half, BF), S(hidden, BF), S(hidden, BF), S(across, BF)],
        scratch_shapes=[
            V(own, F32), V(own, F32), V(square), V(square), *[V(heads)] * 7, V(turned), V(heads), V(turned), V(own), V(own), V(own),
            V(square), V(square), V(hidden), V(hidden), V(across), V(across), V((256, 1408)), V(hidden), V(hidden), V(own, F32),
            V(own), V(own), V(half),
            D(11), D(2, 9), D(22),
        ],
        compiler_params=pltpu.CompilerParams(collective_id=4, has_side_effects=True, vmem_limit_bytes=63 << 20),
        cost_estimate=pl.CostEstimate(flops=40 * 10**9, bytes_accessed=60 << 20, transcendentals=5 << 20),
    )(tokens, vf, wq, wk, wv, wo, wg, wu, wd, gain_attn, gain_mlp, cot, cos, sin)


def ring_place(dp):
    core, x, z = lax.rem(dp, 2), lax.rem(lax.div(dp, 2), 2), lax.div(dp, 4)
    place = z + x * (7 - 2 * z)

    def device(where):
        side = lax.div(where, 4)
        return ((where + side * (7 - 2 * where)) * 2 + side) * 2 + core

    turn_no = lax.rem(place + core * (8 - 2 * place), 8)
    after = device(lax.rem(place + 1 + 6 * core, 8))
    before = device(lax.rem(place + 7 - 6 * core, 8))
    cube = (dp + 1 - 2 * core, dp + 2 - 4 * x, dp + 4 - 8 * lax.rem(z, 2), dp + 8 - 16 * lax.div(z, 2))
    return core, turn_no, after, before, cube


def remote(src, dst, send, recv, dp):
    return pltpu.make_async_remote_copy(
        src, dst, send, recv, device_id={"dp": dp}, device_id_type=pl.DeviceIdType.MESH
    )


class Ring:
    def __init__(self, place, takes, outs, own, sib, slots, sems):
        self.core, self.turn_no, self.after, self.before, self.cube = place
        self.takes, self.outs, self.own, self.sib, self.slots = takes, outs, own, sib, slots
        self.trade, self.rs, self.ag, self.over, self.keep = sems

    def piece(self, g, chunk):
        size = self.slots[g].shape[1]
        return pl.ds(pl.multiple_of(chunk * size, size), size)

    def traded(self, g, n):
        at = self.piece(g, lax.rem(15 + lax.rem(8 - self.turn_no, 8) - n, 8))
        return remote(
            self.takes[g](1 - self.core).at[at], self.sib[g].at[at], self.trade.at[0, g, n], self.trade.at[1, g, n], self.cube[0]
        )

    def trade_all(self):
        for n in range(8):
            for g in range(len(self.takes)):
                self.traded(g, n).start()

    def total(self, g, chunk):
        at = self.piece(g, chunk)
        return self.own[g][at, :].astype(F32) + self.sib[g][at, :].astype(F32)

    def first(self, g, chunk):
        return remote(
            self.own[g].at[self.piece(g, chunk)], self.slots[g].at[0], self.rs.at[0, g, 0], self.rs.at[1, g, 0], self.after
        )

    def begin(self, g):
        self.traded(g, 0).wait_recv()
        chunk = lax.rem(self.turn_no + 7, 8)
        self.own[g][self.piece(g, chunk), :] = self.total(g, chunk).astype(BF)
        self.first(g, chunk).start()

    def add(self, g, t):
        chunk = lax.rem(self.turn_no + 14 - t, 8)
        self.traded(g, t + 1).wait_recv()
        remote(self.slots[g].at[t], self.slots[g].at[t], self.rs.at[0, g, t], self.rs.at[1, g, t], self.after).wait_recv()
        self.slots[g][t] = (self.slots[g][t].astype(F32) + self.total(g, chunk)).astype(BF)

    def add_on(self, g, t):
        self.add(g, t)
        remote(self.slots[g].at[t], self.slots[g].at[t + 1], self.rs.at[0, g, t + 1], self.rs.at[1, g, t + 1], self.after).start()

    def spot(self, g, chunk):
        return self.outs[g](self.core, chunk)

    def turn_over(self, g):
        self.add(g, 6)
        spot = self.spot(g, self.turn_no)
        last = self.slots[g].at[6]
        remote(last, spot, self.ag.at[0, g, 0], self.ag.at[1, g, 0], self.after).start()
        remote(last, spot, self.over.at[0, g, 0], self.over.at[1, g, 0], self.cube[0]).start()
        pltpu.make_async_copy(last, spot, self.keep.at[g]).start()

    def pass_on(self, g, t):
        spot = self.spot(g, lax.rem(self.turn_no + 15 - t, 8))
        remote(spot, spot, self.ag.at[0, g, t], self.ag.at[1, g, t], self.after).wait_recv()

        @pl.when(t < 6)
        def _():
            remote(spot, spot, self.ag.at[0, g, t + 1], self.ag.at[1, g, t + 1], self.after).start()

        remote(spot, spot, self.over.at[0, g, t + 1], self.over.at[1, g, t + 1], self.cube[0]).start()

    def end(self, g):
        spot = self.spot(g, self.turn_no)
        pltpu.make_async_copy(self.slots[g].at[6], spot, self.keep.at[g]).wait()

        def finish(t, _):
            remote(self.slots[g].at[0], self.slots[g].at[0], self.rs.at[0, g, t], self.rs.at[1, g, t], self.after).wait_send()
            remote(spot, spot, self.ag.at[0, g, t], self.ag.at[1, g, t], self.after).wait_send()
            return _

        lax.fori_loop(0, 7, finish, 0)

        def crossed(t, _):
            self.traded(g, t).wait_send()
            there = self.outs[g](1 - self.core, lax.rem(self.turn_no + t, 8))
            remote(spot, there, self.over.at[0, g, t], self.over.at[1, g, t], self.cube[0]).wait()
            return _

        lax.fori_loop(0, 8, crossed, 0)


def strip(ref, axis, halves, length):
    if axis == 0:
        return lambda core, chunk: ref.at[pl.ds(pl.multiple_of(core * halves + chunk * length, length), length)]
    return lambda core, chunk: ref.at[
        pl.ds(pl.multiple_of(chunk * length, length), length), pl.ds(pl.multiple_of(core * halves, halves), halves)
    ]


def half_of(ref, axis, halves):
    if axis == 0:
        return lambda core: ref.at[pl.ds(pl.multiple_of(core * halves, halves), halves)]
    return lambda core: ref.at[:, pl.ds(pl.multiple_of(core * halves, halves), halves)]


def norm_back_rows(values, gain, grad_in):
    factor = lax.rsqrt(jnp.mean(values * values, axis=-1, keepdims=True) + EPS)
    normed = values * factor
    grad_normed = grad_in * gain
    grad = factor * (grad_normed - normed * jnp.mean(grad_normed * normed, axis=-1, keepdims=True))
    return grad, jnp.sum(grad_in * normed, axis=0, keepdims=True)


def back_kernel(
    own6_h, send6_h, recv6_h, own4_h, send4_h, middle_h, cot_h, tokens_h, gain_attn_ref, gain_mlp_ref,
    wo_h, wq_h, wk_h, wv_h, q_h, k_h, v_h, o_h, ot_h, xt_h, lse_ref, cos_ref, sin_ref, gg_h, gu_h, gd_h,
    out_h, gt_h, gf_h, rq_h, rk_h, rv_h, ro_h, rg_h, ru_h, rd_h, gains_ref,
    f1, f2, f3, recv6, recv4, recv8, send8, c, wo, wq, wk, wv, q, k, v, o, ot, xt,
    dq, dk, dv, do, kt, dka, dva, dl, own8, dwq, dwk, dwv, dwo,
    mg, mu, md, sg, su, sd, lg, lu, ld, bq, bk, bv, bo, aq, ak, av, ao,
    load, ysem, trade1, rs1, ag1, over1, keep1, trade2, rs2, ag2, over2, keep2, gain_in, gain_sem, store,
):
    dp, tp = lax.axis_index("dp"), lax.axis_index("tp")
    place = ring_place(dp)
    core, turn_no, after, before, cube = place
    mesh_id = pl.DeviceIdType.MESH
    barrier = pltpu.get_barrier_semaphore()
    for other in (*cube, after, before):
        pl.semaphore_signal(barrier, inc=1, device_id={"dp": other}, device_id_type=mesh_id)
    pl.semaphore_signal(barrier, inc=1, device_id={"tp": 1 - tp}, device_id_type=mesh_id)

    loads = {}

    def fetch(name, src, dst):
        loads[name] = pltpu.make_async_copy(src, dst, load.at[len(loads)])
        loads[name].start()

    one = Ring(
        place, (half_of(gd_h, 1, 512), half_of(gg_h, 0, 512), half_of(gu_h, 0, 512)),
        (strip(rd_h, 1, 512, 176), strip(rg_h, 0, 512, 64), strip(ru_h, 0, 512, 64)),
        (md, mg, mu), (sd, sg, su), (ld, lg, lu), (trade1, rs1, ag1, over1, keep1),
    )
    two = Ring(
        place, (half_of(dwq, 0, 512), half_of(dwk, 0, 512), half_of(dwv, 0, 512), half_of(dwo, 0, 256)),
        (strip(rq_h, 0, 512, 64), strip(rk_h, 0, 512, 64), strip(rv_h, 0, 512, 64), strip(ro_h, 0, 256, 32)),
        (half_of(dwq, 0, 512)(core), half_of(dwk, 0, 512)(core), half_of(dwv, 0, 512)(core), half_of(dwo, 0, 256)(core)),
        (bq, bk, bv, bo), (aq, ak, av, ao), (trade2, rs2, ag2, over2, keep2),
    )
    for g, (whole, mine) in enumerate(((gd_h, md), (gg_h, mg), (gu_h, mu))):
        fetch(("m", g), one.takes[g](core), mine)
    for name, src, dst in (
        ("own6", own6_h, f1), ("recv6", recv6_h, recv6.at[pl.ds(0, BLK)]), ("middle", middle_h, f2), ("cot", cot_h, f3), ("k", k_h, k), ("wo", wo_h, wo), ("o", o_h, o),
        ("q", q_h, q), ("v", v_h, v), ("wq", wq_h, wq), ("wk", wk_h, wk), ("wv", wv_h, wv), ("ot", ot_h, ot), ("xt", xt_h, xt),
    ):
        fetch(name, src, dst)
    pl.semaphore_wait(barrier, 7)

    def peer(n, src, dst):
        return pltpu.make_async_remote_copy(
            src, dst, ysem.at[0, n], ysem.at[1, n], device_id={"tp": 1 - tp}, device_id_type=mesh_id
        )

    half = lambda b: pl.ds(b * BLK, BLK)
    six = peer(0, send6_h.at[half(1)], recv6.at[half(1)])
    six.start()
    one.trade_all()
    for g in range(3):
        loads["m", g].wait()
        one.begin(g)

    lane = lax.broadcasted_iota(jnp.int32, (BLK, 128), 1)
    causal = lax.broadcasted_iota(jnp.int32, (BLK, BLK), 0) <= lax.broadcasted_iota(jnp.int32, (BLK, BLK), 1)
    gain_mlp, gain_attn = gain_mlp_ref[...], gain_attn_ref[...]
    dka[...] = jnp.zeros_like(dka)
    dva[...] = jnp.zeros_like(dva)
    loads["k"].wait()
    for j in range(4):
        kt[:, rows(j)] = k[rows(j), :].T

    def one_piece(n):
        step, g = divmod(n, 3)
        if step < 6:
            one.add_on(g, step)
        elif step == 6:
            one.turn_over(g)
        else:
            one.pass_on(g, step - 7)

    def two_step(g, step):
        if step < 6:
            two.add_on(g, step)
        elif step == 6:
            two.turn_over(g)
        else:
            two.pass_on(g, step - 7)

    def branch_back(m):
        at = pl.ds(pl.multiple_of(m * BLK, BLK), BLK)
        low = nt(c[at, :], wo[...]).astype(BF)
        do[at, :] = low
        prod = (low.astype(F32) * o[at, :].astype(F32)).T
        for h in range(8):
            dl[h : h + 1, at] = jnp.sum(prod[h * 64 : h * 64 + 64, :], axis=0, keepdims=True)

    def attend_back(m, p):
        cols = pl.ds(pl.multiple_of(p * 128, 128), 128)
        i = POS_OF[m]
        qb, dob = q[rows(i), cols], do[rows(m), cols]
        parts = []
        for h in range(2):
            mine = (lane < 64) == (h == 0)
            qm = jnp.where(mine, qb, jnp.zeros_like(qb))
            dom = jnp.where(mine, dob, jnp.zeros_like(dob))
            lse = lse_ref[lax.div(p, 2), pl.ds(2 * lax.rem(p, 2) + h, 1), rows(i)]
            delta = dl[pl.ds(2 * p + h, 1), rows(m)]
            head = pl.ds(pl.multiple_of(p * 128 + h * 64, 64), 64)
            dqt = None
            for j in range(i + 1):
                weights = jnp.exp(nt(k[rows(j), cols], qm) - lse)
                if j == i:
                    weights = jnp.where(causal, weights, 0.0)
                ds = (weights * (nt(v[rows(j), cols], dom) - delta)).astype(BF)
                dva[rows(j), cols] = dva[rows(j), cols] + nn(weights.astype(BF), dom)
                dka[rows(j), cols] = dka[rows(j), cols] + nn(ds, qm)
                part = nn(kt[head, rows(j)], ds)
                dqt = part if dqt is None else dqt + part
            parts.append(dqt)
        grad = (jnp.concatenate(parts, axis=0).T * 0.125).astype(BF).astype(F32)
        dq[rows(m), cols] = turn(grad, cos_ref[rows(m), :], -sin_ref[rows(m), :], lane).astype(BF)

    def block_back(side_of, b, pieces):
        branch_back(side_of(tp) * 2 + b)

        def pair(p, carry):
            for side in range(2):

                @pl.when(tp == side)
                def _():
                    attend_back(side_of(side) * 2 + b, p)

            for late, n in enumerate(pieces):
                if n is not None:

                    @pl.when(p == late)
                    def _():
                        one_piece(n)

            return carry

        lax.fori_loop(0, 4, pair, 0)

    for name in ("own6", "recv6", "middle", "cot", "wo", "o", "q", "v"):
        loads[name].wait()
    gain_sum = jnp.zeros((1, 1024), F32)
    seven = []
    for b in range(2):
        if b == 1:
            six.wait_recv()
            seven[0].start()

        def rows_back(n, total):
            at = pl.ds(pl.multiple_of(b * BLK + n * 64, 64), 64)
            grad_in = f1[at, :] + recv6[at, :].astype(F32)
            grad, part = norm_back_rows(f2[at, :], gain_mlp, grad_in)
            grad = f3[at, :] + grad
            f1[at, :] = grad
            c[pl.ds(pl.multiple_of(tp * 512 + b * BLK + n * 64, 64), 64), :] = grad.astype(BF)
            return total + part

        gain_sum = lax.fori_loop(0, 4, rows_back, gain_sum)
        mine = c.at[pl.ds(pl.multiple_of(tp * 512 + b * BLK, BLK), BLK)]
        seven.append(peer(2 + b, mine, mine))
        if b == 1:
            seven[1].start()
        block_back(lambda side: side, b, ((None, None, None, 0), (2, 3, 4, 5))[b])
        one_piece((1, 6)[b])
    late = pltpu.make_async_copy(own4_h, f3, load.at[len(loads)])
    late.start()
    fetch_tokens = pltpu.make_async_copy(tokens_h, f2, load.at[len(loads) + 1])
    fetch_tokens.start()
    gains_ref[...] = jnp.zeros_like(gains_ref)
    gains_ref[0:1, :] = gain_sum
    four = peer(4, send4_h, recv4)
    for b in range(2):
        seven[b].wait_recv()
        if b == 1:
            four.start()
        block_back(lambda side: 1 - side, b, range(7 + 5 * b, 11 + 5 * b))
        one_piece(11 + 5 * b)
    for m in range(4):
        at = rows(POS_OF[m])
        cosine, sine = cos_ref[rows(m), :], -sin_ref[rows(m), :]
        for t in range(4):
            cols = slice(t * 128, t * 128 + 128)
            grad = dka[at, cols].astype(BF).astype(F32)
            dk[rows(m), cols] = turn(grad, cosine, sine, lane).astype(BF)
        dv[rows(m), :] = (0.5 * dva[at, :].astype(BF).astype(F32)).astype(BF)
    keep_gf = pltpu.make_async_copy(dv, gf_h, store.at[0])
    keep_gf.start()
    one_piece(17)
    for name in ("wq", "wk", "wv", "xt", "ot"):
        loads[name].wait()

    def into_rows(at):
        return nt(dq[at, :], wq[...]) + nt(dk[at, :], wk[...]) + nt(dv[at, :], wv[...])

    for which in range(2):
        side = (1 - core) * (1 - which) + core * which
        at = pl.ds(pl.multiple_of(side * 512, 512), 512)
        for n, (dst, src) in enumerate(((dwq, dq), (dwk, dk), (dwv, dv))):
            dst[at, :] = nn(xt[at, :], src[...]).astype(BF)
            if n < 2:
                one_piece(18 + 2 * which + n)
        at = pl.ds(pl.multiple_of(side * 256, 256), 256)
        dwo[at, :] = nn(ot[at, :], c[...]).astype(BF)
        if which == 0:
            two.trade_all()
    for g in range(4):
        two.begin(g)
    eight = []
    for b in range(2):
        at = pl.ds(pl.multiple_of((1 - tp) * 512 + b * BLK, BLK), BLK)
        send8[half(b), :] = into_rows(at).astype(BF)
        eight.append(peer(5 + b, send8.at[half(b)], recv8.at[half(b)]))
        eight[b].start()
        one_piece(22 + b)

    def gain_swap(n):
        where = {"tp": 1 - tp} if n == 4 else {"dp": cube[n]}
        return pltpu.make_async_remote_copy(
            gains_ref, gain_in.at[n], gain_sem.at[0, n], gain_sem.at[1, n], device_id=where, device_id_type=mesh_id
        )

    def rows_last(b, total):
        eight[b].wait_recv()

        def body(n, total):
            at = pl.ds(pl.multiple_of(b * BLK + n * 64, 64), 64)
            grad, part = norm_back_rows(f2[at, :], gain_attn, own8[at, :] + recv8[at, :].astype(F32))
            f1[at, :] = f1[at, :] + grad
            return total + part

        return lax.fori_loop(0, 4, body, total)

    keep_out = pltpu.make_async_copy(f3, out_h, store.at[1])
    keep_gt = pltpu.make_async_copy(f1, gt_h, store.at[2])
    gain_sum = jnp.zeros((1, 1024), F32)
    for step in range(14):
        for g in range(4):
            two_step(g, step)
        for n in range(24 + PACE[step], 24 + PACE[step + 1]):
            one_piece(n)
        if step < 2:
            at = pl.ds(pl.multiple_of(tp * 512 + step * BLK, BLK), BLK)
            own8[half(step), :] = into_rows(at)
        if step == 2:
            late.wait()
            fetch_tokens.wait()
        if step in (5, 6):
            gain_sum = rows_last(step - 5, gain_sum)
        if step == 6:
            gains_ref[1:2, :] = gain_sum
            keep_gt.start()
        if step == 7:
            four.wait_recv()

            def out_rows(n, carry):
                at = pl.ds(pl.multiple_of(n * 64, 64), 64)
                f3[at, :] = f3[at, :] + recv4[at, :].astype(F32)
                return carry

            lax.fori_loop(0, 8, out_rows, 0)
            keep_out.start()
        if step > 8:
            gain_swap(step - 9).wait()
            gains_ref[...] = gains_ref[...] + gain_in[step - 9]
        if 8 <= step < 13:
            gain_swap(step - 8).start()
    for g in range(3):
        one.end(g)
    for g in range(4):
        two.end(g)
    for copy in (six, *seven, *eight, four):
        copy.wait_send()
    for copy in (keep_gf, keep_out, keep_gt):
        copy.wait()


PACE = (0, 2, 4, 6, 8, 10, 12, 14, 16, 18, 18, 18, 18, 18, 18)


def back(own6, send6, recv6, own4, send4, middle, cot, tokens, gain_attn, gain_mlp, wo, wq, wk, wv, q, k, v, o, ot, xt, lse, cos, sin, gg, gu, gd):
    V = lambda shape, kind=BF: pltpu.VMEM(shape, kind)
    D = lambda *shape: pltpu.SemaphoreType.DMA(shape)
    hbm, vmem = pl.BlockSpec(memory_space=pl.ANY), pl.BlockSpec(memory_space=pltpu.VMEM)
    S = jax.ShapeDtypeStruct
    wide = (1024, 1024)
    return pl.pallas_call(
        back_kernel,
        in_specs=[hbm] * 8 + [vmem] * 2 + [hbm] * 10 + [vmem] * 3 + [hbm] * 3,
        out_specs=[hbm] * 10 + [vmem],
        out_shape=[S((512, 1024), F32), S((512, 1024), F32), S((1024, 512), BF), *[S((1024, 512), BF)] * 3, S((512, 1024), BF),
                   S((1024, 1408), BF), S((1024, 1408), BF), S((1408, 1024), BF), S((8, 1024), F32)],
        scratch_shapes=[
            *[V((512, 1024), F32)] * 3, *[V((512, 1024))] * 4, V(wide), V((512, 1024)), *[V((1024, 512))] * 7, V((512, 1024)), V(wide),
            *[V((1024, 512))] * 4, V((512, 1024)), *[V((1024, 512), F32)] * 2, V((8, 1024), F32), V((512, 1024), F32),
            *[V((1024, 512))] * 3, V((512, 1024)),
            *[V((512, 1408)), V((512, 1408)), V((1408, 512))] * 2, V((7, 64, 1408)), V((7, 64, 1408)), V((7, 176, 512)),
            *[V((512, 512))] * 3, V((256, 1024)), *[V((7, 64, 512))] * 3, V((7, 32, 1024)),
            D(20), D(2, 7), D(2, 3, 8), D(2, 3, 7), D(2, 3, 7), D(2, 3, 8), D(3), D(2, 4, 8), D(2, 4, 7), D(2, 4, 7), D(2, 4, 8), D(4),
            V((5, 8, 1024), F32), D(2, 5), D(3),
        ],
        compiler_params=pltpu.CompilerParams(collective_id=3, has_side_effects=True, vmem_limit_bytes=62 << 20),
        cost_estimate=pl.CostEstimate(flops=30 * 10**9, bytes_accessed=60 << 20, transcendentals=5 << 20),
    )(own6, send6, recv6, own4, send4, middle, cot, tokens, gain_attn, gain_mlp, wo, wq, wk, wv, q, k, v, o, ot, xt, lse, cos, sin, gg, gu, gd)


PIECES = 4


def finish_kernel(*refs):
    gains_ref, ins, outs, wide = refs[0], refs[1:11], refs[11:21], refs[23:39]
    through, load, store = refs[39:]
    for n in range(2):
        refs[21 + n][...] = gains_ref[n : n + 1, :]
    into = [pltpu.make_async_copy(ins[n], through.at[n], load.at[8, n]) for n in range(2)]
    whole = [pltpu.make_async_copy(through.at[n], outs[n], store.at[n, 0]) for n in range(2)]
    for copy in into:
        copy.start()
    low, high = wide[:8], wide[8:]
    order = (5, 6, 7, 1, 2, 3, 4, 0)

    def part(ref, piece):
        size = ref.shape[0] // PIECES
        return ref.at[pl.ds(piece * size, size)]

    for a in order:
        for piece in range(PIECES):
            pltpu.make_async_copy(part(ins[a + 2], piece), part(low[a], piece), load.at[a, piece]).start()
    for n in range(2):
        into[n].wait()
        whole[n].start()
    for a in order:
        for piece in range(PIECES):
            pltpu.make_async_copy(part(ins[a + 2], piece), part(low[a], piece), load.at[a, piece]).wait()
            size = low[a].shape[0] // PIECES

            def widen(n, carry):
                at = pl.ds(pl.multiple_of(piece * size + n * 16, 16), 16)
                high[a][at, :] = low[a][at, :].astype(F32)
                return carry

            lax.fori_loop(0, size // 16, widen, 0, unroll=2)
            pltpu.make_async_copy(part(high[a], piece), part(outs[a + 2], piece), store.at[a + 2, piece]).start()
    for a in order:
        for piece in range(PIECES):
            pltpu.make_async_copy(part(high[a], piece), part(outs[a + 2], piece), store.at[a + 2, piece]).wait()
    for copy in whole:
        copy.wait()


def finish(gains, *arrays):
    hbm, vmem = pl.BlockSpec(memory_space=pl.ANY), pl.BlockSpec(memory_space=pltpu.VMEM)
    return pl.pallas_call(
        finish_kernel,
        in_specs=[vmem] + [hbm] * 10,
        out_specs=[hbm] * 10 + [vmem] * 2,
        out_shape=[jax.ShapeDtypeStruct(a.shape, F32) for a in arrays] + [jax.ShapeDtypeStruct((1, 1024), F32)] * 2,
        scratch_shapes=[
            *[pltpu.VMEM(a.shape, BF) for a in arrays[2:]], *[pltpu.VMEM(a.shape, F32) for a in arrays[2:]],
            pltpu.VMEM((2, *arrays[0].shape), F32), pltpu.SemaphoreType.DMA((9, PIECES)), pltpu.SemaphoreType.DMA((10, PIECES)),
        ],
        compiler_params=pltpu.CompilerParams(vmem_limit_bytes=60 << 20),
        cost_estimate=pl.CostEstimate(flops=10**7, bytes_accessed=48 << 20, transcendentals=0),
    )(gains, *arrays)

def local_pair(
    tokens,
    v_first,
    w_query,
    w_key,
    w_value,
    w_out,
    w_gate,
    w_up,
    w_down,
    gain_attn,
    gain_mlp,
    seq_lens,
    cotangent,
):
    cosine, sine = tables()
    (query, keys, mixed_values, attended, attended_t, normed_t, row_lse, middle, base, send_out, own_in, send_in, got_in,
     grad_gate, grad_up, grad_down) = front(
        tokens, v_first, w_query, w_key, w_value, w_out, w_gate, w_up, w_down, gain_attn[None], gain_mlp[None], cotangent, cosine, sine
    )
    layer_out, grad_tokens, grad_first, *low_grads, gains = back(
        own_in, send_in, got_in, base, send_out, middle, cotangent, tokens, gain_attn[None], gain_mlp[None], w_out, w_query, w_key, w_value,
        query, keys, mixed_values, attended, attended_t, normed_t, row_lse, cosine, sine, grad_gate, grad_up, grad_down,
    )
    layer_out, grad_tokens, grad_first, *wide, gain_mlp_grad, gain_attn_grad = finish(gains, layer_out, grad_tokens, grad_first, *low_grads)
    grad_gain_mlp, grad_gain_attn = gain_mlp_grad[0], gain_attn_grad[0]
    return (layer_out, grad_tokens, grad_first, *wide, grad_gain_attn, grad_gain_mlp)


def local(
    tokens,
    v_first,
    w_query,
    w_key,
    w_value,
    w_out,
    w_gate,
    w_up,
    w_down,
    gain_attn,
    gain_mlp,
    seq_lens,
    cotangent,
):
    tp_count = lax.axis_size("tp")
    row_share = tokens.shape[0]
    doc_ids, positions = layout(seq_lens[0], row_share, tp_count)
    normed_attn = lax.all_gather(
        normalize(tokens, gain_attn).astype(jnp.bfloat16), "tp", axis=0, tiled=True
    )
    query = rotate(
        jnp.dot(normed_attn, w_query, preferred_element_type=jnp.float32), positions, HDIM, 1.0
    ).astype(jnp.bfloat16)
    keys = rotate(
        jnp.dot(normed_attn, w_key, preferred_element_type=jnp.float32), positions, HDIM, 1.0
    ).astype(jnp.bfloat16)
    value_pre = jnp.dot(normed_attn, w_value, preferred_element_type=jnp.float32)
    mixed_values = (0.5 * value_pre + 0.5 * v_first.astype(jnp.float32)).astype(jnp.bfloat16)
    attended, row_lse = attention_forward(query, keys, mixed_values, doc_ids, positions, HDIM)
    middle = tokens + lax.psum_scatter(
        jnp.dot(attended, w_out, preferred_element_type=jnp.float32),
        "tp",
        scatter_dimension=0,
        tiled=True,
    )
    normed_mlp = normalize(middle, gain_mlp).astype(jnp.bfloat16)
    grad_branch = cotangent.astype(jnp.bfloat16)
    mlp_rows = lax.all_gather(normed_mlp, "tp", axis=0, tiled=True)
    gate = jnp.dot(mlp_rows, w_gate, preferred_element_type=jnp.float32)
    up_values = jnp.dot(mlp_rows, w_up, preferred_element_type=jnp.float32)
    hidden = (jax.nn.silu(gate) * up_values).astype(jnp.bfloat16)
    layer_out = middle + lax.psum_scatter(
        jnp.dot(hidden, w_down, preferred_element_type=jnp.float32).astype(jnp.bfloat16),
        "tp",
        scatter_dimension=0,
        tiled=True,
    ).astype(jnp.float32)
    cot_rows = lax.all_gather(grad_branch, "tp", axis=0, tiled=True)
    grad_down = inner_rows(hidden, cot_rows)
    gate_grad, up_grad = swiglu_back(gate, up_values, outer_cols(cot_rows, w_down))
    grad_gate = inner_rows(mlp_rows, gate_grad)
    grad_up = inner_rows(mlp_rows, up_grad)
    grad_mlp_in = lax.psum_scatter(
        (outer_cols(gate_grad, w_gate) + outer_cols(up_grad, w_up)).astype(jnp.bfloat16),
        "tp",
        scatter_dimension=0,
        tiled=True,
    ).astype(jnp.float32)
    middle_back, grad_gain_mlp = normalize_back(middle, gain_mlp, grad_mlp_in)
    grad_middle = cotangent + middle_back
    attn_cot_rows = lax.all_gather(grad_middle.astype(jnp.bfloat16), "tp", axis=0, tiled=True)
    grad_output = inner_rows(attended, attn_cot_rows)
    grad_attended = outer_cols(attn_cot_rows, w_out).astype(jnp.bfloat16)
    query_grad, key_grad, mixed_grad = attention_backward(
        query, keys, mixed_values, grad_attended, row_lse, doc_ids, positions, HDIM
    )
    half_mixed = 0.5 * mixed_grad.astype(jnp.float32)
    value_grad = half_mixed.astype(jnp.bfloat16)
    query_pre_grad = rotate(query_grad.astype(jnp.float32), positions, HDIM, -1.0).astype(
        jnp.bfloat16
    )
    key_pre_grad = rotate(key_grad.astype(jnp.float32), positions, HDIM, -1.0).astype(jnp.bfloat16)
    grad_query = inner_rows(normed_attn, query_pre_grad)
    grad_key = inner_rows(normed_attn, key_pre_grad)
    grad_value = inner_rows(normed_attn, value_grad)
    grad_attn_in = lax.psum_scatter(
        (
            outer_cols(query_pre_grad, w_query)
            + outer_cols(key_pre_grad, w_key)
            + outer_cols(value_grad, w_value)
        ).astype(jnp.bfloat16),
        "tp",
        scatter_dimension=0,
        tiled=True,
    ).astype(jnp.float32)
    tokens_back, grad_gain_attn = normalize_back(tokens, gain_attn, grad_attn_in)
    grad_tokens = grad_middle + tokens_back
    grad_query, grad_key, grad_value, grad_output, grad_gate, grad_up, grad_down = (
        lax.psum(grad_query.astype(jnp.bfloat16), "dp").astype(jnp.float32),
        lax.psum(grad_key.astype(jnp.bfloat16), "dp").astype(jnp.float32),
        lax.psum(grad_value.astype(jnp.bfloat16), "dp").astype(jnp.float32),
        lax.psum(grad_output.astype(jnp.bfloat16), "dp").astype(jnp.float32),
        lax.psum(grad_gate.astype(jnp.bfloat16), "dp").astype(jnp.float32),
        lax.psum(grad_up.astype(jnp.bfloat16), "dp").astype(jnp.float32),
        lax.psum(grad_down.astype(jnp.bfloat16), "dp").astype(jnp.float32),
    )
    grad_gain_attn, grad_gain_mlp = lax.psum((grad_gain_attn, grad_gain_mlp), ("dp", "tp"))
    return (
        layer_out,
        grad_tokens,
        half_mixed,
        grad_query,
        grad_key,
        grad_value,
        grad_output,
        grad_gate,
        grad_up,
        grad_down,
        grad_gain_attn,
        grad_gain_mlp,
    )


def solution(mesh):
    in_specs = (
        P(("dp", "tp"), None),
        P("dp", "tp"),
        P(None, "tp"),
        P(None, "tp"),
        P(None, "tp"),
        P("tp", None),
        P(None, "tp"),
        P(None, "tp"),
        P("tp", None),
        P(),
        P(),
        P("dp", None),
        P(("dp", "tp"), None),
    )
    out_specs = (
        P(("dp", "tp"), None),
        P(("dp", "tp"), None),
        P("dp", "tp"),
        P(None, "tp"),
        P(None, "tp"),
        P(None, "tp"),
        P("tp", None),
        P(None, "tp"),
        P(None, "tp"),
        P("tp", None),
        P(),
        P(),
    )

    def step(*args):
        tokens, seq_lens = args[0], args[11]
        pair = mesh.shape["tp"] == 2 and mesh.shape["dp"] == 16 and seq_lens.shape[1] == 1 and tokens.shape == (512, 1024)
        return (local_pair if pair else local)(*args)

    return jax.shard_map(step, mesh=mesh, in_specs=in_specs, out_specs=out_specs, check_vma=False)
```

```python
import functools

import jax
import jax.numpy as jnp
import numpy as np
from jax import lax
from jax.experimental import pallas as pl
from jax.experimental.pallas import tpu as pltpu
from jax.sharding import PartitionSpec as P

HDIM = 64


EPS = 1e-06


def layout(seq_row, row_share, tp_count):
    group_rows = row_share * tp_count
    row_ids = jnp.arange(group_rows, dtype=jnp.int32)
    device = row_ids // row_share
    local_row = row_ids % row_share
    pieces = seq_row // (2 * tp_count)
    slot_ends = jnp.cumsum(2 * pieces)
    starts = slot_ends - 2 * pieces
    offset = local_row[:, None] - starts[None, :]
    inside = (offset >= 0) & (offset < 2 * pieces[None, :])
    first_half = offset < pieces[None, :]
    mirror = 2 * tp_count - 1 - device[:, None]
    position = jnp.where(
        first_half,
        device[:, None] * pieces[None, :] + offset,
        mirror * pieces[None, :] + offset - pieces[None, :],
    )
    slot_ids = jnp.arange(seq_row.shape[0], dtype=jnp.int32)
    doc_ids = jnp.sum(jnp.where(inside, slot_ids[None, :], 0), axis=1)
    positions = jnp.sum(jnp.where(inside, position, 0), axis=1)
    return (doc_ids, positions)


def rotate(values, positions, head_dim, turn_sign):
    row_count, width_all = values.shape
    half_dim = head_dim // 2
    shaped = values.reshape(row_count, width_all // head_dim, head_dim)
    freqs = 10000.0 ** (-jnp.arange(half_dim, dtype=jnp.float32) / half_dim)
    angles = positions.astype(jnp.float32)[:, None] * freqs[None, :]
    cosine = jnp.cos(angles)[:, None, :]
    sine = turn_sign * jnp.sin(angles)[:, None, :]
    front = shaped[..., :half_dim]
    behind = shaped[..., half_dim:]
    turned = jnp.concatenate(
        [front * cosine - behind * sine, behind * cosine + front * sine], axis=-1
    )
    return turned.reshape(row_count, width_all)


def normalize(values, gain):
    return values * lax.rsqrt(jnp.mean(values * values, axis=-1, keepdims=True) + EPS) * gain


def normalize_back(values, gain, grad_in):
    factor = lax.rsqrt(jnp.mean(values * values, axis=-1, keepdims=True) + EPS)
    normed = values * factor
    grad_normed = grad_in * gain
    grad_values = factor * (
        grad_normed - normed * jnp.mean(grad_normed * normed, axis=-1, keepdims=True)
    )
    return (grad_values, jnp.sum(grad_in * normed, axis=0))


def inner_rows(left, right):
    return lax.dot_general(
        left, right, (((0,), (0,)), ((), ())), preferred_element_type=jnp.float32
    )


def outer_cols(left, right):
    return lax.dot_general(
        left, right, (((1,), (1,)), ((), ())), preferred_element_type=jnp.float32
    )


def swiglu_back(gate, up_values, grad_hidden):
    sigma = jax.nn.sigmoid(gate)
    grad_gate = grad_hidden * up_values * (sigma * (1.0 + gate * (1.0 - sigma)))
    grad_upper = grad_hidden * (gate * sigma)
    return (grad_gate.astype(jnp.bfloat16), grad_upper.astype(jnp.bfloat16))


def block_mask(doc_ids, positions, first_row, block_rows):
    row_doc = lax.dynamic_slice_in_dim(doc_ids, first_row, block_rows, 0)
    row_pos = lax.dynamic_slice_in_dim(positions, first_row, block_rows, 0)
    return (row_doc[:, None] == doc_ids[None, :]) & (positions[None, :] <= row_pos[:, None])


def attention_forward(query, keys, values, doc_ids, positions, head_dim):
    group_rows, width_local = query.shape
    head_count = width_local // head_dim
    block_rows = min(512, group_rows)
    block_count = group_rows // block_rows
    score_scale = head_dim ** (-0.5)
    key_heads = keys.reshape(group_rows, head_count, head_dim)
    value_heads = values.reshape(group_rows, head_count, head_dim)

    def forward_block(block_index):
        first_row = block_index * block_rows
        query_rows = lax.dynamic_slice_in_dim(query, first_row, block_rows, 0).reshape(
            block_rows, head_count, head_dim
        )
        scores = (
            jnp.einsum("qhd,khd->hqk", query_rows, key_heads, preferred_element_type=jnp.float32)
            * score_scale
        )
        allowed = block_mask(doc_ids, positions, first_row, block_rows)
        scores = jnp.where(allowed[None], scores, -1e30)
        row_max = jnp.max(scores, axis=-1, keepdims=True)
        exponent = jnp.exp(scores - row_max)
        row_total = jnp.sum(exponent, axis=-1, keepdims=True)
        weights = (exponent / row_total).astype(jnp.bfloat16)
        mixture = jnp.einsum(
            "hqk,khd->qhd", weights, value_heads, preferred_element_type=jnp.float32
        )
        return (
            mixture.astype(jnp.bfloat16).reshape(block_rows, width_local),
            (row_max + jnp.log(row_total))[..., 0],
        )

    mixture, row_lse = lax.map(forward_block, jnp.arange(block_count, dtype=jnp.int32))
    return (mixture.reshape(group_rows, width_local), row_lse)


def attention_backward(query, keys, values, grad_mixture, row_lse, doc_ids, positions, head_dim):
    group_rows, width_local = query.shape
    head_count = width_local // head_dim
    block_rows = min(512, group_rows)
    block_count = group_rows // block_rows
    score_scale = head_dim ** (-0.5)
    key_heads = keys.reshape(group_rows, head_count, head_dim)
    value_heads = values.reshape(group_rows, head_count, head_dim)

    def backward_block(carry, block_index):
        key_total, value_total = carry
        first_row = block_index * block_rows
        query_rows = lax.dynamic_slice_in_dim(query, first_row, block_rows, 0).reshape(
            block_rows, head_count, head_dim
        )
        grad_rows = lax.dynamic_slice_in_dim(grad_mixture, first_row, block_rows, 0).reshape(
            block_rows, head_count, head_dim
        )
        scores = (
            jnp.einsum("qhd,khd->hqk", query_rows, key_heads, preferred_element_type=jnp.float32)
            * score_scale
        )
        allowed = block_mask(doc_ids, positions, first_row, block_rows)
        scores = jnp.where(allowed[None], scores, -1e30)
        weights = jnp.exp(scores - row_lse[block_index][..., None])
        weights_low = weights.astype(jnp.bfloat16)
        grad_weights = jnp.einsum(
            "qhd,khd->hqk", grad_rows, value_heads, preferred_element_type=jnp.float32
        )
        weighted_sum = jnp.sum(weights * grad_weights, axis=-1, keepdims=True)
        score_grad = (weights * (grad_weights - weighted_sum)).astype(jnp.bfloat16)
        query_grad = (
            jnp.einsum("hqk,khd->qhd", score_grad, key_heads, preferred_element_type=jnp.float32)
            * score_scale
        )
        key_total = (
            key_total
            + jnp.einsum("hqk,qhd->khd", score_grad, query_rows, preferred_element_type=jnp.float32)
            * score_scale
        )
        value_total = value_total + jnp.einsum(
            "hqk,qhd->khd", weights_low, grad_rows, preferred_element_type=jnp.float32
        )
        return (
            (key_total, value_total),
            query_grad.astype(jnp.bfloat16).reshape(block_rows, width_local),
        )

    zero_heads = jnp.zeros((group_rows, head_count, head_dim), jnp.float32)
    (key_total, value_total), query_grad = lax.scan(
        backward_block, (zero_heads, zero_heads), jnp.arange(block_count, dtype=jnp.int32)
    )
    return (
        query_grad.reshape(group_rows, width_local),
        key_total.reshape(group_rows, width_local).astype(jnp.bfloat16),
        value_total.reshape(group_rows, width_local).astype(jnp.bfloat16),
    )


BF, F32 = jnp.bfloat16, jnp.float32
BLK = 256
POS_OF = (0, 3, 1, 2)
NT = (((1,), (1,)), ((), ()))

def nt(a, b):
    return lax.dot_general(a, b, NT, preferred_element_type=F32)

def nn(a, b):
    return jnp.dot(a, b, preferred_element_type=F32)

def rows(block):
    return pl.ds(block * BLK, BLK)

def turn(u, cosine, sine, lane):
    near = jnp.where(lane % 64 < 32, pltpu.roll(u, 96, 1), pltpu.roll(u, 32, 1))
    return u * cosine + near * sine

FIRST = {}
for _m in range(4):
    for _j in range(POS_OF[_m] + 1):
        FIRST.setdefault(_j, (_m, 0))

def tables():
    pos = np.zeros(1024, np.float32)
    for m in range(4):
        pos[m*256:(m+1)*256] = POS_OF[m]*256 + np.arange(256)
    freqs = np.float32(10000.0) ** (-np.arange(32, dtype=np.float32) / np.float32(32))
    ang = pos[:, None] * freqs[None]
    c, s = np.cos(ang.astype(np.float32)), np.sin(ang.astype(np.float32))
    return np.tile(c, (1, 4)).astype(np.float32), np.concatenate([-s, s, -s, s], 1).astype(np.float32)


def block_place(m):
    late = lax.div(m, 2)
    return m * 3 - late * (5 + 2 * (m - 2))


def norm_rows(values, gain):
    return values * lax.rsqrt(jnp.mean(values * values, axis=-1, keepdims=True) + EPS) * gain


TILES = ((0, 512), (512, 512), (1024, 384))


def front_kernel(
    tokens_h, vf_h, wq_h, wk_h, wv_h, wo_h, wg_h, wu_h, wd_h, gain_attn_ref, gain_mlp_ref, cot_h, cos_ref, sin_ref,
    q_h, k_h, v_h, o_h, ot_h, xt_h, lse_ref, middle_h, base_h, send4_h, own6_h, send6_h, recv6_h, gg_h, gu_h, gd_h,
    tok, cot, x, xt, wq, wk, wv, vf, q, k, v, vt, o, ot, wo, recv2, send2, c, x2t, wg, wu, wd,
    ht, hid, gg, ug, base, send4, send6, recv6,
    load, ysem, store, gsem,
):
    tp = lax.axis_index("tp")
    mesh_id = pl.DeviceIdType.MESH
    barrier = pltpu.get_barrier_semaphore()
    pl.semaphore_signal(barrier, inc=1, device_id={"tp": 1 - tp}, device_id_type=mesh_id)
    loads = {}

    def fetch(name, src, dst):
        loads[name] = pltpu.make_async_copy(src, dst, load.at[len(loads)])
        loads[name].start()

    half = lambda b: pl.ds(b * BLK, BLK)
    quarter = lambda n: pl.ds(n * 128, 128)
    for n in range(4):
        fetch(("tok", n), tokens_h.at[quarter(n)], tok.at[quarter(n)])
    for name, src, dst in (
        ("wq", wq_h, wq), ("wk", wk_h, wk), ("wv", wv_h, wv), ("vf", vf_h, vf), ("cot", cot_h, cot), ("wo", wo_h, wo),
        ("wg", wg_h, wg), ("wu", wu_h, wu), ("wd", wd_h, wd),
    ):
        fetch(name, src, dst)
    stores = []

    def keep(src, dst):
        stores.append(pltpu.make_async_copy(src, dst, store.at[len(stores)]))
        stores[-1].start()

    def peer(n, src, dst):
        return pltpu.make_async_remote_copy(
            src, dst, ysem.at[0, n], ysem.at[1, n], device_id={"tp": 1 - tp}, device_id_type=mesh_id
        )

    def mine(b):
        return pl.ds(pl.multiple_of(tp * 512 + b * BLK, BLK), BLK)

    def theirs(b):
        return pl.ds(pl.multiple_of((1 - tp) * 512 + b * BLK, BLK), BLK)

    lane = lax.broadcasted_iota(jnp.int32, (BLK, 128), 1)
    causal = lax.broadcasted_iota(jnp.int32, (BLK, BLK), 0) <= lax.broadcasted_iota(jnp.int32, (BLK, BLK), 1)
    gain_attn, gain_mlp = gain_attn_ref[...], gain_mlp_ref[...]

    def first(n, here, there):
        return pltpu.make_async_remote_copy(
            here, there, gsem.at[0, n], gsem.at[1, n], device_id={"tp": 1 - tp}, device_id_type=mesh_id
        )

    for n in range(4):
        loads["tok", n].wait()
        at = pl.ds(pl.multiple_of(tp * 512 + n * 128, 128), 128)
        x[at, :] = norm_rows(tok[quarter(n), :], gain_attn).astype(BF)
        if n == 0:
            pl.semaphore_wait(barrier, 1)
        first(n, x.at[at], x.at[at]).start()
    loads["cot"].wait()
    for b in range(2):
        c[mine(b), :] = cot[half(b), :].astype(BF)
    for name in ("wq", "wk", "wv", "vf"):
        loads[name].wait()

    def project(m):
        row = pl.ds(pl.multiple_of(m * BLK, BLK), BLK)
        at = pl.ds(pl.multiple_of(block_place(m) * BLK, BLK), BLK)
        xm = x[row, :]
        cosine, sine = cos_ref[row, :], sin_ref[row, :]
        qf, kf = nn(xm, wq[...]), nn(xm, wk[...])
        low = (0.5 * nn(xm, wv[...]) + 0.5 * vf[row, :].astype(F32)).astype(BF)
        for t in range(4):
            cols = slice(t * 128, t * 128 + 128)
            q[at, cols] = turn(qf[:, cols], cosine, sine, lane).astype(BF) * 0.125
            k[at, cols] = turn(kf[:, cols], cosine, sine, lane).astype(BF)
        v[at, :] = low
        vt[:, at] = low.T
        xt[:, row] = xm.T

    def project_mine(b, carry):
        project(tp * 2 + b)
        return carry

    lax.fori_loop(0, 2, project_mine, 0)

    def project_theirs(b, carry):
        for n in range(2):
            first(2 * b + n, x.at[quarter(0)], x.at[quarter(0)]).wait_recv()
        project((1 - tp) * 2 + b)
        return carry

    lax.fori_loop(0, 2, project_theirs, 0)
    cots = [peer(2 + b, c.at[mine(b)], c.at[mine(b)]) for b in range(2)]
    cots[0].start()
    for src, dst in ((q, q_h), (k, k_h), (v, v_h), (xt, xt_h)):
        keep(src, dst)
    lse_ref[...] = jnp.zeros_like(lse_ref)
    loads["wo"].wait()

    def attend(m):
        i = POS_OF[m]

        def pair(p, carry):
            cols = pl.ds(pl.multiple_of(p * 128, 128), 128)
            qb = q[rows(i), cols]
            parts = []
            for h in range(2):
                qm = jnp.where((lane < 64) == (h == 0), qb, jnp.zeros_like(qb))
                scores = [nt(k[rows(j), cols], qm) for j in range(i + 1)]
                scores[i] = jnp.where(causal, scores[i], -1e30)
                top = functools.reduce(jnp.maximum, [jnp.max(s, axis=0, keepdims=True) for s in scores])
                es = [jnp.exp(s - top) for s in scores]
                total = functools.reduce(jnp.add, [jnp.sum(e, axis=0, keepdims=True) for e in es])
                head = pl.ds(pl.multiple_of(p * 128 + h * 64, 64), 64)
                mix = functools.reduce(jnp.add, [nn(vt[head, rows(j)], es[j].astype(BF)) for j in range(i + 1)])
                parts.append(mix * (1.0 / total))
                lse_ref[lax.div(p, 2), pl.ds(2 * lax.rem(p, 2) + h, 1), rows(i)] = top + jnp.log(total)
            flat = jnp.concatenate(parts, axis=0)
            ot[cols, rows(m)] = flat.astype(BF)
            o[rows(m), cols] = flat.T.astype(BF)
            return carry

        lax.fori_loop(0, 4, pair, 0)

    twos = [peer(4 + b, send2.at[half(b)], recv2.at[half(b)]) for b in range(2)]
    for b in range(2):
        for side in range(2):

            @pl.when(tp == side)
            def _():
                attend((1 - side) * 2 + b)

        send2[half(b), :] = nn(o[theirs(b), :], wo[...]).astype(BF)
        twos[b].start()
    for side in range(2):

        @pl.when(tp == side)
        def _():
            attend(side * 2)
            attend(side * 2 + 1)

    keep(o, o_h)
    keep(ot, ot_h)
    for name in ("wg", "wu", "wd"):
        loads[name].wait()

    def gated(at):
        xm, cm = x[at, :], c[at, :]
        x2t[:, at] = xm.T
        for first, size in TILES:
            cols = slice(first, first + size)
            gate, up = nn(xm, wg[:, cols]), nn(xm, wu[:, cols])
            sigma = lax.logistic(gate)
            smooth = gate * sigma
            low = (smooth * up).astype(BF)
            hid[:, cols] = low
            ht[cols, at] = low.T
            back = nt(cm, wd[cols, :])
            gg[at, cols] = (back * up * (sigma * (1.0 + gate * (1.0 - sigma)))).astype(BF)
            ug[at, cols] = (back * smooth).astype(BF)
        return nn(hid[...], wd[...]), nt(gg[at, :], wg[...]) + nt(ug[at, :], wu[...])

    spots = tuple((rows(t // 2), slice(t % 2 * 512, t % 2 * 512 + TILES[t][1])) for t in range(3))

    def gated_up(at):
        xm = x[at, :]
        x2t[:, at] = xm.T
        for (first, size), spot in zip(TILES, spots):
            cols = slice(first, first + size)
            gate, up = nn(xm, wg[:, cols]), nn(xm, wu[:, cols])
            tok[spot] = gate
            base[spot] = up
            low = (gate * lax.logistic(gate) * up).astype(BF)
            hid[:, cols] = low
            ht[cols, at] = low.T
        return nn(hid[...], wd[...])

    def gated_down(at):
        cm = c[at, :]
        for (first, size), spot in zip(TILES, spots):
            cols = slice(first, first + size)
            gate, up = tok[spot], base[spot]
            sigma = lax.logistic(gate)
            back = nt(cm, wd[cols, :])
            gg[at, cols] = (back * up * (sigma * (1.0 + gate * (1.0 - sigma)))).astype(BF)
            ug[at, cols] = (back * (gate * sigma)).astype(BF)
        return nt(gg[at, :], wg[...]) + nt(ug[at, :], wu[...])

    def block_mine(b, carry):
        here = pl.ds(pl.multiple_of(b * BLK, BLK), BLK)
        at = mine(b)
        peer(4 + b, send2.at[half(0)], recv2.at[half(0)]).wait_recv()
        middle = tok[here, :] + nn(o[at, :], wo[...]) + recv2[here, :].astype(F32)
        tok[here, :] = middle
        for n in range(2):
            first(2 * b + n, x.at[quarter(0)], x.at[quarter(0)]).wait_send()
        x[at, :] = norm_rows(middle, gain_mlp).astype(BF)
        peer(6 + b, x.at[at], x.at[at]).start()
        branch, grad_in = gated(at)
        base[here, :] = tok[here, :] + branch
        cot[here, :] = grad_in
        return carry

    lax.fori_loop(0, 2, block_mine, 0)
    keep(tok, middle_h)
    keep(base, base_h)
    keep(cot, own6_h)
    for copy in stores[:9]:
        copy.wait()
    columns = lambda t: slice(TILES[t][0], sum(TILES[t]))
    across = [(buf.at[:, : TILES[t][1]], gg, columns(t), gg_h) for t, buf in enumerate((wq, wk, wv))]
    across += [(buf.at[:, : TILES[t][1]], ug, columns(t), gu_h) for t, buf in enumerate((q, k, v))]
    down = [(buf.at[: TILES[t][1]], columns(t)) for t, buf in enumerate((ot, wo, recv2))]

    def gather(at, fresh):
        for buf, cols in down:
            new = nn(ht[cols, at], c[at, :])
            buf[...] = (new if fresh else buf[...].astype(F32) + new).astype(BF)

        def body(n, carry):
            tile = pl.ds(pl.multiple_of(n * BLK, BLK), BLK)
            turned = x2t[tile, at]
            for buf, right, cols, _ in across:
                new = nn(turned, right[at, cols])
                buf[tile, :] = (new if fresh else buf[tile, :].astype(F32) + new).astype(BF)
            return carry

        lax.fori_loop(0, 4, body, 0)

    gather(pl.ds(pl.multiple_of(tp * 512, 512), 512), True)
    for b in range(2):
        peer(6 + b, x.at[half(0)], x.at[half(0)]).wait_recv()
        if b == 1:
            cots[1].start()
        send4[half(b), :] = gated_up(theirs(b)).astype(BF)
        peer(2 + b, c.at[half(0)], c.at[half(0)]).wait_recv()
        if b == 1:
            peer(8, send6.at[half(0)], recv6.at[half(0)]).start()
        send6[half(b), :] = gated_down(theirs(b)).astype(BF)
        if b == 1:
            keep(send6, send6_h)
            keep(send4, send4_h)
        gather(theirs(b), False)
    last = [(buf, gd_h.at[cols]) for buf, cols in down] + [(buf, out.at[:, cols]) for buf, _, cols, out in across]
    for buf, out in last:
        keep(buf, out)
    peer(8, send6.at[half(0)], recv6.at[half(0)]).wait_recv()
    keep(recv6, recv6_h)
    for b in range(2):
        for n in (2, 4, 6):
            peer(n + b, recv6.at[half(0)], recv6.at[half(0)]).wait_send()
    peer(8, send6.at[half(0)], recv6.at[half(0)]).wait_send()
    for copy in stores[9:]:
        copy.wait()


def front(tokens, vf, wq, wk, wv, wo, wg, wu, wd, gain_attn, gain_mlp, cot, cos, sin):
    V = lambda shape, kind=BF: pltpu.VMEM(shape, kind)
    D = lambda *shape: pltpu.SemaphoreType.DMA(shape)
    hbm, vmem = pl.BlockSpec(memory_space=pl.ANY), pl.BlockSpec(memory_space=pltpu.VMEM)
    S = jax.ShapeDtypeStruct
    own, heads, turned, square = (512, 1024), (1024, 512), (512, 1024), (1024, 1024)
    hidden, across, half = (1024, 1408), (1408, 1024), (256, 1024)
    return pl.pallas_call(
        front_kernel,
        in_specs=[hbm] * 9 + [vmem] * 2 + [hbm] + [vmem] * 2,
        out_specs=[hbm] * 6 + [vmem] + [hbm] * 9,
        out_shape=[*[S(heads, BF)] * 4, S(turned, BF), S(square, BF), S((2, 8, 1024), F32), S(own, F32), S(own, F32), S(own, BF),
                   S(own, F32), S(own, BF), S(half, BF), S(hidden, BF), S(hidden, BF), S(across, BF)],
        scratch_shapes=[
            V(own, F32), V(own, F32), V(square), V(square), *[V(heads)] * 7, V(turned), V(heads), V(turned), V(own), V(own), V(own),
            V(square), V(square), V(hidden), V(hidden), V(across), V(across), V((256, 1408)), V(hidden), V(hidden), V(own, F32),
            V(own), V(own), V(half),
            D(13), D(2, 9), D(22), D(2, 4),
        ],
        compiler_params=pltpu.CompilerParams(collective_id=4, has_side_effects=True, vmem_limit_bytes=63 << 20),
        cost_estimate=pl.CostEstimate(flops=40 * 10**9, bytes_accessed=60 << 20, transcendentals=5 << 20),
    )(tokens, vf, wq, wk, wv, wo, wg, wu, wd, gain_attn, gain_mlp, cot, cos, sin)


def ring_place(dp):
    core, x, z = lax.rem(dp, 2), lax.rem(lax.div(dp, 2), 2), lax.div(dp, 4)
    place = z + x * (7 - 2 * z)

    def device(where):
        side = lax.div(where, 4)
        return ((where + side * (7 - 2 * where)) * 2 + side) * 2 + core

    turn_no = lax.rem(place + core * (8 - 2 * place), 8)
    after = device(lax.rem(place + 1 + 6 * core, 8))
    before = device(lax.rem(place + 7 - 6 * core, 8))
    cube = (dp + 1 - 2 * core, dp + 2 - 4 * x, dp + 4 - 8 * lax.rem(z, 2), dp + 8 - 16 * lax.div(z, 2))
    return core, turn_no, after, before, cube


def remote(src, dst, send, recv, dp):
    return pltpu.make_async_remote_copy(
        src, dst, send, recv, device_id={"dp": dp}, device_id_type=pl.DeviceIdType.MESH
    )


class Ring:
    def __init__(self, place, takes, outs, own, sib, slots, sems):
        self.core, self.turn_no, self.after, self.before, self.cube = place
        self.takes, self.outs, self.own, self.sib, self.slots = takes, outs, own, sib, slots
        self.trade, self.rs, self.ag, self.over, self.keep = sems

    def piece(self, g, chunk):
        size = self.slots[g].shape[1]
        return pl.ds(pl.multiple_of(chunk * size, size), size)

    def traded(self, g, n):
        at = self.piece(g, lax.rem(15 + lax.rem(8 - self.turn_no, 8) - n, 8))
        return remote(
            self.takes[g](1 - self.core).at[at], self.sib[g].at[at], self.trade.at[0, g, n], self.trade.at[1, g, n], self.cube[0]
        )

    def trade_all(self):
        for n in range(8):
            for g in range(len(self.takes)):
                self.traded(g, n).start()

    def total(self, g, chunk):
        at = self.piece(g, chunk)
        return self.own[g][at, :].astype(F32) + self.sib[g][at, :].astype(F32)

    def first(self, g, chunk):
        return remote(
            self.own[g].at[self.piece(g, chunk)], self.slots[g].at[0], self.rs.at[0, g, 0], self.rs.at[1, g, 0], self.after
        )

    def begin(self, g):
        self.traded(g, 0).wait_recv()
        chunk = lax.rem(self.turn_no + 7, 8)
        self.own[g][self.piece(g, chunk), :] = self.total(g, chunk).astype(BF)
        self.first(g, chunk).start()

    def add(self, g, t):
        chunk = lax.rem(self.turn_no + 14 - t, 8)
        self.traded(g, t + 1).wait_recv()
        remote(self.slots[g].at[t], self.slots[g].at[t], self.rs.at[0, g, t], self.rs.at[1, g, t], self.after).wait_recv()
        self.slots[g][t] = (self.slots[g][t].astype(F32) + self.total(g, chunk)).astype(BF)

    def add_on(self, g, t):
        self.add(g, t)
        remote(self.slots[g].at[t], self.slots[g].at[t + 1], self.rs.at[0, g, t + 1], self.rs.at[1, g, t + 1], self.after).start()

    def spot(self, g, chunk):
        return self.outs[g](self.core, chunk)

    def turn_over(self, g):
        self.add(g, 6)
        spot = self.spot(g, self.turn_no)
        last = self.slots[g].at[6]
        remote(last, spot, self.ag.at[0, g, 0], self.ag.at[1, g, 0], self.after).start()
        remote(last, spot, self.over.at[0, g, 0], self.over.at[1, g, 0], self.cube[0]).start()
        pltpu.make_async_copy(last, spot, self.keep.at[g]).start()

    def pass_on(self, g, t):
        spot = self.spot(g, lax.rem(self.turn_no + 15 - t, 8))
        remote(spot, spot, self.ag.at[0, g, t], self.ag.at[1, g, t], self.after).wait_recv()

        @pl.when(t < 6)
        def _():
            remote(spot, spot, self.ag.at[0, g, t + 1], self.ag.at[1, g, t + 1], self.after).start()

        remote(spot, spot, self.over.at[0, g, t + 1], self.over.at[1, g, t + 1], self.cube[0]).start()

    def end(self, g):
        spot = self.spot(g, self.turn_no)
        pltpu.make_async_copy(self.slots[g].at[6], spot, self.keep.at[g]).wait()

        def finish(t, _):
            remote(self.slots[g].at[0], self.slots[g].at[0], self.rs.at[0, g, t], self.rs.at[1, g, t], self.after).wait_send()
            remote(spot, spot, self.ag.at[0, g, t], self.ag.at[1, g, t], self.after).wait_send()
            return _

        lax.fori_loop(0, 7, finish, 0)

        def crossed(t, _):
            self.traded(g, t).wait_send()
            there = self.outs[g](1 - self.core, lax.rem(self.turn_no + t, 8))
            remote(spot, there, self.over.at[0, g, t], self.over.at[1, g, t], self.cube[0]).wait()
            return _

        lax.fori_loop(0, 8, crossed, 0)


def strip(ref, axis, halves, length):
    if axis == 0:
        return lambda core, chunk: ref.at[pl.ds(pl.multiple_of(core * halves + chunk * length, length), length)]
    return lambda core, chunk: ref.at[
        pl.ds(pl.multiple_of(chunk * length, length), length), pl.ds(pl.multiple_of(core * halves, halves), halves)
    ]


def half_of(ref, axis, halves):
    if axis == 0:
        return lambda core: ref.at[pl.ds(pl.multiple_of(core * halves, halves), halves)]
    return lambda core: ref.at[:, pl.ds(pl.multiple_of(core * halves, halves), halves)]


def norm_back_rows(values, gain, grad_in):
    factor = lax.rsqrt(jnp.mean(values * values, axis=-1, keepdims=True) + EPS)
    normed = values * factor
    grad_normed = grad_in * gain
    grad = factor * (grad_normed - normed * jnp.mean(grad_normed * normed, axis=-1, keepdims=True))
    return grad, jnp.sum(grad_in * normed, axis=0, keepdims=True)


def back_kernel(
    own6_h, send6_h, recv6_h, own4_h, send4_h, middle_h, cot_h, tokens_h, gain_attn_ref, gain_mlp_ref,
    wo_h, wq_h, wk_h, wv_h, q_h, k_h, v_h, o_h, ot_h, xt_h, lse_ref, cos_ref, sin_ref, gg_h, gu_h, gd_h,
    out_h, gt_h, gf_h, rq_h, rk_h, rv_h, ro_h, rg_h, ru_h, rd_h, gains_ref,
    f1, f2, f3, recv6, recv4, recv8, send8, c, wo, wq, wk, wv, q, k, v, o, ot, xt,
    dq, dk, dv, do, kt, dka, dva, dl, own8, dwq, dwk, dwv, dwo,
    mg, mu, md, sg, su, sd, lg, lu, ld, bq, bk, bv, bo, aq, ak, av, ao,
    load, ysem, trade1, rs1, ag1, over1, keep1, trade2, rs2, ag2, over2, keep2, gain_in, gain_sem, store,
):
    dp, tp = lax.axis_index("dp"), lax.axis_index("tp")
    place = ring_place(dp)
    core, turn_no, after, before, cube = place
    mesh_id = pl.DeviceIdType.MESH
    barrier = pltpu.get_barrier_semaphore()
    for other in (*cube, after, before):
        pl.semaphore_signal(barrier, inc=1, device_id={"dp": other}, device_id_type=mesh_id)
    pl.semaphore_signal(barrier, inc=1, device_id={"tp": 1 - tp}, device_id_type=mesh_id)

    loads = {}

    def fetch(name, src, dst):
        loads[name] = pltpu.make_async_copy(src, dst, load.at[len(loads)])
        loads[name].start()

    one = Ring(
        place, (half_of(gd_h, 1, 512), half_of(gg_h, 0, 512), half_of(gu_h, 0, 512)),
        (strip(rd_h, 1, 512, 176), strip(rg_h, 0, 512, 64), strip(ru_h, 0, 512, 64)),
        (md, mg, mu), (sd, sg, su), (ld, lg, lu), (trade1, rs1, ag1, over1, keep1),
    )
    two = Ring(
        place, (half_of(dwq, 0, 512), half_of(dwk, 0, 512), half_of(dwv, 0, 512), half_of(dwo, 0, 256)),
        (strip(rq_h, 0, 512, 64), strip(rk_h, 0, 512, 64), strip(rv_h, 0, 512, 64), strip(ro_h, 0, 256, 32)),
        (half_of(dwq, 0, 512)(core), half_of(dwk, 0, 512)(core), half_of(dwv, 0, 512)(core), half_of(dwo, 0, 256)(core)),
        (bq, bk, bv, bo), (aq, ak, av, ao), (trade2, rs2, ag2, over2, keep2),
    )
    for g, (whole, mine) in enumerate(((gd_h, md), (gg_h, mg), (gu_h, mu))):
        fetch(("m", g), one.takes[g](core), mine)
    for name, src, dst in (
        ("own6", own6_h, f1), ("recv6", recv6_h, recv6.at[pl.ds(0, BLK)]), ("middle", middle_h, f2), ("cot", cot_h, f3), ("k", k_h, k), ("wo", wo_h, wo), ("o", o_h, o),
        ("q", q_h, q), ("v", v_h, v), ("wq", wq_h, wq), ("wk", wk_h, wk), ("wv", wv_h, wv), ("ot", ot_h, ot), ("xt", xt_h, xt),
    ):
        fetch(name, src, dst)
    pl.semaphore_wait(barrier, 7)

    def peer(n, src, dst):
        return pltpu.make_async_remote_copy(
            src, dst, ysem.at[0, n], ysem.at[1, n], device_id={"tp": 1 - tp}, device_id_type=mesh_id
        )

    half = lambda b: pl.ds(b * BLK, BLK)
    six = peer(0, send6_h.at[half(1)], recv6.at[half(1)])
    six.start()
    one.trade_all()
    for g in range(3):
        loads["m", g].wait()
        one.begin(g)

    lane = lax.broadcasted_iota(jnp.int32, (BLK, 128), 1)
    causal = lax.broadcasted_iota(jnp.int32, (BLK, BLK), 0) <= lax.broadcasted_iota(jnp.int32, (BLK, BLK), 1)
    gain_mlp, gain_attn = gain_mlp_ref[...], gain_attn_ref[...]
    dka[...] = jnp.zeros_like(dka)
    dva[...] = jnp.zeros_like(dva)
    loads["k"].wait()
    for j in range(4):
        kt[:, rows(j)] = k[rows(j), :].T

    def one_piece(n):
        step, g = divmod(n, 3)
        if step < 6:
            one.add_on(g, step)
        elif step == 6:
            one.turn_over(g)
        else:
            one.pass_on(g, step - 7)

    def two_step(g, step):
        if step < 6:
            two.add_on(g, step)
        elif step == 6:
            two.turn_over(g)
        else:
            two.pass_on(g, step - 7)

    def branch_back(m):
        at = pl.ds(pl.multiple_of(m * BLK, BLK), BLK)
        low = nt(c[at, :], wo[...]).astype(BF)
        do[at, :] = low
        prod = (low.astype(F32) * o[at, :].astype(F32)).T
        for h in range(8):
            dl[h : h + 1, at] = jnp.sum(prod[h * 64 : h * 64 + 64, :], axis=0, keepdims=True)

    def attend_back(m, p):
        cols = pl.ds(pl.multiple_of(p * 128, 128), 128)
        i = POS_OF[m]
        qb, dob = q[rows(i), cols], do[rows(m), cols]
        parts = []
        for h in range(2):
            mine = (lane < 64) == (h == 0)
            qm = jnp.where(mine, qb, jnp.zeros_like(qb))
            dom = jnp.where(mine, dob, jnp.zeros_like(dob))
            lse = lse_ref[lax.div(p, 2), pl.ds(2 * lax.rem(p, 2) + h, 1), rows(i)]
            delta = dl[pl.ds(2 * p + h, 1), rows(m)]
            head = pl.ds(pl.multiple_of(p * 128 + h * 64, 64), 64)
            dqt = None
            for j in range(i + 1):
                weights = jnp.exp(nt(k[rows(j), cols], qm) - lse)
                if j == i:
                    weights = jnp.where(causal, weights, 0.0)
                ds = (weights * (nt(v[rows(j), cols], dom) - delta)).astype(BF)
                dva[rows(j), cols] = dva[rows(j), cols] + nn(weights.astype(BF), dom)
                dka[rows(j), cols] = dka[rows(j), cols] + nn(ds, qm)
                part = nn(kt[head, rows(j)], ds)
                dqt = part if dqt is None else dqt + part
            parts.append(dqt)
        grad = (jnp.concatenate(parts, axis=0).T * 0.125).astype(BF).astype(F32)
        dq[rows(m), cols] = turn(grad, cos_ref[rows(m), :], -sin_ref[rows(m), :], lane).astype(BF)

    def block_back(side_of, b, pieces):
        branch_back(side_of(tp) * 2 + b)

        def pair(p, carry):
            for side in range(2):

                @pl.when(tp == side)
                def _():
                    attend_back(side_of(side) * 2 + b, p)

            for late, n in enumerate(pieces):
                if n is not None:

                    @pl.when(p == late)
                    def _():
                        one_piece(n)

            return carry

        lax.fori_loop(0, 4, pair, 0)

    for name in ("own6", "recv6", "middle", "cot", "wo", "o", "q", "v"):
        loads[name].wait()
    gain_sum = jnp.zeros((1, 1024), F32)
    seven = []
    for b in range(2):
        if b == 1:
            six.wait_recv()
            seven[0].start()

        def rows_back(n, total):
            at = pl.ds(pl.multiple_of(b * BLK + n * 64, 64), 64)
            grad_in = f1[at, :] + recv6[at, :].astype(F32)
            grad, part = norm_back_rows(f2[at, :], gain_mlp, grad_in)
            grad = f3[at, :] + grad
            f1[at, :] = grad
            c[pl.ds(pl.multiple_of(tp * 512 + b * BLK + n * 64, 64), 64), :] = grad.astype(BF)
            return total + part

        gain_sum = lax.fori_loop(0, 4, rows_back, gain_sum)
        mine = c.at[pl.ds(pl.multiple_of(tp * 512 + b * BLK, BLK), BLK)]
        seven.append(peer(2 + b, mine, mine))
        if b == 1:
            seven[1].start()
        block_back(lambda side: side, b, ((None, None, None, 0), (2, 3, 4, 5))[b])
        one_piece((1, 6)[b])
    late = pltpu.make_async_copy(own4_h, f3, load.at[len(loads)])
    late.start()
    fetch_tokens = pltpu.make_async_copy(tokens_h, f2, load.at[len(loads) + 1])
    fetch_tokens.start()
    gains_ref[...] = jnp.zeros_like(gains_ref)
    gains_ref[0:1, :] = gain_sum
    four = peer(4, send4_h, recv4)
    for b in range(2):
        seven[b].wait_recv()
        if b == 1:
            four.start()
        block_back(lambda side: 1 - side, b, range(7 + 5 * b, 11 + 5 * b))
        one_piece(11 + 5 * b)
    for m in range(4):
        at = rows(POS_OF[m])
        cosine, sine = cos_ref[rows(m), :], -sin_ref[rows(m), :]
        for t in range(4):
            cols = slice(t * 128, t * 128 + 128)
            grad = dka[at, cols].astype(BF).astype(F32)
            dk[rows(m), cols] = turn(grad, cosine, sine, lane).astype(BF)
        dv[rows(m), :] = (0.5 * dva[at, :].astype(BF).astype(F32)).astype(BF)
    keep_gf = pltpu.make_async_copy(dv, gf_h, store.at[0])
    keep_gf.start()
    one_piece(17)
    for name in ("wq", "wk", "wv", "xt", "ot"):
        loads[name].wait()

    def into_rows(at):
        return nt(dq[at, :], wq[...]) + nt(dk[at, :], wk[...]) + nt(dv[at, :], wv[...])

    for which in range(2):
        side = (1 - core) * (1 - which) + core * which
        at = pl.ds(pl.multiple_of(side * 512, 512), 512)
        for n, (dst, src) in enumerate(((dwq, dq), (dwk, dk), (dwv, dv))):
            dst[at, :] = nn(xt[at, :], src[...]).astype(BF)
            if n < 2:
                one_piece(18 + 2 * which + n)
        at = pl.ds(pl.multiple_of(side * 256, 256), 256)
        dwo[at, :] = nn(ot[at, :], c[...]).astype(BF)
        if which == 0:
            two.trade_all()
    for g in range(4):
        two.begin(g)
    eight = []
    for b in range(2):
        at = pl.ds(pl.multiple_of((1 - tp) * 512 + b * BLK, BLK), BLK)
        send8[half(b), :] = into_rows(at).astype(BF)
        eight.append(peer(5 + b, send8.at[half(b)], recv8.at[half(b)]))
        eight[b].start()
        one_piece(22 + b)

    def gain_swap(n):
        where = {"tp": 1 - tp} if n == 4 else {"dp": cube[n]}
        return pltpu.make_async_remote_copy(
            gains_ref, gain_in.at[n], gain_sem.at[0, n], gain_sem.at[1, n], device_id=where, device_id_type=mesh_id
        )

    def rows_last(b, total):
        eight[b].wait_recv()

        def body(n, total):
            at = pl.ds(pl.multiple_of(b * BLK + n * 64, 64), 64)
            grad, part = norm_back_rows(f2[at, :], gain_attn, own8[at, :] + recv8[at, :].astype(F32))
            f1[at, :] = f1[at, :] + grad
            return total + part

        return lax.fori_loop(0, 4, body, total)

    keep_out = pltpu.make_async_copy(f3, out_h, store.at[1])
    keep_gt = pltpu.make_async_copy(f1, gt_h, store.at[2])
    gain_sum = jnp.zeros((1, 1024), F32)
    for step in range(14):
        for g in range(4):
            two_step(g, step)
        for n in range(24 + PACE[step], 24 + PACE[step + 1]):
            one_piece(n)
        if step < 2:
            at = pl.ds(pl.multiple_of(tp * 512 + step * BLK, BLK), BLK)
            own8[half(step), :] = into_rows(at)
        if step == 2:
            late.wait()
            fetch_tokens.wait()
        if step in (5, 6):
            gain_sum = rows_last(step - 5, gain_sum)
        if step == 6:
            gains_ref[1:2, :] = gain_sum
            keep_gt.start()
        if step == 7:
            four.wait_recv()

            def out_rows(n, carry):
                at = pl.ds(pl.multiple_of(n * 64, 64), 64)
                f3[at, :] = f3[at, :] + recv4[at, :].astype(F32)
                return carry

            lax.fori_loop(0, 8, out_rows, 0)
            keep_out.start()
        if step > 8:
            gain_swap(step - 9).wait()
            gains_ref[...] = gains_ref[...] + gain_in[step - 9]
        if 8 <= step < 13:
            gain_swap(step - 8).start()
    for g in range(3):
        one.end(g)
    for g in range(4):
        two.end(g)
    for copy in (six, *seven, *eight, four):
        copy.wait_send()
    for copy in (keep_gf, keep_out, keep_gt):
        copy.wait()


PACE = (0, 1, 2, 4, 5, 6, 8, 9, 10, 12, 13, 14, 16, 17, 18)


def back(own6, send6, recv6, own4, send4, middle, cot, tokens, gain_attn, gain_mlp, wo, wq, wk, wv, q, k, v, o, ot, xt, lse, cos, sin, gg, gu, gd):
    V = lambda shape, kind=BF: pltpu.VMEM(shape, kind)
    D = lambda *shape: pltpu.SemaphoreType.DMA(shape)
    hbm, vmem = pl.BlockSpec(memory_space=pl.ANY), pl.BlockSpec(memory_space=pltpu.VMEM)
    S = jax.ShapeDtypeStruct
    wide = (1024, 1024)
    return pl.pallas_call(
        back_kernel,
        in_specs=[hbm] * 8 + [vmem] * 2 + [hbm] * 10 + [vmem] * 3 + [hbm] * 3,
        out_specs=[hbm] * 10 + [vmem],
        out_shape=[S((512, 1024), F32), S((512, 1024), F32), S((1024, 512), BF), *[S((1024, 512), BF)] * 3, S((512, 1024), BF),
                   S((1024, 1408), BF), S((1024, 1408), BF), S((1408, 1024), BF), S((8, 1024), F32)],
        scratch_shapes=[
            *[V((512, 1024), F32)] * 3, *[V((512, 1024))] * 4, V(wide), V((512, 1024)), *[V((1024, 512))] * 7, V((512, 1024)), V(wide),
            *[V((1024, 512))] * 4, V((512, 1024)), *[V((1024, 512), F32)] * 2, V((8, 1024), F32), V((512, 1024), F32),
            *[V((1024, 512))] * 3, V((512, 1024)),
            *[V((512, 1408)), V((512, 1408)), V((1408, 512))] * 2, V((7, 64, 1408)), V((7, 64, 1408)), V((7, 176, 512)),
            *[V((512, 512))] * 3, V((256, 1024)), *[V((7, 64, 512))] * 3, V((7, 32, 1024)),
            D(20), D(2, 7), D(2, 3, 8), D(2, 3, 7), D(2, 3, 7), D(2, 3, 8), D(3), D(2, 4, 8), D(2, 4, 7), D(2, 4, 7), D(2, 4, 8), D(4),
            V((5, 8, 1024), F32), D(2, 5), D(3),
        ],
        compiler_params=pltpu.CompilerParams(collective_id=3, has_side_effects=True, vmem_limit_bytes=62 << 20),
        cost_estimate=pl.CostEstimate(flops=30 * 10**9, bytes_accessed=60 << 20, transcendentals=5 << 20),
    )(own6, send6, recv6, own4, send4, middle, cot, tokens, gain_attn, gain_mlp, wo, wq, wk, wv, q, k, v, o, ot, xt, lse, cos, sin, gg, gu, gd)


PIECES = 8


def finish_kernel(*refs):
    gains_ref, ins, outs, wide = refs[0], refs[1:11], refs[11:21], refs[23:39]
    sums, through, load, store = refs[39:]
    fetch = pltpu.make_async_copy(gains_ref, sums, load.at[8, 2])
    fetch.start()
    gains = [pltpu.make_async_copy(sums.at[pl.ds(n, 1)], refs[21 + n], store.at[n, 1]) for n in range(2)]
    into = [pltpu.make_async_copy(ins[n], through.at[n], load.at[8, n]) for n in range(2)]
    whole = [pltpu.make_async_copy(through.at[n], outs[n], store.at[n, 0]) for n in range(2)]
    for copy in into:
        copy.start()
    low, high = wide[:8], wide[8:]
    order = (5, 6, 7, 1, 2, 3, 4, 0)

    def part(ref, piece):
        size = ref.shape[0] // PIECES
        return ref.at[pl.ds(piece * size, size)]

    for a in order:
        for piece in range(PIECES):
            pltpu.make_async_copy(part(ins[a + 2], piece), part(low[a], piece), load.at[a, piece]).start()
    fetch.wait()
    for n in range(2):
        gains[n].start()
        into[n].wait()
        whole[n].start()
    for a in order:
        for piece in range(PIECES):
            pltpu.make_async_copy(part(ins[a + 2], piece), part(low[a], piece), load.at[a, piece]).wait()
            size = low[a].shape[0] // PIECES

            def widen(n, carry):
                at = pl.ds(pl.multiple_of(piece * size + n * 16, 16), 16)
                high[a][at, :] = low[a][at, :].astype(F32)
                return carry

            lax.fori_loop(0, size // 16, widen, 0, unroll=2)
            pltpu.make_async_copy(part(high[a], piece), part(outs[a + 2], piece), store.at[a + 2, piece]).start()
    for a in order:
        for piece in range(PIECES):
            pltpu.make_async_copy(part(high[a], piece), part(outs[a + 2], piece), store.at[a + 2, piece]).wait()
    for copy in (*whole, *gains):
        copy.wait()


def finish(gains, *arrays):
    hbm = pl.BlockSpec(memory_space=pl.ANY)
    return pl.pallas_call(
        finish_kernel,
        in_specs=[hbm] * 11,
        out_specs=[hbm] * 12,
        out_shape=[jax.ShapeDtypeStruct(a.shape, F32) for a in arrays] + [jax.ShapeDtypeStruct((1, 1024), F32)] * 2,
        scratch_shapes=[
            *[pltpu.VMEM(a.shape, BF) for a in arrays[2:]], *[pltpu.VMEM(a.shape, F32) for a in arrays[2:]],
            pltpu.VMEM(gains.shape, F32), pltpu.VMEM((2, *arrays[0].shape), F32), pltpu.SemaphoreType.DMA((9, PIECES)), pltpu.SemaphoreType.DMA((10, PIECES)),
        ],
        compiler_params=pltpu.CompilerParams(vmem_limit_bytes=60 << 20),
        cost_estimate=pl.CostEstimate(flops=10**7, bytes_accessed=48 << 20, transcendentals=0),
    )(gains, *arrays)

def local_pair(
    tokens,
    v_first,
    w_query,
    w_key,
    w_value,
    w_out,
    w_gate,
    w_up,
    w_down,
    gain_attn,
    gain_mlp,
    seq_lens,
    cotangent,
):
    cosine, sine = tables()
    (query, keys, mixed_values, attended, attended_t, normed_t, row_lse, middle, base, send_out, own_in, send_in, got_in,
     grad_gate, grad_up, grad_down) = front(
        tokens, v_first, w_query, w_key, w_value, w_out, w_gate, w_up, w_down, gain_attn[None], gain_mlp[None], cotangent, cosine, sine
    )
    layer_out, grad_tokens, grad_first, *low_grads, gains = back(
        own_in, send_in, got_in, base, send_out, middle, cotangent, tokens, gain_attn[None], gain_mlp[None], w_out, w_query, w_key, w_value,
        query, keys, mixed_values, attended, attended_t, normed_t, row_lse, cosine, sine, grad_gate, grad_up, grad_down,
    )
    layer_out, grad_tokens, grad_first, *wide, gain_mlp_grad, gain_attn_grad = finish(gains, layer_out, grad_tokens, grad_first, *low_grads)
    grad_gain_mlp, grad_gain_attn = gain_mlp_grad[0], gain_attn_grad[0]
    return (layer_out, grad_tokens, grad_first, *wide, grad_gain_attn, grad_gain_mlp)


def local(
    tokens,
    v_first,
    w_query,
    w_key,
    w_value,
    w_out,
    w_gate,
    w_up,
    w_down,
    gain_attn,
    gain_mlp,
    seq_lens,
    cotangent,
):
    tp_count = lax.axis_size("tp")
    row_share = tokens.shape[0]
    doc_ids, positions = layout(seq_lens[0], row_share, tp_count)
    normed_attn = lax.all_gather(
        normalize(tokens, gain_attn).astype(jnp.bfloat16), "tp", axis=0, tiled=True
    )
    query = rotate(
        jnp.dot(normed_attn, w_query, preferred_element_type=jnp.float32), positions, HDIM, 1.0
    ).astype(jnp.bfloat16)
    keys = rotate(
        jnp.dot(normed_attn, w_key, preferred_element_type=jnp.float32), positions, HDIM, 1.0
    ).astype(jnp.bfloat16)
    value_pre = jnp.dot(normed_attn, w_value, preferred_element_type=jnp.float32)
    mixed_values = (0.5 * value_pre + 0.5 * v_first.astype(jnp.float32)).astype(jnp.bfloat16)
    attended, row_lse = attention_forward(query, keys, mixed_values, doc_ids, positions, HDIM)
    middle = tokens + lax.psum_scatter(
        jnp.dot(attended, w_out, preferred_element_type=jnp.float32),
        "tp",
        scatter_dimension=0,
        tiled=True,
    )
    normed_mlp = normalize(middle, gain_mlp).astype(jnp.bfloat16)
    grad_branch = cotangent.astype(jnp.bfloat16)
    mlp_rows = lax.all_gather(normed_mlp, "tp", axis=0, tiled=True)
    gate = jnp.dot(mlp_rows, w_gate, preferred_element_type=jnp.float32)
    up_values = jnp.dot(mlp_rows, w_up, preferred_element_type=jnp.float32)
    hidden = (jax.nn.silu(gate) * up_values).astype(jnp.bfloat16)
    layer_out = middle + lax.psum_scatter(
        jnp.dot(hidden, w_down, preferred_element_type=jnp.float32).astype(jnp.bfloat16),
        "tp",
        scatter_dimension=0,
        tiled=True,
    ).astype(jnp.float32)
    cot_rows = lax.all_gather(grad_branch, "tp", axis=0, tiled=True)
    grad_down = inner_rows(hidden, cot_rows)
    gate_grad, up_grad = swiglu_back(gate, up_values, outer_cols(cot_rows, w_down))
    grad_gate = inner_rows(mlp_rows, gate_grad)
    grad_up = inner_rows(mlp_rows, up_grad)
    grad_mlp_in = lax.psum_scatter(
        (outer_cols(gate_grad, w_gate) + outer_cols(up_grad, w_up)).astype(jnp.bfloat16),
        "tp",
        scatter_dimension=0,
        tiled=True,
    ).astype(jnp.float32)
    middle_back, grad_gain_mlp = normalize_back(middle, gain_mlp, grad_mlp_in)
    grad_middle = cotangent + middle_back
    attn_cot_rows = lax.all_gather(grad_middle.astype(jnp.bfloat16), "tp", axis=0, tiled=True)
    grad_output = inner_rows(attended, attn_cot_rows)
    grad_attended = outer_cols(attn_cot_rows, w_out).astype(jnp.bfloat16)
    query_grad, key_grad, mixed_grad = attention_backward(
        query, keys, mixed_values, grad_attended, row_lse, doc_ids, positions, HDIM
    )
    half_mixed = 0.5 * mixed_grad.astype(jnp.float32)
    value_grad = half_mixed.astype(jnp.bfloat16)
    query_pre_grad = rotate(query_grad.astype(jnp.float32), positions, HDIM, -1.0).astype(
        jnp.bfloat16
    )
    key_pre_grad = rotate(key_grad.astype(jnp.float32), positions, HDIM, -1.0).astype(jnp.bfloat16)
    grad_query = inner_rows(normed_attn, query_pre_grad)
    grad_key = inner_rows(normed_attn, key_pre_grad)
    grad_value = inner_rows(normed_attn, value_grad)
    grad_attn_in = lax.psum_scatter(
        (
            outer_cols(query_pre_grad, w_query)
            + outer_cols(key_pre_grad, w_key)
            + outer_cols(value_grad, w_value)
        ).astype(jnp.bfloat16),
        "tp",
        scatter_dimension=0,
        tiled=True,
    ).astype(jnp.float32)
    tokens_back, grad_gain_attn = normalize_back(tokens, gain_attn, grad_attn_in)
    grad_tokens = grad_middle + tokens_back
    grad_query, grad_key, grad_value, grad_output, grad_gate, grad_up, grad_down = (
        lax.psum(grad_query.astype(jnp.bfloat16), "dp").astype(jnp.float32),
        lax.psum(grad_key.astype(jnp.bfloat16), "dp").astype(jnp.float32),
        lax.psum(grad_value.astype(jnp.bfloat16), "dp").astype(jnp.float32),
        lax.psum(grad_output.astype(jnp.bfloat16), "dp").astype(jnp.float32),
        lax.psum(grad_gate.astype(jnp.bfloat16), "dp").astype(jnp.float32),
        lax.psum(grad_up.astype(jnp.bfloat16), "dp").astype(jnp.float32),
        lax.psum(grad_down.astype(jnp.bfloat16), "dp").astype(jnp.float32),
    )
    grad_gain_attn, grad_gain_mlp = lax.psum((grad_gain_attn, grad_gain_mlp), ("dp", "tp"))
    return (
        layer_out,
        grad_tokens,
        half_mixed,
        grad_query,
        grad_key,
        grad_value,
        grad_output,
        grad_gate,
        grad_up,
        grad_down,
        grad_gain_attn,
        grad_gain_mlp,
    )


def solution(mesh):
    in_specs = (
        P(("dp", "tp"), None),
        P("dp", "tp"),
        P(None, "tp"),
        P(None, "tp"),
        P(None, "tp"),
        P("tp", None),
        P(None, "tp"),
        P(None, "tp"),
        P("tp", None),
        P(),
        P(),
        P("dp", None),
        P(("dp", "tp"), None),
    )
    out_specs = (
        P(("dp", "tp"), None),
        P(("dp", "tp"), None),
        P("dp", "tp"),
        P(None, "tp"),
        P(None, "tp"),
        P(None, "tp"),
        P("tp", None),
        P(None, "tp"),
        P(None, "tp"),
        P("tp", None),
        P(),
        P(),
    )

    def step(*args):
        tokens, seq_lens = args[0], args[11]
        pair = mesh.shape["tp"] == 2 and mesh.shape["dp"] == 16 and seq_lens.shape[1] == 1 and tokens.shape == (512, 1024)
        return (local_pair if pair else local)(*args)

    return jax.shard_map(step, mesh=mesh, in_specs=in_specs, out_specs=out_specs, check_vma=False)
```

```python
import functools

import jax
import jax.numpy as jnp
import numpy as np
from jax import lax
from jax.experimental import pallas as pl
from jax.experimental.pallas import tpu as pltpu
from jax.sharding import PartitionSpec as P

HDIM = 64


EPS = 1e-06


def layout(seq_row, row_share, tp_count):
    group_rows = row_share * tp_count
    row_ids = jnp.arange(group_rows, dtype=jnp.int32)
    device = row_ids // row_share
    local_row = row_ids % row_share
    pieces = seq_row // (2 * tp_count)
    slot_ends = jnp.cumsum(2 * pieces)
    starts = slot_ends - 2 * pieces
    offset = local_row[:, None] - starts[None, :]
    inside = (offset >= 0) & (offset < 2 * pieces[None, :])
    first_half = offset < pieces[None, :]
    mirror = 2 * tp_count - 1 - device[:, None]
    position = jnp.where(
        first_half,
        device[:, None] * pieces[None, :] + offset,
        mirror * pieces[None, :] + offset - pieces[None, :],
    )
    slot_ids = jnp.arange(seq_row.shape[0], dtype=jnp.int32)
    doc_ids = jnp.sum(jnp.where(inside, slot_ids[None, :], 0), axis=1)
    positions = jnp.sum(jnp.where(inside, position, 0), axis=1)
    return (doc_ids, positions)


def rotate(values, positions, head_dim, turn_sign):
    row_count, width_all = values.shape
    half_dim = head_dim // 2
    shaped = values.reshape(row_count, width_all // head_dim, head_dim)
    freqs = 10000.0 ** (-jnp.arange(half_dim, dtype=jnp.float32) / half_dim)
    angles = positions.astype(jnp.float32)[:, None] * freqs[None, :]
    cosine = jnp.cos(angles)[:, None, :]
    sine = turn_sign * jnp.sin(angles)[:, None, :]
    front = shaped[..., :half_dim]
    behind = shaped[..., half_dim:]
    turned = jnp.concatenate(
        [front * cosine - behind * sine, behind * cosine + front * sine], axis=-1
    )
    return turned.reshape(row_count, width_all)


def normalize(values, gain):
    return values * lax.rsqrt(jnp.mean(values * values, axis=-1, keepdims=True) + EPS) * gain


def normalize_back(values, gain, grad_in):
    factor = lax.rsqrt(jnp.mean(values * values, axis=-1, keepdims=True) + EPS)
    normed = values * factor
    grad_normed = grad_in * gain
    grad_values = factor * (
        grad_normed - normed * jnp.mean(grad_normed * normed, axis=-1, keepdims=True)
    )
    return (grad_values, jnp.sum(grad_in * normed, axis=0))


def inner_rows(left, right):
    return lax.dot_general(
        left, right, (((0,), (0,)), ((), ())), preferred_element_type=jnp.float32
    )


def outer_cols(left, right):
    return lax.dot_general(
        left, right, (((1,), (1,)), ((), ())), preferred_element_type=jnp.float32
    )


def swiglu_back(gate, up_values, grad_hidden):
    sigma = jax.nn.sigmoid(gate)
    grad_gate = grad_hidden * up_values * (sigma * (1.0 + gate * (1.0 - sigma)))
    grad_upper = grad_hidden * (gate * sigma)
    return (grad_gate.astype(jnp.bfloat16), grad_upper.astype(jnp.bfloat16))


def block_mask(doc_ids, positions, first_row, block_rows):
    row_doc = lax.dynamic_slice_in_dim(doc_ids, first_row, block_rows, 0)
    row_pos = lax.dynamic_slice_in_dim(positions, first_row, block_rows, 0)
    return (row_doc[:, None] == doc_ids[None, :]) & (positions[None, :] <= row_pos[:, None])


def attention_forward(query, keys, values, doc_ids, positions, head_dim):
    group_rows, width_local = query.shape
    head_count = width_local // head_dim
    block_rows = min(512, group_rows)
    block_count = group_rows // block_rows
    score_scale = head_dim ** (-0.5)
    key_heads = keys.reshape(group_rows, head_count, head_dim)
    value_heads = values.reshape(group_rows, head_count, head_dim)

    def forward_block(block_index):
        first_row = block_index * block_rows
        query_rows = lax.dynamic_slice_in_dim(query, first_row, block_rows, 0).reshape(
            block_rows, head_count, head_dim
        )
        scores = (
            jnp.einsum("qhd,khd->hqk", query_rows, key_heads, preferred_element_type=jnp.float32)
            * score_scale
        )
        allowed = block_mask(doc_ids, positions, first_row, block_rows)
        scores = jnp.where(allowed[None], scores, -1e30)
        row_max = jnp.max(scores, axis=-1, keepdims=True)
        exponent = jnp.exp(scores - row_max)
        row_total = jnp.sum(exponent, axis=-1, keepdims=True)
        weights = (exponent / row_total).astype(jnp.bfloat16)
        mixture = jnp.einsum(
            "hqk,khd->qhd", weights, value_heads, preferred_element_type=jnp.float32
        )
        return (
            mixture.astype(jnp.bfloat16).reshape(block_rows, width_local),
            (row_max + jnp.log(row_total))[..., 0],
        )

    mixture, row_lse = lax.map(forward_block, jnp.arange(block_count, dtype=jnp.int32))
    return (mixture.reshape(group_rows, width_local), row_lse)


def attention_backward(query, keys, values, grad_mixture, row_lse, doc_ids, positions, head_dim):
    group_rows, width_local = query.shape
    head_count = width_local // head_dim
    block_rows = min(512, group_rows)
    block_count = group_rows // block_rows
    score_scale = head_dim ** (-0.5)
    key_heads = keys.reshape(group_rows, head_count, head_dim)
    value_heads = values.reshape(group_rows, head_count, head_dim)

    def backward_block(carry, block_index):
        key_total, value_total = carry
        first_row = block_index * block_rows
        query_rows = lax.dynamic_slice_in_dim(query, first_row, block_rows, 0).reshape(
            block_rows, head_count, head_dim
        )
        grad_rows = lax.dynamic_slice_in_dim(grad_mixture, first_row, block_rows, 0).reshape(
            block_rows, head_count, head_dim
        )
        scores = (
            jnp.einsum("qhd,khd->hqk", query_rows, key_heads, preferred_element_type=jnp.float32)
            * score_scale
        )
        allowed = block_mask(doc_ids, positions, first_row, block_rows)
        scores = jnp.where(allowed[None], scores, -1e30)
        weights = jnp.exp(scores - row_lse[block_index][..., None])
        weights_low = weights.astype(jnp.bfloat16)
        grad_weights = jnp.einsum(
            "qhd,khd->hqk", grad_rows, value_heads, preferred_element_type=jnp.float32
        )
        weighted_sum = jnp.sum(weights * grad_weights, axis=-1, keepdims=True)
        score_grad = (weights * (grad_weights - weighted_sum)).astype(jnp.bfloat16)
        query_grad = (
            jnp.einsum("hqk,khd->qhd", score_grad, key_heads, preferred_element_type=jnp.float32)
            * score_scale
        )
        key_total = (
            key_total
            + jnp.einsum("hqk,qhd->khd", score_grad, query_rows, preferred_element_type=jnp.float32)
            * score_scale
        )
        value_total = value_total + jnp.einsum(
            "hqk,qhd->khd", weights_low, grad_rows, preferred_element_type=jnp.float32
        )
        return (
            (key_total, value_total),
            query_grad.astype(jnp.bfloat16).reshape(block_rows, width_local),
        )

    zero_heads = jnp.zeros((group_rows, head_count, head_dim), jnp.float32)
    (key_total, value_total), query_grad = lax.scan(
        backward_block, (zero_heads, zero_heads), jnp.arange(block_count, dtype=jnp.int32)
    )
    return (
        query_grad.reshape(group_rows, width_local),
        key_total.reshape(group_rows, width_local).astype(jnp.bfloat16),
        value_total.reshape(group_rows, width_local).astype(jnp.bfloat16),
    )


BF, F32 = jnp.bfloat16, jnp.float32
BLK = 256
POS_OF = (0, 3, 1, 2)
NT = (((1,), (1,)), ((), ()))

def nt(a, b):
    return lax.dot_general(a, b, NT, preferred_element_type=F32)

def nn(a, b):
    return jnp.dot(a, b, preferred_element_type=F32)

def rows(block):
    return pl.ds(block * BLK, BLK)

def turn(u, cosine, sine, lane):
    near = jnp.where(lane % 64 < 32, pltpu.roll(u, 96, 1), pltpu.roll(u, 32, 1))
    return u * cosine + near * sine

FIRST = {}
for _m in range(4):
    for _j in range(POS_OF[_m] + 1):
        FIRST.setdefault(_j, (_m, 0))

def tables():
    pos = np.zeros(1024, np.float32)
    for m in range(4):
        pos[m*256:(m+1)*256] = POS_OF[m]*256 + np.arange(256)
    freqs = np.float32(10000.0) ** (-np.arange(32, dtype=np.float32) / np.float32(32))
    ang = pos[:, None] * freqs[None]
    c, s = np.cos(ang.astype(np.float32)), np.sin(ang.astype(np.float32))
    return np.tile(c, (1, 4)).astype(np.float32), np.concatenate([-s, s, -s, s], 1).astype(np.float32)


def block_place(m):
    late = lax.div(m, 2)
    return m * 3 - late * (5 + 2 * (m - 2))


def norm_rows(values, gain):
    return values * lax.rsqrt(jnp.mean(values * values, axis=-1, keepdims=True) + EPS) * gain


TILES = ((0, 512), (512, 512), (1024, 384))


def front_kernel(
    tokens_h, vf_h, wq_h, wk_h, wv_h, wo_h, wg_h, wu_h, wd_h, gain_attn_h, gain_mlp_h, cot_h, cos_h, sin_h,
    q_h, k_h, v_h, o_h, ot_h, xt_h, lse_h, middle_h, base_h, send4_h, own6_h, send6_h, recv6_h, gg_h, gu_h, gd_h,
    tok, cot, x, xt, wq, wk, wv, vf, q, k, v, vt, o, ot, wo, recv2, send2, c, x2t, wg, wu, wd,
    ht, hid, gg, ug, base, send4, send6, recv6,
    gain_attn_ref, gain_mlp_ref, cos_ref, sin_ref, lse_ref, load, ysem, store, gsem,
):
    tp = lax.axis_index("tp")
    mesh_id = pl.DeviceIdType.MESH
    barrier = pltpu.get_barrier_semaphore()
    pl.semaphore_signal(barrier, inc=1, device_id={"tp": 1 - tp}, device_id_type=mesh_id)
    loads = {}

    def fetch(name, src, dst):
        loads[name] = pltpu.make_async_copy(src, dst, load.at[len(loads)])
        loads[name].start()

    half = lambda b: pl.ds(b * BLK, BLK)
    quarter = lambda n: pl.ds(n * 128, 128)
    fetch("gain_attn", gain_attn_h, gain_attn_ref)
    for n in range(4):
        fetch(("tok", n), tokens_h.at[quarter(n)], tok.at[quarter(n)])
    for name, src, dst in (
        ("wq", wq_h, wq), ("wk", wk_h, wk), ("wv", wv_h, wv), ("vf", vf_h, vf), ("cos", cos_h, cos_ref), ("sin", sin_h, sin_ref), ("gain_mlp", gain_mlp_h, gain_mlp_ref), ("cot", cot_h, cot), ("wo", wo_h, wo),
        ("wg", wg_h, wg), ("wu", wu_h, wu), ("wd", wd_h, wd),
    ):
        fetch(name, src, dst)
    stores = []

    def keep(src, dst):
        stores.append(pltpu.make_async_copy(src, dst, store.at[len(stores)]))
        stores[-1].start()

    def peer(n, src, dst):
        return pltpu.make_async_remote_copy(
            src, dst, ysem.at[0, n], ysem.at[1, n], device_id={"tp": 1 - tp}, device_id_type=mesh_id
        )

    def mine(b):
        return pl.ds(pl.multiple_of(tp * 512 + b * BLK, BLK), BLK)

    def theirs(b):
        return pl.ds(pl.multiple_of((1 - tp) * 512 + b * BLK, BLK), BLK)

    lane = lax.broadcasted_iota(jnp.int32, (BLK, 128), 1)
    causal = lax.broadcasted_iota(jnp.int32, (BLK, BLK), 0) <= lax.broadcasted_iota(jnp.int32, (BLK, BLK), 1)
    loads["gain_attn"].wait()
    gain_attn = gain_attn_ref[...]

    def first(n, here, there):
        return pltpu.make_async_remote_copy(
            here, there, gsem.at[0, n], gsem.at[1, n], device_id={"tp": 1 - tp}, device_id_type=mesh_id
        )

    for n in range(4):
        loads["tok", n].wait()
        at = pl.ds(pl.multiple_of(tp * 512 + n * 128, 128), 128)
        x[at, :] = norm_rows(tok[quarter(n), :], gain_attn).astype(BF)
        if n == 0:
            pl.semaphore_wait(barrier, 1)
        first(n, x.at[at], x.at[at]).start()
    loads["cot"].wait()
    for b in range(2):
        c[mine(b), :] = cot[half(b), :].astype(BF)
    for name in ("wq", "wk", "wv", "vf", "cos", "sin", "gain_mlp"):
        loads[name].wait()

    def project(m):
        row = pl.ds(pl.multiple_of(m * BLK, BLK), BLK)
        at = pl.ds(pl.multiple_of(block_place(m) * BLK, BLK), BLK)
        xm = x[row, :]
        cosine, sine = cos_ref[row, :], sin_ref[row, :]
        qf, kf = nn(xm, wq[...]), nn(xm, wk[...])
        low = (0.5 * nn(xm, wv[...]) + 0.5 * vf[row, :].astype(F32)).astype(BF)
        for t in range(4):
            cols = slice(t * 128, t * 128 + 128)
            q[at, cols] = turn(qf[:, cols], cosine, sine, lane).astype(BF) * 0.125
            k[at, cols] = turn(kf[:, cols], cosine, sine, lane).astype(BF)
        v[at, :] = low
        vt[:, at] = low.T
        xt[:, row] = xm.T

    def project_mine(b, carry):
        project(tp * 2 + b)
        return carry

    lax.fori_loop(0, 2, project_mine, 0)

    def project_theirs(b, carry):
        for n in range(2):
            first(2 * b + n, x.at[quarter(0)], x.at[quarter(0)]).wait_recv()
        project((1 - tp) * 2 + b)
        return carry

    lax.fori_loop(0, 2, project_theirs, 0)
    cots = [peer(2 + b, c.at[mine(b)], c.at[mine(b)]) for b in range(2)]
    cots[0].start()
    for src, dst in ((q, q_h), (k, k_h), (v, v_h), (xt, xt_h)):
        keep(src, dst)
    lse_ref[...] = jnp.zeros_like(lse_ref)
    loads["wo"].wait()

    def attend(m):
        i = POS_OF[m]

        def pair(p, carry):
            cols = pl.ds(pl.multiple_of(p * 128, 128), 128)
            qb = q[rows(i), cols]
            parts = []
            for h in range(2):
                qm = jnp.where((lane < 64) == (h == 0), qb, jnp.zeros_like(qb))
                scores = [nt(k[rows(j), cols], qm) for j in range(i + 1)]
                scores[i] = jnp.where(causal, scores[i], -1e30)
                top = functools.reduce(jnp.maximum, [jnp.max(s, axis=0, keepdims=True) for s in scores])
                es = [jnp.exp(s - top) for s in scores]
                total = functools.reduce(jnp.add, [jnp.sum(e, axis=0, keepdims=True) for e in es])
                head = pl.ds(pl.multiple_of(p * 128 + h * 64, 64), 64)
                mix = functools.reduce(jnp.add, [nn(vt[head, rows(j)], es[j].astype(BF)) for j in range(i + 1)])
                parts.append(mix * (1.0 / total))
                lse_ref[lax.div(p, 2), pl.ds(2 * lax.rem(p, 2) + h, 1), rows(i)] = top + jnp.log(total)
            flat = jnp.concatenate(parts, axis=0)
            ot[cols, rows(m)] = flat.astype(BF)
            o[rows(m), cols] = flat.T.astype(BF)
            return carry

        lax.fori_loop(0, 4, pair, 0)

    twos = [peer(4 + b, send2.at[half(b)], recv2.at[half(b)]) for b in range(2)]
    for b in range(2):
        for side in range(2):

            @pl.when(tp == side)
            def _():
                attend((1 - side) * 2 + b)

        send2[half(b), :] = nn(o[theirs(b), :], wo[...]).astype(BF)
        twos[b].start()
    for side in range(2):

        @pl.when(tp == side)
        def _():
            attend(side * 2)
            attend(side * 2 + 1)

    keep(o, o_h)
    keep(ot, ot_h)
    keep(lse_ref, lse_h)
    for name in ("wg", "wu", "wd"):
        loads[name].wait()

    def gated(at):
        xm, cm = x[at, :], c[at, :]
        x2t[:, at] = xm.T
        for first, size in TILES:
            cols = slice(first, first + size)
            gate, up = nn(xm, wg[:, cols]), nn(xm, wu[:, cols])
            sigma = lax.logistic(gate)
            smooth = gate * sigma
            low = (smooth * up).astype(BF)
            hid[:, cols] = low
            ht[cols, at] = low.T
            back = nt(cm, wd[cols, :])
            gg[at, cols] = (back * up * (sigma * (1.0 + gate * (1.0 - sigma)))).astype(BF)
            ug[at, cols] = (back * smooth).astype(BF)
        return nn(hid[...], wd[...]), nt(gg[at, :], wg[...]) + nt(ug[at, :], wu[...])

    spots = tuple((rows(t // 2), slice(t % 2 * 512, t % 2 * 512 + TILES[t][1])) for t in range(3))

    def gated_up(at):
        xm = x[at, :]
        x2t[:, at] = xm.T
        for (first, size), spot in zip(TILES, spots):
            cols = slice(first, first + size)
            gate, up = nn(xm, wg[:, cols]), nn(xm, wu[:, cols])
            tok[spot] = gate
            base[spot] = up
            low = (gate * lax.logistic(gate) * up).astype(BF)
            hid[:, cols] = low
            ht[cols, at] = low.T
        return nn(hid[...], wd[...])

    def gated_down(at):
        cm = c[at, :]
        for (first, size), spot in zip(TILES, spots):
            cols = slice(first, first + size)
            gate, up = tok[spot], base[spot]
            sigma = lax.logistic(gate)
            back = nt(cm, wd[cols, :])
            gg[at, cols] = (back * up * (sigma * (1.0 + gate * (1.0 - sigma)))).astype(BF)
            ug[at, cols] = (back * (gate * sigma)).astype(BF)
        return nt(gg[at, :], wg[...]) + nt(ug[at, :], wu[...])

    def block_mine(b, carry):
        here = pl.ds(pl.multiple_of(b * BLK, BLK), BLK)
        at = mine(b)
        peer(4 + b, send2.at[half(0)], recv2.at[half(0)]).wait_recv()
        middle = tok[here, :] + nn(o[at, :], wo[...]) + recv2[here, :].astype(F32)
        tok[here, :] = middle
        for n in range(2):
            first(2 * b + n, x.at[quarter(0)], x.at[quarter(0)]).wait_send()
        x[at, :] = norm_rows(middle, gain_mlp_ref[...]).astype(BF)
        peer(6 + b, x.at[at], x.at[at]).start()
        branch, grad_in = gated(at)
        base[here, :] = tok[here, :] + branch
        cot[here, :] = grad_in
        return carry

    lax.fori_loop(0, 2, block_mine, 0)
    keep(tok, middle_h)
    keep(base, base_h)
    keep(cot, own6_h)
    for copy in stores[:10]:
        copy.wait()
    columns = lambda t: slice(TILES[t][0], sum(TILES[t]))
    across = [(buf.at[:, : TILES[t][1]], gg, columns(t), gg_h) for t, buf in enumerate((wq, wk, wv))]
    across += [(buf.at[:, : TILES[t][1]], ug, columns(t), gu_h) for t, buf in enumerate((q, k, v))]
    down = [(buf.at[: TILES[t][1]], columns(t)) for t, buf in enumerate((ot, wo, recv2))]

    def gather(at, fresh):
        for buf, cols in down:
            new = nn(ht[cols, at], c[at, :])
            buf[...] = (new if fresh else buf[...].astype(F32) + new).astype(BF)

        def body(n, carry):
            tile = pl.ds(pl.multiple_of(n * BLK, BLK), BLK)
            turned = x2t[tile, at]
            for buf, right, cols, _ in across:
                new = nn(turned, right[at, cols])
                buf[tile, :] = (new if fresh else buf[tile, :].astype(F32) + new).astype(BF)
            return carry

        lax.fori_loop(0, 4, body, 0)

    gather(pl.ds(pl.multiple_of(tp * 512, 512), 512), True)
    for b in range(2):
        peer(6 + b, x.at[half(0)], x.at[half(0)]).wait_recv()
        if b == 1:
            cots[1].start()
        send4[half(b), :] = gated_up(theirs(b)).astype(BF)
        peer(2 + b, c.at[half(0)], c.at[half(0)]).wait_recv()
        if b == 1:
            peer(8, send6.at[half(0)], recv6.at[half(0)]).start()
        send6[half(b), :] = gated_down(theirs(b)).astype(BF)
        if b == 1:
            keep(send6, send6_h)
            keep(send4, send4_h)
        gather(theirs(b), False)
    last = [(buf, gd_h.at[cols]) for buf, cols in down] + [(buf, out.at[:, cols]) for buf, _, cols, out in across]
    for buf, out in last:
        keep(buf, out)
    peer(8, send6.at[half(0)], recv6.at[half(0)]).wait_recv()
    keep(recv6, recv6_h)
    for b in range(2):
        for n in (2, 4, 6):
            peer(n + b, recv6.at[half(0)], recv6.at[half(0)]).wait_send()
    peer(8, send6.at[half(0)], recv6.at[half(0)]).wait_send()
    for copy in stores[10:]:
        copy.wait()


def front(tokens, vf, wq, wk, wv, wo, wg, wu, wd, gain_attn, gain_mlp, cot, cos, sin):
    V = lambda shape, kind=BF: pltpu.VMEM(shape, kind)
    D = lambda *shape: pltpu.SemaphoreType.DMA(shape)
    hbm = pl.BlockSpec(memory_space=pl.ANY)
    S = jax.ShapeDtypeStruct
    own, heads, turned, square = (512, 1024), (1024, 512), (512, 1024), (1024, 1024)
    hidden, across, half = (1024, 1408), (1408, 1024), (256, 1024)
    return pl.pallas_call(
        front_kernel,
        in_specs=[hbm] * 14,
        out_specs=[hbm] * 16,
        out_shape=[*[S(heads, BF)] * 4, S(turned, BF), S(square, BF), S((2, 8, 1024), F32), S(own, F32), S(own, F32), S(own, BF),
                   S(own, F32), S(own, BF), S(half, BF), S(hidden, BF), S(hidden, BF), S(across, BF)],
        scratch_shapes=[
            V(own, F32), V(own, F32), V(square), V(square), *[V(heads)] * 7, V(turned), V(heads), V(turned), V(own), V(own), V(own),
            V(square), V(square), V(hidden), V(hidden), V(across), V(across), V((256, 1408)), V(hidden), V(hidden), V(own, F32),
            V(own), V(own), V(half),
            *[V((1, 1024), F32)] * 2, *[V((1024, 128), F32)] * 2, V((2, 8, 1024), F32),
            D(17), D(2, 9), D(23), D(2, 4),
        ],
        compiler_params=pltpu.CompilerParams(collective_id=4, has_side_effects=True, vmem_limit_bytes=63 << 20),
        cost_estimate=pl.CostEstimate(flops=40 * 10**9, bytes_accessed=60 << 20, transcendentals=5 << 20),
    )(tokens, vf, wq, wk, wv, wo, wg, wu, wd, gain_attn, gain_mlp, cot, cos, sin)


def ring_place(dp):
    core, x, z = lax.rem(dp, 2), lax.rem(lax.div(dp, 2), 2), lax.div(dp, 4)
    place = z + x * (7 - 2 * z)

    def device(where):
        side = lax.div(where, 4)
        return ((where + side * (7 - 2 * where)) * 2 + side) * 2 + core

    turn_no = lax.rem(place + core * (8 - 2 * place), 8)
    after = device(lax.rem(place + 1 + 6 * core, 8))
    before = device(lax.rem(place + 7 - 6 * core, 8))
    cube = (dp + 1 - 2 * core, dp + 2 - 4 * x, dp + 4 - 8 * lax.rem(z, 2), dp + 8 - 16 * lax.div(z, 2))
    return core, turn_no, after, before, cube


def remote(src, dst, send, recv, dp):
    return pltpu.make_async_remote_copy(
        src, dst, send, recv, device_id={"dp": dp}, device_id_type=pl.DeviceIdType.MESH
    )


class Ring:
    def __init__(self, place, takes, outs, own, sib, slots, sems):
        self.core, self.turn_no, self.after, self.before, self.cube = place
        self.takes, self.outs, self.own, self.sib, self.slots = takes, outs, own, sib, slots
        self.trade, self.rs, self.ag, self.over, self.keep = sems

    def piece(self, g, chunk):
        size = self.slots[g].shape[1]
        return pl.ds(pl.multiple_of(chunk * size, size), size)

    def traded(self, g, n):
        at = self.piece(g, lax.rem(15 + lax.rem(8 - self.turn_no, 8) - n, 8))
        return remote(
            self.takes[g](1 - self.core).at[at], self.sib[g].at[at], self.trade.at[0, g, n], self.trade.at[1, g, n], self.cube[0]
        )

    def trade_all(self):
        for n in range(8):
            for g in range(len(self.takes)):
                self.traded(g, n).start()

    def total(self, g, chunk):
        at = self.piece(g, chunk)
        return self.own[g][at, :].astype(F32) + self.sib[g][at, :].astype(F32)

    def first(self, g, chunk):
        return remote(
            self.own[g].at[self.piece(g, chunk)], self.slots[g].at[0], self.rs.at[0, g, 0], self.rs.at[1, g, 0], self.after
        )

    def begin(self, g):
        self.traded(g, 0).wait_recv()
        chunk = lax.rem(self.turn_no + 7, 8)
        self.own[g][self.piece(g, chunk), :] = self.total(g, chunk).astype(BF)
        self.first(g, chunk).start()

    def add(self, g, t):
        chunk = lax.rem(self.turn_no + 14 - t, 8)
        self.traded(g, t + 1).wait_recv()
        remote(self.slots[g].at[t], self.slots[g].at[t], self.rs.at[0, g, t], self.rs.at[1, g, t], self.after).wait_recv()
        self.slots[g][t] = (self.slots[g][t].astype(F32) + self.total(g, chunk)).astype(BF)

    def add_on(self, g, t):
        self.add(g, t)
        remote(self.slots[g].at[t], self.slots[g].at[t + 1], self.rs.at[0, g, t + 1], self.rs.at[1, g, t + 1], self.after).start()

    def spot(self, g, chunk):
        return self.outs[g](self.core, chunk)

    def turn_over(self, g):
        self.add(g, 6)
        spot = self.spot(g, self.turn_no)
        last = self.slots[g].at[6]
        remote(last, spot, self.ag.at[0, g, 0], self.ag.at[1, g, 0], self.after).start()
        remote(last, spot, self.over.at[0, g, 0], self.over.at[1, g, 0], self.cube[0]).start()
        pltpu.make_async_copy(last, spot, self.keep.at[g]).start()

    def pass_on(self, g, t):
        spot = self.spot(g, lax.rem(self.turn_no + 15 - t, 8))
        remote(spot, spot, self.ag.at[0, g, t], self.ag.at[1, g, t], self.after).wait_recv()

        @pl.when(t < 6)
        def _():
            remote(spot, spot, self.ag.at[0, g, t + 1], self.ag.at[1, g, t + 1], self.after).start()

        remote(spot, spot, self.over.at[0, g, t + 1], self.over.at[1, g, t + 1], self.cube[0]).start()

    def end(self, g):
        spot = self.spot(g, self.turn_no)
        pltpu.make_async_copy(self.slots[g].at[6], spot, self.keep.at[g]).wait()

        def finish(t, _):
            remote(self.slots[g].at[0], self.slots[g].at[0], self.rs.at[0, g, t], self.rs.at[1, g, t], self.after).wait_send()
            remote(spot, spot, self.ag.at[0, g, t], self.ag.at[1, g, t], self.after).wait_send()
            return _

        lax.fori_loop(0, 7, finish, 0)

        def crossed(t, _):
            self.traded(g, t).wait_send()
            there = self.outs[g](1 - self.core, lax.rem(self.turn_no + t, 8))
            remote(spot, there, self.over.at[0, g, t], self.over.at[1, g, t], self.cube[0]).wait()
            return _

        lax.fori_loop(0, 8, crossed, 0)


def strip(ref, axis, halves, length):
    if axis == 0:
        return lambda core, chunk: ref.at[pl.ds(pl.multiple_of(core * halves + chunk * length, length), length)]
    return lambda core, chunk: ref.at[
        pl.ds(pl.multiple_of(chunk * length, length), length), pl.ds(pl.multiple_of(core * halves, halves), halves)
    ]


def half_of(ref, axis, halves):
    if axis == 0:
        return lambda core: ref.at[pl.ds(pl.multiple_of(core * halves, halves), halves)]
    return lambda core: ref.at[:, pl.ds(pl.multiple_of(core * halves, halves), halves)]


def norm_back_rows(values, gain, grad_in):
    factor = lax.rsqrt(jnp.mean(values * values, axis=-1, keepdims=True) + EPS)
    normed = values * factor
    grad_normed = grad_in * gain
    grad = factor * (grad_normed - normed * jnp.mean(grad_normed * normed, axis=-1, keepdims=True))
    return grad, jnp.sum(grad_in * normed, axis=0, keepdims=True)


def back_kernel(
    own6_h, send6_h, recv6_h, own4_h, send4_h, middle_h, cot_h, tokens_h, gain_attn_h, gain_mlp_h,
    wo_h, wq_h, wk_h, wv_h, q_h, k_h, v_h, o_h, ot_h, xt_h, lse_h, cos_h, sin_h, gg_h, gu_h, gd_h,
    out_h, gt_h, gf_h, rq_h, rk_h, rv_h, ro_h, rg_h, ru_h, rd_h, gains_h,
    f1, f2, f3, recv6, recv4, recv8, send8, c, wo, wq, wk, wv, q, k, v, o, ot, xt,
    dq, dk, dv, do, kt, dka, dva, dl, own8, dwq, dwk, dwv, dwo,
    mg, mu, md, sg, su, sd, lg, lu, ld, bq, bk, bv, bo, aq, ak, av, ao,
    load, ysem, trade1, rs1, ag1, over1, keep1, trade2, rs2, ag2, over2, keep2, gain_in, gain_sem, store,
    gain_attn_ref, gain_mlp_ref, lse_ref, cos_ref, sin_ref, gains_ref,
):
    dp, tp = lax.axis_index("dp"), lax.axis_index("tp")
    place = ring_place(dp)
    core, turn_no, after, before, cube = place
    mesh_id = pl.DeviceIdType.MESH
    barrier = pltpu.get_barrier_semaphore()
    for other in (*cube, after, before):
        pl.semaphore_signal(barrier, inc=1, device_id={"dp": other}, device_id_type=mesh_id)
    pl.semaphore_signal(barrier, inc=1, device_id={"tp": 1 - tp}, device_id_type=mesh_id)

    loads = {}

    def fetch(name, src, dst):
        loads[name] = pltpu.make_async_copy(src, dst, load.at[len(loads)])
        loads[name].start()

    one = Ring(
        place, (half_of(gd_h, 1, 512), half_of(gg_h, 0, 512), half_of(gu_h, 0, 512)),
        (strip(rd_h, 1, 512, 176), strip(rg_h, 0, 512, 64), strip(ru_h, 0, 512, 64)),
        (md, mg, mu), (sd, sg, su), (ld, lg, lu), (trade1, rs1, ag1, over1, keep1),
    )
    two = Ring(
        place, (half_of(dwq, 0, 512), half_of(dwk, 0, 512), half_of(dwv, 0, 512), half_of(dwo, 0, 256)),
        (strip(rq_h, 0, 512, 64), strip(rk_h, 0, 512, 64), strip(rv_h, 0, 512, 64), strip(ro_h, 0, 256, 32)),
        (half_of(dwq, 0, 512)(core), half_of(dwk, 0, 512)(core), half_of(dwv, 0, 512)(core), half_of(dwo, 0, 256)(core)),
        (bq, bk, bv, bo), (aq, ak, av, ao), (trade2, rs2, ag2, over2, keep2),
    )
    for g, (whole, mine) in enumerate(((gd_h, md), (gg_h, mg), (gu_h, mu))):
        fetch(("m", g), one.takes[g](core), mine)
    for name, src, dst in (
        ("gain_attn", gain_attn_h, gain_attn_ref), ("gain_mlp", gain_mlp_h, gain_mlp_ref), ("own6", own6_h, f1), ("recv6", recv6_h, recv6.at[pl.ds(0, BLK)]), ("middle", middle_h, f2), ("cot", cot_h, f3), ("k", k_h, k), ("lse", lse_h, lse_ref), ("cos", cos_h, cos_ref), ("sin", sin_h, sin_ref), ("wo", wo_h, wo), ("o", o_h, o),
        ("q", q_h, q), ("v", v_h, v), ("wq", wq_h, wq), ("wk", wk_h, wk), ("wv", wv_h, wv), ("ot", ot_h, ot), ("xt", xt_h, xt),
    ):
        fetch(name, src, dst)
    pl.semaphore_wait(barrier, 7)

    def peer(n, src, dst):
        return pltpu.make_async_remote_copy(
            src, dst, ysem.at[0, n], ysem.at[1, n], device_id={"tp": 1 - tp}, device_id_type=mesh_id
        )

    half = lambda b: pl.ds(b * BLK, BLK)
    six = peer(0, send6_h.at[half(1)], recv6.at[half(1)])
    six.start()
    one.trade_all()
    for g in range(3):
        loads["m", g].wait()
        one.begin(g)

    lane = lax.broadcasted_iota(jnp.int32, (BLK, 128), 1)
    causal = lax.broadcasted_iota(jnp.int32, (BLK, BLK), 0) <= lax.broadcasted_iota(jnp.int32, (BLK, BLK), 1)
    for name in ("gain_attn", "gain_mlp", "lse", "cos", "sin"):
        loads[name].wait()
    gain_mlp, gain_attn = gain_mlp_ref[...], gain_attn_ref[...]
    dka[...] = jnp.zeros_like(dka)
    dva[...] = jnp.zeros_like(dva)
    loads["k"].wait()
    for j in range(4):
        kt[:, rows(j)] = k[rows(j), :].T

    def one_piece(n):
        step, g = divmod(n, 3)
        if step < 6:
            one.add_on(g, step)
        elif step == 6:
            one.turn_over(g)
        else:
            one.pass_on(g, step - 7)

    def two_step(g, step):
        if step < 6:
            two.add_on(g, step)
        elif step == 6:
            two.turn_over(g)
        else:
            two.pass_on(g, step - 7)

    def branch_back(m):
        at = pl.ds(pl.multiple_of(m * BLK, BLK), BLK)
        low = nt(c[at, :], wo[...]).astype(BF)
        do[at, :] = low
        prod = (low.astype(F32) * o[at, :].astype(F32)).T
        for h in range(8):
            dl[h : h + 1, at] = jnp.sum(prod[h * 64 : h * 64 + 64, :], axis=0, keepdims=True)

    def attend_back(m, p):
        cols = pl.ds(pl.multiple_of(p * 128, 128), 128)
        i = POS_OF[m]
        qb, dob = q[rows(i), cols], do[rows(m), cols]
        parts = []
        for h in range(2):
            mine = (lane < 64) == (h == 0)
            qm = jnp.where(mine, qb, jnp.zeros_like(qb))
            dom = jnp.where(mine, dob, jnp.zeros_like(dob))
            lse = lse_ref[lax.div(p, 2), pl.ds(2 * lax.rem(p, 2) + h, 1), rows(i)]
            delta = dl[pl.ds(2 * p + h, 1), rows(m)]
            head = pl.ds(pl.multiple_of(p * 128 + h * 64, 64), 64)
            dqt = None
            for j in range(i + 1):
                weights = jnp.exp(nt(k[rows(j), cols], qm) - lse)
                if j == i:
                    weights = jnp.where(causal, weights, 0.0)
                ds = (weights * (nt(v[rows(j), cols], dom) - delta)).astype(BF)
                dva[rows(j), cols] = dva[rows(j), cols] + nn(weights.astype(BF), dom)
                dka[rows(j), cols] = dka[rows(j), cols] + nn(ds, qm)
                part = nn(kt[head, rows(j)], ds)
                dqt = part if dqt is None else dqt + part
            parts.append(dqt)
        grad = (jnp.concatenate(parts, axis=0).T * 0.125).astype(BF).astype(F32)
        dq[rows(m), cols] = turn(grad, cos_ref[rows(m), :], -sin_ref[rows(m), :], lane).astype(BF)

    def block_back(side_of, b, pieces):
        branch_back(side_of(tp) * 2 + b)

        def pair(p, carry):
            for side in range(2):

                @pl.when(tp == side)
                def _():
                    attend_back(side_of(side) * 2 + b, p)

            for late, n in enumerate(pieces):
                if n is not None:

                    @pl.when(p == late)
                    def _():
                        one_piece(n)

            return carry

        lax.fori_loop(0, 4, pair, 0)

    for name in ("own6", "recv6", "middle", "cot", "wo", "o", "q", "v"):
        loads[name].wait()
    gain_sum = jnp.zeros((1, 1024), F32)
    seven = []
    for b in range(2):
        if b == 1:
            six.wait_recv()
            seven[0].start()

        def rows_back(n, total):
            at = pl.ds(pl.multiple_of(b * BLK + n * 64, 64), 64)
            grad_in = f1[at, :] + recv6[at, :].astype(F32)
            grad, part = norm_back_rows(f2[at, :], gain_mlp, grad_in)
            grad = f3[at, :] + grad
            f1[at, :] = grad
            c[pl.ds(pl.multiple_of(tp * 512 + b * BLK + n * 64, 64), 64), :] = grad.astype(BF)
            return total + part

        gain_sum = lax.fori_loop(0, 4, rows_back, gain_sum)
        mine = c.at[pl.ds(pl.multiple_of(tp * 512 + b * BLK, BLK), BLK)]
        seven.append(peer(2 + b, mine, mine))
        if b == 1:
            seven[1].start()
        block_back(lambda side: side, b, ((None, None, None, 0), (2, 3, 4, 5))[b])
        one_piece((1, 6)[b])
    late = pltpu.make_async_copy(own4_h, f3, load.at[len(loads)])
    late.start()
    fetch_tokens = pltpu.make_async_copy(tokens_h, f2, load.at[len(loads) + 1])
    fetch_tokens.start()
    gains_ref[...] = jnp.zeros_like(gains_ref)
    gains_ref[0:1, :] = gain_sum
    four = peer(4, send4_h, recv4)
    for b in range(2):
        seven[b].wait_recv()
        if b == 1:
            four.start()
        block_back(lambda side: 1 - side, b, range(7 + 5 * b, 11 + 5 * b))
        one_piece(11 + 5 * b)
    for m in range(4):
        at = rows(POS_OF[m])
        cosine, sine = cos_ref[rows(m), :], -sin_ref[rows(m), :]
        for t in range(4):
            cols = slice(t * 128, t * 128 + 128)
            grad = dka[at, cols].astype(BF).astype(F32)
            dk[rows(m), cols] = turn(grad, cosine, sine, lane).astype(BF)
        dv[rows(m), :] = (0.5 * dva[at, :].astype(BF).astype(F32)).astype(BF)
    keep_gf = pltpu.make_async_copy(dv, gf_h, store.at[0])
    keep_gf.start()
    one_piece(17)
    for name in ("wq", "wk", "wv", "xt", "ot"):
        loads[name].wait()

    def into_rows(at):
        return nt(dq[at, :], wq[...]) + nt(dk[at, :], wk[...]) + nt(dv[at, :], wv[...])

    for which in range(2):
        side = (1 - core) * (1 - which) + core * which
        at = pl.ds(pl.multiple_of(side * 512, 512), 512)
        for n, (dst, src) in enumerate(((dwq, dq), (dwk, dk), (dwv, dv))):
            dst[at, :] = nn(xt[at, :], src[...]).astype(BF)
            if n < 2:
                one_piece(18 + 2 * which + n)
        at = pl.ds(pl.multiple_of(side * 256, 256), 256)
        dwo[at, :] = nn(ot[at, :], c[...]).astype(BF)
        if which == 0:
            two.trade_all()
    for g in range(4):
        two.begin(g)
    eight = []
    for b in range(2):
        at = pl.ds(pl.multiple_of((1 - tp) * 512 + b * BLK, BLK), BLK)
        send8[half(b), :] = into_rows(at).astype(BF)
        eight.append(peer(5 + b, send8.at[half(b)], recv8.at[half(b)]))
        eight[b].start()
        one_piece(22 + b)

    def gain_swap(n):
        where = {"tp": 1 - tp} if n == 4 else {"dp": cube[n]}
        return pltpu.make_async_remote_copy(
            gains_ref, gain_in.at[n], gain_sem.at[0, n], gain_sem.at[1, n], device_id=where, device_id_type=mesh_id
        )

    def rows_last(b, total):
        eight[b].wait_recv()

        def body(n, total):
            at = pl.ds(pl.multiple_of(b * BLK + n * 64, 64), 64)
            grad, part = norm_back_rows(f2[at, :], gain_attn, own8[at, :] + recv8[at, :].astype(F32))
            f1[at, :] = f1[at, :] + grad
            return total + part

        return lax.fori_loop(0, 4, body, total)

    keep_out = pltpu.make_async_copy(f3, out_h, store.at[1])
    keep_gt = pltpu.make_async_copy(f1, gt_h, store.at[2])
    gain_sum = jnp.zeros((1, 1024), F32)
    for step in range(14):
        for g in range(4):
            two_step(g, step)
        for n in range(24 + PACE[step], 24 + PACE[step + 1]):
            one_piece(n)
        if step < 2:
            at = pl.ds(pl.multiple_of(tp * 512 + step * BLK, BLK), BLK)
            own8[half(step), :] = into_rows(at)
        if step == 2:
            late.wait()
            fetch_tokens.wait()
        if step in (5, 6):
            gain_sum = rows_last(step - 5, gain_sum)
        if step == 6:
            gains_ref[1:2, :] = gain_sum
            keep_gt.start()
        if step == 7:
            four.wait_recv()

            def out_rows(n, carry):
                at = pl.ds(pl.multiple_of(n * 64, 64), 64)
                f3[at, :] = f3[at, :] + recv4[at, :].astype(F32)
                return carry

            lax.fori_loop(0, 8, out_rows, 0)
            keep_out.start()
        if step > 8:
            gain_swap(step - 9).wait()
            gains_ref[...] = gains_ref[...] + gain_in[step - 9]
        if 8 <= step < 13:
            gain_swap(step - 8).start()
    keep_gains = pltpu.make_async_copy(gains_ref, gains_h, store.at[3])
    keep_gains.start()
    for g in range(3):
        one.end(g)
    for g in range(4):
        two.end(g)
    for copy in (six, *seven, *eight, four):
        copy.wait_send()
    for copy in (keep_gf, keep_out, keep_gt, keep_gains):
        copy.wait()


PACE = (0, 1, 2, 4, 5, 6, 8, 9, 10, 12, 13, 14, 16, 17, 18)


def back(own6, send6, recv6, own4, send4, middle, cot, tokens, gain_attn, gain_mlp, wo, wq, wk, wv, q, k, v, o, ot, xt, lse, cos, sin, gg, gu, gd):
    V = lambda shape, kind=BF: pltpu.VMEM(shape, kind)
    D = lambda *shape: pltpu.SemaphoreType.DMA(shape)
    hbm = pl.BlockSpec(memory_space=pl.ANY)
    S = jax.ShapeDtypeStruct
    wide = (1024, 1024)
    return pl.pallas_call(
        back_kernel,
        in_specs=[hbm] * 26,
        out_specs=[hbm] * 11,
        out_shape=[S((512, 1024), F32), S((512, 1024), F32), S((1024, 512), BF), *[S((1024, 512), BF)] * 3, S((512, 1024), BF),
                   S((1024, 1408), BF), S((1024, 1408), BF), S((1408, 1024), BF), S((8, 1024), F32)],
        scratch_shapes=[
            *[V((512, 1024), F32)] * 3, *[V((512, 1024))] * 4, V(wide), V((512, 1024)), *[V((1024, 512))] * 7, V((512, 1024)), V(wide),
            *[V((1024, 512))] * 4, V((512, 1024)), *[V((1024, 512), F32)] * 2, V((8, 1024), F32), V((512, 1024), F32),
            *[V((1024, 512))] * 3, V((512, 1024)),
            *[V((512, 1408)), V((512, 1408)), V((1408, 512))] * 2, V((7, 64, 1408)), V((7, 64, 1408)), V((7, 176, 512)),
            *[V((512, 512))] * 3, V((256, 1024)), *[V((7, 64, 512))] * 3, V((7, 32, 1024)),
            D(24), D(2, 7), D(2, 3, 8), D(2, 3, 7), D(2, 3, 7), D(2, 3, 8), D(3), D(2, 4, 8), D(2, 4, 7), D(2, 4, 7), D(2, 4, 8), D(4),
            V((5, 8, 1024), F32), D(2, 5), D(4),
            *[V((1, 1024), F32)] * 2, V((2, 8, 1024), F32), *[V((1024, 128), F32)] * 2, V((8, 1024), F32),
        ],
        compiler_params=pltpu.CompilerParams(collective_id=3, has_side_effects=True, vmem_limit_bytes=62 << 20),
        cost_estimate=pl.CostEstimate(flops=30 * 10**9, bytes_accessed=60 << 20, transcendentals=5 << 20),
    )(own6, send6, recv6, own4, send4, middle, cot, tokens, gain_attn, gain_mlp, wo, wq, wk, wv, q, k, v, o, ot, xt, lse, cos, sin, gg, gu, gd)


PIECES = 4


def finish_kernel(*refs):
    gains_ref, ins, outs, wide = refs[0], refs[1:11], refs[11:21], refs[23:39]
    sums, through, load, store = refs[39:]
    fetch = pltpu.make_async_copy(gains_ref, sums, load.at[8, 2])
    fetch.start()
    gains = [pltpu.make_async_copy(sums.at[pl.ds(n, 1)], refs[21 + n], store.at[n, 1]) for n in range(2)]
    into = [pltpu.make_async_copy(ins[n], through.at[n], load.at[8, n]) for n in range(2)]
    whole = [pltpu.make_async_copy(through.at[n], outs[n], store.at[n, 0]) for n in range(2)]
    for copy in into:
        copy.start()
    low, high = wide[:8], wide[8:]
    order = (5, 6, 7, 1, 2, 3, 4, 0)

    def part(ref, piece):
        size = ref.shape[0] // PIECES
        return ref.at[pl.ds(piece * size, size)]

    for a in order:
        for piece in range(PIECES):
            pltpu.make_async_copy(part(ins[a + 2], piece), part(low[a], piece), load.at[a, piece]).start()
    fetch.wait()
    for n in range(2):
        gains[n].start()
        into[n].wait()
        whole[n].start()
    for a in order:
        for piece in range(PIECES):
            pltpu.make_async_copy(part(ins[a + 2], piece), part(low[a], piece), load.at[a, piece]).wait()
            size = low[a].shape[0] // PIECES

            def widen(n, carry):
                at = pl.ds(pl.multiple_of(piece * size + n * 16, 16), 16)
                high[a][at, :] = low[a][at, :].astype(F32)
                return carry

            lax.fori_loop(0, size // 16, widen, 0, unroll=4)
            pltpu.make_async_copy(part(high[a], piece), part(outs[a + 2], piece), store.at[a + 2, piece]).start()
    for a in order:
        for piece in range(PIECES):
            pltpu.make_async_copy(part(high[a], piece), part(outs[a + 2], piece), store.at[a + 2, piece]).wait()
    for copy in (*whole, *gains):
        copy.wait()


def finish(gains, *arrays):
    hbm = pl.BlockSpec(memory_space=pl.ANY)
    return pl.pallas_call(
        finish_kernel,
        in_specs=[hbm] * 11,
        out_specs=[hbm] * 12,
        out_shape=[jax.ShapeDtypeStruct(a.shape, F32) for a in arrays] + [jax.ShapeDtypeStruct((1, 1024), F32)] * 2,
        scratch_shapes=[
            *[pltpu.VMEM(a.shape, BF) for a in arrays[2:]], *[pltpu.VMEM(a.shape, F32) for a in arrays[2:]],
            pltpu.VMEM(gains.shape, F32), pltpu.VMEM((2, *arrays[0].shape), F32), pltpu.SemaphoreType.DMA((9, PIECES)), pltpu.SemaphoreType.DMA((10, PIECES)),
        ],
        compiler_params=pltpu.CompilerParams(vmem_limit_bytes=60 << 20),
        cost_estimate=pl.CostEstimate(flops=10**7, bytes_accessed=48 << 20, transcendentals=0),
    )(gains, *arrays)

def local_pair(
    tokens,
    v_first,
    w_query,
    w_key,
    w_value,
    w_out,
    w_gate,
    w_up,
    w_down,
    gain_attn,
    gain_mlp,
    seq_lens,
    cotangent,
):
    cosine, sine = tables()
    (query, keys, mixed_values, attended, attended_t, normed_t, row_lse, middle, base, send_out, own_in, send_in, got_in,
     grad_gate, grad_up, grad_down) = front(
        tokens, v_first, w_query, w_key, w_value, w_out, w_gate, w_up, w_down, gain_attn[None], gain_mlp[None], cotangent, cosine, sine
    )
    layer_out, grad_tokens, grad_first, *low_grads, gains = back(
        own_in, send_in, got_in, base, send_out, middle, cotangent, tokens, gain_attn[None], gain_mlp[None], w_out, w_query, w_key, w_value,
        query, keys, mixed_values, attended, attended_t, normed_t, row_lse, cosine, sine, grad_gate, grad_up, grad_down,
    )
    layer_out, grad_tokens, grad_first, *wide, gain_mlp_grad, gain_attn_grad = finish(gains, layer_out, grad_tokens, grad_first, *low_grads)
    grad_gain_mlp, grad_gain_attn = gain_mlp_grad[0], gain_attn_grad[0]
    return (layer_out, grad_tokens, grad_first, *wide, grad_gain_attn, grad_gain_mlp)


def local(
    tokens,
    v_first,
    w_query,
    w_key,
    w_value,
    w_out,
    w_gate,
    w_up,
    w_down,
    gain_attn,
    gain_mlp,
    seq_lens,
    cotangent,
):
    tp_count = lax.axis_size("tp")
    row_share = tokens.shape[0]
    doc_ids, positions = layout(seq_lens[0], row_share, tp_count)
    normed_attn = lax.all_gather(
        normalize(tokens, gain_attn).astype(jnp.bfloat16), "tp", axis=0, tiled=True
    )
    query = rotate(
        jnp.dot(normed_attn, w_query, preferred_element_type=jnp.float32), positions, HDIM, 1.0
    ).astype(jnp.bfloat16)
    keys = rotate(
        jnp.dot(normed_attn, w_key, preferred_element_type=jnp.float32), positions, HDIM, 1.0
    ).astype(jnp.bfloat16)
    value_pre = jnp.dot(normed_attn, w_value, preferred_element_type=jnp.float32)
    mixed_values = (0.5 * value_pre + 0.5 * v_first.astype(jnp.float32)).astype(jnp.bfloat16)
    attended, row_lse = attention_forward(query, keys, mixed_values, doc_ids, positions, HDIM)
    middle = tokens + lax.psum_scatter(
        jnp.dot(attended, w_out, preferred_element_type=jnp.float32),
        "tp",
        scatter_dimension=0,
        tiled=True,
    )
    normed_mlp = normalize(middle, gain_mlp).astype(jnp.bfloat16)
    grad_branch = cotangent.astype(jnp.bfloat16)
    mlp_rows = lax.all_gather(normed_mlp, "tp", axis=0, tiled=True)
    gate = jnp.dot(mlp_rows, w_gate, preferred_element_type=jnp.float32)
    up_values = jnp.dot(mlp_rows, w_up, preferred_element_type=jnp.float32)
    hidden = (jax.nn.silu(gate) * up_values).astype(jnp.bfloat16)
    layer_out = middle + lax.psum_scatter(
        jnp.dot(hidden, w_down, preferred_element_type=jnp.float32).astype(jnp.bfloat16),
        "tp",
        scatter_dimension=0,
        tiled=True,
    ).astype(jnp.float32)
    cot_rows = lax.all_gather(grad_branch, "tp", axis=0, tiled=True)
    grad_down = inner_rows(hidden, cot_rows)
    gate_grad, up_grad = swiglu_back(gate, up_values, outer_cols(cot_rows, w_down))
    grad_gate = inner_rows(mlp_rows, gate_grad)
    grad_up = inner_rows(mlp_rows, up_grad)
    grad_mlp_in = lax.psum_scatter(
        (outer_cols(gate_grad, w_gate) + outer_cols(up_grad, w_up)).astype(jnp.bfloat16),
        "tp",
        scatter_dimension=0,
        tiled=True,
    ).astype(jnp.float32)
    middle_back, grad_gain_mlp = normalize_back(middle, gain_mlp, grad_mlp_in)
    grad_middle = cotangent + middle_back
    attn_cot_rows = lax.all_gather(grad_middle.astype(jnp.bfloat16), "tp", axis=0, tiled=True)
    grad_output = inner_rows(attended, attn_cot_rows)
    grad_attended = outer_cols(attn_cot_rows, w_out).astype(jnp.bfloat16)
    query_grad, key_grad, mixed_grad = attention_backward(
        query, keys, mixed_values, grad_attended, row_lse, doc_ids, positions, HDIM
    )
    half_mixed = 0.5 * mixed_grad.astype(jnp.float32)
    value_grad = half_mixed.astype(jnp.bfloat16)
    query_pre_grad = rotate(query_grad.astype(jnp.float32), positions, HDIM, -1.0).astype(
        jnp.bfloat16
    )
    key_pre_grad = rotate(key_grad.astype(jnp.float32), positions, HDIM, -1.0).astype(jnp.bfloat16)
    grad_query = inner_rows(normed_attn, query_pre_grad)
    grad_key = inner_rows(normed_attn, key_pre_grad)
    grad_value = inner_rows(normed_attn, value_grad)
    grad_attn_in = lax.psum_scatter(
        (
            outer_cols(query_pre_grad, w_query)
            + outer_cols(key_pre_grad, w_key)
            + outer_cols(value_grad, w_value)
        ).astype(jnp.bfloat16),
        "tp",
        scatter_dimension=0,
        tiled=True,
    ).astype(jnp.float32)
    tokens_back, grad_gain_attn = normalize_back(tokens, gain_attn, grad_attn_in)
    grad_tokens = grad_middle + tokens_back
    grad_query, grad_key, grad_value, grad_output, grad_gate, grad_up, grad_down = (
        lax.psum(grad_query.astype(jnp.bfloat16), "dp").astype(jnp.float32),
        lax.psum(grad_key.astype(jnp.bfloat16), "dp").astype(jnp.float32),
        lax.psum(grad_value.astype(jnp.bfloat16), "dp").astype(jnp.float32),
        lax.psum(grad_output.astype(jnp.bfloat16), "dp").astype(jnp.float32),
        lax.psum(grad_gate.astype(jnp.bfloat16), "dp").astype(jnp.float32),
        lax.psum(grad_up.astype(jnp.bfloat16), "dp").astype(jnp.float32),
        lax.psum(grad_down.astype(jnp.bfloat16), "dp").astype(jnp.float32),
    )
    grad_gain_attn, grad_gain_mlp = lax.psum((grad_gain_attn, grad_gain_mlp), ("dp", "tp"))
    return (
        layer_out,
        grad_tokens,
        half_mixed,
        grad_query,
        grad_key,
        grad_value,
        grad_output,
        grad_gate,
        grad_up,
        grad_down,
        grad_gain_attn,
        grad_gain_mlp,
    )


def solution(mesh):
    in_specs = (
        P(("dp", "tp"), None),
        P("dp", "tp"),
        P(None, "tp"),
        P(None, "tp"),
        P(None, "tp"),
        P("tp", None),
        P(None, "tp"),
        P(None, "tp"),
        P("tp", None),
        P(),
        P(),
        P("dp", None),
        P(("dp", "tp"), None),
    )
    out_specs = (
        P(("dp", "tp"), None),
        P(("dp", "tp"), None),
        P("dp", "tp"),
        P(None, "tp"),
        P(None, "tp"),
        P(None, "tp"),
        P("tp", None),
        P(None, "tp"),
        P(None, "tp"),
        P("tp", None),
        P(),
        P(),
    )

    def step(*args):
        tokens, seq_lens = args[0], args[11]
        pair = mesh.shape["tp"] == 2 and mesh.shape["dp"] == 16 and seq_lens.shape[1] == 1 and tokens.shape == (512, 1024)
        return (local_pair if pair else local)(*args)

    return jax.shard_map(step, mesh=mesh, in_specs=in_specs, out_specs=out_specs, check_vma=False)
```

```python
import functools

import jax
import jax.numpy as jnp
import numpy as np
from jax import lax
from jax.experimental import pallas as pl
from jax.experimental.pallas import tpu as pltpu
from jax.sharding import PartitionSpec as P

HDIM = 64


EPS = 1e-06


def layout(seq_row, row_share, tp_count):
    group_rows = row_share * tp_count
    row_ids = jnp.arange(group_rows, dtype=jnp.int32)
    device = row_ids // row_share
    local_row = row_ids % row_share
    pieces = seq_row // (2 * tp_count)
    slot_ends = jnp.cumsum(2 * pieces)
    starts = slot_ends - 2 * pieces
    offset = local_row[:, None] - starts[None, :]
    inside = (offset >= 0) & (offset < 2 * pieces[None, :])
    first_half = offset < pieces[None, :]
    mirror = 2 * tp_count - 1 - device[:, None]
    position = jnp.where(
        first_half,
        device[:, None] * pieces[None, :] + offset,
        mirror * pieces[None, :] + offset - pieces[None, :],
    )
    slot_ids = jnp.arange(seq_row.shape[0], dtype=jnp.int32)
    doc_ids = jnp.sum(jnp.where(inside, slot_ids[None, :], 0), axis=1)
    positions = jnp.sum(jnp.where(inside, position, 0), axis=1)
    return (doc_ids, positions)


def rotate(values, positions, head_dim, turn_sign):
    row_count, width_all = values.shape
    half_dim = head_dim // 2
    shaped = values.reshape(row_count, width_all // head_dim, head_dim)
    freqs = 10000.0 ** (-jnp.arange(half_dim, dtype=jnp.float32) / half_dim)
    angles = positions.astype(jnp.float32)[:, None] * freqs[None, :]
    cosine = jnp.cos(angles)[:, None, :]
    sine = turn_sign * jnp.sin(angles)[:, None, :]
    front = shaped[..., :half_dim]
    behind = shaped[..., half_dim:]
    turned = jnp.concatenate(
        [front * cosine - behind * sine, behind * cosine + front * sine], axis=-1
    )
    return turned.reshape(row_count, width_all)


def normalize(values, gain):
    return values * lax.rsqrt(jnp.mean(values * values, axis=-1, keepdims=True) + EPS) * gain


def normalize_back(values, gain, grad_in):
    factor = lax.rsqrt(jnp.mean(values * values, axis=-1, keepdims=True) + EPS)
    normed = values * factor
    grad_normed = grad_in * gain
    grad_values = factor * (
        grad_normed - normed * jnp.mean(grad_normed * normed, axis=-1, keepdims=True)
    )
    return (grad_values, jnp.sum(grad_in * normed, axis=0))


def inner_rows(left, right):
    return lax.dot_general(
        left, right, (((0,), (0,)), ((), ())), preferred_element_type=jnp.float32
    )


def outer_cols(left, right):
    return lax.dot_general(
        left, right, (((1,), (1,)), ((), ())), preferred_element_type=jnp.float32
    )


def swiglu_back(gate, up_values, grad_hidden):
    sigma = jax.nn.sigmoid(gate)
    grad_gate = grad_hidden * up_values * (sigma * (1.0 + gate * (1.0 - sigma)))
    grad_upper = grad_hidden * (gate * sigma)
    return (grad_gate.astype(jnp.bfloat16), grad_upper.astype(jnp.bfloat16))


def block_mask(doc_ids, positions, first_row, block_rows):
    row_doc = lax.dynamic_slice_in_dim(doc_ids, first_row, block_rows, 0)
    row_pos = lax.dynamic_slice_in_dim(positions, first_row, block_rows, 0)
    return (row_doc[:, None] == doc_ids[None, :]) & (positions[None, :] <= row_pos[:, None])


def attention_forward(query, keys, values, doc_ids, positions, head_dim):
    group_rows, width_local = query.shape
    head_count = width_local // head_dim
    block_rows = min(512, group_rows)
    block_count = group_rows // block_rows
    score_scale = head_dim ** (-0.5)
    key_heads = keys.reshape(group_rows, head_count, head_dim)
    value_heads = values.reshape(group_rows, head_count, head_dim)

    def forward_block(block_index):
        first_row = block_index * block_rows
        query_rows = lax.dynamic_slice_in_dim(query, first_row, block_rows, 0).reshape(
            block_rows, head_count, head_dim
        )
        scores = (
            jnp.einsum("qhd,khd->hqk", query_rows, key_heads, preferred_element_type=jnp.float32)
            * score_scale
        )
        allowed = block_mask(doc_ids, positions, first_row, block_rows)
        scores = jnp.where(allowed[None], scores, -1e30)
        row_max = jnp.max(scores, axis=-1, keepdims=True)
        exponent = jnp.exp(scores - row_max)
        row_total = jnp.sum(exponent, axis=-1, keepdims=True)
        weights = (exponent / row_total).astype(jnp.bfloat16)
        mixture = jnp.einsum(
            "hqk,khd->qhd", weights, value_heads, preferred_element_type=jnp.float32
        )
        return (
            mixture.astype(jnp.bfloat16).reshape(block_rows, width_local),
            (row_max + jnp.log(row_total))[..., 0],
        )

    mixture, row_lse = lax.map(forward_block, jnp.arange(block_count, dtype=jnp.int32))
    return (mixture.reshape(group_rows, width_local), row_lse)


def attention_backward(query, keys, values, grad_mixture, row_lse, doc_ids, positions, head_dim):
    group_rows, width_local = query.shape
    head_count = width_local // head_dim
    block_rows = min(512, group_rows)
    block_count = group_rows // block_rows
    score_scale = head_dim ** (-0.5)
    key_heads = keys.reshape(group_rows, head_count, head_dim)
    value_heads = values.reshape(group_rows, head_count, head_dim)

    def backward_block(carry, block_index):
        key_total, value_total = carry
        first_row = block_index * block_rows
        query_rows = lax.dynamic_slice_in_dim(query, first_row, block_rows, 0).reshape(
            block_rows, head_count, head_dim
        )
        grad_rows = lax.dynamic_slice_in_dim(grad_mixture, first_row, block_rows, 0).reshape(
            block_rows, head_count, head_dim
        )
        scores = (
            jnp.einsum("qhd,khd->hqk", query_rows, key_heads, preferred_element_type=jnp.float32)
            * score_scale
        )
        allowed = block_mask(doc_ids, positions, first_row, block_rows)
        scores = jnp.where(allowed[None], scores, -1e30)
        weights = jnp.exp(scores - row_lse[block_index][..., None])
        weights_low = weights.astype(jnp.bfloat16)
        grad_weights = jnp.einsum(
            "qhd,khd->hqk", grad_rows, value_heads, preferred_element_type=jnp.float32
        )
        weighted_sum = jnp.sum(weights * grad_weights, axis=-1, keepdims=True)
        score_grad = (weights * (grad_weights - weighted_sum)).astype(jnp.bfloat16)
        query_grad = (
            jnp.einsum("hqk,khd->qhd", score_grad, key_heads, preferred_element_type=jnp.float32)
            * score_scale
        )
        key_total = (
            key_total
            + jnp.einsum("hqk,qhd->khd", score_grad, query_rows, preferred_element_type=jnp.float32)
            * score_scale
        )
        value_total = value_total + jnp.einsum(
            "hqk,qhd->khd", weights_low, grad_rows, preferred_element_type=jnp.float32
        )
        return (
            (key_total, value_total),
            query_grad.astype(jnp.bfloat16).reshape(block_rows, width_local),
        )

    zero_heads = jnp.zeros((group_rows, head_count, head_dim), jnp.float32)
    (key_total, value_total), query_grad = lax.scan(
        backward_block, (zero_heads, zero_heads), jnp.arange(block_count, dtype=jnp.int32)
    )
    return (
        query_grad.reshape(group_rows, width_local),
        key_total.reshape(group_rows, width_local).astype(jnp.bfloat16),
        value_total.reshape(group_rows, width_local).astype(jnp.bfloat16),
    )


BF, F32 = jnp.bfloat16, jnp.float32
BLK = 256
POS_OF = (0, 3, 1, 2)
NT = (((1,), (1,)), ((), ()))

def nt(a, b):
    return lax.dot_general(a, b, NT, preferred_element_type=F32)

def nn(a, b):
    return jnp.dot(a, b, preferred_element_type=F32)

def rows(block):
    return pl.ds(block * BLK, BLK)

def turn(u, cosine, sine, lane):
    near = jnp.where(lane % 64 < 32, pltpu.roll(u, 96, 1), pltpu.roll(u, 32, 1))
    return u * cosine + near * sine

FIRST = {}
for _m in range(4):
    for _j in range(POS_OF[_m] + 1):
        FIRST.setdefault(_j, (_m, 0))

def tables():
    pos = np.zeros(1024, np.float32)
    for m in range(4):
        pos[m*256:(m+1)*256] = POS_OF[m]*256 + np.arange(256)
    freqs = np.float32(10000.0) ** (-np.arange(32, dtype=np.float32) / np.float32(32))
    ang = pos[:, None] * freqs[None]
    c, s = np.cos(ang.astype(np.float32)), np.sin(ang.astype(np.float32))
    return np.tile(c, (1, 4)).astype(np.float32), np.concatenate([-s, s, -s, s], 1).astype(np.float32)


def block_place(m):
    late = lax.div(m, 2)
    return m * 3 - late * (5 + 2 * (m - 2))


def norm_rows(values, gain):
    return values * lax.rsqrt(jnp.mean(values * values, axis=-1, keepdims=True) + EPS) * gain


TILES = ((0, 512), (512, 512), (1024, 384))


def front_kernel(
    tokens_h, vf_h, wq_h, wk_h, wv_h, wo_h, wg_h, wu_h, wd_h, gain_attn_h, gain_mlp_h, cot_h, cos_h, sin_h,
    q_h, k_h, v_h, o_h, ot_h, xt_h, lse_h, middle_h, base_h, send4_h, own6_h, send6_h, recv6_h, gg_h, gu_h, gd_h,
    tok, cot, x, xt, wq, wk, wv, vf, q, k, v, vt, o, ot, wo, recv2, send2, c, x2t, wg, wu, wd,
    ht, hid, gg, ug, base, send4, send6, recv6,
    gain_attn_ref, gain_mlp_ref, cos_ref, sin_ref, lse_ref, load, ysem, store, gsem,
):
    tp = lax.axis_index("tp")
    mesh_id = pl.DeviceIdType.MESH
    barrier = pltpu.get_barrier_semaphore()
    pl.semaphore_signal(barrier, inc=1, device_id={"tp": 1 - tp}, device_id_type=mesh_id)
    loads = {}

    def fetch(name, src, dst):
        loads[name] = pltpu.make_async_copy(src, dst, load.at[len(loads)])
        loads[name].start()

    half = lambda b: pl.ds(b * BLK, BLK)
    quarter = lambda n: pl.ds(n * 128, 128)
    fetch("gain_attn", gain_attn_h, gain_attn_ref)
    for n in range(4):
        fetch(("tok", n), tokens_h.at[quarter(n)], tok.at[quarter(n)])
    for name, src, dst in (
        ("wq", wq_h, wq), ("wk", wk_h, wk), ("wv", wv_h, wv), ("vf", vf_h, vf), ("cos", cos_h, cos_ref), ("sin", sin_h, sin_ref), ("gain_mlp", gain_mlp_h, gain_mlp_ref), ("cot", cot_h, cot), ("wo", wo_h, wo),
        ("wg", wg_h, wg), ("wu", wu_h, wu), ("wd", wd_h, wd),
    ):
        fetch(name, src, dst)
    stores = []

    def keep(src, dst):
        stores.append(pltpu.make_async_copy(src, dst, store.at[len(stores)]))
        stores[-1].start()

    def peer(n, src, dst):
        return pltpu.make_async_remote_copy(
            src, dst, ysem.at[0, n], ysem.at[1, n], device_id={"tp": 1 - tp}, device_id_type=mesh_id
        )

    def mine(b):
        return pl.ds(pl.multiple_of(tp * 512 + b * BLK, BLK), BLK)

    def theirs(b):
        return pl.ds(pl.multiple_of((1 - tp) * 512 + b * BLK, BLK), BLK)

    lane = lax.broadcasted_iota(jnp.int32, (BLK, 128), 1)
    causal = lax.broadcasted_iota(jnp.int32, (BLK, BLK), 0) <= lax.broadcasted_iota(jnp.int32, (BLK, BLK), 1)
    loads["gain_attn"].wait()
    gain_attn = gain_attn_ref[...]

    def first(n, here, there):
        return pltpu.make_async_remote_copy(
            here, there, gsem.at[0, n], gsem.at[1, n], device_id={"tp": 1 - tp}, device_id_type=mesh_id
        )

    for n in range(4):
        loads["tok", n].wait()
        at = pl.ds(pl.multiple_of(tp * 512 + n * 128, 128), 128)
        x[at, :] = norm_rows(tok[quarter(n), :], gain_attn).astype(BF)
        if n == 0:
            pl.semaphore_wait(barrier, 1)
        first(n, x.at[at], x.at[at]).start()
    loads["cot"].wait()
    for b in range(2):
        c[mine(b), :] = cot[half(b), :].astype(BF)
    for name in ("wq", "wk", "wv", "vf", "cos", "sin", "gain_mlp"):
        loads[name].wait()

    def project(m):
        row = pl.ds(pl.multiple_of(m * BLK, BLK), BLK)
        at = pl.ds(pl.multiple_of(block_place(m) * BLK, BLK), BLK)
        xm = x[row, :]
        cosine, sine = cos_ref[row, :], sin_ref[row, :]
        qf, kf = nn(xm, wq[...]), nn(xm, wk[...])
        low = (0.5 * nn(xm, wv[...]) + 0.5 * vf[row, :].astype(F32)).astype(BF)
        for t in range(4):
            cols = slice(t * 128, t * 128 + 128)
            q[at, cols] = turn(qf[:, cols], cosine, sine, lane).astype(BF) * 0.125
            k[at, cols] = turn(kf[:, cols], cosine, sine, lane).astype(BF)
        v[at, :] = low
        vt[:, at] = low.T
        xt[:, row] = xm.T

    def project_mine(b, carry):
        project(tp * 2 + b)
        return carry

    lax.fori_loop(0, 2, project_mine, 0)

    def project_theirs(b, carry):
        for n in range(2):
            first(2 * b + n, x.at[quarter(0)], x.at[quarter(0)]).wait_recv()
        project((1 - tp) * 2 + b)
        return carry

    lax.fori_loop(0, 2, project_theirs, 0)
    cots = [peer(2 + b, c.at[mine(b)], c.at[mine(b)]) for b in range(2)]
    cots[0].start()
    for src, dst in ((q, q_h), (k, k_h), (v, v_h), (xt, xt_h)):
        keep(src, dst)
    lse_ref[...] = jnp.zeros_like(lse_ref)
    loads["wo"].wait()

    def attend(m):
        i = POS_OF[m]

        def pair(p, carry):
            cols = pl.ds(pl.multiple_of(p * 128, 128), 128)
            qb = q[rows(i), cols]
            parts = []
            for h in range(2):
                qm = jnp.where((lane < 64) == (h == 0), qb, jnp.zeros_like(qb))
                scores = [nt(k[rows(j), cols], qm) for j in range(i + 1)]
                scores[i] = jnp.where(causal, scores[i], -1e30)
                top = functools.reduce(jnp.maximum, [jnp.max(s, axis=0, keepdims=True) for s in scores])
                es = [jnp.exp(s - top) for s in scores]
                total = functools.reduce(jnp.add, [jnp.sum(e, axis=0, keepdims=True) for e in es])
                head = pl.ds(pl.multiple_of(p * 128 + h * 64, 64), 64)
                mix = functools.reduce(jnp.add, [nn(vt[head, rows(j)], es[j].astype(BF)) for j in range(i + 1)])
                parts.append(mix * (1.0 / total))
                lse_ref[lax.div(p, 2), pl.ds(2 * lax.rem(p, 2) + h, 1), rows(i)] = top + jnp.log(total)
            flat = jnp.concatenate(parts, axis=0)
            ot[cols, rows(m)] = flat.astype(BF)
            o[rows(m), cols] = flat.T.astype(BF)
            return carry

        lax.fori_loop(0, 4, pair, 0)

    twos = [peer(4 + b, send2.at[half(b)], recv2.at[half(b)]) for b in range(2)]
    for b in range(2):
        for side in range(2):

            @pl.when(tp == side)
            def _():
                attend((1 - side) * 2 + b)

        send2[half(b), :] = nn(o[theirs(b), :], wo[...]).astype(BF)
        twos[b].start()
    for side in range(2):

        @pl.when(tp == side)
        def _():
            attend(side * 2)
            attend(side * 2 + 1)

    keep(o, o_h)
    keep(ot, ot_h)
    keep(lse_ref, lse_h)
    for name in ("wg", "wu", "wd"):
        loads[name].wait()

    def gated(at):
        xm, cm = x[at, :], c[at, :]
        x2t[:, at] = xm.T
        for first, size in TILES:
            cols = slice(first, first + size)
            gate, up = nn(xm, wg[:, cols]), nn(xm, wu[:, cols])
            sigma = lax.logistic(gate)
            smooth = gate * sigma
            low = (smooth * up).astype(BF)
            hid[:, cols] = low
            ht[cols, at] = low.T
            back = nt(cm, wd[cols, :])
            gg[at, cols] = (back * up * (sigma * (1.0 + gate * (1.0 - sigma)))).astype(BF)
            ug[at, cols] = (back * smooth).astype(BF)
        return nn(hid[...], wd[...]), nt(gg[at, :], wg[...]) + nt(ug[at, :], wu[...])

    spots = tuple((rows(t // 2), slice(t % 2 * 512, t % 2 * 512 + TILES[t][1])) for t in range(3))

    def gated_up(at):
        xm = x[at, :]
        x2t[:, at] = xm.T
        for (first, size), spot in zip(TILES, spots):
            cols = slice(first, first + size)
            gate, up = nn(xm, wg[:, cols]), nn(xm, wu[:, cols])
            tok[spot] = gate
            base[spot] = up
            low = (gate * lax.logistic(gate) * up).astype(BF)
            hid[:, cols] = low
            ht[cols, at] = low.T
        return nn(hid[...], wd[...])

    def gated_down(at):
        cm = c[at, :]
        for (first, size), spot in zip(TILES, spots):
            cols = slice(first, first + size)
            gate, up = tok[spot], base[spot]
            sigma = lax.logistic(gate)
            back = nt(cm, wd[cols, :])
            gg[at, cols] = (back * up * (sigma * (1.0 + gate * (1.0 - sigma)))).astype(BF)
            ug[at, cols] = (back * (gate * sigma)).astype(BF)
        return nt(gg[at, :], wg[...]) + nt(ug[at, :], wu[...])

    def block_mine(b, carry):
        here = pl.ds(pl.multiple_of(b * BLK, BLK), BLK)
        at = mine(b)
        peer(4 + b, send2.at[half(0)], recv2.at[half(0)]).wait_recv()
        middle = tok[here, :] + nn(o[at, :], wo[...]) + recv2[here, :].astype(F32)
        tok[here, :] = middle
        for n in range(2):
            first(2 * b + n, x.at[quarter(0)], x.at[quarter(0)]).wait_send()
        x[at, :] = norm_rows(middle, gain_mlp_ref[...]).astype(BF)
        peer(6 + b, x.at[at], x.at[at]).start()
        branch, grad_in = gated(at)
        base[here, :] = tok[here, :] + branch
        cot[here, :] = grad_in
        return carry

    lax.fori_loop(0, 2, block_mine, 0)
    keep(tok, middle_h)
    keep(base, base_h)
    keep(cot, own6_h)
    for copy in stores[:10]:
        copy.wait()
    columns = lambda t: slice(TILES[t][0], sum(TILES[t]))
    across = [(buf.at[:, : TILES[t][1]], gg, columns(t), gg_h) for t, buf in enumerate((wq, wk, wv))]
    across += [(buf.at[:, : TILES[t][1]], ug, columns(t), gu_h) for t, buf in enumerate((q, k, v))]
    down = [(buf.at[: TILES[t][1]], columns(t)) for t, buf in enumerate((ot, wo, recv2))]

    def gather(at, fresh):
        for buf, cols in down:
            new = nn(ht[cols, at], c[at, :])
            buf[...] = (new if fresh else buf[...].astype(F32) + new).astype(BF)

        def body(n, carry):
            tile = pl.ds(pl.multiple_of(n * BLK, BLK), BLK)
            turned = x2t[tile, at]
            for buf, right, cols, _ in across:
                new = nn(turned, right[at, cols])
                buf[tile, :] = (new if fresh else buf[tile, :].astype(F32) + new).astype(BF)
            return carry

        lax.fori_loop(0, 4, body, 0)

    gather(pl.ds(pl.multiple_of(tp * 512, 512), 512), True)
    for b in range(2):
        peer(6 + b, x.at[half(0)], x.at[half(0)]).wait_recv()
        if b == 1:
            cots[1].start()
        send4[half(b), :] = gated_up(theirs(b)).astype(BF)
        peer(2 + b, c.at[half(0)], c.at[half(0)]).wait_recv()
        if b == 1:
            peer(8, send6.at[half(0)], recv6.at[half(0)]).start()
        send6[half(b), :] = gated_down(theirs(b)).astype(BF)
        if b == 1:
            keep(send6, send6_h)
            keep(send4, send4_h)
        gather(theirs(b), False)
    last = [(buf, gd_h.at[cols]) for buf, cols in down] + [(buf, out.at[:, cols]) for buf, _, cols, out in across]
    for buf, out in last:
        keep(buf, out)
    peer(8, send6.at[half(0)], recv6.at[half(0)]).wait_recv()
    keep(recv6, recv6_h)
    for b in range(2):
        for n in (2, 4, 6):
            peer(n + b, recv6.at[half(0)], recv6.at[half(0)]).wait_send()
    peer(8, send6.at[half(0)], recv6.at[half(0)]).wait_send()
    for copy in stores[10:]:
        copy.wait()


def front(tokens, vf, wq, wk, wv, wo, wg, wu, wd, gain_attn, gain_mlp, cot, cos, sin):
    V = lambda shape, kind=BF: pltpu.VMEM(shape, kind)
    D = lambda *shape: pltpu.SemaphoreType.DMA(shape)
    hbm = pl.BlockSpec(memory_space=pl.ANY)
    S = jax.ShapeDtypeStruct
    own, heads, turned, square = (512, 1024), (1024, 512), (512, 1024), (1024, 1024)
    hidden, across, half = (1024, 1408), (1408, 1024), (256, 1024)
    return pl.pallas_call(
        front_kernel,
        in_specs=[hbm] * 14,
        out_specs=[hbm] * 16,
        out_shape=[*[S(heads, BF)] * 4, S(turned, BF), S(square, BF), S((2, 8, 1024), F32), S(own, F32), S(own, F32), S(own, BF),
                   S(own, F32), S(own, BF), S(half, BF), S(hidden, BF), S(hidden, BF), S(across, BF)],
        scratch_shapes=[
            V(own, F32), V(own, F32), V(square), V(square), *[V(heads)] * 7, V(turned), V(heads), V(turned), V(own), V(own), V(own),
            V(square), V(square), V(hidden), V(hidden), V(across), V(across), V((256, 1408)), V(hidden), V(hidden), V(own, F32),
            V(own), V(own), V(half),
            *[V((1, 1024), F32)] * 2, *[V((1024, 128), F32)] * 2, V((2, 8, 1024), F32),
            D(17), D(2, 9), D(23), D(2, 4),
        ],
        compiler_params=pltpu.CompilerParams(collective_id=4, has_side_effects=True, vmem_limit_bytes=63 << 20),
        cost_estimate=pl.CostEstimate(flops=40 * 10**9, bytes_accessed=60 << 20, transcendentals=5 << 20),
    )(tokens, vf, wq, wk, wv, wo, wg, wu, wd, gain_attn, gain_mlp, cot, cos, sin)


def ring_place(dp):
    core, x, z = lax.rem(dp, 2), lax.rem(lax.div(dp, 2), 2), lax.div(dp, 4)
    place = z + x * (7 - 2 * z)

    def device(where):
        side = lax.div(where, 4)
        return ((where + side * (7 - 2 * where)) * 2 + side) * 2 + core

    turn_no = lax.rem(place + core * (8 - 2 * place), 8)
    after = device(lax.rem(place + 1 + 6 * core, 8))
    before = device(lax.rem(place + 7 - 6 * core, 8))
    cube = (dp + 1 - 2 * core, dp + 2 - 4 * x, dp + 4 - 8 * lax.rem(z, 2), dp + 8 - 16 * lax.div(z, 2))
    return core, turn_no, after, before, cube


def remote(src, dst, send, recv, dp):
    return pltpu.make_async_remote_copy(
        src, dst, send, recv, device_id={"dp": dp}, device_id_type=pl.DeviceIdType.MESH
    )


class Ring:
    def __init__(self, place, takes, outs, own, sib, slots, sems):
        self.core, self.turn_no, self.after, self.before, self.cube = place
        self.takes, self.outs, self.own, self.sib, self.slots = takes, outs, own, sib, slots
        self.trade, self.rs, self.ag, self.over, self.keep = sems

    def piece(self, g, chunk):
        size = self.slots[g].shape[1]
        return pl.ds(pl.multiple_of(chunk * size, size), size)

    def traded(self, g, n):
        at = self.piece(g, lax.rem(15 + lax.rem(8 - self.turn_no, 8) - n, 8))
        return remote(
            self.takes[g](1 - self.core).at[at], self.sib[g].at[at], self.trade.at[0, g, n], self.trade.at[1, g, n], self.cube[0]
        )

    def trade_all(self, first=0, last=8):
        for n in range(first, last):
            for g in range(len(self.takes)):
                self.traded(g, n).start()

    def total(self, g, chunk):
        at = self.piece(g, chunk)
        return self.own[g][at, :].astype(F32) + self.sib[g][at, :].astype(F32)

    def first(self, g, chunk):
        return remote(
            self.own[g].at[self.piece(g, chunk)], self.slots[g].at[0], self.rs.at[0, g, 0], self.rs.at[1, g, 0], self.after
        )

    def begin(self, g):
        self.traded(g, 0).wait_recv()
        chunk = lax.rem(self.turn_no + 7, 8)
        self.own[g][self.piece(g, chunk), :] = self.total(g, chunk).astype(BF)
        self.first(g, chunk).start()

    def add(self, g, t):
        chunk = lax.rem(self.turn_no + 14 - t, 8)
        self.traded(g, t + 1).wait_recv()
        remote(self.slots[g].at[t], self.slots[g].at[t], self.rs.at[0, g, t], self.rs.at[1, g, t], self.after).wait_recv()
        self.slots[g][t] = (self.slots[g][t].astype(F32) + self.total(g, chunk)).astype(BF)

    def add_on(self, g, t):
        self.add(g, t)
        remote(self.slots[g].at[t], self.slots[g].at[t + 1], self.rs.at[0, g, t + 1], self.rs.at[1, g, t + 1], self.after).start()

    def spot(self, g, chunk):
        return self.outs[g](self.core, chunk)

    def turn_over(self, g):
        self.add(g, 6)
        spot = self.spot(g, self.turn_no)
        last = self.slots[g].at[6]
        remote(last, spot, self.ag.at[0, g, 0], self.ag.at[1, g, 0], self.after).start()
        remote(last, spot, self.over.at[0, g, 0], self.over.at[1, g, 0], self.cube[0]).start()
        pltpu.make_async_copy(last, spot, self.keep.at[g]).start()

    def pass_on(self, g, t):
        spot = self.spot(g, lax.rem(self.turn_no + 15 - t, 8))
        remote(spot, spot, self.ag.at[0, g, t], self.ag.at[1, g, t], self.after).wait_recv()

        @pl.when(t < 6)
        def _():
            remote(spot, spot, self.ag.at[0, g, t + 1], self.ag.at[1, g, t + 1], self.after).start()

        remote(spot, spot, self.over.at[0, g, t + 1], self.over.at[1, g, t + 1], self.cube[0]).start()

    def end(self, g):
        spot = self.spot(g, self.turn_no)
        pltpu.make_async_copy(self.slots[g].at[6], spot, self.keep.at[g]).wait()

        def finish(t, _):
            remote(self.slots[g].at[0], self.slots[g].at[0], self.rs.at[0, g, t], self.rs.at[1, g, t], self.after).wait_send()
            remote(spot, spot, self.ag.at[0, g, t], self.ag.at[1, g, t], self.after).wait_send()
            return _

        lax.fori_loop(0, 7, finish, 0)

        def crossed(t, _):
            self.traded(g, t).wait_send()
            there = self.outs[g](1 - self.core, lax.rem(self.turn_no + t, 8))
            remote(spot, there, self.over.at[0, g, t], self.over.at[1, g, t], self.cube[0]).wait()
            return _

        lax.fori_loop(0, 8, crossed, 0)


def strip(ref, axis, halves, length):
    if axis == 0:
        return lambda core, chunk: ref.at[pl.ds(pl.multiple_of(core * halves + chunk * length, length), length)]
    return lambda core, chunk: ref.at[
        pl.ds(pl.multiple_of(chunk * length, length), length), pl.ds(pl.multiple_of(core * halves, halves), halves)
    ]


def half_of(ref, axis, halves):
    if axis == 0:
        return lambda core: ref.at[pl.ds(pl.multiple_of(core * halves, halves), halves)]
    return lambda core: ref.at[:, pl.ds(pl.multiple_of(core * halves, halves), halves)]


def norm_back_rows(values, gain, grad_in):
    factor = lax.rsqrt(jnp.mean(values * values, axis=-1, keepdims=True) + EPS)
    normed = values * factor
    grad_normed = grad_in * gain
    grad = factor * (grad_normed - normed * jnp.mean(grad_normed * normed, axis=-1, keepdims=True))
    return grad, jnp.sum(grad_in * normed, axis=0, keepdims=True)


def back_kernel(
    own6_h, send6_h, recv6_h, own4_h, send4_h, middle_h, cot_h, tokens_h, gain_attn_h, gain_mlp_h,
    wo_h, wq_h, wk_h, wv_h, q_h, k_h, v_h, o_h, ot_h, xt_h, lse_h, cos_h, sin_h, gg_h, gu_h, gd_h,
    out_h, gt_h, gf_h, rq_h, rk_h, rv_h, ro_h, rg_h, ru_h, rd_h, gains_h,
    f1, f2, f3, recv6, recv4, recv8, send8, c, wo, wq, wk, wv, q, k, v, o, ot, xt,
    dq, dk, dv, do, kt, dka, dva, dl, own8, dwq, dwk, dwv, dwo,
    mg, mu, md, sg, su, sd, lg, lu, ld, bq, bk, bv, bo, aq, ak, av, ao,
    load, ysem, trade1, rs1, ag1, over1, keep1, trade2, rs2, ag2, over2, keep2, gain_in, gain_sem, store,
    gain_attn_ref, gain_mlp_ref, lse_ref, cos_ref, sin_ref, gains_ref,
):
    dp, tp = lax.axis_index("dp"), lax.axis_index("tp")
    place = ring_place(dp)
    core, turn_no, after, before, cube = place
    mesh_id = pl.DeviceIdType.MESH
    barrier = pltpu.get_barrier_semaphore()
    for other in (*cube, after, before):
        pl.semaphore_signal(barrier, inc=1, device_id={"dp": other}, device_id_type=mesh_id)
    pl.semaphore_signal(barrier, inc=1, device_id={"tp": 1 - tp}, device_id_type=mesh_id)

    loads = {}

    def fetch(name, src, dst):
        loads[name] = pltpu.make_async_copy(src, dst, load.at[len(loads)])
        loads[name].start()

    one = Ring(
        place, (half_of(gd_h, 1, 512), half_of(gg_h, 0, 512), half_of(gu_h, 0, 512)),
        (strip(rd_h, 1, 512, 176), strip(rg_h, 0, 512, 64), strip(ru_h, 0, 512, 64)),
        (md, mg, mu), (sd, sg, su), (ld, lg, lu), (trade1, rs1, ag1, over1, keep1),
    )
    two = Ring(
        place, (half_of(dwq, 0, 512), half_of(dwk, 0, 512), half_of(dwv, 0, 512), half_of(dwo, 0, 256)),
        (strip(rq_h, 0, 512, 64), strip(rk_h, 0, 512, 64), strip(rv_h, 0, 512, 64), strip(ro_h, 0, 256, 32)),
        (half_of(dwq, 0, 512)(core), half_of(dwk, 0, 512)(core), half_of(dwv, 0, 512)(core), half_of(dwo, 0, 256)(core)),
        (bq, bk, bv, bo), (aq, ak, av, ao), (trade2, rs2, ag2, over2, keep2),
    )
    for g, (whole, mine) in enumerate(((gd_h, md), (gg_h, mg), (gu_h, mu))):
        fetch(("m", g), one.takes[g](core), mine)
    for name, src, dst in (
        ("gain_attn", gain_attn_h, gain_attn_ref), ("gain_mlp", gain_mlp_h, gain_mlp_ref), ("own6", own6_h, f1), ("recv6", recv6_h, recv6.at[pl.ds(0, BLK)]), ("middle", middle_h, f2), ("cot", cot_h, f3), ("k", k_h, k), ("lse", lse_h, lse_ref), ("cos", cos_h, cos_ref), ("sin", sin_h, sin_ref), ("wo", wo_h, wo), ("o", o_h, o),
        ("q", q_h, q), ("v", v_h, v), ("wq", wq_h, wq), ("wk", wk_h, wk), ("wv", wv_h, wv), ("ot", ot_h, ot), ("xt", xt_h, xt),
    ):
        fetch(name, src, dst)
    pl.semaphore_wait(barrier, 7)

    def peer(n, src, dst):
        return pltpu.make_async_remote_copy(
            src, dst, ysem.at[0, n], ysem.at[1, n], device_id={"tp": 1 - tp}, device_id_type=mesh_id
        )

    half = lambda b: pl.ds(b * BLK, BLK)
    six = peer(0, send6_h.at[half(1)], recv6.at[half(1)])
    six.start()
    one.trade_all(0, 2)
    for g in range(3):
        loads["m", g].wait()
        one.begin(g)
    one.trade_all(2, 8)

    lane = lax.broadcasted_iota(jnp.int32, (BLK, 128), 1)
    causal = lax.broadcasted_iota(jnp.int32, (BLK, BLK), 0) <= lax.broadcasted_iota(jnp.int32, (BLK, BLK), 1)
    for name in ("gain_attn", "gain_mlp", "lse", "cos", "sin"):
        loads[name].wait()
    gain_mlp, gain_attn = gain_mlp_ref[...], gain_attn_ref[...]
    dka[...] = jnp.zeros_like(dka)
    dva[...] = jnp.zeros_like(dva)
    loads["k"].wait()
    for j in range(4):
        kt[:, rows(j)] = k[rows(j), :].T

    def one_piece(n):
        step, g = divmod(n, 3)
        if step < 6:
            one.add_on(g, step)
        elif step == 6:
            one.turn_over(g)
        else:
            one.pass_on(g, step - 7)

    def two_step(g, step):
        if step < 6:
            two.add_on(g, step)
        elif step == 6:
            two.turn_over(g)
        else:
            two.pass_on(g, step - 7)

    def branch_back(m):
        at = pl.ds(pl.multiple_of(m * BLK, BLK), BLK)
        low = nt(c[at, :], wo[...]).astype(BF)
        do[at, :] = low
        prod = (low.astype(F32) * o[at, :].astype(F32)).T
        for h in range(8):
            dl[h : h + 1, at] = jnp.sum(prod[h * 64 : h * 64 + 64, :], axis=0, keepdims=True)

    def attend_back(m, p):
        cols = pl.ds(pl.multiple_of(p * 128, 128), 128)
        i = POS_OF[m]
        qb, dob = q[rows(i), cols], do[rows(m), cols]
        parts = []
        for h in range(2):
            mine = (lane < 64) == (h == 0)
            qm = jnp.where(mine, qb, jnp.zeros_like(qb))
            dom = jnp.where(mine, dob, jnp.zeros_like(dob))
            lse = lse_ref[lax.div(p, 2), pl.ds(2 * lax.rem(p, 2) + h, 1), rows(i)]
            delta = dl[pl.ds(2 * p + h, 1), rows(m)]
            head = pl.ds(pl.multiple_of(p * 128 + h * 64, 64), 64)
            dqt = None
            for j in range(i + 1):
                weights = jnp.exp(nt(k[rows(j), cols], qm) - lse)
                if j == i:
                    weights = jnp.where(causal, weights, 0.0)
                ds = (weights * (nt(v[rows(j), cols], dom) - delta)).astype(BF)
                dva[rows(j), cols] = dva[rows(j), cols] + nn(weights.astype(BF), dom)
                dka[rows(j), cols] = dka[rows(j), cols] + nn(ds, qm)
                part = nn(kt[head, rows(j)], ds)
                dqt = part if dqt is None else dqt + part
            parts.append(dqt)
        grad = (jnp.concatenate(parts, axis=0).T * 0.125).astype(BF).astype(F32)
        dq[rows(m), cols] = turn(grad, cos_ref[rows(m), :], -sin_ref[rows(m), :], lane).astype(BF)

    def block_back(side_of, b, pieces):
        branch_back(side_of(tp) * 2 + b)

        def pair(p, carry):
            for side in range(2):

                @pl.when(tp == side)
                def _():
                    attend_back(side_of(side) * 2 + b, p)

            for late, n in enumerate(pieces):
                if n is not None:

                    @pl.when(p == late)
                    def _():
                        one_piece(n)

            return carry

        lax.fori_loop(0, 4, pair, 0)

    for name in ("own6", "recv6", "middle", "cot", "wo", "o", "q", "v"):
        loads[name].wait()
    gain_sum = jnp.zeros((1, 1024), F32)
    seven = []
    for b in range(2):
        if b == 1:
            six.wait_recv()
            seven[0].start()

        def rows_back(n, total):
            at = pl.ds(pl.multiple_of(b * BLK + n * 64, 64), 64)
            grad_in = f1[at, :] + recv6[at, :].astype(F32)
            grad, part = norm_back_rows(f2[at, :], gain_mlp, grad_in)
            grad = f3[at, :] + grad
            f1[at, :] = grad
            c[pl.ds(pl.multiple_of(tp * 512 + b * BLK + n * 64, 64), 64), :] = grad.astype(BF)
            return total + part

        gain_sum = lax.fori_loop(0, 4, rows_back, gain_sum)
        mine = c.at[pl.ds(pl.multiple_of(tp * 512 + b * BLK, BLK), BLK)]
        seven.append(peer(2 + b, mine, mine))
        if b == 1:
            seven[1].start()
        block_back(lambda side: side, b, ((None, None, None, 0), (2, 3, 4, 5))[b])
        one_piece((1, 6)[b])
    late = pltpu.make_async_copy(own4_h, f3, load.at[len(loads)])
    late.start()
    fetch_tokens = pltpu.make_async_copy(tokens_h, f2, load.at[len(loads) + 1])
    fetch_tokens.start()
    gains_ref[...] = jnp.zeros_like(gains_ref)
    gains_ref[0:1, :] = gain_sum
    four = peer(4, send4_h, recv4)
    for b in range(2):
        seven[b].wait_recv()
        if b == 1:
            four.start()
        block_back(lambda side: 1 - side, b, range(7 + 5 * b, 11 + 5 * b))
        one_piece(11 + 5 * b)
    for m in range(4):
        at = rows(POS_OF[m])
        cosine, sine = cos_ref[rows(m), :], -sin_ref[rows(m), :]
        for t in range(4):
            cols = slice(t * 128, t * 128 + 128)
            grad = dka[at, cols].astype(BF).astype(F32)
            dk[rows(m), cols] = turn(grad, cosine, sine, lane).astype(BF)
        dv[rows(m), :] = (0.5 * dva[at, :].astype(BF).astype(F32)).astype(BF)
    keep_gf = pltpu.make_async_copy(dv, gf_h, store.at[0])
    keep_gf.start()
    one_piece(17)
    for name in ("wq", "wk", "wv", "xt", "ot"):
        loads[name].wait()

    def into_rows(at):
        return nt(dq[at, :], wq[...]) + nt(dk[at, :], wk[...]) + nt(dv[at, :], wv[...])

    for which in range(2):
        side = (1 - core) * (1 - which) + core * which
        at = pl.ds(pl.multiple_of(side * 512, 512), 512)
        for n, (dst, src) in enumerate(((dwq, dq), (dwk, dk), (dwv, dv))):
            dst[at, :] = nn(xt[at, :], src[...]).astype(BF)
            if n < 2:
                one_piece(18 + 2 * which + n)
        at = pl.ds(pl.multiple_of(side * 256, 256), 256)
        dwo[at, :] = nn(ot[at, :], c[...]).astype(BF)
        if which == 0:
            two.trade_all()
    for g in range(4):
        two.begin(g)
    eight = []
    for b in range(2):
        at = pl.ds(pl.multiple_of((1 - tp) * 512 + b * BLK, BLK), BLK)
        send8[half(b), :] = into_rows(at).astype(BF)
        eight.append(peer(5 + b, send8.at[half(b)], recv8.at[half(b)]))
        eight[b].start()
        one_piece(22 + b)

    def gain_swap(n):
        where = {"tp": 1 - tp} if n == 4 else {"dp": cube[n]}
        return pltpu.make_async_remote_copy(
            gains_ref, gain_in.at[n], gain_sem.at[0, n], gain_sem.at[1, n], device_id=where, device_id_type=mesh_id
        )

    def rows_last(b, total):
        eight[b].wait_recv()

        def body(n, total):
            at = pl.ds(pl.multiple_of(b * BLK + n * 64, 64), 64)
            grad, part = norm_back_rows(f2[at, :], gain_attn, own8[at, :] + recv8[at, :].astype(F32))
            f1[at, :] = f1[at, :] + grad
            return total + part

        return lax.fori_loop(0, 4, body, total)

    keep_out = pltpu.make_async_copy(f3, out_h, store.at[1])
    keep_gt = pltpu.make_async_copy(f1, gt_h, store.at[2])
    gain_sum = jnp.zeros((1, 1024), F32)
    for step in range(14):
        for g in range(4):
            two_step(g, step)
        for n in range(24 + PACE[step], 24 + PACE[step + 1]):
            one_piece(n)
        if step < 2:
            at = pl.ds(pl.multiple_of(tp * 512 + step * BLK, BLK), BLK)
            own8[half(step), :] = into_rows(at)
        if step == 2:
            late.wait()
            fetch_tokens.wait()
        if step in (5, 6):
            gain_sum = rows_last(step - 5, gain_sum)
        if step == 6:
            gains_ref[1:2, :] = gain_sum
            keep_gt.start()
        if step == 7:
            four.wait_recv()

            def out_rows(n, carry):
                at = pl.ds(pl.multiple_of(n * 64, 64), 64)
                f3[at, :] = f3[at, :] + recv4[at, :].astype(F32)
                return carry

            lax.fori_loop(0, 8, out_rows, 0)
            keep_out.start()
        if step > 8:
            gain_swap(step - 9).wait()
            gains_ref[...] = gains_ref[...] + gain_in[step - 9]
        if 8 <= step < 13:
            gain_swap(step - 8).start()
    keep_gains = pltpu.make_async_copy(gains_ref, gains_h, store.at[3])
    keep_gains.start()
    for g in range(3):
        one.end(g)
    for g in range(4):
        two.end(g)
    for copy in (six, *seven, *eight, four):
        copy.wait_send()
    for copy in (keep_gf, keep_out, keep_gt, keep_gains):
        copy.wait()


PACE = (0, 1, 2, 4, 5, 6, 8, 9, 10, 12, 13, 14, 16, 17, 18)


def back(own6, send6, recv6, own4, send4, middle, cot, tokens, gain_attn, gain_mlp, wo, wq, wk, wv, q, k, v, o, ot, xt, lse, cos, sin, gg, gu, gd):
    V = lambda shape, kind=BF: pltpu.VMEM(shape, kind)
    D = lambda *shape: pltpu.SemaphoreType.DMA(shape)
    hbm = pl.BlockSpec(memory_space=pl.ANY)
    S = jax.ShapeDtypeStruct
    wide = (1024, 1024)
    return pl.pallas_call(
        back_kernel,
        in_specs=[hbm] * 26,
        out_specs=[hbm] * 11,
        out_shape=[S((512, 1024), F32), S((512, 1024), F32), S((1024, 512), BF), *[S((1024, 512), BF)] * 3, S((512, 1024), BF),
                   S((1024, 1408), BF), S((1024, 1408), BF), S((1408, 1024), BF), S((8, 1024), F32)],
        scratch_shapes=[
            *[V((512, 1024), F32)] * 3, *[V((512, 1024))] * 4, V(wide), V((512, 1024)), *[V((1024, 512))] * 7, V((512, 1024)), V(wide),
            *[V((1024, 512))] * 4, V((512, 1024)), *[V((1024, 512), F32)] * 2, V((8, 1024), F32), V((512, 1024), F32),
            *[V((1024, 512))] * 3, V((512, 1024)),
            *[V((512, 1408)), V((512, 1408)), V((1408, 512))] * 2, V((7, 64, 1408)), V((7, 64, 1408)), V((7, 176, 512)),
            *[V((512, 512))] * 3, V((256, 1024)), *[V((7, 64, 512))] * 3, V((7, 32, 1024)),
            D(24), D(2, 7), D(2, 3, 8), D(2, 3, 7), D(2, 3, 7), D(2, 3, 8), D(3), D(2, 4, 8), D(2, 4, 7), D(2, 4, 7), D(2, 4, 8), D(4),
            V((5, 8, 1024), F32), D(2, 5), D(4),
            *[V((1, 1024), F32)] * 2, V((2, 8, 1024), F32), *[V((1024, 128), F32)] * 2, V((8, 1024), F32),
        ],
        compiler_params=pltpu.CompilerParams(collective_id=3, has_side_effects=True, vmem_limit_bytes=62 << 20),
        cost_estimate=pl.CostEstimate(flops=30 * 10**9, bytes_accessed=60 << 20, transcendentals=5 << 20),
    )(own6, send6, recv6, own4, send4, middle, cot, tokens, gain_attn, gain_mlp, wo, wq, wk, wv, q, k, v, o, ot, xt, lse, cos, sin, gg, gu, gd)


PIECES = 4


def finish_kernel(*refs):
    gains_ref, ins, outs, wide = refs[0], refs[1:11], refs[11:21], refs[23:39]
    sums, through, load, store = refs[39:]
    fetch = pltpu.make_async_copy(gains_ref, sums, load.at[8, 2])
    fetch.start()
    gains = [pltpu.make_async_copy(sums.at[pl.ds(n, 1)], refs[21 + n], store.at[n, 1]) for n in range(2)]
    into = [pltpu.make_async_copy(ins[n], through.at[n], load.at[8, n]) for n in range(2)]
    whole = [pltpu.make_async_copy(through.at[n], outs[n], store.at[n, 0]) for n in range(2)]
    for copy in into:
        copy.start()
    low, high = wide[:8], wide[8:]
    order = (5, 6, 7, 1, 2, 3, 4, 0)

    def part(ref, piece):
        size = ref.shape[0] // PIECES
        return ref.at[pl.ds(piece * size, size)]

    for a in order:
        for piece in range(PIECES):
            pltpu.make_async_copy(part(ins[a + 2], piece), part(low[a], piece), load.at[a, piece]).start()
    fetch.wait()
    for n in range(2):
        gains[n].start()
        into[n].wait()
        whole[n].start()
    for a in order:
        for piece in range(PIECES):
            pltpu.make_async_copy(part(ins[a + 2], piece), part(low[a], piece), load.at[a, piece]).wait()
            size = low[a].shape[0] // PIECES

            def widen(n, carry):
                at = pl.ds(pl.multiple_of(piece * size + n * 16, 16), 16)
                high[a][at, :] = low[a][at, :].astype(F32)
                return carry

            lax.fori_loop(0, size // 16, widen, 0, unroll=4)
            pltpu.make_async_copy(part(high[a], piece), part(outs[a + 2], piece), store.at[a + 2, piece]).start()
    for a in order:
        for piece in range(PIECES):
            pltpu.make_async_copy(part(high[a], piece), part(outs[a + 2], piece), store.at[a + 2, piece]).wait()
    for copy in (*whole, *gains):
        copy.wait()


def finish(gains, *arrays):
    hbm = pl.BlockSpec(memory_space=pl.ANY)
    return pl.pallas_call(
        finish_kernel,
        in_specs=[hbm] * 11,
        out_specs=[hbm] * 12,
        out_shape=[jax.ShapeDtypeStruct(a.shape, F32) for a in arrays] + [jax.ShapeDtypeStruct((1, 1024), F32)] * 2,
        scratch_shapes=[
            *[pltpu.VMEM(a.shape, BF) for a in arrays[2:]], *[pltpu.VMEM(a.shape, F32) for a in arrays[2:]],
            pltpu.VMEM(gains.shape, F32), pltpu.VMEM((2, *arrays[0].shape), F32), pltpu.SemaphoreType.DMA((9, PIECES)), pltpu.SemaphoreType.DMA((10, PIECES)),
        ],
        compiler_params=pltpu.CompilerParams(vmem_limit_bytes=60 << 20),
        cost_estimate=pl.CostEstimate(flops=10**7, bytes_accessed=48 << 20, transcendentals=0),
    )(gains, *arrays)

def local_pair(
    tokens,
    v_first,
    w_query,
    w_key,
    w_value,
    w_out,
    w_gate,
    w_up,
    w_down,
    gain_attn,
    gain_mlp,
    seq_lens,
    cotangent,
):
    cosine, sine = tables()
    (query, keys, mixed_values, attended, attended_t, normed_t, row_lse, middle, base, send_out, own_in, send_in, got_in,
     grad_gate, grad_up, grad_down) = front(
        tokens, v_first, w_query, w_key, w_value, w_out, w_gate, w_up, w_down, gain_attn[None], gain_mlp[None], cotangent, cosine, sine
    )
    layer_out, grad_tokens, grad_first, *low_grads, gains = back(
        own_in, send_in, got_in, base, send_out, middle, cotangent, tokens, gain_attn[None], gain_mlp[None], w_out, w_query, w_key, w_value,
        query, keys, mixed_values, attended, attended_t, normed_t, row_lse, cosine, sine, grad_gate, grad_up, grad_down,
    )
    layer_out, grad_tokens, grad_first, *wide, gain_mlp_grad, gain_attn_grad = finish(gains, layer_out, grad_tokens, grad_first, *low_grads)
    grad_gain_mlp, grad_gain_attn = gain_mlp_grad[0], gain_attn_grad[0]
    return (layer_out, grad_tokens, grad_first, *wide, grad_gain_attn, grad_gain_mlp)


def local(
    tokens,
    v_first,
    w_query,
    w_key,
    w_value,
    w_out,
    w_gate,
    w_up,
    w_down,
    gain_attn,
    gain_mlp,
    seq_lens,
    cotangent,
):
    tp_count = lax.axis_size("tp")
    row_share = tokens.shape[0]
    doc_ids, positions = layout(seq_lens[0], row_share, tp_count)
    normed_attn = lax.all_gather(
        normalize(tokens, gain_attn).astype(jnp.bfloat16), "tp", axis=0, tiled=True
    )
    query = rotate(
        jnp.dot(normed_attn, w_query, preferred_element_type=jnp.float32), positions, HDIM, 1.0
    ).astype(jnp.bfloat16)
    keys = rotate(
        jnp.dot(normed_attn, w_key, preferred_element_type=jnp.float32), positions, HDIM, 1.0
    ).astype(jnp.bfloat16)
    value_pre = jnp.dot(normed_attn, w_value, preferred_element_type=jnp.float32)
    mixed_values = (0.5 * value_pre + 0.5 * v_first.astype(jnp.float32)).astype(jnp.bfloat16)
    attended, row_lse = attention_forward(query, keys, mixed_values, doc_ids, positions, HDIM)
    middle = tokens + lax.psum_scatter(
        jnp.dot(attended, w_out, preferred_element_type=jnp.float32),
        "tp",
        scatter_dimension=0,
        tiled=True,
    )
    normed_mlp = normalize(middle, gain_mlp).astype(jnp.bfloat16)
    grad_branch = cotangent.astype(jnp.bfloat16)
    mlp_rows = lax.all_gather(normed_mlp, "tp", axis=0, tiled=True)
    gate = jnp.dot(mlp_rows, w_gate, preferred_element_type=jnp.float32)
    up_values = jnp.dot(mlp_rows, w_up, preferred_element_type=jnp.float32)
    hidden = (jax.nn.silu(gate) * up_values).astype(jnp.bfloat16)
    layer_out = middle + lax.psum_scatter(
        jnp.dot(hidden, w_down, preferred_element_type=jnp.float32).astype(jnp.bfloat16),
        "tp",
        scatter_dimension=0,
        tiled=True,
    ).astype(jnp.float32)
    cot_rows = lax.all_gather(grad_branch, "tp", axis=0, tiled=True)
    grad_down = inner_rows(hidden, cot_rows)
    gate_grad, up_grad = swiglu_back(gate, up_values, outer_cols(cot_rows, w_down))
    grad_gate = inner_rows(mlp_rows, gate_grad)
    grad_up = inner_rows(mlp_rows, up_grad)
    grad_mlp_in = lax.psum_scatter(
        (outer_cols(gate_grad, w_gate) + outer_cols(up_grad, w_up)).astype(jnp.bfloat16),
        "tp",
        scatter_dimension=0,
        tiled=True,
    ).astype(jnp.float32)
    middle_back, grad_gain_mlp = normalize_back(middle, gain_mlp, grad_mlp_in)
    grad_middle = cotangent + middle_back
    attn_cot_rows = lax.all_gather(grad_middle.astype(jnp.bfloat16), "tp", axis=0, tiled=True)
    grad_output = inner_rows(attended, attn_cot_rows)
    grad_attended = outer_cols(attn_cot_rows, w_out).astype(jnp.bfloat16)
    query_grad, key_grad, mixed_grad = attention_backward(
        query, keys, mixed_values, grad_attended, row_lse, doc_ids, positions, HDIM
    )
    half_mixed = 0.5 * mixed_grad.astype(jnp.float32)
    value_grad = half_mixed.astype(jnp.bfloat16)
    query_pre_grad = rotate(query_grad.astype(jnp.float32), positions, HDIM, -1.0).astype(
        jnp.bfloat16
    )
    key_pre_grad = rotate(key_grad.astype(jnp.float32), positions, HDIM, -1.0).astype(jnp.bfloat16)
    grad_query = inner_rows(normed_attn, query_pre_grad)
    grad_key = inner_rows(normed_attn, key_pre_grad)
    grad_value = inner_rows(normed_attn, value_grad)
    grad_attn_in = lax.psum_scatter(
        (
            outer_cols(query_pre_grad, w_query)
            + outer_cols(key_pre_grad, w_key)
            + outer_cols(value_grad, w_value)
        ).astype(jnp.bfloat16),
        "tp",
        scatter_dimension=0,
        tiled=True,
    ).astype(jnp.float32)
    tokens_back, grad_gain_attn = normalize_back(tokens, gain_attn, grad_attn_in)
    grad_tokens = grad_middle + tokens_back
    grad_query, grad_key, grad_value, grad_output, grad_gate, grad_up, grad_down = (
        lax.psum(grad_query.astype(jnp.bfloat16), "dp").astype(jnp.float32),
        lax.psum(grad_key.astype(jnp.bfloat16), "dp").astype(jnp.float32),
        lax.psum(grad_value.astype(jnp.bfloat16), "dp").astype(jnp.float32),
        lax.psum(grad_output.astype(jnp.bfloat16), "dp").astype(jnp.float32),
        lax.psum(grad_gate.astype(jnp.bfloat16), "dp").astype(jnp.float32),
        lax.psum(grad_up.astype(jnp.bfloat16), "dp").astype(jnp.float32),
        lax.psum(grad_down.astype(jnp.bfloat16), "dp").astype(jnp.float32),
    )
    grad_gain_attn, grad_gain_mlp = lax.psum((grad_gain_attn, grad_gain_mlp), ("dp", "tp"))
    return (
        layer_out,
        grad_tokens,
        half_mixed,
        grad_query,
        grad_key,
        grad_value,
        grad_output,
        grad_gate,
        grad_up,
        grad_down,
        grad_gain_attn,
        grad_gain_mlp,
    )


def solution(mesh):
    in_specs = (
        P(("dp", "tp"), None),
        P("dp", "tp"),
        P(None, "tp"),
        P(None, "tp"),
        P(None, "tp"),
        P("tp", None),
        P(None, "tp"),
        P(None, "tp"),
        P("tp", None),
        P(),
        P(),
        P("dp", None),
        P(("dp", "tp"), None),
    )
    out_specs = (
        P(("dp", "tp"), None),
        P(("dp", "tp"), None),
        P("dp", "tp"),
        P(None, "tp"),
        P(None, "tp"),
        P(None, "tp"),
        P("tp", None),
        P(None, "tp"),
        P(None, "tp"),
        P("tp", None),
        P(),
        P(),
    )

    def step(*args):
        tokens, seq_lens = args[0], args[11]
        pair = mesh.shape["tp"] == 2 and mesh.shape["dp"] == 16 and seq_lens.shape[1] == 1 and tokens.shape == (512, 1024)
        return (local_pair if pair else local)(*args)

    return jax.shard_map(step, mesh=mesh, in_specs=in_specs, out_specs=out_specs, check_vma=False)
```
